32 devices in a mesh: span: 16 (over z, x, core), rad: 2 (over y).
Axes of the slice: x: 2, y: 2, z: 4, core: 2. Of those that a mesh axis runs over, the one named last changes fastest.
Arguments:
- fields: float32 [2, 8, 384, 8192], P(None, None, 'rad', 'span'), may hold values from -6 to 6
- mode_group: int32 [168, 16], P(None, 'span'), may hold values from 0 to 1, as said below
- half_step: float32 [2], replicated, may hold values from 0.05 to 0.5
- decay: float32 [2, 384], replicated, may hold values from 0.1 to 10
- eigen_inverse: float32 [2, 384, 384], replicated, may hold values from -0.3125 to 0.3125
- eigen_vectors: float32 [2, 384, 384], replicated, may hold values from -0.3125 to 0.3125
Outputs:
- solved_modes: float32 [16, 2, 168, 2, 2, 8, 384], P('span', 'rad')
The draws below stay inside these ranges and needn't reach their ends.
Inputs may be any that keep to these rules, and one draw needn't show every extreme that they name: `mode_group`: in every column no group holds more than 168 modes, and one group of every column holds exactly 168.
All inputs are finite; a program needn't handle non-finite values.
Results may differ from the reference program's by a relative error of at most 0.000084.
Values sent between devices are 32-bit elements; how exact they have to be, the bound alone decides.
No kernel may reach another device: no remote copies, remote signals or barrier semaphores. Data moves between devices by JAX's collectives and lax.ppermute only.
A program may use at most 128 MiB of HBM per device.

```python
import math
import jax
import jax.numpy as jnp
import numpy as np
from jax import lax

AZ = 8
R = 384
NZ = 8192
KEEP = 2688
SECTIONS = 4
BKEEP = 168
CAP = 168
N_SPAN = 16
N_RAD = 2


def draw_mode_group(key, part):
    key = jax.random.fold_in(key, 7)
    column_keys = jax.random.split(key, N_SPAN)

    def one_column(column_key):
        heavy_key, order_key = jax.random.split(column_key)
        heavy_group = jax.random.randint(heavy_key, (), 0, N_RAD)
        ordering = jax.random.permutation(order_key, BKEEP)
        position = jnp.arange(BKEEP)
        others = heavy_group + 1 + jnp.maximum(position - CAP, 0) % max(N_RAD - 1, 1)
        assigned = jnp.where(position < CAP, heavy_group, others % N_RAD).astype(jnp.int32)
        return jnp.zeros((BKEEP,), jnp.int32).at[ordering].set(assigned)
    return jax.vmap(one_column)(column_keys).T.astype(jnp.int32)


def block_levels(rng, dims, cuts, smallest, high):
    def one(dim, parts):
        heights = jax.random.uniform(jax.random.fold_in(jax.random.fold_in(rng, 6), dim), (parts,), jnp.float32, smallest / len(cuts), high / len(cuts))
        return jnp.repeat(jnp.exp(heights), dims[dim] // parts).reshape((-1,) + (1,) * (len(dims) - dim - 1))

    level = one(*cuts[0])
    for cut in cuts[1:]:
        level = level * one(*cut)
    return level


def noise(key, shape, spread, most, shards=(), held_as=jnp.bfloat16):
    result = spread * jax.random.normal(key, shape, jnp.float32)
    if shards:
        result = result * block_levels(key, shape, shards, -0.22, 0.18)
    return jnp.clip(result, -most, most).astype(held_as)


def setup_inputs(seed: int = 0) -> dict:
    key_list = jax.random.split(jax.random.key(seed), 7)
    return {
        "fields": noise(key_list[0], (2, AZ, R, NZ), 1.0, 6.0, ((2, 2), (3, 16)), jnp.float32),
        "mode_group": draw_mode_group(jax.random.fold_in(key_list[6], 71), 0),
        "half_step": jnp.clip(jnp.exp(jax.random.uniform(key_list[2], (2,), jnp.float32, math.log(0.05), math.log(0.5))), 0.05, 0.5),
        "decay": jnp.clip(jnp.exp(jax.random.uniform(key_list[3], (2, R), jnp.float32, math.log(0.1), math.log(10.0))), 0.1, 10.0),
        "eigen_inverse": noise(key_list[4], (2, R, R), R ** -0.5, 0.3125, (), jnp.float32),
        "eigen_vectors": noise(key_list[5], (2, R, R), R ** -0.5, 0.3125, (), jnp.float32),
    }


precise = lax.Precision.HIGHEST

def reversed_order():
    position = np.arange(N_SPAN)
    flipped = np.zeros(N_SPAN, dtype=np.int32)
    for section_bit in range(SECTIONS):
        flipped = flipped + (position >> section_bit & 1) * 2 ** (SECTIONS - 1 - section_bit)
    return flipped.astype(np.int32)

def reference(fields, mode_group, half_step, decay, eigen_inverse, eigen_vectors):
    spectrum = jnp.fft.fft(fields, axis=-1)[..., :KEEP] / math.sqrt(NZ)
    real_part = jnp.real(spectrum).astype(jnp.float32)
    imag_part = jnp.imag(spectrum).astype(jnp.float32)
    wave_square = (jnp.arange(KEEP, dtype=jnp.float32) * (math.pi / KEEP)) ** 2
    damping = half_step[:, None, None] * (decay[:, :, None] + wave_square[None, None, :])
    factor = (1.0 - damping) / (1.0 + damping)

    def solve_part(part):
        inner_part = jnp.einsum('fir,fark->faik', eigen_inverse, part, precision=precise)
        inner_part = inner_part * factor[:, None, :, :]
        return jnp.einsum('fri,faik->fark', eigen_vectors, inner_part, precision=precise)
    solved = jnp.stack([solve_part(real_part), solve_part(imag_part)])
    reversal = reversed_order()
    arranged = solved.reshape(2, 2, AZ, R, BKEEP, N_SPAN)[..., reversal]
    groups = jnp.arange(N_RAD, dtype=jnp.int32)
    member = (mode_group[None, :, :] == groups[:, None, None]).astype(jnp.int32)
    ranking = jnp.cumsum(member, axis=1, dtype=jnp.int32) - member
    slot_index = jnp.arange(CAP, dtype=jnp.int32)
    placing = (member[None] * (ranking[None] == slot_index[:, None, None, None])).astype(jnp.float32)
    return jnp.einsum('sgbi,cfarbi->igscfar', placing, arranged, precision=precise)
```

```python
import math

import jax
import jax.numpy as jnp
import ml_dtypes
import numpy as np
from jax import lax
from jax.experimental import pallas as pl
from jax.experimental.pallas import tpu as pltpu
from jax.sharding import PartitionSpec as P

KEEP = 2688


precise = lax.Precision.HIGHEST
contract_rows = (((1,), (1,)), ((), ()))


def partner_2(value, axis, distance):
    mask = 2**distance
    pairs = [(source, source ^ mask) for source in range(lax.axis_size(axis))]
    return lax.ppermute(value, axis, pairs)


def bit_reverse(value, bit_count):
    flipped = jnp.zeros_like(value)
    for section_bit in range(bit_count):
        flipped = flipped + (value >> section_bit & 1) * 2 ** (bit_count - 1 - section_bit)
    return flipped


def section_angles(device, section_bit):
    upper_half = device >> section_bit & 1 == 1
    twiddle_index = jnp.where(upper_half, device % 2**section_bit, 0)
    angles = twiddle_index.astype(jnp.float32) * (2.0 * math.pi / 2 ** (section_bit + 1))
    sign_factor = jnp.where(upper_half, -1.0, 1.0).astype(jnp.float32)
    return (sign_factor, jnp.cos(angles), jnp.sin(angles))


def butterfly(fields, bit_count):
    device = lax.axis_index("span")
    top_bit = bit_count - 1
    partner = partner_2(fields, "span", top_bit)
    sign_factor, cosine, sine_value = section_angles(device, top_bit)
    difference = partner + sign_factor * fields
    real_part = difference * cosine
    imag_part = -difference * sine_value
    for section_bit in range(bit_count - 2, -1, -1):
        other_real, other_imag = partner_2((real_part, imag_part), "span", section_bit)
        sign_factor, cosine, sine_value = section_angles(device, section_bit)
        diff_real = other_real + sign_factor * real_part
        diff_imag = other_imag + sign_factor * imag_part
        real_part = diff_real * cosine + diff_imag * sine_value
        imag_part = diff_imag * cosine - diff_real * sine_value
    return (real_part, imag_part)


def mode_transform(real_part, imag_part, bit_count):
    groups = lax.axis_size("span")
    line_width = real_part.shape[3]
    full_length = line_width * groups
    kept_modes = KEEP // groups
    residue = bit_reverse(lax.axis_index("span"), bit_count)
    mode_index = residue + groups * jnp.arange(kept_modes, dtype=jnp.int32)
    phases = mode_index[:, None] * jnp.arange(line_width, dtype=jnp.int32)[None, :] % full_length
    angles = phases.astype(jnp.float32) * (2.0 * math.pi / full_length)
    normalizer = 1.0 / math.sqrt(full_length)
    cosine_table = jnp.cos(angles) * normalizer
    sine_table = jnp.sin(angles) * normalizer
    line_real = real_part.reshape(-1, line_width)
    line_imag = imag_part.reshape(-1, line_width)
    cos_real = lax.dot_general(cosine_table, line_real, contract_rows, precision=precise)
    cos_imag = lax.dot_general(cosine_table, line_imag, contract_rows, precision=precise)
    sin_real = lax.dot_general(sine_table, line_real, contract_rows, precision=precise)
    sin_imag = lax.dot_general(sine_table, line_imag, contract_rows, precision=precise)
    return (jnp.stack([cos_real + sin_imag, cos_imag - sin_real]), mode_index)


def placement_table(column, group_count, capacity):
    groups = jnp.arange(group_count, dtype=jnp.int32)
    member = (column[None, :] == groups[:, None]).astype(jnp.int32)
    ranking = jnp.cumsum(member, axis=1, dtype=jnp.int32) - member
    slot_index = jnp.arange(capacity, dtype=jnp.int32)
    return member[None] * (ranking[None] == slot_index[:, None, None])


def damping_factor(half_step, decay, wave_index):
    wave_square = (wave_index.astype(jnp.float32) * (math.pi / KEEP)) ** 2
    damping = half_step[None, :, None] * (decay[None, :, :] + wave_square[:, None, None])
    return (1.0 - damping) / (1.0 + damping)


def on_device_any(fields, mode_group, half_step, decay, eigen_inverse, eigen_vectors):
    bit_count = lax.axis_size("span").bit_length() - 1
    real_part, imag_part = butterfly(fields, bit_count)
    spectra, mode_index = mode_transform(real_part, imag_part, bit_count)
    kept_modes = spectra.shape[1]
    group_count = lax.axis_size("rad")
    capacity = min(kept_modes, 2 * kept_modes // group_count)
    planes = fields.shape[1]
    radial_rows = fields.shape[2]
    arranged = spectra.reshape(2, kept_modes, 2, planes, radial_rows)
    placing = placement_table(mode_group[:, 0], group_count, capacity)
    placing_float = placing.astype(jnp.float32)
    packed = jnp.einsum("sgb,cbfal->scfagl", placing_float, arranged, precision=precise)
    packed = packed.reshape(capacity, 2, 2, planes, group_count * radial_rows)
    regrouped = lax.all_to_all(packed, "rad", split_axis=4, concat_axis=4, tiled=True)
    own_slots = lax.dynamic_index_in_dim(placing, lax.axis_index("rad"), 1, keepdims=False)
    slot_modes = jnp.sum(own_slots * mode_index[None, :], axis=1)
    factor = damping_factor(half_step, decay, slot_modes)
    inner_part = jnp.einsum("scfar,fir->scfai", regrouped, eigen_inverse, precision=precise)
    inner_part = inner_part * factor[:, None, :, None, :]
    result = jnp.einsum("scfai,fri->scfar", inner_part, eigen_vectors, precision=precise)
    return result.reshape(1, 1, capacity, 2, 2, planes, group_count * radial_rows)


HALF = 8
BLOCK = 64
VMEM_BYTES = 32 * 1024 * 1024


def flip3(value):
    return (value & 1) << 2 | value & 2 | value >> 2


def swap_span(value, distance):
    pairs = [(source, source ^ distance) for source in range(lax.axis_size("span"))]
    return lax.ppermute(value, "span", pairs)


def swap_rad(value):
    return lax.ppermute(value, "rad", [(0, 1), (1, 0)])


def split_pair(value):
    high = value.astype(jnp.bfloat16)
    low = (value - high.astype(jnp.float32)).astype(jnp.bfloat16)
    return high, low


def dot_rows(left, right):
    return lax.dot_general(left, right, contract_rows, preferred_element_type=jnp.float32)


def dot_split(left, right):
    left_high, left_low = left
    right_high, right_low = right
    total = dot_rows(left_high, right_high)
    total = total + dot_rows(left_low, right_high)
    return total + dot_rows(left_high, right_low)


def transform_8(real, imag):
    root = math.sqrt(0.5)
    er, ei, orr, oi = [], [], [], []
    for j in range(4):
        er.append(real[j] + real[j + 4])
        ei.append(imag[j] + imag[j + 4])
        dr = real[j] - real[j + 4]
        di = imag[j] - imag[j + 4]
        if j == 0:
            orr.append(dr)
            oi.append(di)
        elif j == 1:
            orr.append((dr + di) * root)
            oi.append((di - dr) * root)
        elif j == 2:
            orr.append(di)
            oi.append(-dr)
        else:
            orr.append((di - dr) * root)
            oi.append((-di - dr) * root)

    def transform_4(r, i):
        ar, ai = r[0] + r[2], i[0] + i[2]
        br, bi = r[0] - r[2], i[0] - i[2]
        cr, ci = r[1] + r[3], i[1] + i[3]
        dr, di = r[1] - r[3], i[1] - i[3]
        return [(ar + cr, ai + ci), (br + di, bi - dr), (ar - cr, ai - ci), (br - di, bi + dr)]

    even = transform_4(er, ei)
    odd = transform_4(orr, oi)
    return [even[q // 2] if q % 2 == 0 else odd[q // 2] for q in range(8)]


def half_sums_kernel(place, *refs):
    pieces = refs[:HALF]
    cos_turn, sin_turn, table_high, table_low, out, ordered, high, low = refs[HALF:]
    me, parity = place[0], place[1]
    sign = place[2].astype(jnp.float32)
    width = pieces[0].shape[-1]
    modes = out.shape[1]
    for distance in range(HALF):
        ordered[me ^ distance] = pieces[distance][...]

    turn_real, turn_imag = [], []
    for j in range(HALF):
        angle = 2.0 * math.pi * j / 16
        turn_real.append(sign * jnp.where(parity == 1, math.cos(angle), 1.0))
        turn_imag.append(sign * jnp.where(parity == 1, -math.sin(angle), 0.0))

    def one_block(step, carry):
        rows = pl.ds(pl.multiple_of(step * 16, 16), 16)
        lower = pl.ds(pl.multiple_of(BLOCK + step * 16, 16), 16)
        for lane in range(0, width, 128):
            real, imag = [], []
            for j in range(HALF):
                value = ordered[j, rows, lane : lane + 128]
                real.append(value * turn_real[j])
                imag.append(value * turn_imag[j])
            sums = transform_8(real, imag)
            for q in range(HALF):
                sum_real, sum_imag = sums[q]
                cosine = cos_turn[parity, q : q + 1, lane : lane + 128]
                sine = sin_turn[parity, q : q + 1, lane : lane + 128]
                real_high, real_low = split_pair(sum_real * cosine + sum_imag * sine)
                imag_high, imag_low = split_pair(sum_imag * cosine - sum_real * sine)
                high[q, rows, lane : lane + 128] = real_high
                high[q, rows, width + lane : width + lane + 128] = imag_high
                high[q, lower, lane : lane + 128] = imag_high
                high[q, lower, width + lane : width + lane + 128] = -real_high
                low[q, rows, lane : lane + 128] = real_low
                low[q, rows, width + lane : width + lane + 128] = imag_low
                low[q, lower, lane : lane + 128] = imag_low
                low[q, lower, width + lane : width + lane + 128] = -real_low
        return carry

    lax.fori_loop(0, BLOCK // 16, one_block, 0)
    table = (table_high[...], table_low[...])
    for q in range(0, HALF, 2):
        lines_high = high[q : q + 2].reshape(4 * BLOCK, 2 * width)
        lines_low = low[q : q + 2].reshape(4 * BLOCK, 2 * width)
        result = dot_split(table, (lines_high, lines_low))
        out[flip3(q)] = result[:modes, : 2 * BLOCK]
        out[flip3(q + 1)] = result[:modes, 2 * BLOCK :]


def half_sums(place, pieces, tables, modes):
    width = pieces[0].shape[-1]
    vmem = pl.BlockSpec(memory_space=pltpu.VMEM)
    rows = tables[2].shape[0]
    return pl.pallas_call(
        half_sums_kernel,
        out_shape=jax.ShapeDtypeStruct((HALF, modes, 2 * BLOCK), jnp.float32),
        in_specs=[pl.BlockSpec(memory_space=pltpu.SMEM)] + [vmem] * (HALF + 4),
        out_specs=vmem,
        scratch_shapes=[
            pltpu.VMEM((HALF, BLOCK, width), jnp.float32),
            pltpu.VMEM((HALF, 2 * BLOCK, 2 * width), jnp.bfloat16),
            pltpu.VMEM((HALF, 2 * BLOCK, 2 * width), jnp.bfloat16),
        ],
        cost_estimate=pl.CostEstimate(
            flops=6 * rows * HALF * 4 * BLOCK * width,
            bytes_accessed=HALF * BLOCK * (width + 2 * modes) * 4,
            transcendentals=0,
        ),
        compiler_params=pltpu.CompilerParams(vmem_limit_bytes=VMEM_BYTES),
        name="half_sums",
    )(place, *pieces, *tables)


def gather_planes_kernel(place, *refs):
    out, ordered = refs[HALF:]
    for distance in range(HALF):
        ordered[place[0] ^ distance] = refs[distance][...]
    for plane in range(HALF):
        out[:, plane, :] = ordered[plane]


def gather_planes(place, pieces):
    modes, lanes = pieces[0].shape
    vmem = pl.BlockSpec(memory_space=pltpu.VMEM)
    return pl.pallas_call(
        gather_planes_kernel,
        out_shape=jax.ShapeDtypeStruct((modes, HALF, lanes), jnp.float32),
        in_specs=[pl.BlockSpec(memory_space=pltpu.SMEM)] + [vmem] * HALF,
        out_specs=vmem,
        scratch_shapes=[pltpu.VMEM((HALF, modes, lanes), jnp.float32)],
        cost_estimate=pl.CostEstimate(
            flops=0, bytes_accessed=8 * HALF * modes * lanes, transcendentals=0
        ),
        compiler_params=pltpu.CompilerParams(vmem_limit_bytes=VMEM_BYTES),
        name="gather_planes",
    )(place, *pieces)


def solve_kernel(count, place, *refs):
    blocks = refs[: 2 * count]
    inverse, vectors, factor = refs[2 * count : 2 * count + 3]
    out = refs[-1]
    modes = out.shape[0]
    radial = out.shape[-1]

    @pl.when(place[3] == 1)
    def _():
        inverse_pair = split_pair(inverse[0])
        vectors_pair = split_pair(vectors[0])
        scale = jnp.broadcast_to(factor[0][:, None, :], (modes, HALF, radial))
        scale = scale.reshape(modes * HALF, radial)
        whole = [block[...].reshape(modes * HALF, 2 * BLOCK) for block in blocks]
        for part in range(2):
            lanes = slice(part * BLOCK, (part + 1) * BLOCK)
            lines = jnp.concatenate([value[:, lanes] for value in whole], axis=1)
            inner = dot_split(split_pair(lines), inverse_pair) * scale
            solved = dot_split(split_pair(inner), vectors_pair)
            out[:, part, 0] = solved.reshape(modes, HALF, radial)

    @pl.when(place[3] != 1)
    def _():
        out[...] = jnp.zeros_like(out)


def solve(place, field, blocks, inverse, vectors, factor, earlier):
    modes = blocks[0].shape[0]
    radial = inverse.shape[-1]
    step = modes // 3
    line = pl.BlockSpec((step, HALF, 2 * BLOCK), lambda i: (i, 0, 0))
    matrix = pl.BlockSpec((1, radial, radial), lambda i: (field, 0, 0))
    in_specs = [pl.BlockSpec(memory_space=pltpu.SMEM)] + [line] * len(blocks)
    in_specs += [matrix, matrix, pl.BlockSpec((1, step, radial), lambda i: (field, i, 0))]
    operands = [place, *blocks, inverse, vectors, factor]
    aliases = {}
    if earlier is not None:
        aliases = {len(operands): 0}
        operands.append(earlier)
        in_specs.append(pl.BlockSpec(memory_space=pl.ANY))

    def kernel(*refs):
        kept = refs if earlier is None else refs[: len(operands) - 1] + refs[-1:]
        solve_kernel(len(blocks) // 2, *kept)

    return pl.pallas_call(
        kernel,
        grid=(3,),
        out_shape=jax.ShapeDtypeStruct((modes, 2, 2, HALF, radial), jnp.float32),
        in_specs=in_specs,
        out_specs=pl.BlockSpec((step, 2, 1, HALF, radial), lambda i: (i, 0, field, 0, 0)),
        input_output_aliases=aliases,
        cost_estimate=pl.CostEstimate(
            flops=24 * modes * HALF * radial * radial,
            bytes_accessed=16 * modes * HALF * radial,
            transcendentals=0,
        ),
        compiler_params=pltpu.CompilerParams(vmem_limit_bytes=VMEM_BYTES),
        name="solve",
    )(*operands)


def mode_tables(width, modes):
    cells = np.arange(width)
    residue = 2 * np.arange(HALF)[None, :, None] + np.arange(2)[:, None, None]
    turn = 2.0 * np.pi * residue * cells / (2 * HALF * width)
    padded = -(-modes // 16) * 16
    angle = 2.0 * np.pi * (np.arange(padded)[:, None] * cells[None, :] % width) / width
    table = np.concatenate([np.cos(angle), np.sin(angle)], axis=1)
    table = table / math.sqrt(2 * HALF * width)
    table[modes:] = 0.0
    high = table.astype(np.float32).astype(ml_dtypes.bfloat16)
    low = (table - high.astype(np.float64)).astype(np.float32).astype(ml_dtypes.bfloat16)
    return (np.cos(turn).astype(np.float32), np.sin(turn).astype(np.float32), high, low)


def on_device_halves(fields, mode_group, half_step, decay, eigen_inverse, eigen_vectors):
    span = lax.axis_index("span")
    rad = lax.axis_index("rad")
    me = span & 7
    half = span >> 3
    rows = fields.shape[2]
    width = fields.shape[3]
    modes = KEEP // 16
    tables = mode_tables(width, modes)

    heavy = (mode_group[0, 0] == rad).astype(jnp.int32)
    one = jnp.ones_like(me)
    place_send = jnp.stack([me, 1 - half, one, heavy])
    place_keep = jnp.stack([me, half, 1 - 2 * half, heavy])

    mode_index = bit_reverse(span, 4) + 16 * jnp.arange(modes, dtype=jnp.int32)
    factor = damping_factor(half_step, decay, mode_index).transpose(1, 0, 2)
    own = lax.dynamic_slice_in_dim(eigen_inverse, rad * rows, rows, 2)
    other = lax.dynamic_slice_in_dim(eigen_inverse, (1 - rad) * rows, rows, 2)
    inverse = jnp.concatenate([own, other], axis=2)

    units = [(field, start) for field in range(2) for start in range(0, rows, BLOCK)]

    def raw_pieces(unit, after):
        field, start = unit
        source = fields
        if after is not None:
            source, after = lax.optimization_barrier((fields, after))
        result = []
        for distance in range(HALF):
            piece = lax.dynamic_slice(
                source, (field, me ^ distance, start, 0), (1, 1, BLOCK, width)
            ).reshape(BLOCK, width)
            result.append(piece if distance == 0 else swap_span(piece, distance))
        return result, after

    raw = {0: raw_pieces(units[0], None)[0], 1: raw_pieces(units[1], None)[0]}
    lines = []
    result = None
    per_field = rows // BLOCK
    for number, unit in enumerate(units):
        pieces = raw.pop(number)
        sent = half_sums(place_send, pieces, tables, modes)
        if number + 2 < len(units):
            raw[number + 2], sent = raw_pieces(units[number + 2], sent)
        came = swap_span(sent, HALF)
        kept = half_sums(place_keep, pieces, tables, modes)
        arrived = []
        for distance in range(HALF):
            index = me ^ distance
            total = lax.dynamic_index_in_dim(kept, index, 0, keepdims=False)
            total = total + lax.dynamic_index_in_dim(came, index, 0, keepdims=False)
            arrived.append(total if distance == 0 else swap_span(total, distance))
        mine = gather_planes(place_keep, arrived)
        lines.append((mine, swap_rad(mine)))
        if len(lines) == per_field:
            blocks = [pair[0] for pair in lines] + [pair[1] for pair in lines]
            result = solve(place_keep, unit[0], blocks, inverse, eigen_vectors, factor, result)
            lines = []
    return result[None, None]


def solution(mesh):
    placed = (P(None, None, "rad", "span"), P(None, "span"), P(), P(), P(), P())
    halves = mesh.shape["span"] == 2 * HALF and mesh.shape["rad"] == 2
    return jax.shard_map(
        on_device_halves if halves else on_device_any,
        mesh=mesh,
        in_specs=placed,
        out_specs=P("span", "rad", None, None, None, None, None),
        check_vma=False,
    )
```

```python
import math

import jax
import jax.numpy as jnp
import ml_dtypes
import numpy as np
from jax import lax
from jax.experimental import pallas as pl
from jax.experimental.pallas import tpu as pltpu
from jax.sharding import PartitionSpec as P

KEEP = 2688


precise = lax.Precision.HIGHEST
contract_rows = (((1,), (1,)), ((), ()))


def partner_2(value, axis, distance):
    mask = 2**distance
    pairs = [(source, source ^ mask) for source in range(lax.axis_size(axis))]
    return lax.ppermute(value, axis, pairs)


def bit_reverse(value, bit_count):
    flipped = jnp.zeros_like(value)
    for section_bit in range(bit_count):
        flipped = flipped + (value >> section_bit & 1) * 2 ** (bit_count - 1 - section_bit)
    return flipped


def section_angles(device, section_bit):
    upper_half = device >> section_bit & 1 == 1
    twiddle_index = jnp.where(upper_half, device % 2**section_bit, 0)
    angles = twiddle_index.astype(jnp.float32) * (2.0 * math.pi / 2 ** (section_bit + 1))
    sign_factor = jnp.where(upper_half, -1.0, 1.0).astype(jnp.float32)
    return (sign_factor, jnp.cos(angles), jnp.sin(angles))


def butterfly(fields, bit_count):
    device = lax.axis_index("span")
    top_bit = bit_count - 1
    partner = partner_2(fields, "span", top_bit)
    sign_factor, cosine, sine_value = section_angles(device, top_bit)
    difference = partner + sign_factor * fields
    real_part = difference * cosine
    imag_part = -difference * sine_value
    for section_bit in range(bit_count - 2, -1, -1):
        other_real, other_imag = partner_2((real_part, imag_part), "span", section_bit)
        sign_factor, cosine, sine_value = section_angles(device, section_bit)
        diff_real = other_real + sign_factor * real_part
        diff_imag = other_imag + sign_factor * imag_part
        real_part = diff_real * cosine + diff_imag * sine_value
        imag_part = diff_imag * cosine - diff_real * sine_value
    return (real_part, imag_part)


def mode_transform(real_part, imag_part, bit_count):
    groups = lax.axis_size("span")
    line_width = real_part.shape[3]
    full_length = line_width * groups
    kept_modes = KEEP // groups
    residue = bit_reverse(lax.axis_index("span"), bit_count)
    mode_index = residue + groups * jnp.arange(kept_modes, dtype=jnp.int32)
    phases = mode_index[:, None] * jnp.arange(line_width, dtype=jnp.int32)[None, :] % full_length
    angles = phases.astype(jnp.float32) * (2.0 * math.pi / full_length)
    normalizer = 1.0 / math.sqrt(full_length)
    cosine_table = jnp.cos(angles) * normalizer
    sine_table = jnp.sin(angles) * normalizer
    line_real = real_part.reshape(-1, line_width)
    line_imag = imag_part.reshape(-1, line_width)
    cos_real = lax.dot_general(cosine_table, line_real, contract_rows, precision=precise)
    cos_imag = lax.dot_general(cosine_table, line_imag, contract_rows, precision=precise)
    sin_real = lax.dot_general(sine_table, line_real, contract_rows, precision=precise)
    sin_imag = lax.dot_general(sine_table, line_imag, contract_rows, precision=precise)
    return (jnp.stack([cos_real + sin_imag, cos_imag - sin_real]), mode_index)


def placement_table(column, group_count, capacity):
    groups = jnp.arange(group_count, dtype=jnp.int32)
    member = (column[None, :] == groups[:, None]).astype(jnp.int32)
    ranking = jnp.cumsum(member, axis=1, dtype=jnp.int32) - member
    slot_index = jnp.arange(capacity, dtype=jnp.int32)
    return member[None] * (ranking[None] == slot_index[:, None, None])


def damping_factor(half_step, decay, wave_index):
    wave_square = (wave_index.astype(jnp.float32) * (math.pi / KEEP)) ** 2
    damping = half_step[None, :, None] * (decay[None, :, :] + wave_square[:, None, None])
    return (1.0 - damping) / (1.0 + damping)


def on_device_any(fields, mode_group, half_step, decay, eigen_inverse, eigen_vectors):
    bit_count = lax.axis_size("span").bit_length() - 1
    real_part, imag_part = butterfly(fields, bit_count)
    spectra, mode_index = mode_transform(real_part, imag_part, bit_count)
    kept_modes = spectra.shape[1]
    group_count = lax.axis_size("rad")
    capacity = min(kept_modes, 2 * kept_modes // group_count)
    planes = fields.shape[1]
    radial_rows = fields.shape[2]
    arranged = spectra.reshape(2, kept_modes, 2, planes, radial_rows)
    placing = placement_table(mode_group[:, 0], group_count, capacity)
    placing_float = placing.astype(jnp.float32)
    packed = jnp.einsum("sgb,cbfal->scfagl", placing_float, arranged, precision=precise)
    packed = packed.reshape(capacity, 2, 2, planes, group_count * radial_rows)
    regrouped = lax.all_to_all(packed, "rad", split_axis=4, concat_axis=4, tiled=True)
    own_slots = lax.dynamic_index_in_dim(placing, lax.axis_index("rad"), 1, keepdims=False)
    slot_modes = jnp.sum(own_slots * mode_index[None, :], axis=1)
    factor = damping_factor(half_step, decay, slot_modes)
    inner_part = jnp.einsum("scfar,fir->scfai", regrouped, eigen_inverse, precision=precise)
    inner_part = inner_part * factor[:, None, :, None, :]
    result = jnp.einsum("scfai,fri->scfar", inner_part, eigen_vectors, precision=precise)
    return result.reshape(1, 1, capacity, 2, 2, planes, group_count * radial_rows)


HALF = 8
BLOCK = 64
VMEM_BYTES = 32 * 1024 * 1024


def flip3(value):
    return (value & 1) << 2 | value & 2 | value >> 2


def swap_span(value, distance):
    pairs = [(source, source ^ distance) for source in range(lax.axis_size("span"))]
    return lax.ppermute(value, "span", pairs)


def swap_rad(value):
    return lax.ppermute(value, "rad", [(0, 1), (1, 0)])


def split_pair(value):
    high = value.astype(jnp.bfloat16)
    low = (value - high.astype(jnp.float32)).astype(jnp.bfloat16)
    return high, low


def dot_rows(left, right):
    return lax.dot_general(left, right, contract_rows, preferred_element_type=jnp.float32)


def dot_split(left, right):
    left_high, left_low = left
    right_high, right_low = right
    total = dot_rows(left_high, right_high)
    total = total + dot_rows(left_low, right_high)
    return total + dot_rows(left_high, right_low)


def transform_8(real, imag):
    root = math.sqrt(0.5)
    er, ei, orr, oi = [], [], [], []
    for j in range(4):
        er.append(real[j] + real[j + 4])
        ei.append(imag[j] + imag[j + 4])
        dr = real[j] - real[j + 4]
        di = imag[j] - imag[j + 4]
        if j == 0:
            orr.append(dr)
            oi.append(di)
        elif j == 1:
            orr.append((dr + di) * root)
            oi.append((di - dr) * root)
        elif j == 2:
            orr.append(di)
            oi.append(-dr)
        else:
            orr.append((di - dr) * root)
            oi.append((-di - dr) * root)

    def transform_4(r, i):
        ar, ai = r[0] + r[2], i[0] + i[2]
        br, bi = r[0] - r[2], i[0] - i[2]
        cr, ci = r[1] + r[3], i[1] + i[3]
        dr, di = r[1] - r[3], i[1] - i[3]
        return [(ar + cr, ai + ci), (br + di, bi - dr), (ar - cr, ai - ci), (br - di, bi + dr)]

    even = transform_4(er, ei)
    odd = transform_4(orr, oi)
    return [even[q // 2] if q % 2 == 0 else odd[q // 2] for q in range(8)]


def half_sums_kernel(place, own, core, other_x, other_z, *refs):
    cos_turn, sin_turn, table_high, table_low, out, ordered, high, low = refs
    me, parity = place[0], place[1]
    sign = place[2].astype(jnp.float32)
    width = own.shape[-1]
    modes = out.shape[1]
    ordered[me] = own[0, 0]
    ordered[me ^ 1] = core[0]
    for index in range(2):
        ordered[me ^ (2 + index)] = other_x[index, 0]
    for index in range(4):
        ordered[me ^ (4 + index)] = other_z[index]

    turn_real, turn_imag = [], []
    for j in range(HALF):
        angle = 2.0 * math.pi * j / 16
        turn_real.append(sign * jnp.where(parity == 1, math.cos(angle), 1.0))
        turn_imag.append(sign * jnp.where(parity == 1, -math.sin(angle), 0.0))

    def one_block(step, carry):
        rows = pl.ds(pl.multiple_of(step * 16, 16), 16)
        lower = pl.ds(pl.multiple_of(BLOCK + step * 16, 16), 16)
        for lane in range(0, width, 128):
            real, imag = [], []
            for j in range(HALF):
                value = ordered[j, rows, lane : lane + 128]
                real.append(value * turn_real[j])
                imag.append(value * turn_imag[j])
            sums = transform_8(real, imag)
            for q in range(HALF):
                sum_real, sum_imag = sums[q]
                cosine = cos_turn[parity, q : q + 1, lane : lane + 128]
                sine = sin_turn[parity, q : q + 1, lane : lane + 128]
                real_high, real_low = split_pair(sum_real * cosine + sum_imag * sine)
                imag_high, imag_low = split_pair(sum_imag * cosine - sum_real * sine)
                high[q, rows, lane : lane + 128] = real_high
                high[q, rows, width + lane : width + lane + 128] = imag_high
                high[q, lower, lane : lane + 128] = imag_high
                high[q, lower, width + lane : width + lane + 128] = -real_high
                low[q, rows, lane : lane + 128] = real_low
                low[q, rows, width + lane : width + lane + 128] = imag_low
                low[q, lower, lane : lane + 128] = imag_low
                low[q, lower, width + lane : width + lane + 128] = -real_low
        return carry

    lax.fori_loop(0, BLOCK // 16, one_block, 0)
    table = (table_high[...], table_low[...])
    for q in range(0, HALF, 2):
        lines_high = high[q : q + 2].reshape(4 * BLOCK, 2 * width)
        lines_low = low[q : q + 2].reshape(4 * BLOCK, 2 * width)
        result = dot_split(table, (lines_high, lines_low))
        out[me ^ flip3(q)] = result[:modes, : 2 * BLOCK]
        out[me ^ flip3(q + 1)] = result[:modes, 2 * BLOCK :]


def half_sums(place, unit, fields, core, other_x, other_z, tables, modes):
    field, block, inner = unit
    width = fields.shape[-1]
    rows = tables[2].shape[0]

    def full(array):
        return pl.BlockSpec(array.shape, lambda i, place: (0,) * array.ndim)

    grid_spec = pltpu.PrefetchScalarGridSpec(
        num_scalar_prefetch=1,
        grid=(1,),
        in_specs=[
            pl.BlockSpec((1, 1, BLOCK, width), lambda i, place: (field, place[0], block, 0)),
            pl.BlockSpec((1, BLOCK, width), lambda i, place: (0, inner, 0)),
            pl.BlockSpec((2, 1, BLOCK, width), lambda i, place: (0, 0, inner, 0)),
            pl.BlockSpec((4, BLOCK, width), lambda i, place: (0, inner, 0)),
        ]
        + [full(table) for table in tables],
        out_specs=pl.BlockSpec((HALF, modes, 2 * BLOCK), lambda i, place: (0, 0, 0)),
        scratch_shapes=[
            pltpu.VMEM((HALF, BLOCK, width), jnp.float32),
            pltpu.VMEM((HALF, 2 * BLOCK, 2 * width), jnp.bfloat16),
            pltpu.VMEM((HALF, 2 * BLOCK, 2 * width), jnp.bfloat16),
        ],
    )
    return pl.pallas_call(
        half_sums_kernel,
        out_shape=jax.ShapeDtypeStruct((HALF, modes, 2 * BLOCK), jnp.float32),
        grid_spec=grid_spec,
        cost_estimate=pl.CostEstimate(
            flops=6 * rows * HALF * 4 * BLOCK * width,
            bytes_accessed=HALF * BLOCK * (width + 2 * modes) * 4,
            transcendentals=0,
        ),
        compiler_params=pltpu.CompilerParams(vmem_limit_bytes=VMEM_BYTES),
        name="half_sums",
    )(place, fields, core, other_x, other_z, *tables)


def gather_planes_kernel(place, *refs):
    own, from_z, out, ordered = refs[0], refs[1], refs[-2], refs[-1]
    me = place[0]
    ordered[me] = own[0]
    ordered[me ^ 4] = from_z[0]
    for distance in range(1, 4):
        for index in range(2):
            ordered[me ^ (distance + 4 * index)] = refs[1 + distance][index]
    for plane in range(HALF):
        out[:, plane, :] = ordered[plane]


def gather_planes(place, own, from_z, others):
    modes, lanes = own.shape[-2:]
    one = pl.BlockSpec((1, modes, lanes), lambda i: (0, 0, 0))
    two = pl.BlockSpec((2, modes, lanes), lambda i: (0, 0, 0))
    return pl.pallas_call(
        gather_planes_kernel,
        grid=(1,),
        out_shape=jax.ShapeDtypeStruct((modes, HALF, lanes), jnp.float32),
        in_specs=[pl.BlockSpec(memory_space=pltpu.SMEM), one, one, two, two, two],
        out_specs=pl.BlockSpec((modes, HALF, lanes), lambda i: (0, 0, 0)),
        scratch_shapes=[pltpu.VMEM((HALF, modes, lanes), jnp.float32)],
        cost_estimate=pl.CostEstimate(
            flops=0, bytes_accessed=8 * HALF * modes * lanes, transcendentals=0
        ),
        compiler_params=pltpu.CompilerParams(vmem_limit_bytes=VMEM_BYTES),
        name="gather_planes",
    )(place, own, from_z, *others)


def solve_kernel(count, place, *refs):
    blocks = refs[: 2 * count]
    inverse, vectors, factor = refs[2 * count : 2 * count + 3]
    out = refs[-1]
    modes = out.shape[0]
    radial = out.shape[-1]

    @pl.when(place[3] == 1)
    def _():
        inverse_pair = split_pair(inverse[0])
        vectors_pair = split_pair(vectors[0])
        scale = jnp.broadcast_to(factor[0][:, None, :], (modes, HALF, radial))
        scale = scale.reshape(modes * HALF, radial)
        whole = [block[...].reshape(modes * HALF, 2 * BLOCK) for block in blocks]
        for part in range(2):
            lanes = slice(part * BLOCK, (part + 1) * BLOCK)
            lines = jnp.concatenate([value[:, lanes] for value in whole], axis=1)
            inner = dot_split(split_pair(lines), inverse_pair) * scale
            solved = dot_split(split_pair(inner), vectors_pair)
            out[:, part, 0] = solved.reshape(modes, HALF, radial)

    @pl.when(place[3] != 1)
    def _():
        out[...] = jnp.zeros_like(out)


def solve(place, field, blocks, inverse, vectors, factor, earlier):
    modes = blocks[0].shape[0]
    radial = inverse.shape[-1]
    step = modes // 3
    line = pl.BlockSpec((step, HALF, 2 * BLOCK), lambda i: (i, 0, 0))
    matrix = pl.BlockSpec((1, radial, radial), lambda i: (field, 0, 0))
    in_specs = [pl.BlockSpec(memory_space=pltpu.SMEM)] + [line] * len(blocks)
    in_specs += [matrix, matrix, pl.BlockSpec((1, step, radial), lambda i: (field, i, 0))]
    operands = [place, *blocks, inverse, vectors, factor]
    aliases = {}
    if earlier is not None:
        aliases = {len(operands): 0}
        operands.append(earlier)
        in_specs.append(pl.BlockSpec(memory_space=pl.ANY))

    def kernel(*refs):
        kept = refs if earlier is None else refs[: len(operands) - 1] + refs[-1:]
        solve_kernel(len(blocks) // 2, *kept)

    return pl.pallas_call(
        kernel,
        grid=(3,),
        out_shape=jax.ShapeDtypeStruct((modes, 2, 2, HALF, radial), jnp.float32),
        in_specs=in_specs,
        out_specs=pl.BlockSpec((step, 2, 1, HALF, radial), lambda i: (i, 0, field, 0, 0)),
        input_output_aliases=aliases,
        cost_estimate=pl.CostEstimate(
            flops=24 * modes * HALF * radial * radial,
            bytes_accessed=16 * modes * HALF * radial,
            transcendentals=0,
        ),
        compiler_params=pltpu.CompilerParams(vmem_limit_bytes=VMEM_BYTES),
        name="solve",
    )(*operands)


def mode_tables(width, modes):
    cells = np.arange(width)
    residue = 2 * np.arange(HALF)[None, :, None] + np.arange(2)[:, None, None]
    turn = 2.0 * np.pi * residue * cells / (2 * HALF * width)
    padded = -(-modes // 16) * 16
    angle = 2.0 * np.pi * (np.arange(padded)[:, None] * cells[None, :] % width) / width
    table = np.concatenate([np.cos(angle), np.sin(angle)], axis=1)
    table = table / math.sqrt(2 * HALF * width)
    table[modes:] = 0.0
    high = table.astype(np.float32).astype(ml_dtypes.bfloat16)
    low = (table - high.astype(np.float64)).astype(np.float32).astype(ml_dtypes.bfloat16)
    return (np.cos(turn).astype(np.float32), np.sin(turn).astype(np.float32), high, low)


def on_device_halves(fields, mode_group, half_step, decay, eigen_inverse, eigen_vectors):
    span = lax.axis_index("span")
    rad = lax.axis_index("rad")
    me = span & 7
    half = span >> 3
    rows = fields.shape[2]
    width = fields.shape[3]
    modes = KEEP // 16
    tables = mode_tables(width, modes)

    heavy = (mode_group[0, 0] == rad).astype(jnp.int32)
    one = jnp.ones_like(me)
    place_send = jnp.stack([me, 1 - half, one, heavy])
    place_keep = jnp.stack([me, half, 1 - 2 * half, heavy])

    mode_index = bit_reverse(span, 4) + 16 * jnp.arange(modes, dtype=jnp.int32)
    factor = damping_factor(half_step, decay, mode_index).transpose(1, 0, 2)
    own = lax.dynamic_slice_in_dim(eigen_inverse, rad * rows, rows, 2)
    other = lax.dynamic_slice_in_dim(eigen_inverse, (1 - rad) * rows, rows, 2)
    inverse = jnp.concatenate([own, other], axis=2)

    groups = [(0, 0, BLOCK), (0, BLOCK, rows - BLOCK), (1, 0, rows)]
    units = []
    for group, (field, start, count) in enumerate(groups):
        for inner in range(count // BLOCK):
            units.append((group, (field, start // BLOCK + inner, inner)))
    total = len(units)
    per_field = rows // BLOCK

    def plane_rows(group, distance):
        field, start, count = groups[group]
        piece = lax.dynamic_slice(
            fields, (field, me ^ distance, start, 0), (1, 1, count, width)
        )
        return piece.reshape(count, width)

    def swap_core(group):
        return swap_span(jnp.stack([plane_rows(group, d) for d in (1, 3, 5, 7)]), 1)

    def swap_x(group):
        away = jnp.stack([plane_rows(group, d) for d in (2, 6)])
        return swap_span(jnp.stack([away, core[group][1::2]]), 2)

    def swap_z(group):
        away = [plane_rows(group, 4)[None], core[group][2:3], other_x[group][:, 1]]
        return swap_span(jnp.concatenate(away), 4)

    def sums(place, number):
        group, unit = units[number]
        cells = (core[group], other_x[group], other_z[group])
        return half_sums(place, unit, fields, *cells, tables, modes)

    def finish(kept, came):
        near = kept[:4] + came[:4]
        from_z = swap_span(kept[4:] + came[4:], 4)
        others = []
        for distance in range(1, 4):
            away = jnp.stack([near[distance], from_z[distance]])
            others.append(swap_span(away, distance))
        return gather_planes(place_keep, near, from_z, others)

    def tie(*slots):
        values = lax.optimization_barrier([store[key] for store, key in slots])
        for (store, key), value in zip(slots, values):
            store[key] = value

    core, other_x, other_z = {}, {}, {}
    sent, kept, came, mine, other = {}, {}, {}, {}, {}
    for group in range(3):
        core[group] = swap_core(group)
    other_x[0] = swap_x(0)
    other_z[0] = swap_z(0)
    other_x[1] = swap_x(1)
    sent[0] = sums(place_send, 0)
    tie((sent, 0), (other_x, 1), (core, 2))
    result = None
    for step in range(total):
        came[step] = swap_span(sent[step], HALF)
        kept[step] = sums(place_keep, step)
        tied = [(came, step), (kept, step)]
        if step == 0:
            other_z[1] = swap_z(1)
            other_x[2] = swap_x(2)
            tied += [(other_z, 1), (other_x, 2)]
        if step == 1:
            other_z[2] = swap_z(2)
        if step == 2:
            tied += [(other_z, 2)]
        if step >= 1:
            mine[step - 1] = finish(kept[step - 1], came[step - 1])
            tied += [(mine, step - 1)]
        if step >= 2:
            other[step - 2] = swap_rad(mine[step - 2])
            tied += [(other, step - 2)]
        if step + 1 < total:
            sent[step + 1] = sums(place_send, step + 1)
            tied += [(sent, step + 1)]
        tie(*tied)
    mine[total - 1] = finish(kept[total - 1], came[total - 1])
    other[total - 2] = swap_rad(mine[total - 2])
    other[total - 1] = swap_rad(mine[total - 1])
    for first in (0, per_field):
        numbers = range(first, first + per_field)
        blocks = [mine[n] for n in numbers] + [other[n] for n in numbers]
        field = units[first][1][0]
        result = solve(place_keep, field, blocks, inverse, eigen_vectors, factor, result)
    return result[None, None]


def solution(mesh):
    placed = (P(None, None, "rad", "span"), P(None, "span"), P(), P(), P(), P())
    halves = mesh.shape["span"] == 2 * HALF and mesh.shape["rad"] == 2
    return jax.shard_map(
        on_device_halves if halves else on_device_any,
        mesh=mesh,
        in_specs=placed,
        out_specs=P("span", "rad", None, None, None, None, None),
        check_vma=False,
    )
```

```python
import functools
import math

import jax
import jax.numpy as jnp
import numpy as np
from jax import lax
from jax.experimental import pallas as pl
from jax.experimental.pallas import tpu as pltpu
from jax.sharding import PartitionSpec as P

KEEP = 2688


precise = lax.Precision.HIGHEST
contract_rows = (((1,), (1,)), ((), ()))


def partner_2(value, axis, distance):
    mask = 2**distance
    pairs = [(source, source ^ mask) for source in range(lax.axis_size(axis))]
    return lax.ppermute(value, axis, pairs)


def bit_reverse(value, bit_count):
    flipped = jnp.zeros_like(value)
    for section_bit in range(bit_count):
        flipped = flipped + (value >> section_bit & 1) * 2 ** (bit_count - 1 - section_bit)
    return flipped


def section_angles(device, section_bit):
    upper_half = device >> section_bit & 1 == 1
    twiddle_index = jnp.where(upper_half, device % 2**section_bit, 0)
    angles = twiddle_index.astype(jnp.float32) * (2.0 * math.pi / 2 ** (section_bit + 1))
    sign_factor = jnp.where(upper_half, -1.0, 1.0).astype(jnp.float32)
    return (sign_factor, jnp.cos(angles), jnp.sin(angles))


def butterfly(fields, bit_count):
    device = lax.axis_index("span")
    top_bit = bit_count - 1
    partner = partner_2(fields, "span", top_bit)
    sign_factor, cosine, sine_value = section_angles(device, top_bit)
    difference = partner + sign_factor * fields
    real_part = difference * cosine
    imag_part = -difference * sine_value
    for section_bit in range(bit_count - 2, -1, -1):
        other_real, other_imag = partner_2((real_part, imag_part), "span", section_bit)
        sign_factor, cosine, sine_value = section_angles(device, section_bit)
        diff_real = other_real + sign_factor * real_part
        diff_imag = other_imag + sign_factor * imag_part
        real_part = diff_real * cosine + diff_imag * sine_value
        imag_part = diff_imag * cosine - diff_real * sine_value
    return (real_part, imag_part)


def mode_transform(real_part, imag_part, bit_count):
    groups = lax.axis_size("span")
    line_width = real_part.shape[3]
    full_length = line_width * groups
    kept_modes = KEEP // groups
    residue = bit_reverse(lax.axis_index("span"), bit_count)
    mode_index = residue + groups * jnp.arange(kept_modes, dtype=jnp.int32)
    phases = mode_index[:, None] * jnp.arange(line_width, dtype=jnp.int32)[None, :] % full_length
    angles = phases.astype(jnp.float32) * (2.0 * math.pi / full_length)
    normalizer = 1.0 / math.sqrt(full_length)
    cosine_table = jnp.cos(angles) * normalizer
    sine_table = jnp.sin(angles) * normalizer
    line_real = real_part.reshape(-1, line_width)
    line_imag = imag_part.reshape(-1, line_width)
    cos_real = lax.dot_general(cosine_table, line_real, contract_rows, precision=precise)
    cos_imag = lax.dot_general(cosine_table, line_imag, contract_rows, precision=precise)
    sin_real = lax.dot_general(sine_table, line_real, contract_rows, precision=precise)
    sin_imag = lax.dot_general(sine_table, line_imag, contract_rows, precision=precise)
    return (jnp.stack([cos_real + sin_imag, cos_imag - sin_real]), mode_index)


def placement_table(column, group_count, capacity):
    groups = jnp.arange(group_count, dtype=jnp.int32)
    member = (column[None, :] == groups[:, None]).astype(jnp.int32)
    ranking = jnp.cumsum(member, axis=1, dtype=jnp.int32) - member
    slot_index = jnp.arange(capacity, dtype=jnp.int32)
    return member[None] * (ranking[None] == slot_index[:, None, None])


def damping_factor(half_step, decay, wave_index):
    wave_square = (wave_index.astype(jnp.float32) * (math.pi / KEEP)) ** 2
    damping = half_step[None, :, None] * (decay[None, :, :] + wave_square[:, None, None])
    return (1.0 - damping) / (1.0 + damping)


def on_device_any(fields, mode_group, half_step, decay, eigen_inverse, eigen_vectors):
    bit_count = lax.axis_size("span").bit_length() - 1
    real_part, imag_part = butterfly(fields, bit_count)
    spectra, mode_index = mode_transform(real_part, imag_part, bit_count)
    kept_modes = spectra.shape[1]
    group_count = lax.axis_size("rad")
    capacity = min(kept_modes, 2 * kept_modes // group_count)
    planes = fields.shape[1]
    radial_rows = fields.shape[2]
    arranged = spectra.reshape(2, kept_modes, 2, planes, radial_rows)
    placing = placement_table(mode_group[:, 0], group_count, capacity)
    placing_float = placing.astype(jnp.float32)
    packed = jnp.einsum("sgb,cbfal->scfagl", placing_float, arranged, precision=precise)
    packed = packed.reshape(capacity, 2, 2, planes, group_count * radial_rows)
    regrouped = lax.all_to_all(packed, "rad", split_axis=4, concat_axis=4, tiled=True)
    own_slots = lax.dynamic_index_in_dim(placing, lax.axis_index("rad"), 1, keepdims=False)
    slot_modes = jnp.sum(own_slots * mode_index[None, :], axis=1)
    factor = damping_factor(half_step, decay, slot_modes)
    inner_part = jnp.einsum("scfar,fir->scfai", regrouped, eigen_inverse, precision=precise)
    inner_part = inner_part * factor[:, None, :, None, :]
    result = jnp.einsum("scfai,fri->scfar", inner_part, eigen_vectors, precision=precise)
    return result.reshape(1, 1, capacity, 2, 2, planes, group_count * radial_rows)


HALF = 8
BLOCK = 64
PARTS = 3
LAST_PARTS = (2, 1)
VMEM_BYTES = 32 * 1024 * 1024


def flip3(value):
    return (value & 1) << 2 | value & 2 | value >> 2


def swap_span(value, distance):
    pairs = [(source, source ^ distance) for source in range(lax.axis_size("span"))]
    return lax.ppermute(value, "span", pairs)


def swap_rad(value):
    return lax.ppermute(value, "rad", [(0, 1), (1, 0)])


def split_pair(value):
    high = value.astype(jnp.bfloat16)
    low = (value - high.astype(jnp.float32)).astype(jnp.bfloat16)
    return high, low


def dot_rows(left, right):
    return lax.dot_general(left, right, contract_rows, preferred_element_type=jnp.float32)


def dot_split(left, right):
    left_high, left_low = left
    right_high, right_low = right
    total = dot_rows(left_high, right_high)
    total = total + dot_rows(left_low, right_high)
    return total + dot_rows(left_high, right_low)


def transform_8(real, imag):
    root = math.sqrt(0.5)
    er, ei, orr, oi = [], [], [], []
    for j in range(4):
        er.append(real[j] + real[j + 4])
        ei.append(imag[j] + imag[j + 4])
        dr = real[j] - real[j + 4]
        di = imag[j] - imag[j + 4]
        if j == 0:
            orr.append(dr)
            oi.append(di)
        elif j == 1:
            orr.append((dr + di) * root)
            oi.append((di - dr) * root)
        elif j == 2:
            orr.append(di)
            oi.append(-dr)
        else:
            orr.append((di - dr) * root)
            oi.append((-di - dr) * root)

    def transform_4(r, i):
        ar, ai = r[0] + r[2], i[0] + i[2]
        br, bi = r[0] - r[2], i[0] - i[2]
        cr, ci = r[1] + r[3], i[1] + i[3]
        dr, di = r[1] - r[3], i[1] - i[3]
        return [(ar + cr, ai + ci), (br + di, bi - dr), (ar - cr, ai - ci), (br - di, bi + dr)]

    even = transform_4(er, ei)
    odd = transform_4(orr, oi)
    return [even[q // 2] if q % 2 == 0 else odd[q // 2] for q in range(8)]


def half_sums_kernel(counts, place, own, *refs):
    cells, refs = refs[: len(counts)], refs[len(counts) :]
    cos_turn, sin_turn, table_rows = refs[:3]
    outs, (ordered, high, low) = refs[3:-3], refs[-3:]
    me, parity = place[0], place[1]
    sign = place[2].astype(jnp.float32)
    width = own.shape[-1]
    ordered[me] = own[0, 0]
    distance = 1
    for ref, count in zip(cells, counts):
        for index in range(count):
            ordered[me ^ distance] = ref[index].reshape(ordered.shape[1:])
            distance += 1

    turn_real, turn_imag = [], []
    for j in range(HALF):
        angle = 2.0 * math.pi * j / 16
        turn_real.append(sign * jnp.where(parity == 1, math.cos(angle), 1.0))
        turn_imag.append(sign * jnp.where(parity == 1, -math.sin(angle), 0.0))

    def one_block(step, carry):
        rows = pl.ds(pl.multiple_of(step * 16, 16), 16)
        lower = pl.ds(pl.multiple_of(BLOCK + step * 16, 16), 16)
        for lane in range(0, width, 128):
            real, imag = [], []
            for j in range(HALF):
                value = ordered[j, rows, lane : lane + 128]
                real.append(value * turn_real[j])
                imag.append(value * turn_imag[j])
            sums = transform_8(real, imag)
            for q in range(HALF):
                sum_real, sum_imag = sums[q]
                cosine = cos_turn[parity, q : q + 1, lane : lane + 128]
                sine = sin_turn[parity, q : q + 1, lane : lane + 128]
                real_high, real_low = split_pair(sum_real * cosine + sum_imag * sine)
                imag_high, imag_low = split_pair(sum_imag * cosine - sum_real * sine)
                high[q, rows, lane : lane + 128] = real_high
                high[q, rows, width + lane : width + lane + 128] = imag_high
                high[q, lower, lane : lane + 128] = imag_high
                high[q, lower, width + lane : width + lane + 128] = -real_high
                low[q, rows, lane : lane + 128] = real_low
                low[q, rows, width + lane : width + lane + 128] = imag_low
                low[q, lower, lane : lane + 128] = imag_low
                low[q, lower, width + lane : width + lane + 128] = -real_low
        return carry

    lax.fori_loop(0, BLOCK // 16, one_block, 0)
    table = split_pair(table_rows[...])
    for q in range(0, HALF, 2):
        lines_high = high[q : q + 2].reshape(4 * BLOCK, 2 * width)
        lines_low = low[q : q + 2].reshape(4 * BLOCK, 2 * width)
        result = dot_split(table, (lines_high, lines_low))
        first = 0
        for out in outs:
            rows = slice(first, first + out.shape[1])
            out[me ^ flip3(q)] = result[rows, : 2 * BLOCK]
            out[me ^ flip3(q + 1)] = result[rows, 2 * BLOCK :]
            first += out.shape[1]


def half_sums(place, field, block, fields, cells, tables, parts):
    width = fields.shape[-1]
    rows = tables[2].shape[0]
    counts = [count for _, count, _ in cells]

    def full(array):
        return pl.BlockSpec(array.shape, lambda i, place: (0,) * array.ndim)

    def some(array, count, inner):
        middle = (1,) * (array.ndim - 3)
        first = (0,) * (array.ndim - 2)
        return pl.BlockSpec(
            (count, *middle, BLOCK, width), lambda i, place: (*first, inner, 0)
        )

    grid_spec = pltpu.PrefetchScalarGridSpec(
        num_scalar_prefetch=1,
        grid=(1,),
        in_specs=[
            pl.BlockSpec((1, 1, BLOCK, width), lambda i, place: (field, place[0], block, 0))
        ]
        + [some(*cell) for cell in cells]
        + [full(table) for table in tables],
        out_specs=[
            pl.BlockSpec((HALF, part, 2 * BLOCK), lambda i, place: (0, 0, 0)) for part in parts
        ],
        scratch_shapes=[
            pltpu.VMEM((HALF, BLOCK, width), jnp.float32),
            pltpu.VMEM((HALF, 2 * BLOCK, 2 * width), jnp.bfloat16),
            pltpu.VMEM((HALF, 2 * BLOCK, 2 * width), jnp.bfloat16),
        ],
    )
    return pl.pallas_call(
        functools.partial(half_sums_kernel, counts),
        out_shape=[
            jax.ShapeDtypeStruct((HALF, part, 2 * BLOCK), jnp.float32) for part in parts
        ],
        grid_spec=grid_spec,
        cost_estimate=pl.CostEstimate(
            flops=rows * BLOCK * width,
            bytes_accessed=BLOCK * width * 4,
            transcendentals=0,
        ),
        compiler_params=pltpu.CompilerParams(vmem_limit_bytes=VMEM_BYTES),
        name="half_sums",
    )(place, fields, *[array for array, _, _ in cells], *tables)


def gather_planes_kernel(place, *refs):
    own, from_z, out, ordered = refs[0], refs[1], refs[-2], refs[-1]
    me = place[0]
    ordered[me] = own[0]
    ordered[me ^ 4] = from_z[0]
    for distance in range(1, 4):
        for index in range(2):
            ordered[me ^ (distance + 4 * index)] = refs[1 + distance][index]
    for plane in range(HALF):
        out[:, plane, :] = ordered[plane]


def gather_planes(place, own, from_z, others):
    modes, lanes = own.shape[-2:]
    one = pl.BlockSpec((1, modes, lanes), lambda i: (0, 0, 0))
    two = pl.BlockSpec((2, modes, lanes), lambda i: (0, 0, 0))
    return pl.pallas_call(
        gather_planes_kernel,
        grid=(1,),
        out_shape=jax.ShapeDtypeStruct((modes, HALF, lanes), jnp.float32),
        in_specs=[pl.BlockSpec(memory_space=pltpu.SMEM), one, one, two, two, two],
        out_specs=pl.BlockSpec((modes, HALF, lanes), lambda i: (0, 0, 0)),
        scratch_shapes=[pltpu.VMEM((HALF, modes, lanes), jnp.float32)],
        cost_estimate=pl.CostEstimate(
            flops=0, bytes_accessed=8 * HALF * modes * lanes, transcendentals=0
        ),
        compiler_params=pltpu.CompilerParams(vmem_limit_bytes=VMEM_BYTES),
        name="gather_planes",
    )(place, own, from_z, *others)


def solve_kernel(count, place, *refs):
    blocks = refs[: 2 * count]
    inverse, vectors, factor = refs[2 * count : 2 * count + 3]
    out = refs[-1]
    modes = out.shape[0]
    radial = out.shape[-1]

    @pl.when(place[3] == 1)
    def _():
        inverse_pair = split_pair(inverse[0])
        vectors_pair = split_pair(vectors[0])
        scale = jnp.broadcast_to(factor[0][:, None, :], (modes, HALF, radial))
        scale = scale.reshape(modes * HALF, radial)
        whole = [block[...].reshape(modes * HALF, 2 * BLOCK) for block in blocks]
        for part in range(2):
            lanes = slice(part * BLOCK, (part + 1) * BLOCK)
            lines = jnp.concatenate([value[:, lanes] for value in whole], axis=1)
            inner = dot_split(split_pair(lines), inverse_pair) * scale
            solved = dot_split(split_pair(inner), vectors_pair)
            out[:, part, 0] = solved.reshape(modes, HALF, radial)

    @pl.when(place[3] != 1)
    def _():
        out[...] = jnp.zeros_like(out)


def solve(place, field, first, count, blocks, inverse, vectors, factor, earlier):
    modes = factor.shape[1]
    radial = inverse.shape[-1]
    step = modes // PARTS

    def lines(array):
        offset = first if array.shape[0] == modes else 0
        return pl.BlockSpec((step, HALF, 2 * BLOCK), lambda i: (offset + i, 0, 0))

    matrix = pl.BlockSpec((1, radial, radial), lambda i: (field, 0, 0))
    in_specs = [pl.BlockSpec(memory_space=pltpu.SMEM)] + [lines(block) for block in blocks]
    in_specs += [matrix, matrix]
    in_specs += [pl.BlockSpec((1, step, radial), lambda i: (field, first + i, 0))]
    operands = [place, *blocks, inverse, vectors, factor]
    aliases = {}
    if earlier is not None:
        aliases = {len(operands): 0}
        operands.append(earlier)
        in_specs.append(pl.BlockSpec(memory_space=pl.ANY))

    def kernel(*refs):
        kept = refs if earlier is None else refs[: len(operands) - 1] + refs[-1:]
        solve_kernel(len(blocks) // 2, *kept)

    return pl.pallas_call(
        kernel,
        grid=(count,),
        out_shape=jax.ShapeDtypeStruct((modes, 2, 2, HALF, radial), jnp.float32),
        in_specs=in_specs,
        out_specs=pl.BlockSpec(
            (step, 2, 1, HALF, radial), lambda i: (first + i, 0, field, 0, 0)
        ),
        input_output_aliases=aliases,
        cost_estimate=pl.CostEstimate(
            flops=count * modes * radial * radial,
            bytes_accessed=count * modes * radial,
            transcendentals=0,
        ),
        compiler_params=pltpu.CompilerParams(vmem_limit_bytes=VMEM_BYTES),
        name="solve",
    )(*operands)


def mode_tables(width, modes):
    cells = np.arange(width)
    residue = 2 * np.arange(HALF)[None, :, None] + np.arange(2)[:, None, None]
    turn = 2.0 * np.pi * residue * cells / (2 * HALF * width)
    padded = -(-modes // 16) * 16
    angle = 2.0 * np.pi * (np.arange(padded)[:, None] * cells[None, :] % width) / width
    table = np.concatenate([np.cos(angle), np.sin(angle)], axis=1)
    table = table / math.sqrt(2 * HALF * width)
    table[modes:] = 0.0
    return tuple(array.astype(np.float32) for array in (np.cos(turn), np.sin(turn), table))


def on_device_halves(fields, mode_group, half_step, decay, eigen_inverse, eigen_vectors):
    span = lax.axis_index("span")
    rad = lax.axis_index("rad")
    me = span & 7
    half = span >> 3
    rows = fields.shape[2]
    width = fields.shape[3]
    modes = KEEP // 16
    tables = mode_tables(width, modes)

    heavy = (mode_group[0, 0] == rad).astype(jnp.int32)
    one = jnp.ones_like(me)
    place_send = jnp.stack([me, 1 - half, one, heavy])
    place_keep = jnp.stack([me, half, 1 - 2 * half, heavy])

    mode_index = bit_reverse(span, 4) + 16 * jnp.arange(modes, dtype=jnp.int32)
    factor = damping_factor(half_step, decay, mode_index).transpose(1, 0, 2)
    own = lax.dynamic_slice_in_dim(eigen_inverse, rad * rows, rows, 2)
    other = lax.dynamic_slice_in_dim(eigen_inverse, (1 - rad) * rows, rows, 2)
    inverse = jnp.concatenate([own, other], axis=2)

    units = [(field, block) for field in range(2) for block in range(rows // BLOCK)]
    total = len(units)
    per_field = rows // BLOCK
    last = total - 1

    def plane_rows(source, field, start, count, distance):
        piece = lax.dynamic_slice(
            source, (field, me ^ distance, start, 0), (1, 1, count, width)
        )
        return piece.reshape(count, width)

    def swap_core(source, *rows_of):
        pieces = [plane_rows(source, *rows_of, d) for d in (1, 3, 5, 7)]
        return swap_span(jnp.stack(pieces), 1)

    def away_direct(source, core, inner, field, block):
        picked = slice(inner * BLOCK, (inner + 1) * BLOCK)
        result = []
        for place, distance in ((1, 2), (2, 4), (3, 6)):
            mine = plane_rows(source, field, block * BLOCK, BLOCK, distance)
            result.append(jnp.stack([mine, core[place, picked]]))
        return result

    def swap_direct(away):
        return [swap_span(value, distance) for value, distance in zip(away, (2, 4, 6))]

    def direct_cells(core, inner, arrays):
        return [(core, 1, inner)] + [(array, 2, 0) for array in arrays]

    def away_rows_x(source, core, inner, count):
        rows_of = (1, inner * BLOCK, count * BLOCK)
        mine = jnp.stack([plane_rows(source, *rows_of, d) for d in (2, 6)])
        picked = slice(inner * BLOCK, (inner + count) * BLOCK)
        return jnp.stack([mine, core[1::2, picked]])

    def swap_z(source, core, inner, other_x, place):
        picked = slice(inner * BLOCK, (inner + 1) * BLOCK)
        away = [plane_rows(source, 1, inner * BLOCK, BLOCK, 4)[None], core[2:3, picked]]
        away += [other_x[:, 1, place * BLOCK : (place + 1) * BLOCK]]
        return swap_span(jnp.concatenate(away), 4)

    def finish(kept, came):
        near = kept[:4] + came[:4]
        from_z = swap_span(kept[4:] + came[4:], 4)
        others = []
        for distance in range(1, 4):
            away = jnp.stack([near[distance], from_z[distance]])
            others.append(swap_span(away, distance))
        return gather_planes(place_keep, near, from_z, others)

    def tie(*values):
        return lax.optimization_barrier(values)

    def sums(place, unit):
        step = modes // PARTS
        parts = [step * count for count in LAST_PARTS] if unit == last else [modes]
        return half_sums(place, *units[unit], fields, cells[unit], tables, parts)

    cells = {}
    sent, kept, came, mine, other = {}, {}, {}, {}, {}
    core_1 = swap_core(fields, 0, 0, rows)
    away = [away_direct(fields, core_1, n, *units[n]) for n in range(per_field)]
    arrays = [swap_direct(away[n]) for n in range(2)]
    core_2 = swap_core(fields, 1, 0, rows)
    cells[0] = direct_cells(core_1, 0, arrays[0])
    sent[0] = sums(place_send, 0)
    away_x = [away_rows_x(fields, core_2, 0, 2), away_rows_x(fields, core_2, 2, 1)]
    sent[0], arrays[1], core_2, away, away_x = tie(sent[0], arrays[1], core_2, away, away_x)
    cells[1] = direct_cells(core_1, 1, arrays[1])
    matrices = (inverse, eigen_vectors, factor)
    other_x = {}
    result = None
    for step in range(last):
        came[step] = swap_span(sent[step][0], HALF)
        if step == 0:
            kept[0] = sums(place_keep, 0)
        extra = {}
        if step == 0:
            extra["direct"] = swap_direct(away[2])
        if step < 2:
            extra["x"] = swap_span(away_x[step], 2)
        if 1 <= step <= 3:
            unit = step + 2
            inner = unit - per_field
            source, place = (other_x[0], inner) if inner < 2 else (other_x[1], 0)
            extra["z"] = swap_z(fields, core_2, inner, source, place)
            cells[unit] = [(core_2, 1, inner), (source, 2, place)]
        if step >= 1:
            extra["mine"] = finish(kept[step - 1][0], came[step - 1])
        if step >= 2:
            extra["other"] = swap_rad(mine[step - 2])
        sent[step + 1] = sums(place_send, step + 1)
        kept[step + 1] = sums(place_keep, step + 1)
        came[step], sent[step + 1], kept[step + 1], extra = tie(
            came[step], sent[step + 1], kept[step + 1], extra
        )
        if "direct" in extra:
            cells[2] = direct_cells(core_1, 2, extra["direct"])
        if "x" in extra:
            other_x[step] = extra["x"]
        if "z" in extra:
            cells[step + 2].append((extra["z"], 4, 0))
        if step >= 1:
            mine[step - 1] = extra["mine"]
        if step >= 2:
            other[step - 2] = extra["other"]

    def blocks_of(numbers, part=None):
        chosen = [mine[n] if n != last else mine[n][part] for n in numbers]
        return chosen + [other[n] if n != last else other[n][part] for n in numbers]

    came[last] = [swap_span(part, HALF) for part in sent[last]]
    mine[last - 1] = finish(kept[last - 1][0], came[last - 1])
    other[last - 2] = swap_rad(mine[last - 2])
    result = solve(place_keep, 0, 0, PARTS, blocks_of(range(per_field)), *matrices, None)
    came[last][0], mine[last - 1], other[last - 2], result = tie(
        came[last][0], mine[last - 1], other[last - 2], result
    )
    other[last - 1] = swap_rad(mine[last - 1])
    first = finish(kept[last][0], came[last][0])
    first, came[last][1], other[last - 1] = tie(first, came[last][1], other[last - 1])
    other_first = swap_rad(first)
    second = finish(kept[last][1], came[last][1])
    second, other_first = tie(second, other_first)
    mine[last] = [first, second]
    other[last] = [other_first, swap_rad(second)]
    start = 0
    for part, count in enumerate(LAST_PARTS):
        blocks = blocks_of(range(per_field, total), part)
        result = solve(place_keep, 1, start, count, blocks, *matrices, result)
        start += count
    return result[None, None]


def solution(mesh):
    placed = (P(None, None, "rad", "span"), P(None, "span"), P(), P(), P(), P())
    halves = mesh.shape["span"] == 2 * HALF and mesh.shape["rad"] == 2
    return jax.shard_map(
        on_device_halves if halves else on_device_any,
        mesh=mesh,
        in_specs=placed,
        out_specs=P("span", "rad", None, None, None, None, None),
        check_vma=False,
    )
```

```python
import functools
import math

import jax
import jax.numpy as jnp
import numpy as np
from jax import lax
from jax.experimental import pallas as pl
from jax.experimental.pallas import tpu as pltpu
from jax.sharding import PartitionSpec as P

KEEP = 2688


precise = lax.Precision.HIGHEST
contract_rows = (((1,), (1,)), ((), ()))


def partner_2(value, axis, distance):
    mask = 2**distance
    pairs = [(source, source ^ mask) for source in range(lax.axis_size(axis))]
    return lax.ppermute(value, axis, pairs)


def bit_reverse(value, bit_count):
    flipped = jnp.zeros_like(value)
    for section_bit in range(bit_count):
        flipped = flipped + (value >> section_bit & 1) * 2 ** (bit_count - 1 - section_bit)
    return flipped


def section_angles(device, section_bit):
    upper_half = device >> section_bit & 1 == 1
    twiddle_index = jnp.where(upper_half, device % 2**section_bit, 0)
    angles = twiddle_index.astype(jnp.float32) * (2.0 * math.pi / 2 ** (section_bit + 1))
    sign_factor = jnp.where(upper_half, -1.0, 1.0).astype(jnp.float32)
    return (sign_factor, jnp.cos(angles), jnp.sin(angles))


def butterfly(fields, bit_count):
    device = lax.axis_index("span")
    top_bit = bit_count - 1
    partner = partner_2(fields, "span", top_bit)
    sign_factor, cosine, sine_value = section_angles(device, top_bit)
    difference = partner + sign_factor * fields
    real_part = difference * cosine
    imag_part = -difference * sine_value
    for section_bit in range(bit_count - 2, -1, -1):
        other_real, other_imag = partner_2((real_part, imag_part), "span", section_bit)
        sign_factor, cosine, sine_value = section_angles(device, section_bit)
        diff_real = other_real + sign_factor * real_part
        diff_imag = other_imag + sign_factor * imag_part
        real_part = diff_real * cosine + diff_imag * sine_value
        imag_part = diff_imag * cosine - diff_real * sine_value
    return (real_part, imag_part)


def mode_transform(real_part, imag_part, bit_count):
    groups = lax.axis_size("span")
    line_width = real_part.shape[3]
    full_length = line_width * groups
    kept_modes = KEEP // groups
    residue = bit_reverse(lax.axis_index("span"), bit_count)
    mode_index = residue + groups * jnp.arange(kept_modes, dtype=jnp.int32)
    phases = mode_index[:, None] * jnp.arange(line_width, dtype=jnp.int32)[None, :] % full_length
    angles = phases.astype(jnp.float32) * (2.0 * math.pi / full_length)
    normalizer = 1.0 / math.sqrt(full_length)
    cosine_table = jnp.cos(angles) * normalizer
    sine_table = jnp.sin(angles) * normalizer
    line_real = real_part.reshape(-1, line_width)
    line_imag = imag_part.reshape(-1, line_width)
    cos_real = lax.dot_general(cosine_table, line_real, contract_rows, precision=precise)
    cos_imag = lax.dot_general(cosine_table, line_imag, contract_rows, precision=precise)
    sin_real = lax.dot_general(sine_table, line_real, contract_rows, precision=precise)
    sin_imag = lax.dot_general(sine_table, line_imag, contract_rows, precision=precise)
    return (jnp.stack([cos_real + sin_imag, cos_imag - sin_real]), mode_index)


def placement_table(column, group_count, capacity):
    groups = jnp.arange(group_count, dtype=jnp.int32)
    member = (column[None, :] == groups[:, None]).astype(jnp.int32)
    ranking = jnp.cumsum(member, axis=1, dtype=jnp.int32) - member
    slot_index = jnp.arange(capacity, dtype=jnp.int32)
    return member[None] * (ranking[None] == slot_index[:, None, None])


def damping_factor(half_step, decay, wave_index):
    wave_square = (wave_index.astype(jnp.float32) * (math.pi / KEEP)) ** 2
    damping = half_step[None, :, None] * (decay[None, :, :] + wave_square[:, None, None])
    return (1.0 - damping) / (1.0 + damping)


def on_device_any(fields, mode_group, half_step, decay, eigen_inverse, eigen_vectors):
    bit_count = lax.axis_size("span").bit_length() - 1
    real_part, imag_part = butterfly(fields, bit_count)
    spectra, mode_index = mode_transform(real_part, imag_part, bit_count)
    kept_modes = spectra.shape[1]
    group_count = lax.axis_size("rad")
    capacity = min(kept_modes, 2 * kept_modes // group_count)
    planes = fields.shape[1]
    radial_rows = fields.shape[2]
    arranged = spectra.reshape(2, kept_modes, 2, planes, radial_rows)
    placing = placement_table(mode_group[:, 0], group_count, capacity)
    placing_float = placing.astype(jnp.float32)
    packed = jnp.einsum("sgb,cbfal->scfagl", placing_float, arranged, precision=precise)
    packed = packed.reshape(capacity, 2, 2, planes, group_count * radial_rows)
    regrouped = lax.all_to_all(packed, "rad", split_axis=4, concat_axis=4, tiled=True)
    own_slots = lax.dynamic_index_in_dim(placing, lax.axis_index("rad"), 1, keepdims=False)
    slot_modes = jnp.sum(own_slots * mode_index[None, :], axis=1)
    factor = damping_factor(half_step, decay, slot_modes)
    inner_part = jnp.einsum("scfar,fir->scfai", regrouped, eigen_inverse, precision=precise)
    inner_part = inner_part * factor[:, None, :, None, :]
    result = jnp.einsum("scfai,fri->scfar", inner_part, eigen_vectors, precision=precise)
    return result.reshape(1, 1, capacity, 2, 2, planes, group_count * radial_rows)


HALF = 8
BLOCK = 64
PARTS = 3
LAST_PARTS = (2, 1)
VMEM_BYTES = 56 * 1024 * 1024


def flip3(value):
    return (value & 1) << 2 | value & 2 | value >> 2


def swap_span(value, distance):
    pairs = [(source, source ^ distance) for source in range(lax.axis_size("span"))]
    return lax.ppermute(value, "span", pairs)


def swap_rad(value):
    return lax.ppermute(value, "rad", [(0, 1), (1, 0)])


def split_pair(value):
    high = value.astype(jnp.bfloat16)
    low = (value - high.astype(jnp.float32)).astype(jnp.bfloat16)
    return high, low


def dot_rows(left, right):
    return lax.dot_general(left, right, contract_rows, preferred_element_type=jnp.float32)


def dot_split(left, right):
    left_high, left_low = left
    right_high, right_low = right
    total = dot_rows(left_high, right_high)
    total = total + dot_rows(left_low, right_high)
    return total + dot_rows(left_high, right_low)


def transform_8(real, imag):
    root = math.sqrt(0.5)
    er, ei, orr, oi = [], [], [], []
    for j in range(4):
        er.append(real[j] + real[j + 4])
        ei.append(imag[j] + imag[j + 4])
        dr = real[j] - real[j + 4]
        di = imag[j] - imag[j + 4]
        if j == 0:
            orr.append(dr)
            oi.append(di)
        elif j == 1:
            orr.append((dr + di) * root)
            oi.append((di - dr) * root)
        elif j == 2:
            orr.append(di)
            oi.append(-dr)
        else:
            orr.append((di - dr) * root)
            oi.append((-di - dr) * root)

    def transform_4(r, i):
        ar, ai = r[0] + r[2], i[0] + i[2]
        br, bi = r[0] - r[2], i[0] - i[2]
        cr, ci = r[1] + r[3], i[1] + i[3]
        dr, di = r[1] - r[3], i[1] - i[3]
        return [(ar + cr, ai + ci), (br + di, bi - dr), (ar - cr, ai - ci), (br - di, bi + dr)]

    even = transform_4(er, ei)
    odd = transform_4(orr, oi)
    return [even[q // 2] if q % 2 == 0 else odd[q // 2] for q in range(8)]


def half_sums_kernel(counts, place, own, *refs):
    cells, refs = refs[: len(counts)], refs[len(counts) :]
    cos_turn, sin_turn, table_rows = refs[:3]
    outs, (ordered, high, low) = refs[3:-3], refs[-3:]
    me, parity = place[0], place[1]
    sign = place[2].astype(jnp.float32)
    width = own.shape[-1]
    ordered[me] = own[0, 0]
    distance = 1
    for ref, count in zip(cells, counts):
        for index in range(count):
            ordered[me ^ distance] = ref[index]
            distance += 1

    turn_real, turn_imag = [], []
    for j in range(HALF):
        angle = 2.0 * math.pi * j / 16
        turn_real.append(sign * jnp.where(parity == 1, math.cos(angle), 1.0))
        turn_imag.append(sign * jnp.where(parity == 1, -math.sin(angle), 0.0))

    def one_block(step, carry):
        rows = pl.ds(pl.multiple_of(step * 16, 16), 16)
        lower = pl.ds(pl.multiple_of(BLOCK + step * 16, 16), 16)
        for lane in range(0, width, 128):
            real, imag = [], []
            for j in range(HALF):
                value = ordered[j, rows, lane : lane + 128]
                real.append(value * turn_real[j])
                imag.append(value * turn_imag[j])
            sums = transform_8(real, imag)
            for q in range(HALF):
                sum_real, sum_imag = sums[q]
                cosine = cos_turn[parity, q : q + 1, lane : lane + 128]
                sine = sin_turn[parity, q : q + 1, lane : lane + 128]
                real_high, real_low = split_pair(sum_real * cosine + sum_imag * sine)
                imag_high, imag_low = split_pair(sum_imag * cosine - sum_real * sine)
                high[q, rows, lane : lane + 128] = real_high
                high[q, rows, width + lane : width + lane + 128] = imag_high
                high[q, lower, lane : lane + 128] = imag_high
                high[q, lower, width + lane : width + lane + 128] = -real_high
                low[q, rows, lane : lane + 128] = real_low
                low[q, rows, width + lane : width + lane + 128] = imag_low
                low[q, lower, lane : lane + 128] = imag_low
                low[q, lower, width + lane : width + lane + 128] = -real_low
        return carry

    lax.fori_loop(0, BLOCK // 16, one_block, 0)
    table = split_pair(table_rows[...])
    for q in range(0, HALF, 2):
        lines_high = high[q : q + 2].reshape(4 * BLOCK, 2 * width)
        lines_low = low[q : q + 2].reshape(4 * BLOCK, 2 * width)
        result = dot_split(table, (lines_high, lines_low))
        first = 0
        for out in outs:
            rows = slice(first, first + out.shape[1])
            out[me ^ flip3(q)] = result[rows, : 2 * BLOCK]
            out[me ^ flip3(q + 1)] = result[rows, 2 * BLOCK :]
            first += out.shape[1]


def half_sums(place, field, block, fields, cells, tables, parts):
    width = fields.shape[-1]
    rows = tables[2].shape[0]
    counts = [count or 1 for _, count, _ in cells]

    def full(array):
        return pl.BlockSpec(array.shape, lambda i, place: (0,) * array.ndim)

    def some(_, count, inner):
        if count is None:
            return pl.BlockSpec(
                (1, BLOCK, width), lambda i, place: (place[0] >> 1, inner, 0)
            )
        return pl.BlockSpec((count, BLOCK, width), lambda i, place: (0, inner, 0))

    grid_spec = pltpu.PrefetchScalarGridSpec(
        num_scalar_prefetch=1,
        grid=(1,),
        in_specs=[
            pl.BlockSpec((1, 1, BLOCK, width), lambda i, place: (field, place[0], block, 0))
        ]
        + [some(*cell) for cell in cells]
        + [full(table) for table in tables],
        out_specs=[
            pl.BlockSpec((HALF, part, 2 * BLOCK), lambda i, place: (0, 0, 0)) for part in parts
        ],
        scratch_shapes=[
            pltpu.VMEM((HALF, BLOCK, width), jnp.float32),
            pltpu.VMEM((HALF, 2 * BLOCK, 2 * width), jnp.bfloat16),
            pltpu.VMEM((HALF, 2 * BLOCK, 2 * width), jnp.bfloat16),
        ],
    )
    return pl.pallas_call(
        functools.partial(half_sums_kernel, counts),
        out_shape=[
            jax.ShapeDtypeStruct((HALF, part, 2 * BLOCK), jnp.float32) for part in parts
        ],
        grid_spec=grid_spec,
        cost_estimate=pl.CostEstimate(
            flops=rows * BLOCK * width,
            bytes_accessed=BLOCK * width * 4,
            transcendentals=0,
        ),
        compiler_params=pltpu.CompilerParams(vmem_limit_bytes=VMEM_BYTES),
        name="half_sums",
    )(place, fields, *[array for array, _, _ in cells], *tables)


def gather_planes_kernel(place, *refs):
    own, from_z, out, ordered = refs[0], refs[1], refs[-2], refs[-1]
    me = place[0]
    ordered[me] = own[0]
    ordered[me ^ 4] = from_z[0]
    for distance in range(1, 4):
        for index in range(2):
            ordered[me ^ (distance + 4 * index)] = refs[1 + distance][index]
    for plane in range(HALF):
        out[:, plane, :] = ordered[plane]


def gather_planes(place, own, from_z, others):
    modes, lanes = own.shape[-2:]
    one = pl.BlockSpec((1, modes, lanes), lambda i: (0, 0, 0))
    two = pl.BlockSpec((2, modes, lanes), lambda i: (0, 0, 0))
    return pl.pallas_call(
        gather_planes_kernel,
        grid=(1,),
        out_shape=jax.ShapeDtypeStruct((modes, HALF, lanes), jnp.float32),
        in_specs=[pl.BlockSpec(memory_space=pltpu.SMEM), one, one, two, two, two],
        out_specs=pl.BlockSpec((modes, HALF, lanes), lambda i: (0, 0, 0)),
        scratch_shapes=[pltpu.VMEM((HALF, modes, lanes), jnp.float32)],
        cost_estimate=pl.CostEstimate(
            flops=0, bytes_accessed=8 * HALF * modes * lanes, transcendentals=0
        ),
        compiler_params=pltpu.CompilerParams(vmem_limit_bytes=VMEM_BYTES),
        name="gather_planes",
    )(place, own, from_z, *others)


def solve_kernel(count, place, *refs):
    blocks = refs[: 2 * count]
    inverse, vectors, factor = refs[2 * count : 2 * count + 3]
    out = refs[-1]
    modes = out.shape[0]
    radial = out.shape[-1]

    @pl.when(place[3] == 1)
    def _():
        inverse_pair = split_pair(inverse[0])
        vectors_pair = split_pair(vectors[0])
        scale = jnp.broadcast_to(factor[0][:, None, :], (modes, HALF, radial))
        scale = scale.reshape(modes * HALF, radial)
        whole = [block[...].reshape(modes * HALF, 2 * BLOCK) for block in blocks]
        for part in range(2):
            lanes = slice(part * BLOCK, (part + 1) * BLOCK)
            lines = jnp.concatenate([value[:, lanes] for value in whole], axis=1)
            inner = dot_split(split_pair(lines), inverse_pair) * scale
            solved = dot_split(split_pair(inner), vectors_pair)
            out[:, part, 0] = solved.reshape(modes, HALF, radial)

    @pl.when(place[3] != 1)
    def _():
        out[...] = jnp.zeros_like(out)


def solve(place, field, first, count, blocks, inverse, vectors, factor, earlier):
    modes = factor.shape[1]
    radial = inverse.shape[-1]
    step = modes // PARTS

    def lines(array):
        offset = first if array.shape[0] == modes else 0
        return pl.BlockSpec((step, HALF, 2 * BLOCK), lambda i: (offset + i, 0, 0))

    matrix = pl.BlockSpec((1, radial, radial), lambda i: (field, 0, 0))
    in_specs = [pl.BlockSpec(memory_space=pltpu.SMEM)] + [lines(block) for block in blocks]
    in_specs += [matrix, matrix]
    in_specs += [pl.BlockSpec((1, step, radial), lambda i: (field, first + i, 0))]
    operands = [place, *blocks, inverse, vectors, factor]
    aliases = {}
    if earlier is not None:
        aliases = {len(operands): 0}
        operands.append(earlier)
        in_specs.append(pl.BlockSpec(memory_space=pl.ANY))

    def kernel(*refs):
        kept = refs if earlier is None else refs[: len(operands) - 1] + refs[-1:]
        solve_kernel(len(blocks) // 2, *kept)

    return pl.pallas_call(
        kernel,
        grid=(count,),
        out_shape=jax.ShapeDtypeStruct((modes, 2, 2, HALF, radial), jnp.float32),
        in_specs=in_specs,
        out_specs=pl.BlockSpec(
            (step, 2, 1, HALF, radial), lambda i: (first + i, 0, field, 0, 0)
        ),
        input_output_aliases=aliases,
        cost_estimate=pl.CostEstimate(
            flops=count * modes * radial * radial,
            bytes_accessed=count * modes * radial,
            transcendentals=0,
        ),
        compiler_params=pltpu.CompilerParams(vmem_limit_bytes=VMEM_BYTES),
        name="solve",
    )(*operands)


def mode_tables(width, modes):
    cells = np.arange(width)
    residue = 2 * np.arange(HALF)[None, :, None] + np.arange(2)[:, None, None]
    turn = 2.0 * np.pi * residue * cells / (2 * HALF * width)
    padded = -(-modes // 16) * 16
    angle = 2.0 * np.pi * (np.arange(padded)[:, None] * cells[None, :] % width) / width
    table = np.concatenate([np.cos(angle), np.sin(angle)], axis=1)
    table = table / math.sqrt(2 * HALF * width)
    table[modes:] = 0.0
    return tuple(array.astype(np.float32) for array in (np.cos(turn), np.sin(turn), table))


def on_device_halves(fields, mode_group, half_step, decay, eigen_inverse, eigen_vectors):
    span = lax.axis_index("span")
    rad = lax.axis_index("rad")
    me = span & 7
    half = span >> 3
    rows = fields.shape[2]
    width = fields.shape[3]
    modes = KEEP // 16
    tables = mode_tables(width, modes)

    heavy = (mode_group[0, 0] == rad).astype(jnp.int32)
    one = jnp.ones_like(me)
    place_send = jnp.stack([me, 1 - half, one, heavy])
    place_keep = jnp.stack([me, half, 1 - 2 * half, heavy])

    mode_index = bit_reverse(span, 4) + 16 * jnp.arange(modes, dtype=jnp.int32)
    factor = damping_factor(half_step, decay, mode_index).transpose(1, 0, 2)
    own = lax.dynamic_slice_in_dim(eigen_inverse, rad * rows, rows, 2)
    other = lax.dynamic_slice_in_dim(eigen_inverse, (1 - rad) * rows, rows, 2)
    inverse = jnp.concatenate([own, other], axis=2)

    units = [(field, block) for field in range(2) for block in range(rows // BLOCK)]
    total = len(units)
    per_field = rows // BLOCK
    last = total - 1

    def plane_rows(field, start, count, distance):
        piece = lax.dynamic_slice(
            fields, (field, me ^ distance, start, 0), (1, 1, count, width)
        )
        return piece.reshape(count, width)

    def swap_core(field, start, count):
        paired = fields.reshape(2, 4, 2, rows, width)
        piece = lax.dynamic_slice(
            paired, (field, 0, 1 - (me & 1), start, 0), (1, 4, 1, count, width)
        )
        return swap_span(piece.reshape(4, count, width), 1)

    def core_rows(core, start, count, distance):
        plane = (me ^ distance) >> 1
        piece = lax.dynamic_slice(core, (plane, start, 0), (1, count, width))
        return piece.reshape(count, width)

    def away_direct(core, field, start, count):
        return [
            jnp.stack([plane_rows(field, start, count, d), core_rows(core, 0, count, d)])
            for d in (2, 4, 6)
        ]

    def swap_direct(away):
        return [swap_span(value, distance) for value, distance in zip(away, (2, 4, 6))]

    def direct_cells(core, inner, arrays):
        return [(core, None, inner)] + [(array, 2, inner) for array in arrays]

    def away_x(core, inner, count):
        rows_of = (inner * BLOCK, count * BLOCK)
        return jnp.stack(
            [cells_of(d) for d in (2, 6) for cells_of in (
                lambda d: plane_rows(1, *rows_of, d),
                lambda d: core_rows(core, *rows_of, d),
            )]
        )

    def away_z(core, inner, other_x, place):
        rows_of = (inner * BLOCK, BLOCK)
        away = [plane_rows(1, *rows_of, 4)[None], core_rows(core, *rows_of, 4)[None]]
        away += [other_x[2:, place * BLOCK : (place + 1) * BLOCK]]
        return jnp.concatenate(away)

    def share(kept, came):
        return kept[:4] + came[:4], swap_span(kept[4:] + came[4:], 4)

    def finish(near, from_z):
        others = []
        for distance in range(1, 4):
            away = jnp.stack([near[distance], from_z[distance]])
            others.append(swap_span(away, distance))
        return gather_planes(place_keep, near, from_z, others)

    def tie(*values):
        return lax.optimization_barrier(values)

    def sums(place, unit):
        step = modes // PARTS
        parts = [step * count for count in LAST_PARTS] if unit == last else [modes]
        return half_sums(place, *units[unit], fields, cells[unit], tables, parts)

    cells = {}
    sent, kept, came, mine, other = {}, {}, {}, {}, {}
    core_a = swap_core(0, 0, 2 * BLOCK)
    arrays = swap_direct(away_direct(core_a, 0, 0, 2 * BLOCK))
    cells[0] = direct_cells(core_a, 0, arrays)
    sent[0] = sums(place_send, 0)
    sent[0], me = tie(sent[0], me)
    matrices = (inverse, eigen_vectors, factor)
    other_x = {}
    result = None
    for step in range(last):
        came[step] = swap_span(sent[step][0], HALF)
        extra = {}
        if step == 0:
            core_b = swap_core(0, 2 * BLOCK, BLOCK)
            core_c = swap_core(1, 0, rows)
            away = [away_direct(core_b, 0, 2 * BLOCK, BLOCK), away_x(core_c, 0, 1)]
            away, arrays = tie(away, arrays)
            cells[0] = direct_cells(core_a, 0, arrays)
            cells[1] = direct_cells(core_a, 1, arrays)
            extra["direct"] = swap_direct(away[0])
            extra["x"] = swap_span(away[1], 2)
            extra["away_x"] = away_x(core_c, 1, 2)
            kept[0] = sums(place_keep, 0)
        if step == 1:
            extra["x"] = swap_span(later_x, 2)
        sent[step + 1] = sums(place_send, step + 1)
        kept[step + 1] = sums(place_keep, step + 1)
        if step >= 1:
            near, from_z = share(kept[step - 1][0], came[step - 1])
            if step <= 3:
                unit = step + 2
                inner = unit - per_field
                source, place = (other_x[0], 0) if inner == 0 else (other_x[1], inner - 1)
                away, from_z = tie(away_z(core_c, inner, source, place), from_z)
                extra["z"] = swap_span(away, 4)
                cells[unit] = [(core_c, None, inner), (source, 2, place)]
            from_z, sent[step + 1], kept[step + 1] = tie(
                from_z, sent[step + 1], kept[step + 1]
            )
            extra["mine"] = finish(near, from_z)
        if step >= 2:
            extra["other"] = swap_rad(mine[step - 2])
        came[step], sent[step + 1], kept[step + 1], extra = tie(
            came[step], sent[step + 1], kept[step + 1], extra
        )
        if "direct" in extra:
            cells[2] = direct_cells(core_b, 0, extra["direct"])
            later_x = extra["away_x"]
        if "x" in extra:
            other_x[step] = extra["x"]
        if "z" in extra:
            cells[step + 2].append((extra["z"], 4, 0))
        if step >= 1:
            mine[step - 1] = extra["mine"]
        if step >= 2:
            other[step - 2] = extra["other"]

    def blocks_of(numbers, part=None):
        chosen = [mine[n] if n != last else mine[n][part] for n in numbers]
        return chosen + [other[n] if n != last else other[n][part] for n in numbers]

    came[last] = [swap_span(part, HALF) for part in sent[last]]
    other[last - 2] = swap_rad(mine[last - 2])
    near, from_z = share(kept[last - 1][0], came[last - 1])
    result = solve(place_keep, 0, 0, PARTS, blocks_of(range(per_field)), *matrices, None)
    from_z, result = tie(from_z, result)
    mine[last - 1] = finish(near, from_z)
    came[last][0], mine[last - 1], other[last - 2], result = tie(
        came[last][0], mine[last - 1], other[last - 2], result
    )
    other[last - 1] = swap_rad(mine[last - 1])
    first = finish(*share(kept[last][0], came[last][0]))
    first, came[last][1], other[last - 1] = tie(first, came[last][1], other[last - 1])
    other_first = swap_rad(first)
    second = finish(*share(kept[last][1], came[last][1]))
    second, other_first = tie(second, other_first)
    mine[last] = [first, second]
    other[last] = [other_first, swap_rad(second)]
    start = 0
    for part, count in enumerate(LAST_PARTS):
        blocks = blocks_of(range(per_field, total), part)
        result = solve(place_keep, 1, start, count, blocks, *matrices, result)
        start += count
    return result[None, None]


def solution(mesh):
    placed = (P(None, None, "rad", "span"), P(None, "span"), P(), P(), P(), P())
    halves = mesh.shape["span"] == 2 * HALF and mesh.shape["rad"] == 2
    return jax.shard_map(
        on_device_halves if halves else on_device_any,
        mesh=mesh,
        in_specs=placed,
        out_specs=P("span", "rad", None, None, None, None, None),
        check_vma=False,
    )
```

```python
import functools
import math

import jax
import jax.numpy as jnp
import numpy as np
from jax import lax
from jax.experimental import pallas as pl
from jax.experimental.pallas import tpu as pltpu
from jax.sharding import PartitionSpec as P

KEEP = 2688


precise = lax.Precision.HIGHEST
contract_rows = (((1,), (1,)), ((), ()))


def partner_2(value, axis, distance):
    mask = 2**distance
    pairs = [(source, source ^ mask) for source in range(lax.axis_size(axis))]
    return lax.ppermute(value, axis, pairs)


def bit_reverse(value, bit_count):
    flipped = jnp.zeros_like(value)
    for section_bit in range(bit_count):
        flipped = flipped + (value >> section_bit & 1) * 2 ** (bit_count - 1 - section_bit)
    return flipped


def section_angles(device, section_bit):
    upper_half = device >> section_bit & 1 == 1
    twiddle_index = jnp.where(upper_half, device % 2**section_bit, 0)
    angles = twiddle_index.astype(jnp.float32) * (2.0 * math.pi / 2 ** (section_bit + 1))
    sign_factor = jnp.where(upper_half, -1.0, 1.0).astype(jnp.float32)
    return (sign_factor, jnp.cos(angles), jnp.sin(angles))


def butterfly(fields, bit_count):
    device = lax.axis_index("span")
    top_bit = bit_count - 1
    partner = partner_2(fields, "span", top_bit)
    sign_factor, cosine, sine_value = section_angles(device, top_bit)
    difference = partner + sign_factor * fields
    real_part = difference * cosine
    imag_part = -difference * sine_value
    for section_bit in range(bit_count - 2, -1, -1):
        other_real, other_imag = partner_2((real_part, imag_part), "span", section_bit)
        sign_factor, cosine, sine_value = section_angles(device, section_bit)
        diff_real = other_real + sign_factor * real_part
        diff_imag = other_imag + sign_factor * imag_part
        real_part = diff_real * cosine + diff_imag * sine_value
        imag_part = diff_imag * cosine - diff_real * sine_value
    return (real_part, imag_part)


def mode_transform(real_part, imag_part, bit_count):
    groups = lax.axis_size("span")
    line_width = real_part.shape[3]
    full_length = line_width * groups
    kept_modes = KEEP // groups
    residue = bit_reverse(lax.axis_index("span"), bit_count)
    mode_index = residue + groups * jnp.arange(kept_modes, dtype=jnp.int32)
    phases = mode_index[:, None] * jnp.arange(line_width, dtype=jnp.int32)[None, :] % full_length
    angles = phases.astype(jnp.float32) * (2.0 * math.pi / full_length)
    normalizer = 1.0 / math.sqrt(full_length)
    cosine_table = jnp.cos(angles) * normalizer
    sine_table = jnp.sin(angles) * normalizer
    line_real = real_part.reshape(-1, line_width)
    line_imag = imag_part.reshape(-1, line_width)
    cos_real = lax.dot_general(cosine_table, line_real, contract_rows, precision=precise)
    cos_imag = lax.dot_general(cosine_table, line_imag, contract_rows, precision=precise)
    sin_real = lax.dot_general(sine_table, line_real, contract_rows, precision=precise)
    sin_imag = lax.dot_general(sine_table, line_imag, contract_rows, precision=precise)
    return (jnp.stack([cos_real + sin_imag, cos_imag - sin_real]), mode_index)


def placement_table(column, group_count, capacity):
    groups = jnp.arange(group_count, dtype=jnp.int32)
    member = (column[None, :] == groups[:, None]).astype(jnp.int32)
    ranking = jnp.cumsum(member, axis=1, dtype=jnp.int32) - member
    slot_index = jnp.arange(capacity, dtype=jnp.int32)
    return member[None] * (ranking[None] == slot_index[:, None, None])


def damping_factor(half_step, decay, wave_index):
    wave_square = (wave_index.astype(jnp.float32) * (math.pi / KEEP)) ** 2
    damping = half_step[None, :, None] * (decay[None, :, :] + wave_square[:, None, None])
    return (1.0 - damping) / (1.0 + damping)


def on_device_any(fields, mode_group, half_step, decay, eigen_inverse, eigen_vectors):
    bit_count = lax.axis_size("span").bit_length() - 1
    real_part, imag_part = butterfly(fields, bit_count)
    spectra, mode_index = mode_transform(real_part, imag_part, bit_count)
    kept_modes = spectra.shape[1]
    group_count = lax.axis_size("rad")
    capacity = min(kept_modes, 2 * kept_modes // group_count)
    planes = fields.shape[1]
    radial_rows = fields.shape[2]
    arranged = spectra.reshape(2, kept_modes, 2, planes, radial_rows)
    placing = placement_table(mode_group[:, 0], group_count, capacity)
    placing_float = placing.astype(jnp.float32)
    packed = jnp.einsum("sgb,cbfal->scfagl", placing_float, arranged, precision=precise)
    packed = packed.reshape(capacity, 2, 2, planes, group_count * radial_rows)
    regrouped = lax.all_to_all(packed, "rad", split_axis=4, concat_axis=4, tiled=True)
    own_slots = lax.dynamic_index_in_dim(placing, lax.axis_index("rad"), 1, keepdims=False)
    slot_modes = jnp.sum(own_slots * mode_index[None, :], axis=1)
    factor = damping_factor(half_step, decay, slot_modes)
    inner_part = jnp.einsum("scfar,fir->scfai", regrouped, eigen_inverse, precision=precise)
    inner_part = inner_part * factor[:, None, :, None, :]
    result = jnp.einsum("scfai,fri->scfar", inner_part, eigen_vectors, precision=precise)
    return result.reshape(1, 1, capacity, 2, 2, planes, group_count * radial_rows)


HALF = 8
BLOCK = 64
PARTS = 3
LAST_PARTS = (2, 1)
VMEM_BYTES = 24 * 1024 * 1024


def flip3(value):
    return (value & 1) << 2 | value & 2 | value >> 2


def swap_span(value, distance):
    pairs = [(source, source ^ distance) for source in range(lax.axis_size("span"))]
    return lax.ppermute(value, "span", pairs)


def swap_rad(value):
    return lax.ppermute(value, "rad", [(0, 1), (1, 0)])


def split_pair(value):
    high = value.astype(jnp.bfloat16)
    low = (value - high.astype(jnp.float32)).astype(jnp.bfloat16)
    return high, low


def dot_rows(left, right):
    return lax.dot_general(left, right, contract_rows, preferred_element_type=jnp.float32)


def dot_split(left, right):
    left_high, left_low = left
    right_high, right_low = right
    total = dot_rows(left_high, right_high)
    total = total + dot_rows(left_low, right_high)
    return total + dot_rows(left_high, right_low)


def transform_8(real, imag):
    root = math.sqrt(0.5)
    er, ei, orr, oi = [], [], [], []
    for j in range(4):
        er.append(real[j] + real[j + 4])
        ei.append(imag[j] + imag[j + 4])
        dr = real[j] - real[j + 4]
        di = imag[j] - imag[j + 4]
        if j == 0:
            orr.append(dr)
            oi.append(di)
        elif j == 1:
            orr.append((dr + di) * root)
            oi.append((di - dr) * root)
        elif j == 2:
            orr.append(di)
            oi.append(-dr)
        else:
            orr.append((di - dr) * root)
            oi.append((-di - dr) * root)

    def transform_4(r, i):
        ar, ai = r[0] + r[2], i[0] + i[2]
        br, bi = r[0] - r[2], i[0] - i[2]
        cr, ci = r[1] + r[3], i[1] + i[3]
        dr, di = r[1] - r[3], i[1] - i[3]
        return [(ar + cr, ai + ci), (br + di, bi - dr), (ar - cr, ai - ci), (br - di, bi + dr)]

    even = transform_4(er, ei)
    odd = transform_4(orr, oi)
    return [even[q // 2] if q % 2 == 0 else odd[q // 2] for q in range(8)]


def half_sums_kernel(counts, place, *refs):
    cells, refs = refs[: len(counts)], refs[len(counts) :]
    cos_turn, sin_turn, table_rows = refs[:3]
    outs, (ordered, high, low) = refs[3:-3], refs[-3:]
    me, parity = place[0], place[1]
    sign = place[2].astype(jnp.float32)
    width = ordered.shape[-1]
    distance = 0
    for ref, count in zip(cells, counts):
        for index in range(count):
            ordered[me ^ distance] = ref[index]
            distance += 1

    turn_real, turn_imag = [], []
    for j in range(HALF):
        angle = 2.0 * math.pi * j / 16
        turn_real.append(sign * jnp.where(parity == 1, math.cos(angle), 1.0))
        turn_imag.append(sign * jnp.where(parity == 1, -math.sin(angle), 0.0))

    def one_block(step, carry):
        rows = pl.ds(pl.multiple_of(step * 16, 16), 16)
        lower = pl.ds(pl.multiple_of(BLOCK + step * 16, 16), 16)
        for lane in range(0, width, 128):
            real, imag = [], []
            for j in range(HALF):
                value = ordered[j, rows, lane : lane + 128]
                real.append(value * turn_real[j])
                imag.append(value * turn_imag[j])
            sums = transform_8(real, imag)
            for q in range(HALF):
                sum_real, sum_imag = sums[q]
                cosine = cos_turn[parity, q : q + 1, lane : lane + 128]
                sine = sin_turn[parity, q : q + 1, lane : lane + 128]
                real_high, real_low = split_pair(sum_real * cosine + sum_imag * sine)
                imag_high, imag_low = split_pair(sum_imag * cosine - sum_real * sine)
                high[q, rows, lane : lane + 128] = real_high
                high[q, rows, width + lane : width + lane + 128] = imag_high
                high[q, lower, lane : lane + 128] = imag_high
                high[q, lower, width + lane : width + lane + 128] = -real_high
                low[q, rows, lane : lane + 128] = real_low
                low[q, rows, width + lane : width + lane + 128] = imag_low
                low[q, lower, lane : lane + 128] = imag_low
                low[q, lower, width + lane : width + lane + 128] = -real_low
        return carry

    lax.fori_loop(0, BLOCK // 16, one_block, 0)
    table = split_pair(table_rows[...])
    for q in range(0, HALF, 2):
        lines_high = high[q : q + 2].reshape(4 * BLOCK, 2 * width)
        lines_low = low[q : q + 2].reshape(4 * BLOCK, 2 * width)
        result = dot_split(table, (lines_high, lines_low))
        first = 0
        for out in outs:
            rows = slice(first, first + out.shape[1])
            out[me ^ flip3(q)] = result[rows, : 2 * BLOCK]
            out[me ^ flip3(q + 1)] = result[rows, 2 * BLOCK :]
            first += out.shape[1]


def half_sums(place, cells, tables, parts):
    width = cells[0][0].shape[-1]
    rows = tables[2].shape[0]
    counts = [array.shape[0] if count is None else count for array, count, _ in cells]

    def full(array):
        return pl.BlockSpec(array.shape, lambda i: (0,) * array.ndim)

    def some(count, inner):
        return pl.BlockSpec((count, BLOCK, width), lambda i: (0, inner, 0))

    return pl.pallas_call(
        functools.partial(half_sums_kernel, counts),
        grid=(1,),
        out_shape=[
            jax.ShapeDtypeStruct((HALF, part, 2 * BLOCK), jnp.float32) for part in parts
        ],
        in_specs=[pl.BlockSpec(memory_space=pltpu.SMEM)]
        + [some(count, inner) for count, (_, _, inner) in zip(counts, cells)]
        + [full(table) for table in tables],
        out_specs=[
            pl.BlockSpec((HALF, part, 2 * BLOCK), lambda i: (0, 0, 0)) for part in parts
        ],
        scratch_shapes=[
            pltpu.VMEM((HALF, BLOCK, width), jnp.float32),
            pltpu.VMEM((HALF, 2 * BLOCK, 2 * width), jnp.bfloat16),
            pltpu.VMEM((HALF, 2 * BLOCK, 2 * width), jnp.bfloat16),
        ],
        cost_estimate=pl.CostEstimate(
            flops=rows * BLOCK * width,
            bytes_accessed=BLOCK * width * 4,
            transcendentals=0,
        ),
        compiler_params=pltpu.CompilerParams(vmem_limit_bytes=VMEM_BYTES),
        name="half_sums",
    )(place, *[array for array, _, _ in cells], *tables)


def gather_planes_kernel(place, *refs):
    own, from_z, out, ordered = refs[0], refs[1], refs[-2], refs[-1]
    me = place[0]
    ordered[me] = own[0]
    ordered[me ^ 4] = from_z[0]
    for distance in range(1, 4):
        for index in range(2):
            ordered[me ^ (distance + 4 * index)] = refs[1 + distance][index]
    for plane in range(HALF):
        out[:, plane, :] = ordered[plane]


def gather_planes(place, own, from_z, others):
    modes, lanes = own.shape[-2:]
    one = pl.BlockSpec((1, modes, lanes), lambda i: (0, 0, 0))
    two = pl.BlockSpec((2, modes, lanes), lambda i: (0, 0, 0))
    return pl.pallas_call(
        gather_planes_kernel,
        grid=(1,),
        out_shape=jax.ShapeDtypeStruct((modes, HALF, lanes), jnp.float32),
        in_specs=[pl.BlockSpec(memory_space=pltpu.SMEM), one, one, two, two, two],
        out_specs=pl.BlockSpec((modes, HALF, lanes), lambda i: (0, 0, 0)),
        scratch_shapes=[pltpu.VMEM((HALF, modes, lanes), jnp.float32)],
        cost_estimate=pl.CostEstimate(
            flops=0, bytes_accessed=8 * HALF * modes * lanes, transcendentals=0
        ),
        compiler_params=pltpu.CompilerParams(vmem_limit_bytes=VMEM_BYTES),
        name="gather_planes",
    )(place, own, from_z, *others)


def solve_kernel(count, place, *refs):
    blocks = refs[: 2 * count]
    inverse, vectors, factor = refs[2 * count : 2 * count + 3]
    out = refs[-1]
    modes = out.shape[0]
    radial = out.shape[-1]

    @pl.when(place[3] == 1)
    def _():
        inverse_pair = split_pair(inverse[0])
        vectors_pair = split_pair(vectors[0])
        scale = jnp.broadcast_to(factor[0][:, None, :], (modes, HALF, radial))
        scale = scale.reshape(modes * HALF, radial)
        whole = [block[...].reshape(modes * HALF, 2 * BLOCK) for block in blocks]
        for part in range(2):
            lanes = slice(part * BLOCK, (part + 1) * BLOCK)
            lines = jnp.concatenate([value[:, lanes] for value in whole], axis=1)
            inner = dot_split(split_pair(lines), inverse_pair) * scale
            solved = dot_split(split_pair(inner), vectors_pair)
            out[:, part, 0] = solved.reshape(modes, HALF, radial)

    @pl.when(place[3] != 1)
    def _():
        out[...] = jnp.zeros_like(out)


def solve(place, field, first, count, blocks, inverse, vectors, factor, earlier):
    modes = factor.shape[1]
    radial = inverse.shape[-1]
    step = modes // PARTS

    def lines(array):
        offset = first if array.shape[0] == modes else 0
        return pl.BlockSpec((step, HALF, 2 * BLOCK), lambda i: (offset + i, 0, 0))

    matrix = pl.BlockSpec((1, radial, radial), lambda i: (field, 0, 0))
    in_specs = [pl.BlockSpec(memory_space=pltpu.SMEM)] + [lines(block) for block in blocks]
    in_specs += [matrix, matrix]
    in_specs += [pl.BlockSpec((1, step, radial), lambda i: (field, first + i, 0))]
    operands = [place, *blocks, inverse, vectors, factor]
    aliases = {}
    if earlier is not None:
        aliases = {len(operands): 0}
        operands.append(earlier)
        in_specs.append(pl.BlockSpec(memory_space=pl.ANY))

    def kernel(*refs):
        kept = refs if earlier is None else refs[: len(operands) - 1] + refs[-1:]
        solve_kernel(len(blocks) // 2, *kept)

    return pl.pallas_call(
        kernel,
        grid=(count,),
        out_shape=jax.ShapeDtypeStruct((modes, 2, 2, HALF, radial), jnp.float32),
        in_specs=in_specs,
        out_specs=pl.BlockSpec(
            (step, 2, 1, HALF, radial), lambda i: (first + i, 0, field, 0, 0)
        ),
        input_output_aliases=aliases,
        cost_estimate=pl.CostEstimate(
            flops=count * modes * radial * radial,
            bytes_accessed=count * modes * radial,
            transcendentals=0,
        ),
        compiler_params=pltpu.CompilerParams(vmem_limit_bytes=VMEM_BYTES),
        name="solve",
    )(*operands)


def mode_tables(width, modes):
    cells = np.arange(width)
    residue = 2 * np.arange(HALF)[None, :, None] + np.arange(2)[:, None, None]
    turn = 2.0 * np.pi * residue * cells / (2 * HALF * width)
    padded = -(-modes // 16) * 16
    angle = 2.0 * np.pi * (np.arange(padded)[:, None] * cells[None, :] % width) / width
    table = np.concatenate([np.cos(angle), np.sin(angle)], axis=1)
    table = table / math.sqrt(2 * HALF * width)
    table[modes:] = 0.0
    return tuple(array.astype(np.float32) for array in (np.cos(turn), np.sin(turn), table))


def on_device_halves(fields, mode_group, half_step, decay, eigen_inverse, eigen_vectors):
    span = lax.axis_index("span")
    rad = lax.axis_index("rad")
    me = span & 7
    half = span >> 3
    rows = fields.shape[2]
    width = fields.shape[3]
    modes = KEEP // 16
    tables = mode_tables(width, modes)

    heavy = (mode_group[0, 0] == rad).astype(jnp.int32)
    one = jnp.ones_like(me)
    place_send = jnp.stack([me, 1 - half, one, heavy])
    place_keep = jnp.stack([me, half, 1 - 2 * half, heavy])

    mode_index = bit_reverse(span, 4) + 16 * jnp.arange(modes, dtype=jnp.int32)
    factor = damping_factor(half_step, decay, mode_index).transpose(1, 0, 2)
    own = lax.dynamic_slice_in_dim(eigen_inverse, rad * rows, rows, 2)
    other = lax.dynamic_slice_in_dim(eigen_inverse, (1 - rad) * rows, rows, 2)
    inverse = jnp.concatenate([own, other], axis=2)

    units = [(field, block) for field in range(2) for block in range(rows // BLOCK)]
    total = len(units)
    per_field = rows // BLOCK
    last = total - 1

    def plane_rows(field, start, count, distance):
        piece = lax.dynamic_slice(
            fields, (field, me ^ distance, start, 0), (1, 1, count, width)
        )
        return piece.reshape(count, width)

    def swap_core(field, start, count):
        paired = fields.reshape(2, 4, 2, rows, width)
        piece = lax.dynamic_slice(
            paired, (field, 0, 1 - (me & 1), start, 0), (1, 4, 1, count, width)
        )
        return swap_span(piece.reshape(4, count, width), 1)

    def core_rows(core, start, count, distance):
        plane = (me ^ distance) >> 1
        piece = lax.dynamic_slice(core, (plane, start, 0), (1, count, width))
        return piece.reshape(count, width)

    def away_direct(core, field, start, count):
        return [
            jnp.stack([plane_rows(field, start, count, d), core_rows(core, start, count, d)])
            for d in (2, 4, 6)
        ]

    def swap_direct(away):
        return [swap_span(value, distance) for value, distance in zip(away, (2, 4, 6))]

    def near_cells(core, field, start, core_start):
        mine = plane_rows(field, start, BLOCK, 0)
        return [(mine[None], 1, 0), (core_rows(core, core_start, BLOCK, 0)[None], 1, 0)]

    def away_x(core, inner):
        away = []
        for distance in (2, 6):
            away.append(plane_rows(1, inner * BLOCK, BLOCK, distance))
            away.append(core_rows(core, 0, BLOCK, distance))
        return jnp.stack(away)

    def away_z(core, inner, from_x):
        away = [plane_rows(1, inner * BLOCK, BLOCK, 4)[None]]
        away += [core_rows(core, 0, BLOCK, 4)[None]]
        return jnp.concatenate(away + [from_x[2:]])

    def share(kept, came):
        return kept[:4] + came[:4], swap_span(kept[4:] + came[4:], 4)

    def finish(near, from_z):
        others = []
        for distance in range(1, 4):
            away = jnp.stack([near[distance], from_z[distance]])
            others.append(swap_span(away, distance))
        return gather_planes(place_keep, near, from_z, others)

    def tie(*values):
        return lax.optimization_barrier(values)

    def sums(place, unit):
        step = modes // PARTS
        parts = [step * count for count in LAST_PARTS] if unit == last else [modes]
        return half_sums(place, cells[unit], tables, parts)

    cells = {}
    sent, kept, came, mine, other = {}, {}, {}, {}, {}
    def direct_unit(core, unit, away):
        start = units[unit][1] * BLOCK
        arrays = swap_direct(away)
        return near_cells(core, 0, start, start) + [(array, 2, 0) for array in arrays]

    core_a = swap_core(0, 0, rows)
    away = [away_direct(core_a, 0, n * BLOCK, BLOCK) for n in range(per_field)]
    cells[0] = direct_unit(core_a, 0, away[0])
    sent[0] = sums(place_send, 0)
    core_c = [swap_core(1, 0, BLOCK)]
    sent[0], me, away, core_c = tie(sent[0], me, away, core_c)
    matrices = (inverse, eigen_vectors, factor)
    from_x = {}
    result = None
    for step in range(last):
        came[step] = swap_span(sent[step][0], HALF)
        extra = {}
        if step == 0:
            cells[1] = direct_unit(core_a, 1, away[1])
            first = [array for array, _, _ in cells[1]]
            kept[0] = sums(place_keep, 0)
            first, away[2], kept[0] = tie(first, away[2], kept[0])
            cells[1] = [(array, *cell[1:]) for array, cell in zip(first, cells[1])]
            extra["direct"] = swap_direct(away[2])
            extra["core"] = core_c + [swap_core(1, inner * BLOCK, BLOCK) for inner in (1, 2)]
        if 1 <= step <= 3:
            unit = step + 2
            inner = unit - per_field
            if step == 1:
                from_x[unit] = swap_span(away_x(core_c[0], 0), 2)
            if step < 3:
                extra["x"] = swap_span(away_x(core_c[inner + 1], inner + 1), 2)
        if step != 3:
            sent[step + 1] = sums(place_send, step + 1)
            kept[step + 1] = sums(place_keep, step + 1)
        if step >= 1:
            near, from_z = share(kept[step - 1][0], came[step - 1])
            away = away_z(core_c[inner], inner, from_x[unit]) if step <= 3 else []
            if step == 3:
                from_z, away = tie(from_z, away)
                arrays, from_z = tie([cell[0] for cell in cells[step + 1]], from_z)
                cells[step + 1] = [
                    (array, *cell[1:]) for array, cell in zip(arrays, cells[step + 1])
                ]
                sent[step + 1] = sums(place_send, step + 1)
                kept[step + 1] = sums(place_keep, step + 1)
            else:
                from_z, away, sent[step + 1], kept[step + 1] = tie(
                    from_z, away, sent[step + 1], kept[step + 1]
                )
            if step <= 3:
                extra["z"] = swap_span(away, 4)
                cells[unit] = near_cells(core_c[inner], 1, inner * BLOCK, 0)
                cells[unit] += [(from_x[unit], 2, 0)]
            extra["mine"] = finish(near, from_z)
        if step >= 2:
            extra["other"] = swap_rad(mine[step - 2])
        came[step], sent[step + 1], kept[step + 1], extra = tie(
            came[step], sent[step + 1], kept[step + 1], extra
        )
        if "direct" in extra:
            arrays = [(array, 2, 0) for array in extra["direct"]]
            cells[2] = near_cells(core_a, 0, 2 * BLOCK, 2 * BLOCK) + arrays
            core_c = extra["core"]
        if "x" in extra:
            from_x[step + 3] = extra["x"]
        if "z" in extra:
            cells[step + 2].append((extra["z"], 4, 0))
        if step >= 1:
            mine[step - 1] = extra["mine"]
        if step >= 2:
            other[step - 2] = extra["other"]

    def blocks_of(numbers, part=None):
        chosen = [mine[n] if n != last else mine[n][part] for n in numbers]
        return chosen + [other[n] if n != last else other[n][part] for n in numbers]

    came[last] = [swap_span(part, HALF) for part in sent[last]]
    other[last - 2] = swap_rad(mine[last - 2])
    near, from_z = share(kept[last - 1][0], came[last - 1])
    blocks = blocks_of(range(per_field))
    result = solve(place_keep, 0, 0, 2, blocks, *matrices, None)
    from_z, result = tie(from_z, result)
    mine[last - 1] = finish(near, from_z)
    came[last][0], mine[last - 1], other[last - 2], result = tie(
        came[last][0], mine[last - 1], other[last - 2], result
    )
    other[last - 1] = swap_rad(mine[last - 1])
    near, from_z = share(kept[last][0], came[last][0])
    result = solve(place_keep, 0, 2, 1, blocks, *matrices, result)
    from_z, result = tie(from_z, result)
    first = finish(near, from_z)
    first, came[last][1], other[last - 1] = tie(first, came[last][1], other[last - 1])
    other_first = swap_rad(first)
    second = finish(*share(kept[last][1], came[last][1]))
    second, other_first = tie(second, other_first)
    mine[last] = [first, second]
    other[last] = [other_first, swap_rad(second)]
    start = 0
    for part, count in enumerate(LAST_PARTS):
        blocks = blocks_of(range(per_field, total), part)
        result = solve(place_keep, 1, start, count, blocks, *matrices, result)
        start += count
    return result[None, None]


def solution(mesh):
    placed = (P(None, None, "rad", "span"), P(None, "span"), P(), P(), P(), P())
    halves = mesh.shape["span"] == 2 * HALF and mesh.shape["rad"] == 2
    return jax.shard_map(
        on_device_halves if halves else on_device_any,
        mesh=mesh,
        in_specs=placed,
        out_specs=P("span", "rad", None, None, None, None, None),
        check_vma=False,
    )
```

```python
import functools
import math

import jax
import jax.numpy as jnp
import numpy as np
from jax import lax
from jax.experimental import pallas as pl
from jax.experimental.pallas import tpu as pltpu
from jax.sharding import PartitionSpec as P

KEEP = 2688


precise = lax.Precision.HIGHEST
contract_rows = (((1,), (1,)), ((), ()))


def partner_2(value, axis, distance):
    mask = 2**distance
    pairs = [(source, source ^ mask) for source in range(lax.axis_size(axis))]
    return lax.ppermute(value, axis, pairs)


def bit_reverse(value, bit_count):
    flipped = jnp.zeros_like(value)
    for section_bit in range(bit_count):
        flipped = flipped + (value >> section_bit & 1) * 2 ** (bit_count - 1 - section_bit)
    return flipped


def section_angles(device, section_bit):
    upper_half = device >> section_bit & 1 == 1
    twiddle_index = jnp.where(upper_half, device % 2**section_bit, 0)
    angles = twiddle_index.astype(jnp.float32) * (2.0 * math.pi / 2 ** (section_bit + 1))
    sign_factor = jnp.where(upper_half, -1.0, 1.0).astype(jnp.float32)
    return (sign_factor, jnp.cos(angles), jnp.sin(angles))


def butterfly(fields, bit_count):
    device = lax.axis_index("span")
    top_bit = bit_count - 1
    partner = partner_2(fields, "span", top_bit)
    sign_factor, cosine, sine_value = section_angles(device, top_bit)
    difference = partner + sign_factor * fields
    real_part = difference * cosine
    imag_part = -difference * sine_value
    for section_bit in range(bit_count - 2, -1, -1):
        other_real, other_imag = partner_2((real_part, imag_part), "span", section_bit)
        sign_factor, cosine, sine_value = section_angles(device, section_bit)
        diff_real = other_real + sign_factor * real_part
        diff_imag = other_imag + sign_factor * imag_part
        real_part = diff_real * cosine + diff_imag * sine_value
        imag_part = diff_imag * cosine - diff_real * sine_value
    return (real_part, imag_part)


def mode_transform(real_part, imag_part, bit_count):
    groups = lax.axis_size("span")
    line_width = real_part.shape[3]
    full_length = line_width * groups
    kept_modes = KEEP // groups
    residue = bit_reverse(lax.axis_index("span"), bit_count)
    mode_index = residue + groups * jnp.arange(kept_modes, dtype=jnp.int32)
    phases = mode_index[:, None] * jnp.arange(line_width, dtype=jnp.int32)[None, :] % full_length
    angles = phases.astype(jnp.float32) * (2.0 * math.pi / full_length)
    normalizer = 1.0 / math.sqrt(full_length)
    cosine_table = jnp.cos(angles) * normalizer
    sine_table = jnp.sin(angles) * normalizer
    line_real = real_part.reshape(-1, line_width)
    line_imag = imag_part.reshape(-1, line_width)
    cos_real = lax.dot_general(cosine_table, line_real, contract_rows, precision=precise)
    cos_imag = lax.dot_general(cosine_table, line_imag, contract_rows, precision=precise)
    sin_real = lax.dot_general(sine_table, line_real, contract_rows, precision=precise)
    sin_imag = lax.dot_general(sine_table, line_imag, contract_rows, precision=precise)
    return (jnp.stack([cos_real + sin_imag, cos_imag - sin_real]), mode_index)


def placement_table(column, group_count, capacity):
    groups = jnp.arange(group_count, dtype=jnp.int32)
    member = (column[None, :] == groups[:, None]).astype(jnp.int32)
    ranking = jnp.cumsum(member, axis=1, dtype=jnp.int32) - member
    slot_index = jnp.arange(capacity, dtype=jnp.int32)
    return member[None] * (ranking[None] == slot_index[:, None, None])


def damping_factor(half_step, decay, wave_index):
    wave_square = (wave_index.astype(jnp.float32) * (math.pi / KEEP)) ** 2
    damping = half_step[None, :, None] * (decay[None, :, :] + wave_square[:, None, None])
    return (1.0 - damping) / (1.0 + damping)


def on_device_any(fields, mode_group, half_step, decay, eigen_inverse, eigen_vectors):
    bit_count = lax.axis_size("span").bit_length() - 1
    real_part, imag_part = butterfly(fields, bit_count)
    spectra, mode_index = mode_transform(real_part, imag_part, bit_count)
    kept_modes = spectra.shape[1]
    group_count = lax.axis_size("rad")
    capacity = min(kept_modes, 2 * kept_modes // group_count)
    planes = fields.shape[1]
    radial_rows = fields.shape[2]
    arranged = spectra.reshape(2, kept_modes, 2, planes, radial_rows)
    placing = placement_table(mode_group[:, 0], group_count, capacity)
    placing_float = placing.astype(jnp.float32)
    packed = jnp.einsum("sgb,cbfal->scfagl", placing_float, arranged, precision=precise)
    packed = packed.reshape(capacity, 2, 2, planes, group_count * radial_rows)
    regrouped = lax.all_to_all(packed, "rad", split_axis=4, concat_axis=4, tiled=True)
    own_slots = lax.dynamic_index_in_dim(placing, lax.axis_index("rad"), 1, keepdims=False)
    slot_modes = jnp.sum(own_slots * mode_index[None, :], axis=1)
    factor = damping_factor(half_step, decay, slot_modes)
    inner_part = jnp.einsum("scfar,fir->scfai", regrouped, eigen_inverse, precision=precise)
    inner_part = inner_part * factor[:, None, :, None, :]
    result = jnp.einsum("scfai,fri->scfar", inner_part, eigen_vectors, precision=precise)
    return result.reshape(1, 1, capacity, 2, 2, planes, group_count * radial_rows)


HALF = 8
BLOCK = 64
PARTS = 3
LAST_PARTS = (2, 1)
VMEM_BYTES = 24 * 1024 * 1024


def flip3(value):
    return (value & 1) << 2 | value & 2 | value >> 2


def swap_span(value, distance):
    pairs = [(source, source ^ distance) for source in range(lax.axis_size("span"))]
    return lax.ppermute(value, "span", pairs)


def swap_rad(value):
    return lax.ppermute(value, "rad", [(0, 1), (1, 0)])


def split_pair(value):
    high = value.astype(jnp.bfloat16)
    low = (value - high.astype(jnp.float32)).astype(jnp.bfloat16)
    return high, low


def dot_rows(left, right):
    return lax.dot_general(left, right, contract_rows, preferred_element_type=jnp.float32)


def dot_split(left, right):
    left_high, left_low = left
    right_high, right_low = right
    total = dot_rows(left_high, right_high)
    total = total + dot_rows(left_low, right_high)
    return total + dot_rows(left_high, right_low)


def transform_8(real, imag):
    root = math.sqrt(0.5)
    er, ei, orr, oi = [], [], [], []
    for j in range(4):
        er.append(real[j] + real[j + 4])
        ei.append(imag[j] + imag[j + 4])
        dr = real[j] - real[j + 4]
        di = imag[j] - imag[j + 4]
        if j == 0:
            orr.append(dr)
            oi.append(di)
        elif j == 1:
            orr.append((dr + di) * root)
            oi.append((di - dr) * root)
        elif j == 2:
            orr.append(di)
            oi.append(-dr)
        else:
            orr.append((di - dr) * root)
            oi.append((-di - dr) * root)

    def transform_4(r, i):
        ar, ai = r[0] + r[2], i[0] + i[2]
        br, bi = r[0] - r[2], i[0] - i[2]
        cr, ci = r[1] + r[3], i[1] + i[3]
        dr, di = r[1] - r[3], i[1] - i[3]
        return [(ar + cr, ai + ci), (br + di, bi - dr), (ar - cr, ai - ci), (br - di, bi + dr)]

    even = transform_4(er, ei)
    odd = transform_4(orr, oi)
    return [even[q // 2] if q % 2 == 0 else odd[q // 2] for q in range(8)]


def half_sums_kernel(counts, place, *refs):
    cells, refs = refs[: len(counts)], refs[len(counts) :]
    cos_turn, sin_turn, table_rows = refs[:3]
    outs, (ordered, high, low) = refs[3:-3], refs[-3:]
    me, parity = place[0], place[1]
    sign = place[2].astype(jnp.float32)
    width = ordered.shape[-1]
    distance = 0
    for ref, count in zip(cells, counts):
        for index in range(count):
            ordered[me ^ distance] = ref[index]
            distance += 1

    turn_real, turn_imag = [], []
    for j in range(HALF):
        angle = 2.0 * math.pi * j / 16
        turn_real.append(sign * jnp.where(parity == 1, math.cos(angle), 1.0))
        turn_imag.append(sign * jnp.where(parity == 1, -math.sin(angle), 0.0))

    def one_block(step, carry):
        rows = pl.ds(pl.multiple_of(step * 16, 16), 16)
        lower = pl.ds(pl.multiple_of(BLOCK + step * 16, 16), 16)
        for lane in range(0, width, 128):
            real, imag = [], []
            for j in range(HALF):
                value = ordered[j, rows, lane : lane + 128]
                real.append(value * turn_real[j])
                imag.append(value * turn_imag[j])
            sums = transform_8(real, imag)
            for q in range(HALF):
                sum_real, sum_imag = sums[q]
                cosine = cos_turn[parity, q : q + 1, lane : lane + 128]
                sine = sin_turn[parity, q : q + 1, lane : lane + 128]
                real_high, real_low = split_pair(sum_real * cosine + sum_imag * sine)
                imag_high, imag_low = split_pair(sum_imag * cosine - sum_real * sine)
                high[q, rows, lane : lane + 128] = real_high
                high[q, rows, width + lane : width + lane + 128] = imag_high
                high[q, lower, lane : lane + 128] = imag_high
                high[q, lower, width + lane : width + lane + 128] = -real_high
                low[q, rows, lane : lane + 128] = real_low
                low[q, rows, width + lane : width + lane + 128] = imag_low
                low[q, lower, lane : lane + 128] = imag_low
                low[q, lower, width + lane : width + lane + 128] = -real_low
        return carry

    lax.fori_loop(0, BLOCK // 16, one_block, 0)
    table = split_pair(table_rows[...])
    for q in range(0, HALF, 2):
        lines_high = high[q : q + 2].reshape(4 * BLOCK, 2 * width)
        lines_low = low[q : q + 2].reshape(4 * BLOCK, 2 * width)
        result = dot_split(table, (lines_high, lines_low))
        first = 0
        for out in outs:
            rows = slice(first, first + out.shape[1])
            out[me ^ flip3(q)] = result[rows, : 2 * BLOCK]
            out[me ^ flip3(q + 1)] = result[rows, 2 * BLOCK :]
            first += out.shape[1]


def half_sums(place, cells, tables, parts):
    width = cells[0][0].shape[-1]
    rows = tables[2].shape[0]
    counts = [array.shape[0] if count is None else count for array, count, _ in cells]

    def full(array):
        return pl.BlockSpec(array.shape, lambda i: (0,) * array.ndim)

    def some(count, inner):
        return pl.BlockSpec((count, BLOCK, width), lambda i: (0, inner, 0))

    return pl.pallas_call(
        functools.partial(half_sums_kernel, counts),
        grid=(1,),
        out_shape=[
            jax.ShapeDtypeStruct((HALF, part, 2 * BLOCK), jnp.float32) for part in parts
        ],
        in_specs=[pl.BlockSpec(memory_space=pltpu.SMEM)]
        + [some(count, inner) for count, (_, _, inner) in zip(counts, cells)]
        + [full(table) for table in tables],
        out_specs=[
            pl.BlockSpec((HALF, part, 2 * BLOCK), lambda i: (0, 0, 0)) for part in parts
        ],
        scratch_shapes=[
            pltpu.VMEM((HALF, BLOCK, width), jnp.float32),
            pltpu.VMEM((HALF, 2 * BLOCK, 2 * width), jnp.bfloat16),
            pltpu.VMEM((HALF, 2 * BLOCK, 2 * width), jnp.bfloat16),
        ],
        cost_estimate=pl.CostEstimate(
            flops=rows * BLOCK * width,
            bytes_accessed=BLOCK * width * 4,
            transcendentals=0,
        ),
        compiler_params=pltpu.CompilerParams(vmem_limit_bytes=VMEM_BYTES),
        name="half_sums",
    )(place, *[array for array, _, _ in cells], *tables)


def gather_planes_kernel(place, *refs):
    own, from_z, out, ordered = refs[0], refs[1], refs[-2], refs[-1]
    me = place[0]
    ordered[me] = own[0]
    ordered[me ^ 4] = from_z[0]
    for distance in range(1, 4):
        for index in range(2):
            ordered[me ^ (distance + 4 * index)] = refs[1 + distance][index]
    for plane in range(HALF):
        out[:, plane, :] = ordered[plane]


def gather_planes(place, own, from_z, others):
    modes, lanes = own.shape[-2:]
    one = pl.BlockSpec((1, modes, lanes), lambda i: (0, 0, 0))
    two = pl.BlockSpec((2, modes, lanes), lambda i: (0, 0, 0))
    return pl.pallas_call(
        gather_planes_kernel,
        grid=(1,),
        out_shape=jax.ShapeDtypeStruct((modes, HALF, lanes), jnp.float32),
        in_specs=[pl.BlockSpec(memory_space=pltpu.SMEM), one, one, two, two, two],
        out_specs=pl.BlockSpec((modes, HALF, lanes), lambda i: (0, 0, 0)),
        scratch_shapes=[pltpu.VMEM((HALF, modes, lanes), jnp.float32)],
        cost_estimate=pl.CostEstimate(
            flops=0, bytes_accessed=8 * HALF * modes * lanes, transcendentals=0
        ),
        compiler_params=pltpu.CompilerParams(vmem_limit_bytes=VMEM_BYTES),
        name="gather_planes",
    )(place, own, from_z, *others)


def solve_kernel(count, place, *refs):
    blocks = refs[: 2 * count]
    inverse, vectors, factor = refs[2 * count : 2 * count + 3]
    out = refs[-1]
    modes = out.shape[0]
    radial = out.shape[-1]

    @pl.when(place[3] == 1)
    def _():
        inverse_pair = split_pair(inverse[0])
        vectors_pair = split_pair(vectors[0])
        scale = jnp.broadcast_to(factor[0][:, None, :], (modes, HALF, radial))
        scale = scale.reshape(modes * HALF, radial)
        whole = [block[...].reshape(modes * HALF, 2 * BLOCK) for block in blocks]
        for part in range(2):
            lanes = slice(part * BLOCK, (part + 1) * BLOCK)
            lines = jnp.concatenate([value[:, lanes] for value in whole], axis=1)
            inner = dot_split(split_pair(lines), inverse_pair) * scale
            solved = dot_split(split_pair(inner), vectors_pair)
            out[:, part, 0] = solved.reshape(modes, HALF, radial)

    @pl.when(place[3] != 1)
    def _():
        out[...] = jnp.zeros_like(out)


def solve(place, field, first, count, blocks, inverse, vectors, factor, earlier):
    modes = factor.shape[1]
    radial = inverse.shape[-1]
    step = modes // PARTS

    def lines(array):
        offset = first if array.shape[0] == modes else 0
        return pl.BlockSpec((step, HALF, 2 * BLOCK), lambda i: (offset + i, 0, 0))

    matrix = pl.BlockSpec((1, radial, radial), lambda i: (field, 0, 0))
    in_specs = [pl.BlockSpec(memory_space=pltpu.SMEM)] + [lines(block) for block in blocks]
    in_specs += [matrix, matrix]
    in_specs += [pl.BlockSpec((1, step, radial), lambda i: (field, first + i, 0))]
    operands = [place, *blocks, inverse, vectors, factor]
    aliases = {}
    if earlier is not None:
        aliases = {len(operands): 0}
        operands.append(earlier)
        in_specs.append(pl.BlockSpec(memory_space=pl.ANY))

    def kernel(*refs):
        kept = refs if earlier is None else refs[: len(operands) - 1] + refs[-1:]
        solve_kernel(len(blocks) // 2, *kept)

    return pl.pallas_call(
        kernel,
        grid=(count,),
        out_shape=jax.ShapeDtypeStruct((modes, 2, 2, HALF, radial), jnp.float32),
        in_specs=in_specs,
        out_specs=pl.BlockSpec(
            (step, 2, 1, HALF, radial), lambda i: (first + i, 0, field, 0, 0)
        ),
        input_output_aliases=aliases,
        cost_estimate=pl.CostEstimate(
            flops=count * modes * radial * radial,
            bytes_accessed=count * modes * radial,
            transcendentals=0,
        ),
        compiler_params=pltpu.CompilerParams(vmem_limit_bytes=VMEM_BYTES),
        name="solve",
    )(*operands)


def mode_tables(width, modes):
    cells = np.arange(width)
    residue = 2 * np.arange(HALF)[None, :, None] + np.arange(2)[:, None, None]
    turn = 2.0 * np.pi * residue * cells / (2 * HALF * width)
    padded = -(-modes // 16) * 16
    angle = 2.0 * np.pi * (np.arange(padded)[:, None] * cells[None, :] % width) / width
    table = np.concatenate([np.cos(angle), np.sin(angle)], axis=1)
    table = table / math.sqrt(2 * HALF * width)
    table[modes:] = 0.0
    return tuple(array.astype(np.float32) for array in (np.cos(turn), np.sin(turn), table))


def on_device_halves(fields, mode_group, half_step, decay, eigen_inverse, eigen_vectors):
    span = lax.axis_index("span")
    rad = lax.axis_index("rad")
    me = span & 7
    half = span >> 3
    rows = fields.shape[2]
    width = fields.shape[3]
    modes = KEEP // 16
    tables = mode_tables(width, modes)

    heavy = (mode_group[0, 0] == rad).astype(jnp.int32)
    one = jnp.ones_like(me)
    place_send = jnp.stack([me, 1 - half, one, heavy])
    place_keep = jnp.stack([me, half, 1 - 2 * half, heavy])

    mode_index = bit_reverse(span, 4) + 16 * jnp.arange(modes, dtype=jnp.int32)
    factor = damping_factor(half_step, decay, mode_index).transpose(1, 0, 2)
    own = lax.dynamic_slice_in_dim(eigen_inverse, rad * rows, rows, 2)
    other = lax.dynamic_slice_in_dim(eigen_inverse, (1 - rad) * rows, rows, 2)
    inverse = jnp.concatenate([own, other], axis=2)

    units = [(field, block) for field in range(2) for block in range(rows // BLOCK)]
    total = len(units)
    per_field = rows // BLOCK
    last = total - 1

    def plane_rows(field, start, count, distance):
        piece = lax.dynamic_slice(
            fields, (field, me ^ distance, start, 0), (1, 1, count, width)
        )
        return piece.reshape(count, width)

    def swap_core(field, start, count):
        paired = fields.reshape(2, 4, 2, rows, width)
        piece = lax.dynamic_slice(
            paired, (field, 0, 1 - (me & 1), start, 0), (1, 4, 1, count, width)
        )
        return swap_span(piece.reshape(4, count, width), 1)

    def core_rows(core, start, count, distance):
        plane = (me ^ distance) >> 1
        piece = lax.dynamic_slice(core, (plane, start, 0), (1, count, width))
        return piece.reshape(count, width)

    def away_direct(core, field, start, count):
        return [
            jnp.stack([plane_rows(field, start, count, d), core_rows(core, start, count, d)])
            for d in (2, 4, 6)
        ]

    def swap_direct(away):
        return [swap_span(value, distance) for value, distance in zip(away, (2, 4, 6))]

    def near_cells(core, field, start, core_start):
        mine = plane_rows(field, start, BLOCK, 0)
        return [(mine[None], 1, 0), (core_rows(core, core_start, BLOCK, 0)[None], 1, 0)]

    def away_x(core, inner):
        away = []
        for distance in (2, 6):
            away.append(plane_rows(1, inner * BLOCK, BLOCK, distance))
            away.append(core_rows(core, inner * BLOCK, BLOCK, distance))
        return jnp.stack(away)

    def away_z(core, inner, from_x):
        away = [plane_rows(1, inner * BLOCK, BLOCK, 4)[None]]
        away += [core_rows(core, inner * BLOCK, BLOCK, 4)[None]]
        return jnp.concatenate(away + [from_x[2:]])

    def share(kept, came):
        return kept[:4] + came[:4], swap_span(kept[4:] + came[4:], 4)

    def finish(near, from_z):
        others = []
        for distance in range(1, 4):
            away = jnp.stack([near[distance], from_z[distance]])
            others.append(swap_span(away, distance))
        return gather_planes(place_keep, near, from_z, others)

    def tie(*values):
        return lax.optimization_barrier(values)

    def sums(place, unit):
        step = modes // PARTS
        parts = [step * count for count in LAST_PARTS] if unit == last else [modes]
        return half_sums(place, cells[unit], tables, parts)

    cells = {}
    sent, kept, came, mine, other = {}, {}, {}, {}, {}
    def direct_unit(core, unit, arrays):
        start = units[unit][1] * BLOCK
        return near_cells(core, 0, start, start) + [(array, 2, 0) for array in arrays]

    core_a = swap_core(0, 0, rows)
    away = [away_direct(core_a, 0, n * BLOCK, BLOCK) for n in range(per_field)]
    direct = [swap_direct(away[0])]
    core_c = swap_core(1, 0, rows)
    for unit in range(1, per_field):
        away[unit], direct[unit - 1] = tie(away[unit], direct[unit - 1])
        direct.append(swap_direct(away[unit]))
    away_3, direct[1] = tie(away_x(core_c, 0), direct[1])
    for unit in range(per_field):
        cells[unit] = direct_unit(core_a, unit, direct[unit])
    sent[0] = sums(place_send, 0)
    sent[0], me, core_c = tie(sent[0], me, core_c)
    matrices = (inverse, eigen_vectors, factor)
    result = None
    for step in range(last):
        came[step] = swap_span(sent[step][0], HALF)
        extra = {}
        sent[step + 1] = sums(place_send, step + 1)
        kept[step + 1] = sums(place_keep, step + 1)
        if step == 0:
            kept[0] = sums(place_keep, 0)
            from_x = [swap_span(away_3, 2)]
            kept[0], direct[2], from_x[0] = tie(kept[0], direct[2], from_x[0])
            cells[2] = direct_unit(core_a, 2, direct[2])
        if 1 <= step <= 2:
            extra["x"] = swap_span(away_x(core_c, step), 2)
        if 1 <= step <= 3:
            unit = step + 2
            inner = unit - per_field
            extra["z"] = swap_span(away_z(core_c, inner, from_x[inner]), 4)
            cells[unit] = near_cells(core_c, 1, inner * BLOCK, inner * BLOCK)
            cells[unit] += [(from_x[inner], 2, 0)]
        if step >= 1:
            near, from_z = share(kept[step - 1][0], came[step - 1])
            from_z, sent[step + 1], kept[step + 1] = tie(
                from_z, sent[step + 1], kept[step + 1]
            )
            extra["mine"] = finish(near, from_z)
        if step >= 2:
            extra["other"] = swap_rad(mine[step - 2])
        came[step], sent[step + 1], kept[step + 1], extra = tie(
            came[step], sent[step + 1], kept[step + 1], extra
        )
        if "x" in extra:
            from_x.append(extra["x"])
        if "z" in extra:
            cells[step + 2].append((extra["z"], 4, 0))
        if step >= 1:
            mine[step - 1] = extra["mine"]
        if step >= 2:
            other[step - 2] = extra["other"]

    def blocks_of(numbers, part=None):
        chosen = [mine[n] if n != last else mine[n][part] for n in numbers]
        return chosen + [other[n] if n != last else other[n][part] for n in numbers]

    came[last] = [swap_span(sent[last][0], HALF)]
    other[last - 2] = swap_rad(mine[last - 2])
    near, from_z = share(kept[last - 1][0], came[last - 1])
    blocks = blocks_of(range(per_field))
    result = solve(place_keep, 0, 0, 2, blocks, *matrices, None)
    from_z, result = tie(from_z, result)
    mine[last - 1] = finish(near, from_z)
    came[last][0], sent_second, mine[last - 1], other[last - 2], result = tie(
        came[last][0], sent[last][1], mine[last - 1], other[last - 2], result
    )
    came[last].append(swap_span(sent_second, HALF))
    other[last - 1] = swap_rad(mine[last - 1])
    near, from_z = share(kept[last][0], came[last][0])
    result = solve(place_keep, 0, 2, 1, blocks, *matrices, result)
    from_z, result = tie(from_z, result)
    first = finish(near, from_z)
    first, came[last][1], other[last - 1] = tie(first, came[last][1], other[last - 1])
    other_first = swap_rad(first)
    second = finish(*share(kept[last][1], came[last][1]))
    second, other_first = tie(second, other_first)
    mine[last] = [first, second]
    other[last] = [other_first, swap_rad(second)]
    start = 0
    for part, count in enumerate(LAST_PARTS):
        blocks = blocks_of(range(per_field, total), part)
        result = solve(place_keep, 1, start, count, blocks, *matrices, result)
        start += count
    return result[None, None]


def solution(mesh):
    placed = (P(None, None, "rad", "span"), P(None, "span"), P(), P(), P(), P())
    halves = mesh.shape["span"] == 2 * HALF and mesh.shape["rad"] == 2
    return jax.shard_map(
        on_device_halves if halves else on_device_any,
        mesh=mesh,
        in_specs=placed,
        out_specs=P("span", "rad", None, None, None, None, None),
        check_vma=False,
    )
```

```python
import functools
import math

import jax
import jax.numpy as jnp
import numpy as np
from jax import lax
from jax.experimental import pallas as pl
from jax.experimental.pallas import tpu as pltpu
from jax.sharding import PartitionSpec as P

KEEP = 2688


precise = lax.Precision.HIGHEST
contract_rows = (((1,), (1,)), ((), ()))


def partner_2(value, axis, distance):
    mask = 2**distance
    pairs = [(source, source ^ mask) for source in range(lax.axis_size(axis))]
    return lax.ppermute(value, axis, pairs)


def bit_reverse(value, bit_count):
    flipped = jnp.zeros_like(value)
    for section_bit in range(bit_count):
        flipped = flipped + (value >> section_bit & 1) * 2 ** (bit_count - 1 - section_bit)
    return flipped


def section_angles(device, section_bit):
    upper_half = device >> section_bit & 1 == 1
    twiddle_index = jnp.where(upper_half, device % 2**section_bit, 0)
    angles = twiddle_index.astype(jnp.float32) * (2.0 * math.pi / 2 ** (section_bit + 1))
    sign_factor = jnp.where(upper_half, -1.0, 1.0).astype(jnp.float32)
    return (sign_factor, jnp.cos(angles), jnp.sin(angles))


def butterfly(fields, bit_count):
    device = lax.axis_index("span")
    top_bit = bit_count - 1
    partner = partner_2(fields, "span", top_bit)
    sign_factor, cosine, sine_value = section_angles(device, top_bit)
    difference = partner + sign_factor * fields
    real_part = difference * cosine
    imag_part = -difference * sine_value
    for section_bit in range(bit_count - 2, -1, -1):
        other_real, other_imag = partner_2((real_part, imag_part), "span", section_bit)
        sign_factor, cosine, sine_value = section_angles(device, section_bit)
        diff_real = other_real + sign_factor * real_part
        diff_imag = other_imag + sign_factor * imag_part
        real_part = diff_real * cosine + diff_imag * sine_value
        imag_part = diff_imag * cosine - diff_real * sine_value
    return (real_part, imag_part)


def mode_transform(real_part, imag_part, bit_count):
    groups = lax.axis_size("span")
    line_width = real_part.shape[3]
    full_length = line_width * groups
    kept_modes = KEEP // groups
    residue = bit_reverse(lax.axis_index("span"), bit_count)
    mode_index = residue + groups * jnp.arange(kept_modes, dtype=jnp.int32)
    phases = mode_index[:, None] * jnp.arange(line_width, dtype=jnp.int32)[None, :] % full_length
    angles = phases.astype(jnp.float32) * (2.0 * math.pi / full_length)
    normalizer = 1.0 / math.sqrt(full_length)
    cosine_table = jnp.cos(angles) * normalizer
    sine_table = jnp.sin(angles) * normalizer
    line_real = real_part.reshape(-1, line_width)
    line_imag = imag_part.reshape(-1, line_width)
    cos_real = lax.dot_general(cosine_table, line_real, contract_rows, precision=precise)
    cos_imag = lax.dot_general(cosine_table, line_imag, contract_rows, precision=precise)
    sin_real = lax.dot_general(sine_table, line_real, contract_rows, precision=precise)
    sin_imag = lax.dot_general(sine_table, line_imag, contract_rows, precision=precise)
    return (jnp.stack([cos_real + sin_imag, cos_imag - sin_real]), mode_index)


def placement_table(column, group_count, capacity):
    groups = jnp.arange(group_count, dtype=jnp.int32)
    member = (column[None, :] == groups[:, None]).astype(jnp.int32)
    ranking = jnp.cumsum(member, axis=1, dtype=jnp.int32) - member
    slot_index = jnp.arange(capacity, dtype=jnp.int32)
    return member[None] * (ranking[None] == slot_index[:, None, None])


def damping_factor(half_step, decay, wave_index):
    wave_square = (wave_index.astype(jnp.float32) * (math.pi / KEEP)) ** 2
    damping = half_step[None, :, None] * (decay[None, :, :] + wave_square[:, None, None])
    return (1.0 - damping) / (1.0 + damping)


def on_device_any(fields, mode_group, half_step, decay, eigen_inverse, eigen_vectors):
    bit_count = lax.axis_size("span").bit_length() - 1
    real_part, imag_part = butterfly(fields, bit_count)
    spectra, mode_index = mode_transform(real_part, imag_part, bit_count)
    kept_modes = spectra.shape[1]
    group_count = lax.axis_size("rad")
    capacity = min(kept_modes, 2 * kept_modes // group_count)
    planes = fields.shape[1]
    radial_rows = fields.shape[2]
    arranged = spectra.reshape(2, kept_modes, 2, planes, radial_rows)
    placing = placement_table(mode_group[:, 0], group_count, capacity)
    placing_float = placing.astype(jnp.float32)
    packed = jnp.einsum("sgb,cbfal->scfagl", placing_float, arranged, precision=precise)
    packed = packed.reshape(capacity, 2, 2, planes, group_count * radial_rows)
    regrouped = lax.all_to_all(packed, "rad", split_axis=4, concat_axis=4, tiled=True)
    own_slots = lax.dynamic_index_in_dim(placing, lax.axis_index("rad"), 1, keepdims=False)
    slot_modes = jnp.sum(own_slots * mode_index[None, :], axis=1)
    factor = damping_factor(half_step, decay, slot_modes)
    inner_part = jnp.einsum("scfar,fir->scfai", regrouped, eigen_inverse, precision=precise)
    inner_part = inner_part * factor[:, None, :, None, :]
    result = jnp.einsum("scfai,fri->scfar", inner_part, eigen_vectors, precision=precise)
    return result.reshape(1, 1, capacity, 2, 2, planes, group_count * radial_rows)


HALF = 8
BLOCK = 64
PARTS = 3
LAST_PARTS = (2, 1)
VMEM_BYTES = 24 * 1024 * 1024


def flip3(value):
    return (value & 1) << 2 | value & 2 | value >> 2


def swap_span(value, distance):
    pairs = [(source, source ^ distance) for source in range(lax.axis_size("span"))]
    return lax.ppermute(value, "span", pairs)


def swap_rad(value):
    return lax.ppermute(value, "rad", [(0, 1), (1, 0)])


def split_pair(value):
    high = value.astype(jnp.bfloat16)
    low = (value - high.astype(jnp.float32)).astype(jnp.bfloat16)
    return high, low


def dot_rows(left, right):
    return lax.dot_general(left, right, contract_rows, preferred_element_type=jnp.float32)


def dot_split(left, right):
    left_high, left_low = left
    right_high, right_low = right
    total = dot_rows(left_high, right_high)
    total = total + dot_rows(left_low, right_high)
    return total + dot_rows(left_high, right_low)


def transform_8(real, imag):
    root = math.sqrt(0.5)
    er, ei, orr, oi = [], [], [], []
    for j in range(4):
        er.append(real[j] + real[j + 4])
        ei.append(imag[j] + imag[j + 4])
        dr = real[j] - real[j + 4]
        di = imag[j] - imag[j + 4]
        if j == 0:
            orr.append(dr)
            oi.append(di)
        elif j == 1:
            orr.append((dr + di) * root)
            oi.append((di - dr) * root)
        elif j == 2:
            orr.append(di)
            oi.append(-dr)
        else:
            orr.append((di - dr) * root)
            oi.append((-di - dr) * root)

    def transform_4(r, i):
        ar, ai = r[0] + r[2], i[0] + i[2]
        br, bi = r[0] - r[2], i[0] - i[2]
        cr, ci = r[1] + r[3], i[1] + i[3]
        dr, di = r[1] - r[3], i[1] - i[3]
        return [(ar + cr, ai + ci), (br + di, bi - dr), (ar - cr, ai - ci), (br - di, bi + dr)]

    even = transform_4(er, ei)
    odd = transform_4(orr, oi)
    return [even[q // 2] if q % 2 == 0 else odd[q // 2] for q in range(8)]


def half_sums_kernel(counts, place, *refs):
    cells, refs = refs[: len(counts)], refs[len(counts) :]
    cos_turn, sin_turn, table_rows = refs[:3]
    outs, (ordered, high, low) = refs[3:-3], refs[-3:]
    me, parity = place[0], place[1]
    sign = place[2].astype(jnp.float32)
    width = ordered.shape[-1]
    distance = 0
    for ref, count in zip(cells, counts):
        for index in range(count):
            ordered[me ^ distance] = ref[index]
            distance += 1

    turn_real, turn_imag = [], []
    for j in range(HALF):
        angle = 2.0 * math.pi * j / 16
        turn_real.append(sign * jnp.where(parity == 1, math.cos(angle), 1.0))
        turn_imag.append(sign * jnp.where(parity == 1, -math.sin(angle), 0.0))

    def one_block(step, carry):
        rows = pl.ds(pl.multiple_of(step * 16, 16), 16)
        lower = pl.ds(pl.multiple_of(BLOCK + step * 16, 16), 16)
        for lane in range(0, width, 128):
            real, imag = [], []
            for j in range(HALF):
                value = ordered[j, rows, lane : lane + 128]
                real.append(value * turn_real[j])
                imag.append(value * turn_imag[j])
            sums = transform_8(real, imag)
            for q in range(HALF):
                sum_real, sum_imag = sums[q]
                cosine = cos_turn[parity, q : q + 1, lane : lane + 128]
                sine = sin_turn[parity, q : q + 1, lane : lane + 128]
                real_high, real_low = split_pair(sum_real * cosine + sum_imag * sine)
                imag_high, imag_low = split_pair(sum_imag * cosine - sum_real * sine)
                high[q, rows, lane : lane + 128] = real_high
                high[q, rows, width + lane : width + lane + 128] = imag_high
                high[q, lower, lane : lane + 128] = imag_high
                high[q, lower, width + lane : width + lane + 128] = -real_high
                low[q, rows, lane : lane + 128] = real_low
                low[q, rows, width + lane : width + lane + 128] = imag_low
                low[q, lower, lane : lane + 128] = imag_low
                low[q, lower, width + lane : width + lane + 128] = -real_low
        return carry

    lax.fori_loop(0, BLOCK // 16, one_block, 0)
    table = split_pair(table_rows[...])
    for q in range(0, HALF, 2):
        lines_high = high[q : q + 2].reshape(4 * BLOCK, 2 * width)
        lines_low = low[q : q + 2].reshape(4 * BLOCK, 2 * width)
        result = dot_split(table, (lines_high, lines_low))
        first = 0
        for out in outs:
            rows = slice(first, first + out.shape[1])
            out[me ^ flip3(q)] = result[rows, : 2 * BLOCK]
            out[me ^ flip3(q + 1)] = result[rows, 2 * BLOCK :]
            first += out.shape[1]


def half_sums(place, cells, tables, parts):
    width = cells[0][0].shape[-1]
    rows = tables[2].shape[0]
    counts = [array.shape[0] if count is None else count for array, count, _ in cells]

    def full(array):
        return pl.BlockSpec(array.shape, lambda i: (0,) * array.ndim)

    def some(count, inner):
        return pl.BlockSpec((count, BLOCK, width), lambda i: (0, inner, 0))

    return pl.pallas_call(
        functools.partial(half_sums_kernel, counts),
        grid=(1,),
        out_shape=[
            jax.ShapeDtypeStruct((HALF, part, 2 * BLOCK), jnp.float32) for part in parts
        ],
        in_specs=[pl.BlockSpec(memory_space=pltpu.SMEM)]
        + [some(count, inner) for count, (_, _, inner) in zip(counts, cells)]
        + [full(table) for table in tables],
        out_specs=[
            pl.BlockSpec((HALF, part, 2 * BLOCK), lambda i: (0, 0, 0)) for part in parts
        ],
        scratch_shapes=[
            pltpu.VMEM((HALF, BLOCK, width), jnp.float32),
            pltpu.VMEM((HALF, 2 * BLOCK, 2 * width), jnp.bfloat16),
            pltpu.VMEM((HALF, 2 * BLOCK, 2 * width), jnp.bfloat16),
        ],
        cost_estimate=pl.CostEstimate(
            flops=rows * BLOCK * width,
            bytes_accessed=BLOCK * width * 4,
            transcendentals=0,
        ),
        compiler_params=pltpu.CompilerParams(vmem_limit_bytes=VMEM_BYTES),
        name="half_sums",
    )(place, *[array for array, _, _ in cells], *tables)


def gather_planes_kernel(place, *refs):
    own, from_z, out, ordered = refs[0], refs[1], refs[-2], refs[-1]
    me = place[0]
    ordered[me] = own[0]
    ordered[me ^ 4] = from_z[0]
    for distance in range(1, 4):
        for index in range(2):
            ordered[me ^ (distance + 4 * index)] = refs[1 + distance][index]
    for plane in range(HALF):
        out[:, plane, :] = ordered[plane]


def gather_planes(place, own, from_z, others):
    modes, lanes = own.shape[-2:]
    one = pl.BlockSpec((1, modes, lanes), lambda i: (0, 0, 0))
    two = pl.BlockSpec((2, modes, lanes), lambda i: (0, 0, 0))
    return pl.pallas_call(
        gather_planes_kernel,
        grid=(1,),
        out_shape=jax.ShapeDtypeStruct((modes, HALF, lanes), jnp.float32),
        in_specs=[pl.BlockSpec(memory_space=pltpu.SMEM), one, one, two, two, two],
        out_specs=pl.BlockSpec((modes, HALF, lanes), lambda i: (0, 0, 0)),
        scratch_shapes=[pltpu.VMEM((HALF, modes, lanes), jnp.float32)],
        cost_estimate=pl.CostEstimate(
            flops=0, bytes_accessed=8 * HALF * modes * lanes, transcendentals=0
        ),
        compiler_params=pltpu.CompilerParams(vmem_limit_bytes=VMEM_BYTES),
        name="gather_planes",
    )(place, own, from_z, *others)


def solve_kernel(count, place, *refs):
    blocks = refs[: 2 * count]
    inverse, vectors, factor = refs[2 * count : 2 * count + 3]
    out = refs[-1]
    modes = out.shape[0]
    radial = out.shape[-1]

    @pl.when(place[3] == 1)
    def _():
        inverse_pair = split_pair(inverse[0])
        vectors_pair = split_pair(vectors[0])
        scale = jnp.broadcast_to(factor[0][:, None, :], (modes, HALF, radial))
        scale = scale.reshape(modes * HALF, radial)
        whole = [block[...].reshape(modes * HALF, 2 * BLOCK) for block in blocks]
        for part in range(2):
            lanes = slice(part * BLOCK, (part + 1) * BLOCK)
            lines = jnp.concatenate([value[:, lanes] for value in whole], axis=1)
            inner = dot_split(split_pair(lines), inverse_pair) * scale
            solved = dot_split(split_pair(inner), vectors_pair)
            out[:, part, 0] = solved.reshape(modes, HALF, radial)

    @pl.when(place[3] != 1)
    def _():
        out[...] = jnp.zeros_like(out)


def solve(place, field, first, count, blocks, inverse, vectors, factor, earlier):
    modes = factor.shape[1]
    radial = inverse.shape[-1]
    step = modes // PARTS

    def lines(array):
        offset = first if array.shape[0] == modes else 0
        return pl.BlockSpec((step, HALF, 2 * BLOCK), lambda i: (offset + i, 0, 0))

    matrix = pl.BlockSpec((1, radial, radial), lambda i: (field, 0, 0))
    in_specs = [pl.BlockSpec(memory_space=pltpu.SMEM)] + [lines(block) for block in blocks]
    in_specs += [matrix, matrix]
    in_specs += [pl.BlockSpec((1, step, radial), lambda i: (field, first + i, 0))]
    operands = [place, *blocks, inverse, vectors, factor]
    aliases = {}
    if earlier is not None:
        aliases = {len(operands): 0}
        operands.append(earlier)
        in_specs.append(pl.BlockSpec(memory_space=pl.ANY))

    def kernel(*refs):
        kept = refs if earlier is None else refs[: len(operands) - 1] + refs[-1:]
        solve_kernel(len(blocks) // 2, *kept)

    return pl.pallas_call(
        kernel,
        grid=(count,),
        out_shape=jax.ShapeDtypeStruct((modes, 2, 2, HALF, radial), jnp.float32),
        in_specs=in_specs,
        out_specs=pl.BlockSpec(
            (step, 2, 1, HALF, radial), lambda i: (first + i, 0, field, 0, 0)
        ),
        input_output_aliases=aliases,
        cost_estimate=pl.CostEstimate(
            flops=count * modes * radial * radial,
            bytes_accessed=count * modes * radial,
            transcendentals=0,
        ),
        compiler_params=pltpu.CompilerParams(vmem_limit_bytes=VMEM_BYTES),
        name="solve",
    )(*operands)


def mode_tables(width, modes):
    cells = np.arange(width)
    residue = 2 * np.arange(HALF)[None, :, None] + np.arange(2)[:, None, None]
    turn = 2.0 * np.pi * residue * cells / (2 * HALF * width)
    padded = -(-modes // 16) * 16
    angle = 2.0 * np.pi * (np.arange(padded)[:, None] * cells[None, :] % width) / width
    table = np.concatenate([np.cos(angle), np.sin(angle)], axis=1)
    table = table / math.sqrt(2 * HALF * width)
    table[modes:] = 0.0
    return tuple(array.astype(np.float32) for array in (np.cos(turn), np.sin(turn), table))


def on_device_halves(fields, mode_group, half_step, decay, eigen_inverse, eigen_vectors):
    span = lax.axis_index("span")
    rad = lax.axis_index("rad")
    me = span & 7
    half = span >> 3
    rows = fields.shape[2]
    width = fields.shape[3]
    modes = KEEP // 16
    tables = mode_tables(width, modes)

    heavy = (mode_group[0, 0] == rad).astype(jnp.int32)
    one = jnp.ones_like(me)
    place_send = jnp.stack([me, 1 - half, one, heavy])
    place_keep = jnp.stack([me, half, 1 - 2 * half, heavy])

    mode_index = bit_reverse(span, 4) + 16 * jnp.arange(modes, dtype=jnp.int32)
    factor = damping_factor(half_step, decay, mode_index).transpose(1, 0, 2)
    own = lax.dynamic_slice_in_dim(eigen_inverse, rad * rows, rows, 2)
    other = lax.dynamic_slice_in_dim(eigen_inverse, (1 - rad) * rows, rows, 2)
    inverse = jnp.concatenate([own, other], axis=2)

    units = [(field, block) for field in range(2) for block in range(rows // BLOCK)]
    total = len(units)
    per_field = rows // BLOCK
    last = total - 1

    def plane_rows(field, start, count, distance):
        piece = lax.dynamic_slice(
            fields, (field, me ^ distance, start, 0), (1, 1, count, width)
        )
        return piece.reshape(count, width)

    def swap_core(field, start, count):
        paired = fields.reshape(2, 4, 2, rows, width)
        piece = lax.dynamic_slice(
            paired, (field, 0, 1 - (me & 1), start, 0), (1, 4, 1, count, width)
        )
        return swap_span(piece.reshape(4, count, width), 1)

    def core_rows(core, start, count, distance):
        plane = (me ^ distance) >> 1
        piece = lax.dynamic_slice(core, (plane, start, 0), (1, count, width))
        return piece.reshape(count, width)

    def away_direct(core, field, start, count):
        return [
            jnp.stack([plane_rows(field, start, count, d), core_rows(core, start, count, d)])
            for d in (2, 4, 6)
        ]

    def swap_direct(away):
        return [swap_span(value, distance) for value, distance in zip(away, (2, 4, 6))]

    def near_cells(core, field, start, core_start):
        mine = plane_rows(field, start, BLOCK, 0)
        return [(mine[None], 1, 0), (core_rows(core, core_start, BLOCK, 0)[None], 1, 0)]

    def away_x(core, inner):
        away = []
        for distance in (2, 6):
            away.append(plane_rows(1, inner * BLOCK, BLOCK, distance))
            away.append(core_rows(core, inner * BLOCK, BLOCK, distance))
        return jnp.stack(away)

    def away_z(core, inner, from_x):
        away = [plane_rows(1, inner * BLOCK, BLOCK, 4)[None]]
        away += [core_rows(core, inner * BLOCK, BLOCK, 4)[None]]
        return jnp.concatenate(away + [from_x[2:]])

    def share(kept, came):
        return kept[:4] + came[:4], swap_span(kept[4:] + came[4:], 4)

    def swap_modes(near, from_z):
        return [
            swap_span(jnp.stack([near[distance], from_z[distance]]), distance)
            for distance in range(1, 4)
        ]

    def finish(near, from_z):
        return gather_planes(place_keep, near, from_z, swap_modes(near, from_z))

    def tie(*values):
        return lax.optimization_barrier(values)

    def sums(place, unit):
        step = modes // PARTS
        parts = [step * count for count in LAST_PARTS] if unit == last else [modes]
        return half_sums(place, cells[unit], tables, parts)

    cells = {}
    sent, kept, came, mine, other = {}, {}, {}, {}, {}
    def direct_unit(core, unit, arrays):
        start = units[unit][1] * BLOCK
        return near_cells(core, 0, start, start) + [(array, 2, 0) for array in arrays]

    core_a = swap_core(0, 0, rows)
    away = [away_direct(core_a, 0, n * BLOCK, BLOCK) for n in range(per_field)]
    direct = [swap_direct(away[0])]
    core_c = swap_core(1, 0, rows)
    for unit in range(1, per_field):
        away[unit], direct[unit - 1] = tie(away[unit], direct[unit - 1])
        direct.append(swap_direct(away[unit]))
    away_3, direct[1] = tie(away_x(core_c, 0), direct[1])
    for unit in range(per_field):
        cells[unit] = direct_unit(core_a, unit, direct[unit])
    sent[0] = sums(place_send, 0)
    sent[0], me, core_c = tie(sent[0], me, core_c)
    matrices = (inverse, eigen_vectors, factor)
    result = None
    swapped = {}
    for step in range(last):
        came[step] = swap_span(sent[step][0], HALF)
        extra = {}
        if step == 0:
            kept[0] = sums(place_keep, 0)
            direct[1], kept[0] = tie(direct[1], kept[0])
            cells[1] = direct_unit(core_a, 1, direct[1])
            away[2], away_3, direct[1] = tie(away[2], away_3, direct[1])
            direct[2] = swap_direct(away[2])
            cells[2] = direct_unit(core_a, 2, direct[2])
            from_x = [swap_span(away_3, 2)]
        sent[step + 1] = sums(place_send, step + 1)
        if step >= 1:
            kept[step] = sums(place_keep, step)
        if 1 <= step <= 2:
            extra["x"] = swap_span(away_x(core_c, step), 2)
        if 1 <= step <= 3:
            unit = step + 2
            inner = unit - per_field
            extra["z"] = swap_span(away_z(core_c, inner, from_x[inner]), 4)
            cells[unit] = near_cells(core_c, 1, inner * BLOCK, inner * BLOCK)
            cells[unit] += [(from_x[inner], 2, 0)]
        if step >= 1:
            extra["swapped"] = share(kept[step - 1][0], came[step - 1])
        if step >= 2:
            extra["mine"] = finish(*swapped[step - 2])
        if step == last - 1:
            extra["next"] = finish(*extra["swapped"])
            extra["kept"] = sums(place_keep, last)
        if step >= 3:
            extra["other"] = swap_rad(mine[step - 3])
        came[step], sent[step + 1], kept[step], extra = tie(
            came[step], sent[step + 1], kept[step], extra
        )
        if "x" in extra:
            from_x.append(extra["x"])
        if "z" in extra:
            cells[step + 2].append((extra["z"], 4, 0))
        if step >= 1:
            swapped[step - 1] = extra["swapped"]
        if step >= 2:
            mine[step - 2] = extra["mine"]
        if step >= 3:
            other[step - 3] = extra["other"]
    mine[last - 2], kept[last] = extra["next"], extra["kept"]

    def blocks_of(numbers, part=None):
        chosen = [mine[n] if n != last else mine[n][part] for n in numbers]
        return chosen + [other[n] if n != last else other[n][part] for n in numbers]

    came_first = swap_span(sent[last][0], HALF)
    other[last - 3] = swap_rad(mine[last - 3])
    mine[last - 1] = finish(*share(kept[last - 1][0], came[last - 1]))
    came_first, sent_second, mine[last - 1], other[last - 3] = tie(
        came_first, sent[last][1], mine[last - 1], other[last - 3]
    )
    came_second = swap_span(sent_second, HALF)
    other[last - 2] = swap_rad(mine[last - 2])
    near, from_z = share(kept[last][0], came_first)
    blocks = blocks_of(range(per_field))
    result = solve(place_keep, 0, 0, 2, blocks, *matrices, None)
    others, result = tie(swap_modes(near, from_z), result)
    first = gather_planes(place_keep, near, from_z, others)
    first, came_second, other[last - 2] = tie(first, came_second, other[last - 2])
    other[last - 1] = swap_rad(mine[last - 1])
    other_first = swap_rad(first)
    near, from_z = share(kept[last][1], came_second)
    result = solve(place_keep, 0, 2, 1, blocks, *matrices, result)
    others, result = tie(swap_modes(near, from_z), result)
    second = gather_planes(place_keep, near, from_z, others)
    second, other[last - 1] = tie(second, other[last - 1])
    mine[last] = [first, second]
    other[last] = [other_first, swap_rad(second)]
    start = 0
    for part, count in enumerate(LAST_PARTS):
        blocks = blocks_of(range(per_field, total), part)
        result = solve(place_keep, 1, start, count, blocks, *matrices, result)
        start += count
    return result[None, None]


def solution(mesh):
    placed = (P(None, None, "rad", "span"), P(None, "span"), P(), P(), P(), P())
    halves = mesh.shape["span"] == 2 * HALF and mesh.shape["rad"] == 2
    return jax.shard_map(
        on_device_halves if halves else on_device_any,
        mesh=mesh,
        in_specs=placed,
        out_specs=P("span", "rad", None, None, None, None, None),
        check_vma=False,
    )
```

```python
import functools
import math

import jax
import jax.numpy as jnp
import numpy as np
from jax import lax
from jax.experimental import pallas as pl
from jax.experimental.pallas import tpu as pltpu
from jax.sharding import PartitionSpec as P

KEEP = 2688


precise = lax.Precision.HIGHEST
contract_rows = (((1,), (1,)), ((), ()))


def partner_2(value, axis, distance):
    mask = 2**distance
    pairs = [(source, source ^ mask) for source in range(lax.axis_size(axis))]
    return lax.ppermute(value, axis, pairs)


def bit_reverse(value, bit_count):
    flipped = jnp.zeros_like(value)
    for section_bit in range(bit_count):
        flipped = flipped + (value >> section_bit & 1) * 2 ** (bit_count - 1 - section_bit)
    return flipped


def section_angles(device, section_bit):
    upper_half = device >> section_bit & 1 == 1
    twiddle_index = jnp.where(upper_half, device % 2**section_bit, 0)
    angles = twiddle_index.astype(jnp.float32) * (2.0 * math.pi / 2 ** (section_bit + 1))
    sign_factor = jnp.where(upper_half, -1.0, 1.0).astype(jnp.float32)
    return (sign_factor, jnp.cos(angles), jnp.sin(angles))


def butterfly(fields, bit_count):
    device = lax.axis_index("span")
    top_bit = bit_count - 1
    partner = partner_2(fields, "span", top_bit)
    sign_factor, cosine, sine_value = section_angles(device, top_bit)
    difference = partner + sign_factor * fields
    real_part = difference * cosine
    imag_part = -difference * sine_value
    for section_bit in range(bit_count - 2, -1, -1):
        other_real, other_imag = partner_2((real_part, imag_part), "span", section_bit)
        sign_factor, cosine, sine_value = section_angles(device, section_bit)
        diff_real = other_real + sign_factor * real_part
        diff_imag = other_imag + sign_factor * imag_part
        real_part = diff_real * cosine + diff_imag * sine_value
        imag_part = diff_imag * cosine - diff_real * sine_value
    return (real_part, imag_part)


def mode_transform(real_part, imag_part, bit_count):
    groups = lax.axis_size("span")
    line_width = real_part.shape[3]
    full_length = line_width * groups
    kept_modes = KEEP // groups
    residue = bit_reverse(lax.axis_index("span"), bit_count)
    mode_index = residue + groups * jnp.arange(kept_modes, dtype=jnp.int32)
    phases = mode_index[:, None] * jnp.arange(line_width, dtype=jnp.int32)[None, :] % full_length
    angles = phases.astype(jnp.float32) * (2.0 * math.pi / full_length)
    normalizer = 1.0 / math.sqrt(full_length)
    cosine_table = jnp.cos(angles) * normalizer
    sine_table = jnp.sin(angles) * normalizer
    line_real = real_part.reshape(-1, line_width)
    line_imag = imag_part.reshape(-1, line_width)
    cos_real = lax.dot_general(cosine_table, line_real, contract_rows, precision=precise)
    cos_imag = lax.dot_general(cosine_table, line_imag, contract_rows, precision=precise)
    sin_real = lax.dot_general(sine_table, line_real, contract_rows, precision=precise)
    sin_imag = lax.dot_general(sine_table, line_imag, contract_rows, precision=precise)
    return (jnp.stack([cos_real + sin_imag, cos_imag - sin_real]), mode_index)


def placement_table(column, group_count, capacity):
    groups = jnp.arange(group_count, dtype=jnp.int32)
    member = (column[None, :] == groups[:, None]).astype(jnp.int32)
    ranking = jnp.cumsum(member, axis=1, dtype=jnp.int32) - member
    slot_index = jnp.arange(capacity, dtype=jnp.int32)
    return member[None] * (ranking[None] == slot_index[:, None, None])


def damping_factor(half_step, decay, wave_index):
    wave_square = (wave_index.astype(jnp.float32) * (math.pi / KEEP)) ** 2
    damping = half_step[None, :, None] * (decay[None, :, :] + wave_square[:, None, None])
    return (1.0 - damping) / (1.0 + damping)


def on_device_any(fields, mode_group, half_step, decay, eigen_inverse, eigen_vectors):
    bit_count = lax.axis_size("span").bit_length() - 1
    real_part, imag_part = butterfly(fields, bit_count)
    spectra, mode_index = mode_transform(real_part, imag_part, bit_count)
    kept_modes = spectra.shape[1]
    group_count = lax.axis_size("rad")
    capacity = min(kept_modes, 2 * kept_modes // group_count)
    planes = fields.shape[1]
    radial_rows = fields.shape[2]
    arranged = spectra.reshape(2, kept_modes, 2, planes, radial_rows)
    placing = placement_table(mode_group[:, 0], group_count, capacity)
    placing_float = placing.astype(jnp.float32)
    packed = jnp.einsum("sgb,cbfal->scfagl", placing_float, arranged, precision=precise)
    packed = packed.reshape(capacity, 2, 2, planes, group_count * radial_rows)
    regrouped = lax.all_to_all(packed, "rad", split_axis=4, concat_axis=4, tiled=True)
    own_slots = lax.dynamic_index_in_dim(placing, lax.axis_index("rad"), 1, keepdims=False)
    slot_modes = jnp.sum(own_slots * mode_index[None, :], axis=1)
    factor = damping_factor(half_step, decay, slot_modes)
    inner_part = jnp.einsum("scfar,fir->scfai", regrouped, eigen_inverse, precision=precise)
    inner_part = inner_part * factor[:, None, :, None, :]
    result = jnp.einsum("scfai,fri->scfar", inner_part, eigen_vectors, precision=precise)
    return result.reshape(1, 1, capacity, 2, 2, planes, group_count * radial_rows)


HALF = 8
BLOCK = 64
PARTS = 3
LAST_PARTS = (2, 1)
PLANES = 2
VMEM_BYTES = 24 * 1024 * 1024


def flip3(value):
    return (value & 1) << 2 | value & 2 | value >> 2


def swap_span(value, distance):
    pairs = [(source, source ^ distance) for source in range(lax.axis_size("span"))]
    return lax.ppermute(value, "span", pairs)


def inner_pairs(span_size, distance, inward):
    outer = [*range(4), *range(span_size - 4, span_size)]
    pairs = [(device, device ^ 4 ^ distance) for device in outer]
    return pairs if inward else [(target, source) for source, target in pairs]


def swap_inner(value):
    size = lax.axis_size("span")
    middle = size // 2
    pairs = [(middle - 4 + n, middle + n) for n in range(4)]
    return lax.ppermute(value, "span", pairs + [(target, source) for source, target in pairs])


def send_inner(value, distance=0, inward=True):
    size = lax.axis_size("span")
    return lax.ppermute(value, "span", inner_pairs(size, distance, inward))


def swap_rad(value):
    return lax.ppermute(value, "rad", [(0, 1), (1, 0)])


def split_pair(value):
    high = value.astype(jnp.bfloat16)
    low = (value - high.astype(jnp.float32)).astype(jnp.bfloat16)
    return high, low


def dot_rows(left, right):
    return lax.dot_general(left, right, contract_rows, preferred_element_type=jnp.float32)


def dot_split(left, right):
    left_high, left_low = left
    right_high, right_low = right
    total = dot_rows(left_high, right_high)
    total = total + dot_rows(left_low, right_high)
    return total + dot_rows(left_high, right_low)


def transform_8(real, imag):
    root = math.sqrt(0.5)
    er, ei, orr, oi = [], [], [], []
    for j in range(4):
        er.append(real[j] + real[j + 4])
        ei.append(imag[j] + imag[j + 4])
        dr = real[j] - real[j + 4]
        di = imag[j] - imag[j + 4]
        if j == 0:
            orr.append(dr)
            oi.append(di)
        elif j == 1:
            orr.append((dr + di) * root)
            oi.append((di - dr) * root)
        elif j == 2:
            orr.append(di)
            oi.append(-dr)
        else:
            orr.append((di - dr) * root)
            oi.append((-di - dr) * root)

    def transform_4(r, i):
        ar, ai = r[0] + r[2], i[0] + i[2]
        br, bi = r[0] - r[2], i[0] - i[2]
        cr, ci = r[1] + r[3], i[1] + i[3]
        dr, di = r[1] - r[3], i[1] - i[3]
        return [(ar + cr, ai + ci), (br + di, bi - dr), (ar - cr, ai - ci), (br - di, bi + dr)]

    even = transform_4(er, ei)
    odd = transform_4(orr, oi)
    return [even[q // 2] if q % 2 == 0 else odd[q // 2] for q in range(8)]


def half_sums_kernel(counts, place, *refs):
    cells, refs = refs[: len(counts)], refs[len(counts) :]
    cos_turn, sin_turn, table_rows = refs[:3]
    outs, (ordered, high, low) = refs[3:-3], refs[-3:]
    me, parity, out_me = place[0], place[1], place[4]
    sign = place[2].astype(jnp.float32)
    width = ordered.shape[-1]

    @pl.when(place[5] == 1)
    def _():
        distance = 0
        for ref, count in zip(cells, counts):
            for index in range(count):
                ordered[me ^ distance] = ref[index]
                distance += 1
        sum_half(me, parity, out_me, sign, cos_turn, sin_turn, table_rows, outs, ordered, high, low)


def sum_half(me, parity, out_me, sign, cos_turn, sin_turn, table_rows, outs, ordered, high, low):
    width = ordered.shape[-1]
    turn_real, turn_imag = [], []
    for j in range(HALF):
        angle = 2.0 * math.pi * j / 16
        turn_real.append(sign * jnp.where(parity == 1, math.cos(angle), 1.0))
        turn_imag.append(sign * jnp.where(parity == 1, -math.sin(angle), 0.0))

    def one_block(step, carry):
        rows = pl.ds(pl.multiple_of(step * 16, 16), 16)
        lower = pl.ds(pl.multiple_of(BLOCK + step * 16, 16), 16)
        for lane in range(0, width, 128):
            real, imag = [], []
            for j in range(HALF):
                value = ordered[j, rows, lane : lane + 128]
                real.append(value * turn_real[j])
                imag.append(value * turn_imag[j])
            sums = transform_8(real, imag)
            for q in range(HALF):
                sum_real, sum_imag = sums[q]
                cosine = cos_turn[parity, q : q + 1, lane : lane + 128]
                sine = sin_turn[parity, q : q + 1, lane : lane + 128]
                real_high, real_low = split_pair(sum_real * cosine + sum_imag * sine)
                imag_high, imag_low = split_pair(sum_imag * cosine - sum_real * sine)
                high[q, rows, lane : lane + 128] = real_high
                high[q, rows, width + lane : width + lane + 128] = imag_high
                high[q, lower, lane : lane + 128] = imag_high
                high[q, lower, width + lane : width + lane + 128] = -real_high
                low[q, rows, lane : lane + 128] = real_low
                low[q, rows, width + lane : width + lane + 128] = imag_low
                low[q, lower, lane : lane + 128] = imag_low
                low[q, lower, width + lane : width + lane + 128] = -real_low
        return carry

    lax.fori_loop(0, BLOCK // 16, one_block, 0)
    table = split_pair(table_rows[...])
    for q in range(0, HALF, 2):
        lines_high = high[q : q + 2].reshape(4 * BLOCK, 2 * width)
        lines_low = low[q : q + 2].reshape(4 * BLOCK, 2 * width)
        result = dot_split(table, (lines_high, lines_low))
        first = 0
        for out in outs:
            rows = slice(first, first + out.shape[2])
            out[0, out_me ^ flip3(q)] = result[rows, : 2 * BLOCK]
            out[0, out_me ^ flip3(q + 1)] = result[rows, 2 * BLOCK :]
            first += out.shape[2]


def half_sums(place, cells, tables, parts):
    width = cells[0].shape[-1]
    rows = tables[2].shape[0]
    counts = [array.shape[0] // PLANES for array in cells]

    def full(array):
        return pl.BlockSpec(array.shape, lambda i: (0,) * array.ndim)

    return pl.pallas_call(
        functools.partial(half_sums_kernel, counts),
        grid=(PLANES,),
        out_shape=[
            jax.ShapeDtypeStruct((PLANES, HALF, part, 2 * BLOCK), jnp.float32)
            for part in parts
        ],
        in_specs=[pl.BlockSpec(memory_space=pltpu.SMEM)]
        + [pl.BlockSpec((count, BLOCK, width), lambda i: (i, 0, 0)) for count in counts]
        + [full(table) for table in tables],
        out_specs=[
            pl.BlockSpec((1, HALF, part, 2 * BLOCK), lambda i: (i, 0, 0, 0)) for part in parts
        ],
        scratch_shapes=[
            pltpu.VMEM((HALF, BLOCK, width), jnp.float32),
            pltpu.VMEM((HALF, 2 * BLOCK, 2 * width), jnp.bfloat16),
            pltpu.VMEM((HALF, 2 * BLOCK, 2 * width), jnp.bfloat16),
        ],
        cost_estimate=pl.CostEstimate(
            flops=rows * BLOCK * width,
            bytes_accessed=BLOCK * width * 4,
            transcendentals=0,
        ),
        compiler_params=pltpu.CompilerParams(vmem_limit_bytes=VMEM_BYTES),
        name="half_sums",
    )(place, *cells, *tables)


def gather_planes_kernel(place, *refs):
    out, ordered = refs[-2], refs[-1]
    me = place[0] & 3
    for distance in range(4):
        for plane in range(PLANES):
            piece = refs[0][plane, 0] if distance == 0 else refs[distance][plane]
            ordered[4 * plane + (me ^ distance)] = piece
    for plane in range(HALF):
        out[:, plane, :] = ordered[plane]


def gather_planes(place, own, others):
    modes, lanes = own.shape[-2:]
    two = pl.BlockSpec((PLANES, modes, lanes), lambda i: (0, 0, 0))
    return pl.pallas_call(
        gather_planes_kernel,
        grid=(1,),
        out_shape=jax.ShapeDtypeStruct((modes, HALF, lanes), jnp.float32),
        in_specs=[
            pl.BlockSpec(memory_space=pltpu.SMEM),
            pl.BlockSpec((PLANES, 1, modes, lanes), lambda i: (0, 0, 0, 0)),
            two,
            two,
            two,
        ],
        out_specs=pl.BlockSpec((modes, HALF, lanes), lambda i: (0, 0, 0)),
        scratch_shapes=[pltpu.VMEM((HALF, modes, lanes), jnp.float32)],
        cost_estimate=pl.CostEstimate(
            flops=0, bytes_accessed=8 * modes * lanes, transcendentals=0
        ),
        compiler_params=pltpu.CompilerParams(vmem_limit_bytes=VMEM_BYTES),
        name="gather_planes",
    )(place, own, *others)


def solve_kernel(count, place, *refs):
    blocks = refs[: 2 * count]
    inverse, vectors, factor = refs[2 * count : 2 * count + 3]
    out = refs[-1]
    modes = out.shape[0]
    radial = out.shape[-1]

    @pl.when(place[3] == 1)
    def _():
        inverse_pair = split_pair(inverse[0])
        vectors_pair = split_pair(vectors[0])
        scale = jnp.broadcast_to(factor[0][:, None, :], (modes, HALF, radial))
        scale = scale.reshape(modes * HALF, radial)
        whole = [block[...].reshape(modes * HALF, 2 * BLOCK) for block in blocks]
        for part in range(2):
            lanes = slice(part * BLOCK, (part + 1) * BLOCK)
            lines = jnp.concatenate([value[:, lanes] for value in whole], axis=1)
            inner = dot_split(split_pair(lines), inverse_pair) * scale
            solved = dot_split(split_pair(inner), vectors_pair)
            out[:, part, 0] = solved.reshape(modes, HALF, radial)

    @pl.when(place[3] != 1)
    def _():
        out[...] = jnp.zeros_like(out)


def solve(place, field, first, count, blocks, inverse, vectors, factor, earlier):
    modes = factor.shape[1]
    radial = inverse.shape[-1]
    step = modes // PARTS

    def lines(array):
        offset = first if array.shape[0] == modes else 0
        return pl.BlockSpec((step, HALF, 2 * BLOCK), lambda i: (offset + i, 0, 0))

    matrix = pl.BlockSpec((1, radial, radial), lambda i: (field, 0, 0))
    in_specs = [pl.BlockSpec(memory_space=pltpu.SMEM)] + [lines(block) for block in blocks]
    in_specs += [matrix, matrix]
    in_specs += [pl.BlockSpec((1, step, radial), lambda i: (field, first + i, 0))]
    operands = [place, *blocks, inverse, vectors, factor]
    aliases = {}
    if earlier is not None:
        aliases = {len(operands): 0}
        operands.append(earlier)
        in_specs.append(pl.BlockSpec(memory_space=pl.ANY))

    def kernel(*refs):
        kept = refs if earlier is None else refs[: len(operands) - 1] + refs[-1:]
        solve_kernel(len(blocks) // 2, *kept)

    return pl.pallas_call(
        kernel,
        grid=(count,),
        out_shape=jax.ShapeDtypeStruct((modes, 2, 2, HALF, radial), jnp.float32),
        in_specs=in_specs,
        out_specs=pl.BlockSpec(
            (step, 2, 1, HALF, radial), lambda i: (first + i, 0, field, 0, 0)
        ),
        input_output_aliases=aliases,
        cost_estimate=pl.CostEstimate(
            flops=count * modes * radial * radial,
            bytes_accessed=count * modes * radial,
            transcendentals=0,
        ),
        compiler_params=pltpu.CompilerParams(vmem_limit_bytes=VMEM_BYTES),
        name="solve",
    )(*operands)


def mode_tables(width, modes):
    cells = np.arange(width)
    residue = 2 * np.arange(HALF)[None, :, None] + np.arange(2)[:, None, None]
    turn = 2.0 * np.pi * residue * cells / (2 * HALF * width)
    padded = -(-modes // 16) * 16
    angle = 2.0 * np.pi * (np.arange(padded)[:, None] * cells[None, :] % width) / width
    table = np.concatenate([np.cos(angle), np.sin(angle)], axis=1)
    table = table / math.sqrt(2 * HALF * width)
    table[modes:] = 0.0
    return tuple(array.astype(np.float32) for array in (np.cos(turn), np.sin(turn), table))


def on_device_halves(fields, mode_group, half_step, decay, eigen_inverse, eigen_vectors):
    span = lax.axis_index("span")
    rad = lax.axis_index("rad")
    me = span & 7
    half = span >> 3
    rows = fields.shape[2]
    width = fields.shape[3]
    modes = KEEP // 16
    tables = mode_tables(width, modes)

    heavy = (mode_group[0, 0] == rad).astype(jnp.int32)
    inner_layer = ((me >> 2) != half).astype(jnp.int32)
    one = jnp.ones_like(me)
    place_send = jnp.stack([me, 1 - half, one, heavy, me ^ 4, inner_layer])
    place_keep = jnp.stack([me, half, 1 - 2 * half, heavy, me, inner_layer])

    mode_index = bit_reverse(span, 4) + 16 * jnp.arange(modes, dtype=jnp.int32)
    factor = damping_factor(half_step, decay, mode_index).transpose(1, 0, 2)
    own = lax.dynamic_slice_in_dim(eigen_inverse, rad * rows, rows, 2)
    other = lax.dynamic_slice_in_dim(eigen_inverse, (1 - rad) * rows, rows, 2)
    inverse = jnp.concatenate([own, other], axis=2)

    units = [(field, block) for field in range(2) for block in range(rows // BLOCK)]
    total = len(units)
    per_field = rows // BLOCK
    last = total - 1

    def swap_core(field):
        paired = fields.reshape(2, 4, 2, rows, width)
        piece = lax.dynamic_slice(
            paired, (field, 0, 1 - (me & 1), 0, 0), (1, 4, 1, rows, width)
        )
        return swap_span(piece.reshape(4, rows, width), 1)

    def plane_cells(unit, distance):
        field, block = units[unit]
        pieces = []
        for half_plane in range(PLANES):
            plane = 4 * half_plane + ((me & 3) ^ distance)
            piece = lax.dynamic_slice(
                fields, (field, plane, block * BLOCK, 0), (1, 1, BLOCK, width)
            )
            pieces.append(piece.reshape(1, BLOCK, width))
            piece = lax.dynamic_slice(
                core[field], (plane >> 1, block * BLOCK, 0), (1, BLOCK, width)
            )
            pieces.append(piece)
        return jnp.concatenate(pieces)

    def swap_x(unit):
        return swap_span(plane_cells(unit, 2), 2)

    def away_z(unit, from_x):
        mine = plane_cells(unit, 0)
        return jnp.concatenate([mine[:2], from_x[:2], mine[2:], from_x[2:]])

    def share(kept, came):
        near = kept[:, :4] + came[:, :4]
        from_z = send_inner(kept[:, 4:] + came[:, 4:], inward=False)
        return jnp.where(inner_layer == 1, near, from_z)

    def swap_modes(modes_of):
        return [swap_span(modes_of[:, distance], distance) for distance in range(1, 4)]

    def finish(modes_of):
        return gather_planes(place_keep, modes_of, swap_modes(modes_of))

    def tie(*values):
        return lax.optimization_barrier(values)

    def sums(place, unit):
        step = modes // PARTS
        parts = [step * count for count in LAST_PARTS] if unit == last else [modes]
        return half_sums(place, cells[unit], tables, parts)

    core = [swap_core(0), swap_core(1)]
    cells, from_x, from_z = {}, {}, {}
    sent, kept, came, mine, other = {}, {}, {}, {}, {}
    matrices = (inverse, eigen_vectors, factor)
    result = None

    mine_0, away_0 = plane_cells(0, 0), plane_cells(0, 2)
    direct = [swap_span(away_0, 2), send_inner(mine_0), send_inner(away_0, 2)]
    from_x[1] = swap_x(1)
    from_x[1], direct = tie(from_x[1], direct)
    from_z[1] = send_inner(away_z(1, from_x[1]))
    cells[0] = [mine_0, *direct]
    sent[0] = sums(place_send, 0)
    from_x[2], sent_0 = tie(plane_cells(2, 2), sent[0])
    sent[0] = sent_0
    from_x[2] = swap_span(from_x[2], 2)
    for step in range(last):
        came[step] = swap_inner(sent[step][0])
        extra = {}
        if step == 0:
            kept[0] = sums(place_keep, 0)
            from_x[2], from_z[1], kept[0] = tie(from_x[2], from_z[1], kept[0])
            extra["z"] = send_inner(away_z(2, from_x[2]))
        elif step + 2 < total:
            extra["z"] = send_inner(away_z(step + 2, from_x[step + 2]))
        if step + 3 < total:
            extra["x"] = swap_x(step + 3)
        cells[step + 1] = [plane_cells(step + 1, 0), from_x[step + 1], from_z[step + 1]]
        sent[step + 1] = sums(place_send, step + 1)
        if step >= 1:
            kept[step] = sums(place_keep, step)
            modes_of = share(kept[step - 1][0], came[step - 1])
            modes_of, sent[step + 1] = tie(modes_of, sent[step + 1])
            others, kept[step] = tie(swap_modes(modes_of), kept[step])
            extra["mine"] = gather_planes(place_keep, modes_of, others)
        if step >= 2:
            extra["other"] = swap_rad(mine[step - 2])
        came[step], sent[step + 1], kept[step], extra, me = tie(
            came[step], sent[step + 1], kept[step], extra, me
        )
        if "z" in extra:
            from_z[step + 2] = extra["z"]
        if "x" in extra:
            from_x[step + 3] = extra["x"]
        if "mine" in extra:
            mine[step - 1] = extra["mine"]
        if "other" in extra:
            other[step - 2] = extra["other"]

    def blocks_of(numbers, part=None):
        chosen = [mine[n] if n != last else mine[n][part] for n in numbers]
        return chosen + [other[n] if n != last else other[n][part] for n in numbers]

    came_first = swap_inner(sent[last][0])
    kept[last] = sums(place_keep, last)
    other[last - 2] = swap_rad(mine[last - 2])
    modes_of = share(kept[last - 1][0], came[last - 1])
    modes_of, kept[last] = tie(modes_of, kept[last])
    mine[last - 1] = finish(modes_of)
    came_first, sent_second, mine[last - 1], other[last - 2] = tie(
        came_first, sent[last][1], mine[last - 1], other[last - 2]
    )
    came_second = swap_inner(sent_second)
    other[last - 1] = swap_rad(mine[last - 1])
    modes_of = share(kept[last][0], came_first)
    blocks = blocks_of(range(per_field))
    result = solve(place_keep, 0, 0, 2, blocks, *matrices, None)
    others, result = tie(swap_modes(modes_of), result)
    first = gather_planes(place_keep, modes_of, others)
    first, came_second, other[last - 1] = tie(first, came_second, other[last - 1])
    other_first = swap_rad(first)
    modes_of = share(kept[last][1], came_second)
    result = solve(place_keep, 0, 2, 1, blocks, *matrices, result)
    others, result = tie(swap_modes(modes_of), result)
    second = gather_planes(place_keep, modes_of, others)
    second, other_first = tie(second, other_first)
    mine[last] = [first, second]
    other[last] = [other_first, swap_rad(second)]
    start = 0
    for part, count in enumerate(LAST_PARTS):
        blocks = blocks_of(range(per_field, total), part)
        result = solve(place_keep, 1, start, count, blocks, *matrices, result)
        start += count
    return result[None, None]


def solution(mesh):
    placed = (P(None, None, "rad", "span"), P(None, "span"), P(), P(), P(), P())
    halves = mesh.shape["span"] == 2 * HALF and mesh.shape["rad"] == 2
    return jax.shard_map(
        on_device_halves if halves else on_device_any,
        mesh=mesh,
        in_specs=placed,
        out_specs=P("span", "rad", None, None, None, None, None),
        check_vma=False,
    )
```

```python
import functools
import math

import jax
import jax.numpy as jnp
import numpy as np
from jax import lax
from jax.experimental import pallas as pl
from jax.experimental.pallas import tpu as pltpu
from jax.sharding import PartitionSpec as P

KEEP = 2688


precise = lax.Precision.HIGHEST
contract_rows = (((1,), (1,)), ((), ()))


def partner_2(value, axis, distance):
    mask = 2**distance
    pairs = [(source, source ^ mask) for source in range(lax.axis_size(axis))]
    return lax.ppermute(value, axis, pairs)


def bit_reverse(value, bit_count):
    flipped = jnp.zeros_like(value)
    for section_bit in range(bit_count):
        flipped = flipped + (value >> section_bit & 1) * 2 ** (bit_count - 1 - section_bit)
    return flipped


def section_angles(device, section_bit):
    upper_half = device >> section_bit & 1 == 1
    twiddle_index = jnp.where(upper_half, device % 2**section_bit, 0)
    angles = twiddle_index.astype(jnp.float32) * (2.0 * math.pi / 2 ** (section_bit + 1))
    sign_factor = jnp.where(upper_half, -1.0, 1.0).astype(jnp.float32)
    return (sign_factor, jnp.cos(angles), jnp.sin(angles))


def butterfly(fields, bit_count):
    device = lax.axis_index("span")
    top_bit = bit_count - 1
    partner = partner_2(fields, "span", top_bit)
    sign_factor, cosine, sine_value = section_angles(device, top_bit)
    difference = partner + sign_factor * fields
    real_part = difference * cosine
    imag_part = -difference * sine_value
    for section_bit in range(bit_count - 2, -1, -1):
        other_real, other_imag = partner_2((real_part, imag_part), "span", section_bit)
        sign_factor, cosine, sine_value = section_angles(device, section_bit)
        diff_real = other_real + sign_factor * real_part
        diff_imag = other_imag + sign_factor * imag_part
        real_part = diff_real * cosine + diff_imag * sine_value
        imag_part = diff_imag * cosine - diff_real * sine_value
    return (real_part, imag_part)


def mode_transform(real_part, imag_part, bit_count):
    groups = lax.axis_size("span")
    line_width = real_part.shape[3]
    full_length = line_width * groups
    kept_modes = KEEP // groups
    residue = bit_reverse(lax.axis_index("span"), bit_count)
    mode_index = residue + groups * jnp.arange(kept_modes, dtype=jnp.int32)
    phases = mode_index[:, None] * jnp.arange(line_width, dtype=jnp.int32)[None, :] % full_length
    angles = phases.astype(jnp.float32) * (2.0 * math.pi / full_length)
    normalizer = 1.0 / math.sqrt(full_length)
    cosine_table = jnp.cos(angles) * normalizer
    sine_table = jnp.sin(angles) * normalizer
    line_real = real_part.reshape(-1, line_width)
    line_imag = imag_part.reshape(-1, line_width)
    cos_real = lax.dot_general(cosine_table, line_real, contract_rows, precision=precise)
    cos_imag = lax.dot_general(cosine_table, line_imag, contract_rows, precision=precise)
    sin_real = lax.dot_general(sine_table, line_real, contract_rows, precision=precise)
    sin_imag = lax.dot_general(sine_table, line_imag, contract_rows, precision=precise)
    return (jnp.stack([cos_real + sin_imag, cos_imag - sin_real]), mode_index)


def placement_table(column, group_count, capacity):
    groups = jnp.arange(group_count, dtype=jnp.int32)
    member = (column[None, :] == groups[:, None]).astype(jnp.int32)
    ranking = jnp.cumsum(member, axis=1, dtype=jnp.int32) - member
    slot_index = jnp.arange(capacity, dtype=jnp.int32)
    return member[None] * (ranking[None] == slot_index[:, None, None])


def damping_factor(half_step, decay, wave_index):
    wave_square = (wave_index.astype(jnp.float32) * (math.pi / KEEP)) ** 2
    damping = half_step[None, :, None] * (decay[None, :, :] + wave_square[:, None, None])
    return (1.0 - damping) / (1.0 + damping)


def on_device_any(fields, mode_group, half_step, decay, eigen_inverse, eigen_vectors):
    bit_count = lax.axis_size("span").bit_length() - 1
    real_part, imag_part = butterfly(fields, bit_count)
    spectra, mode_index = mode_transform(real_part, imag_part, bit_count)
    kept_modes = spectra.shape[1]
    group_count = lax.axis_size("rad")
    capacity = min(kept_modes, 2 * kept_modes // group_count)
    planes = fields.shape[1]
    radial_rows = fields.shape[2]
    arranged = spectra.reshape(2, kept_modes, 2, planes, radial_rows)
    placing = placement_table(mode_group[:, 0], group_count, capacity)
    placing_float = placing.astype(jnp.float32)
    packed = jnp.einsum("sgb,cbfal->scfagl", placing_float, arranged, precision=precise)
    packed = packed.reshape(capacity, 2, 2, planes, group_count * radial_rows)
    regrouped = lax.all_to_all(packed, "rad", split_axis=4, concat_axis=4, tiled=True)
    own_slots = lax.dynamic_index_in_dim(placing, lax.axis_index("rad"), 1, keepdims=False)
    slot_modes = jnp.sum(own_slots * mode_index[None, :], axis=1)
    factor = damping_factor(half_step, decay, slot_modes)
    inner_part = jnp.einsum("scfar,fir->scfai", regrouped, eigen_inverse, precision=precise)
    inner_part = inner_part * factor[:, None, :, None, :]
    result = jnp.einsum("scfai,fri->scfar", inner_part, eigen_vectors, precision=precise)
    return result.reshape(1, 1, capacity, 2, 2, planes, group_count * radial_rows)


HALF = 8
BLOCK = 64
PARTS = 3
LAST_PARTS = (2, 1)
VMEM_BYTES = 24 * 1024 * 1024


def flip3(value):
    return (value & 1) << 2 | value & 2 | value >> 2


def swap_span(value, distance):
    pairs = [(source, source ^ distance) for source in range(lax.axis_size("span"))]
    return lax.ppermute(value, "span", pairs)


def swap_rad(value):
    return lax.ppermute(value, "rad", [(0, 1), (1, 0)])


def split_pair(value):
    high = value.astype(jnp.bfloat16)
    low = (value - high.astype(jnp.float32)).astype(jnp.bfloat16)
    return high, low


def dot_rows(left, right):
    return lax.dot_general(left, right, contract_rows, preferred_element_type=jnp.float32)


def dot_split(left, right):
    left_high, left_low = left
    right_high, right_low = right
    total = dot_rows(left_high, right_high)
    total = total + dot_rows(left_low, right_high)
    return total + dot_rows(left_high, right_low)


def transform_8(real, imag):
    root = math.sqrt(0.5)
    er, ei, orr, oi = [], [], [], []
    for j in range(4):
        er.append(real[j] + real[j + 4])
        ei.append(imag[j] + imag[j + 4])
        dr = real[j] - real[j + 4]
        di = imag[j] - imag[j + 4]
        if j == 0:
            orr.append(dr)
            oi.append(di)
        elif j == 1:
            orr.append((dr + di) * root)
            oi.append((di - dr) * root)
        elif j == 2:
            orr.append(di)
            oi.append(-dr)
        else:
            orr.append((di - dr) * root)
            oi.append((-di - dr) * root)

    def transform_4(r, i):
        ar, ai = r[0] + r[2], i[0] + i[2]
        br, bi = r[0] - r[2], i[0] - i[2]
        cr, ci = r[1] + r[3], i[1] + i[3]
        dr, di = r[1] - r[3], i[1] - i[3]
        return [(ar + cr, ai + ci), (br + di, bi - dr), (ar - cr, ai - ci), (br - di, bi + dr)]

    even = transform_4(er, ei)
    odd = transform_4(orr, oi)
    return [even[q // 2] if q % 2 == 0 else odd[q // 2] for q in range(8)]


def half_sums_kernel(where, counts, parts, place, *refs):
    field, start, core_start = where
    fields, core, others = refs[0], refs[1], refs[2 : 2 + len(counts)]
    cos_turn, sin_turn, table_rows = refs[2 + len(counts) : 5 + len(counts)]
    sums_of = refs[5 + len(counts) : -6]
    ordered, high, low, done, in_sems, out_sems = refs[-6:]
    me = place[0, 0]
    width = ordered.shape[-1]
    modes = done.shape[2]
    rows = pl.ds(start, BLOCK)

    sources = [fields.at[field, me, rows], core.at[me >> 1, pl.ds(core_start, BLOCK)]]
    for ref, count in zip(others, counts):
        sources += [ref.at[index] for index in range(count)]
    copies = [
        pltpu.make_async_copy(source, ordered.at[me ^ distance], in_sems.at[distance])
        for distance, source in enumerate(sources)
    ]
    for copy in copies:
        copy.start()
    for copy in copies:
        copy.wait()

    table = split_pair(table_rows[...])
    lane = lax.broadcasted_iota(jnp.int32, (modes, 2 * BLOCK), 1)
    flip = jnp.where(lane < BLOCK, 1.0, -1.0)
    finals = []
    for which in range(done.shape[0]):
        parity = place[which, 1]
        sign = place[which, 2].astype(jnp.float32)
        turn_real, turn_imag = [], []
        for j in range(HALF):
            angle = 2.0 * math.pi * j / 16
            turn_real.append(sign * jnp.where(parity == 1, math.cos(angle), 1.0))
            turn_imag.append(sign * jnp.where(parity == 1, -math.sin(angle), 0.0))

        def one_block(step, carry):
            upper = pl.ds(pl.multiple_of(step * 16, 16), 16)
            lower = pl.ds(pl.multiple_of(BLOCK + step * 16, 16), 16)
            for lane in range(0, width, 128):
                lanes = slice(lane, lane + 128)
                real, imag = [], []
                for j in range(HALF):
                    value = ordered[j, upper, lanes]
                    real.append(value * turn_real[j])
                    imag.append(value * turn_imag[j])
                sums = transform_8(real, imag)
                for q in range(HALF):
                    sum_real, sum_imag = sums[q]
                    cosine = cos_turn[parity, q : q + 1, lanes]
                    sine = sin_turn[parity, q : q + 1, lanes]
                    real_high, real_low = split_pair(sum_real * cosine + sum_imag * sine)
                    imag_high, imag_low = split_pair(sum_imag * cosine - sum_real * sine)
                    high[q, upper, lanes] = real_high
                    high[q, lower, lanes] = imag_high
                    low[q, upper, lanes] = real_low
                    low[q, lower, lanes] = imag_low
            return carry

        lax.fori_loop(0, BLOCK // 16, one_block, 0)
        for q in range(0, HALF, 2):
            lines_high = high[q : q + 2].reshape(4 * BLOCK, width)
            lines_low = low[q : q + 2].reshape(4 * BLOCK, width)
            result = dot_split(table, (lines_high, lines_low))
            for side in range(2):
                lanes = slice(side * 2 * BLOCK, (side + 1) * 2 * BLOCK)
                by_cosine, by_sine = result[:modes, lanes], result[modes:, lanes]
                index = me ^ flip3(q + side)
                done[which, index] = by_cosine + pltpu.roll(by_sine, BLOCK, 1) * flip
                first = 0
                for part, count in enumerate(parts):
                    copy = pltpu.make_async_copy(
                        done.at[which, index, pl.ds(first, count)],
                        sums_of[which * len(parts) + part].at[index],
                        out_sems.at[which, part, q + side],
                    )
                    copy.start()
                    finals.append(copy)
                    first += count
    for copy in finals:
        copy.wait()


def half_sums(places, where, fields, core, others, tables, parts):
    width = fields.shape[-1]
    modes = sum(parts)
    counts = [array.shape[0] for array in others]
    hbm = pl.BlockSpec(memory_space=pltpu.HBM)
    vmem = pl.BlockSpec(memory_space=pltpu.VMEM)
    sums_of = pl.pallas_call(
        functools.partial(half_sums_kernel, where, counts, parts),
        out_shape=[
            jax.ShapeDtypeStruct((HALF, part, 2 * BLOCK), jnp.float32)
            for _ in places
            for part in parts
        ],
        in_specs=[pl.BlockSpec(memory_space=pltpu.SMEM)]
        + [hbm] * (2 + len(others))
        + [vmem] * len(tables),
        out_specs=[hbm] * (len(places) * len(parts)),
        scratch_shapes=[
            pltpu.VMEM((HALF, BLOCK, width), jnp.float32),
            pltpu.VMEM((HALF, 2 * BLOCK, width), jnp.bfloat16),
            pltpu.VMEM((HALF, 2 * BLOCK, width), jnp.bfloat16),
            pltpu.VMEM((len(places), HALF, modes, 2 * BLOCK), jnp.float32),
            pltpu.SemaphoreType.DMA((HALF,)),
            pltpu.SemaphoreType.DMA((len(places), len(parts), HALF)),
        ],
        cost_estimate=pl.CostEstimate(
            flops=modes * BLOCK * width, bytes_accessed=BLOCK * width * 4, transcendentals=0
        ),
        compiler_params=pltpu.CompilerParams(vmem_limit_bytes=VMEM_BYTES),
        name="half_sums",
    )(jnp.stack(places), fields, core, *others, *tables)
    return [sums_of[n : n + len(parts)] for n in range(0, len(sums_of), len(parts))]


def gather_planes_kernel(place, *refs):
    own, from_z, out, ordered = refs[0], refs[1], refs[-2], refs[-1]
    me = place[0]
    ordered[me] = own[0]
    ordered[me ^ 4] = from_z[0]
    for distance in range(1, 4):
        for index in range(2):
            ordered[me ^ (distance + 4 * index)] = refs[1 + distance][index]
    for plane in range(HALF):
        out[:, plane, :] = ordered[plane]


def gather_planes(place, own, from_z, others):
    modes, lanes = own.shape[-2:]
    one = pl.BlockSpec((1, modes, lanes), lambda i: (0, 0, 0))
    two = pl.BlockSpec((2, modes, lanes), lambda i: (0, 0, 0))
    return pl.pallas_call(
        gather_planes_kernel,
        grid=(1,),
        out_shape=jax.ShapeDtypeStruct((modes, HALF, lanes), jnp.float32),
        in_specs=[pl.BlockSpec(memory_space=pltpu.SMEM), one, one, two, two, two],
        out_specs=pl.BlockSpec((modes, HALF, lanes), lambda i: (0, 0, 0)),
        scratch_shapes=[pltpu.VMEM((HALF, modes, lanes), jnp.float32)],
        cost_estimate=pl.CostEstimate(
            flops=0, bytes_accessed=8 * HALF * modes * lanes, transcendentals=0
        ),
        compiler_params=pltpu.CompilerParams(vmem_limit_bytes=VMEM_BYTES),
        name="gather_planes",
    )(place, own, from_z, *others)


def solve_kernel(count, place, *refs):
    blocks = refs[: 2 * count]
    inverse, vectors, factor = refs[2 * count : 2 * count + 3]
    out = refs[-1]
    modes = out.shape[0]
    radial = out.shape[-1]

    @pl.when(place[3] == 1)
    def _():
        inverse_pair = split_pair(inverse[0])
        vectors_pair = split_pair(vectors[0])
        scale = jnp.broadcast_to(factor[0][:, None, :], (modes, HALF, radial))
        scale = scale.reshape(modes * HALF, radial)
        whole = [block[...].reshape(modes * HALF, 2 * BLOCK) for block in blocks]
        for part in range(2):
            lanes = slice(part * BLOCK, (part + 1) * BLOCK)
            lines = jnp.concatenate([value[:, lanes] for value in whole], axis=1)
            inner = dot_split(split_pair(lines), inverse_pair) * scale
            solved = dot_split(split_pair(inner), vectors_pair)
            out[:, part, 0] = solved.reshape(modes, HALF, radial)

    @pl.when(place[3] != 1)
    def _():
        out[...] = jnp.zeros_like(out)


def solve(place, field, first, count, blocks, inverse, vectors, factor, earlier):
    modes = factor.shape[1]
    radial = inverse.shape[-1]
    step = modes // PARTS

    def lines(array):
        offset = first if array.shape[0] == modes else 0
        return pl.BlockSpec((step, HALF, 2 * BLOCK), lambda i: (offset + i, 0, 0))

    matrix = pl.BlockSpec((1, radial, radial), lambda i: (field, 0, 0))
    in_specs = [pl.BlockSpec(memory_space=pltpu.SMEM)] + [lines(block) for block in blocks]
    in_specs += [matrix, matrix]
    in_specs += [pl.BlockSpec((1, step, radial), lambda i: (field, first + i, 0))]
    operands = [place, *blocks, inverse, vectors, factor]
    aliases = {}
    if earlier is not None:
        aliases = {len(operands): 0}
        operands.append(earlier)
        in_specs.append(pl.BlockSpec(memory_space=pl.ANY))

    def kernel(*refs):
        kept = refs if earlier is None else refs[: len(operands) - 1] + refs[-1:]
        solve_kernel(len(blocks) // 2, *kept)

    return pl.pallas_call(
        kernel,
        grid=(count,),
        out_shape=jax.ShapeDtypeStruct((modes, 2, 2, HALF, radial), jnp.float32),
        in_specs=in_specs,
        out_specs=pl.BlockSpec(
            (step, 2, 1, HALF, radial), lambda i: (first + i, 0, field, 0, 0)
        ),
        input_output_aliases=aliases,
        cost_estimate=pl.CostEstimate(
            flops=count * modes * radial * radial,
            bytes_accessed=count * modes * radial,
            transcendentals=0,
        ),
        compiler_params=pltpu.CompilerParams(vmem_limit_bytes=VMEM_BYTES),
        name="solve",
    )(*operands)


def mode_tables(width, modes):
    cells = np.arange(width)
    residue = 2 * np.arange(HALF)[None, :, None] + np.arange(2)[:, None, None]
    turn = 2.0 * np.pi * residue * cells / (2 * HALF * width)
    angle = 2.0 * np.pi * (np.arange(modes)[:, None] * cells[None, :] % width) / width
    table = np.concatenate([np.cos(angle), np.sin(angle)]) / math.sqrt(2 * HALF * width)
    return tuple(array.astype(np.float32) for array in (np.cos(turn), np.sin(turn), table))


def on_device_halves(fields, mode_group, half_step, decay, eigen_inverse, eigen_vectors):
    span = lax.axis_index("span")
    rad = lax.axis_index("rad")
    me = span & 7
    half = span >> 3
    rows = fields.shape[2]
    width = fields.shape[3]
    modes = KEEP // 16
    tables = mode_tables(width, modes)

    heavy = (mode_group[0, 0] == rad).astype(jnp.int32)
    one = jnp.ones_like(me)
    place_send = jnp.stack([me, 1 - half, one, heavy])
    place_keep = jnp.stack([me, half, 1 - 2 * half, heavy])

    mode_index = bit_reverse(span, 4) + 16 * jnp.arange(modes, dtype=jnp.int32)
    factor = damping_factor(half_step, decay, mode_index).transpose(1, 0, 2)
    own = lax.dynamic_slice_in_dim(eigen_inverse, rad * rows, rows, 2)
    other = lax.dynamic_slice_in_dim(eigen_inverse, (1 - rad) * rows, rows, 2)
    inverse = jnp.concatenate([own, other], axis=2)

    units = [(field, block) for field in range(2) for block in range(rows // BLOCK)]
    total = len(units)
    per_field = rows // BLOCK
    last = total - 1

    def plane_rows(field, start, count, distance):
        piece = lax.dynamic_slice(
            fields, (field, me ^ distance, start, 0), (1, 1, count, width)
        )
        return piece.reshape(count, width)

    def swap_core(field, start, count):
        paired = fields.reshape(2, 4, 2, rows, width)
        piece = lax.dynamic_slice(
            paired, (field, 0, 1 - (me & 1), start, 0), (1, 4, 1, count, width)
        )
        return swap_span(piece.reshape(4, count, width), 1)

    def core_rows(core, start, count, distance):
        plane = (me ^ distance) >> 1
        piece = lax.dynamic_slice(core, (plane, start, 0), (1, count, width))
        return piece.reshape(count, width)

    def away_direct(core, field, start, count):
        return [
            jnp.stack([plane_rows(field, start, count, d), core_rows(core, start, count, d)])
            for d in (2, 4, 6)
        ]

    def swap_direct(away):
        return [swap_span(value, distance) for value, distance in zip(away, (2, 4, 6))]

    def away_x(core, inner):
        away = []
        for distance in (2, 6):
            away.append(plane_rows(1, inner * BLOCK, BLOCK, distance))
            away.append(core_rows(core, inner * BLOCK, BLOCK, distance))
        return jnp.stack(away)

    def away_z(core, inner, from_x):
        away = [plane_rows(1, inner * BLOCK, BLOCK, 4)[None]]
        away += [core_rows(core, inner * BLOCK, BLOCK, 4)[None]]
        return jnp.concatenate(away + [from_x[2:]])

    def share(kept, came):
        return kept[:4] + came[:4], swap_span(kept[4:] + came[4:], 4)

    def finish(near, from_z):
        others = []
        for distance in range(1, 4):
            away = jnp.stack([near[distance], from_z[distance]])
            others.append(swap_span(away, distance))
        return gather_planes(place_keep, near, from_z, others)

    def tie(*values):
        return lax.optimization_barrier(values)

    def sums(places, unit):
        step = modes // PARTS
        parts = [step * count for count in LAST_PARTS] if unit == last else [modes]
        field, block = units[unit]
        where = (field, block * BLOCK, block * BLOCK)
        core = core_c if field else core_a
        return half_sums(places, where, fields, core, cells[unit], tables, parts)

    cells = {}
    sent, kept, came, mine, other = {}, {}, {}, {}, {}
    core_a = swap_core(0, 0, rows)
    away = [away_direct(core_a, 0, n * BLOCK, BLOCK) for n in range(per_field)]
    direct = [swap_direct(away[0])]
    core_c = swap_core(1, 0, rows)
    for unit in range(1, per_field):
        away[unit], direct[unit - 1] = tie(away[unit], direct[unit - 1])
        direct.append(swap_direct(away[unit]))
    away_3, direct[1] = tie(away_x(core_c, 0), direct[1])
    cells[0] = direct[0]
    (sent[0],) = sums([place_send], 0)
    sent[0], me = tie(sent[0], me)
    matrices = (inverse, eigen_vectors, factor)
    both = [place_send, place_keep]
    result = None
    for step in range(last):
        came[step] = swap_span(sent[step][0], HALF)
        extra = {}
        if step == 0:
            (kept[0],) = sums([place_keep], 0)
            direct[1], kept[0] = tie(direct[1], kept[0])
            away[2], away_3, cells[1] = tie(away[2], away_3, direct[1])
            cells[2] = swap_direct(away[2])
            from_x = [swap_span(away_3, 2)]
        if 1 <= step <= 2:
            extra["x"] = swap_span(away_x(core_c, step), 2)
        if 1 <= step <= 3:
            unit = step + 2
            inner = unit - per_field
            extra["z"] = swap_span(away_z(core_c, inner, from_x[inner]), 4)
            cells[unit] = [from_x[inner][:2]]
        sent[step + 1], kept[step + 1] = sums(both, step + 1)
        if step >= 1:
            near, from_z = share(kept[step - 1][0], came[step - 1])
            from_z, sent[step + 1], kept[step + 1] = tie(
                from_z, sent[step + 1], kept[step + 1]
            )
            extra["mine"] = finish(near, from_z)
        if step >= 2:
            extra["other"] = swap_rad(mine[step - 2])
        came[step], sent[step + 1], kept[step + 1], extra, me, both = tie(
            came[step], sent[step + 1], kept[step + 1], extra, me, both
        )
        if "x" in extra:
            from_x.append(extra["x"])
        if "z" in extra:
            cells[step + 2].append(extra["z"])
        if step >= 1:
            mine[step - 1] = extra["mine"]
        if step >= 2:
            other[step - 2] = extra["other"]

    def blocks_of(numbers, part=None):
        chosen = [mine[n] if n != last else mine[n][part] for n in numbers]
        return chosen + [other[n] if n != last else other[n][part] for n in numbers]

    came[last] = [swap_span(sent[last][0], HALF)]
    other[last - 2] = swap_rad(mine[last - 2])
    near, from_z = share(kept[last - 1][0], came[last - 1])
    blocks = blocks_of(range(per_field))
    result = solve(place_keep, 0, 0, 2, blocks, *matrices, None)
    from_z, result = tie(from_z, result)
    mine[last - 1] = finish(near, from_z)
    came[last][0], sent_second, mine[last - 1], other[last - 2], result = tie(
        came[last][0], sent[last][1], mine[last - 1], other[last - 2], result
    )
    came[last].append(swap_span(sent_second, HALF))
    other[last - 1] = swap_rad(mine[last - 1])
    near, from_z = share(kept[last][0], came[last][0])
    result = solve(place_keep, 0, 2, 1, blocks, *matrices, result)
    from_z, result = tie(from_z, result)
    first = finish(near, from_z)
    first, came[last][1], other[last - 1] = tie(first, came[last][1], other[last - 1])
    other_first = swap_rad(first)
    second = finish(*share(kept[last][1], came[last][1]))
    second, other_first = tie(second, other_first)
    mine[last] = [first, second]
    other[last] = [other_first, swap_rad(second)]
    start = 0
    for part, count in enumerate(LAST_PARTS):
        blocks = blocks_of(range(per_field, total), part)
        result = solve(place_keep, 1, start, count, blocks, *matrices, result)
        start += count
    return result[None, None]


def solution(mesh):
    placed = (P(None, None, "rad", "span"), P(None, "span"), P(), P(), P(), P())
    halves = mesh.shape["span"] == 2 * HALF and mesh.shape["rad"] == 2
    return jax.shard_map(
        on_device_halves if halves else on_device_any,
        mesh=mesh,
        in_specs=placed,
        out_specs=P("span", "rad", None, None, None, None, None),
        check_vma=False,
    )
```

```python
import functools
import math

import jax
import jax.numpy as jnp
import numpy as np
from jax import lax
from jax.experimental import pallas as pl
from jax.experimental.pallas import tpu as pltpu
from jax.sharding import PartitionSpec as P

KEEP = 2688


precise = lax.Precision.HIGHEST
contract_rows = (((1,), (1,)), ((), ()))


def partner_2(value, axis, distance):
    mask = 2**distance
    pairs = [(source, source ^ mask) for source in range(lax.axis_size(axis))]
    return lax.ppermute(value, axis, pairs)


def bit_reverse(value, bit_count):
    flipped = jnp.zeros_like(value)
    for section_bit in range(bit_count):
        flipped = flipped + (value >> section_bit & 1) * 2 ** (bit_count - 1 - section_bit)
    return flipped


def section_angles(device, section_bit):
    upper_half = device >> section_bit & 1 == 1
    twiddle_index = jnp.where(upper_half, device % 2**section_bit, 0)
    angles = twiddle_index.astype(jnp.float32) * (2.0 * math.pi / 2 ** (section_bit + 1))
    sign_factor = jnp.where(upper_half, -1.0, 1.0).astype(jnp.float32)
    return (sign_factor, jnp.cos(angles), jnp.sin(angles))


def butterfly(fields, bit_count):
    device = lax.axis_index("span")
    top_bit = bit_count - 1
    partner = partner_2(fields, "span", top_bit)
    sign_factor, cosine, sine_value = section_angles(device, top_bit)
    difference = partner + sign_factor * fields
    real_part = difference * cosine
    imag_part = -difference * sine_value
    for section_bit in range(bit_count - 2, -1, -1):
        other_real, other_imag = partner_2((real_part, imag_part), "span", section_bit)
        sign_factor, cosine, sine_value = section_angles(device, section_bit)
        diff_real = other_real + sign_factor * real_part
        diff_imag = other_imag + sign_factor * imag_part
        real_part = diff_real * cosine + diff_imag * sine_value
        imag_part = diff_imag * cosine - diff_real * sine_value
    return (real_part, imag_part)


def mode_transform(real_part, imag_part, bit_count):
    groups = lax.axis_size("span")
    line_width = real_part.shape[3]
    full_length = line_width * groups
    kept_modes = KEEP // groups
    residue = bit_reverse(lax.axis_index("span"), bit_count)
    mode_index = residue + groups * jnp.arange(kept_modes, dtype=jnp.int32)
    phases = mode_index[:, None] * jnp.arange(line_width, dtype=jnp.int32)[None, :] % full_length
    angles = phases.astype(jnp.float32) * (2.0 * math.pi / full_length)
    normalizer = 1.0 / math.sqrt(full_length)
    cosine_table = jnp.cos(angles) * normalizer
    sine_table = jnp.sin(angles) * normalizer
    line_real = real_part.reshape(-1, line_width)
    line_imag = imag_part.reshape(-1, line_width)
    cos_real = lax.dot_general(cosine_table, line_real, contract_rows, precision=precise)
    cos_imag = lax.dot_general(cosine_table, line_imag, contract_rows, precision=precise)
    sin_real = lax.dot_general(sine_table, line_real, contract_rows, precision=precise)
    sin_imag = lax.dot_general(sine_table, line_imag, contract_rows, precision=precise)
    return (jnp.stack([cos_real + sin_imag, cos_imag - sin_real]), mode_index)


def placement_table(column, group_count, capacity):
    groups = jnp.arange(group_count, dtype=jnp.int32)
    member = (column[None, :] == groups[:, None]).astype(jnp.int32)
    ranking = jnp.cumsum(member, axis=1, dtype=jnp.int32) - member
    slot_index = jnp.arange(capacity, dtype=jnp.int32)
    return member[None] * (ranking[None] == slot_index[:, None, None])


def damping_factor(half_step, decay, wave_index):
    wave_square = (wave_index.astype(jnp.float32) * (math.pi / KEEP)) ** 2
    damping = half_step[None, :, None] * (decay[None, :, :] + wave_square[:, None, None])
    return (1.0 - damping) / (1.0 + damping)


def on_device_any(fields, mode_group, half_step, decay, eigen_inverse, eigen_vectors):
    bit_count = lax.axis_size("span").bit_length() - 1
    real_part, imag_part = butterfly(fields, bit_count)
    spectra, mode_index = mode_transform(real_part, imag_part, bit_count)
    kept_modes = spectra.shape[1]
    group_count = lax.axis_size("rad")
    capacity = min(kept_modes, 2 * kept_modes // group_count)
    planes = fields.shape[1]
    radial_rows = fields.shape[2]
    arranged = spectra.reshape(2, kept_modes, 2, planes, radial_rows)
    placing = placement_table(mode_group[:, 0], group_count, capacity)
    placing_float = placing.astype(jnp.float32)
    packed = jnp.einsum("sgb,cbfal->scfagl", placing_float, arranged, precision=precise)
    packed = packed.reshape(capacity, 2, 2, planes, group_count * radial_rows)
    regrouped = lax.all_to_all(packed, "rad", split_axis=4, concat_axis=4, tiled=True)
    own_slots = lax.dynamic_index_in_dim(placing, lax.axis_index("rad"), 1, keepdims=False)
    slot_modes = jnp.sum(own_slots * mode_index[None, :], axis=1)
    factor = damping_factor(half_step, decay, slot_modes)
    inner_part = jnp.einsum("scfar,fir->scfai", regrouped, eigen_inverse, precision=precise)
    inner_part = inner_part * factor[:, None, :, None, :]
    result = jnp.einsum("scfai,fri->scfar", inner_part, eigen_vectors, precision=precise)
    return result.reshape(1, 1, capacity, 2, 2, planes, group_count * radial_rows)


HALF = 8
BLOCK = 64
PARTS = 3
LAST_PARTS = (2, 1)
VMEM_BYTES = 24 * 1024 * 1024


def flip3(value):
    return (value & 1) << 2 | value & 2 | value >> 2


def swap_span(value, distance):
    pairs = [(source, source ^ distance) for source in range(lax.axis_size("span"))]
    return lax.ppermute(value, "span", pairs)


def swap_rad(value):
    return lax.ppermute(value, "rad", [(0, 1), (1, 0)])


def split_pair(value):
    high = value.astype(jnp.bfloat16)
    low = (value - high.astype(jnp.float32)).astype(jnp.bfloat16)
    return high, low


def dot_rows(left, right):
    return lax.dot_general(left, right, contract_rows, preferred_element_type=jnp.float32)


def dot_split(left, right):
    left_high, left_low = left
    right_high, right_low = right
    total = dot_rows(left_high, right_high)
    total = total + dot_rows(left_low, right_high)
    return total + dot_rows(left_high, right_low)


def transform_8(real, imag):
    root = math.sqrt(0.5)
    er, ei, orr, oi = [], [], [], []
    for j in range(4):
        er.append(real[j] + real[j + 4])
        ei.append(imag[j] + imag[j + 4])
        dr = real[j] - real[j + 4]
        di = imag[j] - imag[j + 4]
        if j == 0:
            orr.append(dr)
            oi.append(di)
        elif j == 1:
            orr.append((dr + di) * root)
            oi.append((di - dr) * root)
        elif j == 2:
            orr.append(di)
            oi.append(-dr)
        else:
            orr.append((di - dr) * root)
            oi.append((-di - dr) * root)

    def transform_4(r, i):
        ar, ai = r[0] + r[2], i[0] + i[2]
        br, bi = r[0] - r[2], i[0] - i[2]
        cr, ci = r[1] + r[3], i[1] + i[3]
        dr, di = r[1] - r[3], i[1] - i[3]
        return [(ar + cr, ai + ci), (br + di, bi - dr), (ar - cr, ai - ci), (br - di, bi + dr)]

    even = transform_4(er, ei)
    odd = transform_4(orr, oi)
    return [even[q // 2] if q % 2 == 0 else odd[q // 2] for q in range(8)]


def half_sums_kernel(counts, place, *refs):
    cells, refs = refs[: len(counts)], refs[len(counts) :]
    cos_turn, sin_turn, table_rows = refs[:3]
    outs, (ordered, high, low) = refs[3:-3], refs[-3:]
    me, parity = place[0], place[1]
    sign = place[2].astype(jnp.float32)
    width = ordered.shape[-1]
    distance = 0
    for ref, count in zip(cells, counts):
        for index in range(count):
            ordered[me ^ distance] = ref[index]
            distance += 1

    turn_real, turn_imag = [], []
    for j in range(HALF):
        angle = 2.0 * math.pi * j / 16
        turn_real.append(sign * jnp.where(parity == 1, math.cos(angle), 1.0))
        turn_imag.append(sign * jnp.where(parity == 1, -math.sin(angle), 0.0))

    def one_block(step, carry):
        rows = pl.ds(pl.multiple_of(step * 16, 16), 16)
        lower = pl.ds(pl.multiple_of(BLOCK + step * 16, 16), 16)
        for lane in range(0, width, 128):
            real, imag = [], []
            for j in range(HALF):
                value = ordered[j, rows, lane : lane + 128]
                real.append(value * turn_real[j])
                imag.append(value * turn_imag[j])
            sums = transform_8(real, imag)
            for q in range(HALF):
                sum_real, sum_imag = sums[q]
                cosine = cos_turn[parity, q : q + 1, lane : lane + 128]
                sine = sin_turn[parity, q : q + 1, lane : lane + 128]
                real_high, real_low = split_pair(sum_real * cosine + sum_imag * sine)
                imag_high, imag_low = split_pair(sum_imag * cosine - sum_real * sine)
                high[q, rows, lane : lane + 128] = real_high
                high[q, rows, width + lane : width + lane + 128] = imag_high
                high[q, lower, lane : lane + 128] = imag_high
                high[q, lower, width + lane : width + lane + 128] = -real_high
                low[q, rows, lane : lane + 128] = real_low
                low[q, rows, width + lane : width + lane + 128] = imag_low
                low[q, lower, lane : lane + 128] = imag_low
                low[q, lower, width + lane : width + lane + 128] = -real_low
        return carry

    lax.fori_loop(0, BLOCK // 16, one_block, 0)
    table = split_pair(table_rows[...])
    for q in range(0, HALF, 2):
        lines_high = high[q : q + 2].reshape(4 * BLOCK, 2 * width)
        lines_low = low[q : q + 2].reshape(4 * BLOCK, 2 * width)
        result = dot_split(table, (lines_high, lines_low))
        first = 0
        for out in outs:
            rows = slice(first, first + out.shape[1])
            out[me ^ flip3(q)] = result[rows, : 2 * BLOCK]
            out[me ^ flip3(q + 1)] = result[rows, 2 * BLOCK :]
            first += out.shape[1]


def half_sums(place, cells, tables, parts):
    width = cells[0][0].shape[-1]
    rows = tables[2].shape[0]
    counts = [array.shape[0] if count is None else count for array, count, _ in cells]

    def full(array):
        return pl.BlockSpec(array.shape, lambda i: (0,) * array.ndim)

    def some(count, inner):
        return pl.BlockSpec((count, BLOCK, width), lambda i: (0, inner, 0))

    return pl.pallas_call(
        functools.partial(half_sums_kernel, counts),
        grid=(1,),
        out_shape=[
            jax.ShapeDtypeStruct((HALF, part, 2 * BLOCK), jnp.float32) for part in parts
        ],
        in_specs=[pl.BlockSpec(memory_space=pltpu.SMEM)]
        + [some(count, inner) for count, (_, _, inner) in zip(counts, cells)]
        + [full(table) for table in tables],
        out_specs=[
            pl.BlockSpec((HALF, part, 2 * BLOCK), lambda i: (0, 0, 0)) for part in parts
        ],
        scratch_shapes=[
            pltpu.VMEM((HALF, BLOCK, width), jnp.float32),
            pltpu.VMEM((HALF, 2 * BLOCK, 2 * width), jnp.bfloat16),
            pltpu.VMEM((HALF, 2 * BLOCK, 2 * width), jnp.bfloat16),
        ],
        cost_estimate=pl.CostEstimate(
            flops=rows * BLOCK * width,
            bytes_accessed=BLOCK * width * 4,
            transcendentals=0,
        ),
        compiler_params=pltpu.CompilerParams(vmem_limit_bytes=VMEM_BYTES),
        name="half_sums",
    )(place, *[array for array, _, _ in cells], *tables)


def gather_planes_kernel(place, *refs):
    own, from_z, out, ordered = refs[0], refs[1], refs[-2], refs[-1]
    me = place[0]
    ordered[me] = own[0]
    ordered[me ^ 4] = from_z[0]
    for distance in range(1, 4):
        for index in range(2):
            ordered[me ^ (distance + 4 * index)] = refs[1 + distance][index]
    for plane in range(HALF):
        out[:, plane, :] = ordered[plane]


def gather_planes(place, own, from_z, others):
    modes, lanes = own.shape[-2:]
    one = pl.BlockSpec((1, modes, lanes), lambda i: (0, 0, 0))
    two = pl.BlockSpec((2, modes, lanes), lambda i: (0, 0, 0))
    return pl.pallas_call(
        gather_planes_kernel,
        grid=(1,),
        out_shape=jax.ShapeDtypeStruct((modes, HALF, lanes), jnp.float32),
        in_specs=[pl.BlockSpec(memory_space=pltpu.SMEM), one, one, two, two, two],
        out_specs=pl.BlockSpec((modes, HALF, lanes), lambda i: (0, 0, 0)),
        scratch_shapes=[pltpu.VMEM((HALF, modes, lanes), jnp.float32)],
        cost_estimate=pl.CostEstimate(
            flops=0, bytes_accessed=8 * HALF * modes * lanes, transcendentals=0
        ),
        compiler_params=pltpu.CompilerParams(vmem_limit_bytes=VMEM_BYTES),
        name="gather_planes",
    )(place, own, from_z, *others)


def solve_kernel(count, place, *refs):
    blocks = refs[: 2 * count]
    inverse, vectors, factor = refs[2 * count : 2 * count + 3]
    out = refs[-1]
    modes = out.shape[0]
    radial = out.shape[-1]

    @pl.when(place[3] == 1)
    def _():
        inverse_pair = split_pair(inverse[0])
        vectors_pair = split_pair(vectors[0])
        scale = jnp.broadcast_to(factor[0][:, None, :], (modes, HALF, radial))
        scale = scale.reshape(modes * HALF, radial)
        whole = [block[...].reshape(modes * HALF, 2 * BLOCK) for block in blocks]
        for part in range(2):
            lanes = slice(part * BLOCK, (part + 1) * BLOCK)
            lines = jnp.concatenate([value[:, lanes] for value in whole], axis=1)
            inner = dot_split(split_pair(lines), inverse_pair) * scale
            solved = dot_split(split_pair(inner), vectors_pair)
            out[:, part, 0] = solved.reshape(modes, HALF, radial)

    @pl.when(place[3] != 1)
    def _():
        out[...] = jnp.zeros_like(out)


def solve(place, field, first, count, blocks, inverse, vectors, factor, earlier):
    modes = factor.shape[1]
    radial = inverse.shape[-1]
    step = modes // PARTS

    def lines(array):
        offset = first if array.shape[0] == modes else 0
        return pl.BlockSpec((step, HALF, 2 * BLOCK), lambda i: (offset + i, 0, 0))

    matrix = pl.BlockSpec((1, radial, radial), lambda i: (field, 0, 0))
    in_specs = [pl.BlockSpec(memory_space=pltpu.SMEM)] + [lines(block) for block in blocks]
    in_specs += [matrix, matrix]
    in_specs += [pl.BlockSpec((1, step, radial), lambda i: (field, first + i, 0))]
    operands = [place, *blocks, inverse, vectors, factor]
    aliases = {}
    if earlier is not None:
        aliases = {len(operands): 0}
        operands.append(earlier)
        in_specs.append(pl.BlockSpec(memory_space=pl.ANY))

    def kernel(*refs):
        kept = refs if earlier is None else refs[: len(operands) - 1] + refs[-1:]
        solve_kernel(len(blocks) // 2, *kept)

    return pl.pallas_call(
        kernel,
        grid=(count,),
        out_shape=jax.ShapeDtypeStruct((modes, 2, 2, HALF, radial), jnp.float32),
        in_specs=in_specs,
        out_specs=pl.BlockSpec(
            (step, 2, 1, HALF, radial), lambda i: (first + i, 0, field, 0, 0)
        ),
        input_output_aliases=aliases,
        cost_estimate=pl.CostEstimate(
            flops=count * modes * radial * radial,
            bytes_accessed=count * modes * radial,
            transcendentals=0,
        ),
        compiler_params=pltpu.CompilerParams(vmem_limit_bytes=VMEM_BYTES),
        name="solve",
    )(*operands)


def mode_tables(width, modes):
    cells = np.arange(width)
    residue = 2 * np.arange(HALF)[None, :, None] + np.arange(2)[:, None, None]
    turn = 2.0 * np.pi * residue * cells / (2 * HALF * width)
    padded = -(-modes // 16) * 16
    angle = 2.0 * np.pi * (np.arange(padded)[:, None] * cells[None, :] % width) / width
    table = np.concatenate([np.cos(angle), np.sin(angle)], axis=1)
    table = table / math.sqrt(2 * HALF * width)
    table[modes:] = 0.0
    return tuple(array.astype(np.float32) for array in (np.cos(turn), np.sin(turn), table))


def on_device_halves(fields, mode_group, half_step, decay, eigen_inverse, eigen_vectors):
    span = lax.axis_index("span")
    rad = lax.axis_index("rad")
    me = span & 7
    half = span >> 3
    rows = fields.shape[2]
    width = fields.shape[3]
    modes = KEEP // 16
    tables = mode_tables(width, modes)

    heavy = (mode_group[0, 0] == rad).astype(jnp.int32)
    one = jnp.ones_like(me)
    place_send = jnp.stack([me, 1 - half, one, heavy])
    place_keep = jnp.stack([me, half, 1 - 2 * half, heavy])

    mode_index = bit_reverse(span, 4) + 16 * jnp.arange(modes, dtype=jnp.int32)
    factor = damping_factor(half_step, decay, mode_index).transpose(1, 0, 2)
    own = lax.dynamic_slice_in_dim(eigen_inverse, rad * rows, rows, 2)
    other = lax.dynamic_slice_in_dim(eigen_inverse, (1 - rad) * rows, rows, 2)
    inverse = jnp.concatenate([own, other], axis=2)

    units = [(field, block) for field in range(2) for block in range(rows // BLOCK)]
    total = len(units)
    per_field = rows // BLOCK
    last = total - 1

    def plane_rows(field, start, count, distance):
        piece = lax.dynamic_slice(
            fields, (field, me ^ distance, start, 0), (1, 1, count, width)
        )
        return piece.reshape(count, width)

    def swap_core(field, start, count):
        paired = fields.reshape(2, 4, 2, rows, width)
        piece = lax.dynamic_slice(
            paired, (field, 0, 1 - (me & 1), start, 0), (1, 4, 1, count, width)
        )
        return swap_span(piece.reshape(4, count, width), 1)

    def core_rows(core, start, count, distance):
        plane = (me ^ distance) >> 1
        piece = lax.dynamic_slice(core, (plane, start, 0), (1, count, width))
        return piece.reshape(count, width)

    def away_direct(core, field, start, count):
        return [
            jnp.stack([plane_rows(field, start, count, d), core_rows(core, start, count, d)])
            for d in (2, 4, 6)
        ]

    def swap_direct(away):
        return [swap_span(value, distance) for value, distance in zip(away, (2, 4, 6))]

    def near_cells(core, field, start, core_start):
        mine = plane_rows(field, start, BLOCK, 0)
        return [(mine[None], 1, 0), (core_rows(core, core_start, BLOCK, 0)[None], 1, 0)]

    def away_x(core, inner, count):
        rows_of = (inner * BLOCK, count * BLOCK)
        away = []
        for distance in (2, 6):
            away.append(plane_rows(1, *rows_of, distance))
            away.append(core_rows(core, *rows_of, distance))
        return jnp.stack(away)

    def away_z(core, inner, from_x, place):
        rows_of = (inner * BLOCK, BLOCK)
        away = [plane_rows(1, *rows_of, 4)[None], core_rows(core, *rows_of, 4)[None]]
        away += [from_x[2:, place * BLOCK : (place + 1) * BLOCK]]
        return jnp.concatenate(away)

    def share(kept, came):
        return kept[:4] + came[:4], swap_span(kept[4:] + came[4:], 4)

    def finish(near, from_z):
        others = []
        for distance in range(1, 4):
            away = jnp.stack([near[distance], from_z[distance]])
            others.append(swap_span(away, distance))
        return gather_planes(place_keep, near, from_z, others)

    def tie(*values):
        return lax.optimization_barrier(values)

    def sums(place, unit):
        step = modes // PARTS
        parts = [step * count for count in LAST_PARTS] if unit == last else [modes]
        return half_sums(place, cells[unit], tables, parts)

    cells = {}
    sent, kept, came, mine, other = {}, {}, {}, {}, {}
    def direct_unit(core, unit, arrays):
        start = units[unit][1] * BLOCK
        return near_cells(core, 0, start, start) + [(array, 2, 0) for array in arrays]

    core_a = swap_core(0, 0, rows)
    away = [away_direct(core_a, 0, n * BLOCK, BLOCK) for n in range(per_field)]
    direct = [swap_direct(away[0]), swap_direct(away[1])]
    core_c = swap_core(1, 0, rows)
    cells[0] = direct_unit(core_a, 0, direct[0])
    sent[0] = sums(place_send, 0)
    later_x = [away_x(core_c, 0, 2), away_x(core_c, 2, 1)]
    sent[0], direct[1], away[2], later_x, core_c, me = tie(
        sent[0], direct[1], away[2], later_x, core_c, me
    )
    cells[1] = direct_unit(core_a, 1, direct[1])
    matrices = (inverse, eigen_vectors, factor)
    from_x = []
    result = None
    for step in range(last):
        came[step] = swap_span(sent[step][0], HALF)
        extra = {}
        if step == 0:
            kept[0] = sums(place_keep, 0)
            extra["direct"] = swap_direct(away[2])
        if step < 2:
            extra["x"] = swap_span(later_x[step], 2)
        sent[step + 1] = sums(place_send, step + 1)
        kept[step + 1] = sums(place_keep, step + 1)
        if 1 <= step <= 3:
            unit = step + 2
            inner = unit - per_field
            source, place = (from_x[0], inner) if inner < 2 else (from_x[1], 0)
            extra["z"] = swap_span(away_z(core_c, inner, source, place), 4)
            cells[unit] = near_cells(core_c, 1, inner * BLOCK, inner * BLOCK)
            cells[unit] += [(source, 2, place)]
        if step >= 1:
            near, from_z = share(kept[step - 1][0], came[step - 1])
            from_z, sent[step + 1], kept[step + 1] = tie(
                from_z, sent[step + 1], kept[step + 1]
            )
            extra["mine"] = finish(near, from_z)
        if step >= 2:
            extra["other"] = swap_rad(mine[step - 2])
        came[step], sent[step + 1], kept[step + 1], extra, me = tie(
            came[step], sent[step + 1], kept[step + 1], extra, me
        )
        if "direct" in extra:
            cells[2] = direct_unit(core_a, 2, extra["direct"])
        if "x" in extra:
            from_x.append(extra["x"])
        if "z" in extra:
            cells[step + 2].append((extra["z"], 4, 0))
        if step >= 1:
            mine[step - 1] = extra["mine"]
        if step >= 2:
            other[step - 2] = extra["other"]

    def blocks_of(numbers, part=None):
        chosen = [mine[n] if n != last else mine[n][part] for n in numbers]
        return chosen + [other[n] if n != last else other[n][part] for n in numbers]

    came[last] = [swap_span(part, HALF) for part in sent[last]]
    other[last - 2] = swap_rad(mine[last - 2])
    near, from_z = share(kept[last - 1][0], came[last - 1])
    blocks = blocks_of(range(per_field))
    result = solve(place_keep, 0, 0, 2, blocks, *matrices, None)
    from_z, result = tie(from_z, result)
    mine[last - 1] = finish(near, from_z)
    came[last][0], mine[last - 1], other[last - 2], result = tie(
        came[last][0], mine[last - 1], other[last - 2], result
    )
    other[last - 1] = swap_rad(mine[last - 1])
    near, from_z = share(kept[last][0], came[last][0])
    result = solve(place_keep, 0, 2, 1, blocks, *matrices, result)
    from_z, result = tie(from_z, result)
    first = finish(near, from_z)
    first, came[last][1], other[last - 1] = tie(first, came[last][1], other[last - 1])
    other_first = swap_rad(first)
    second = finish(*share(kept[last][1], came[last][1]))
    second, other_first = tie(second, other_first)
    mine[last] = [first, second]
    other[last] = [other_first, swap_rad(second)]
    start = 0
    for part, count in enumerate(LAST_PARTS):
        blocks = blocks_of(range(per_field, total), part)
        result = solve(place_keep, 1, start, count, blocks, *matrices, result)
        start += count
    return result[None, None]


def solution(mesh):
    placed = (P(None, None, "rad", "span"), P(None, "span"), P(), P(), P(), P())
    halves = mesh.shape["span"] == 2 * HALF and mesh.shape["rad"] == 2
    return jax.shard_map(
        on_device_halves if halves else on_device_any,
        mesh=mesh,
        in_specs=placed,
        out_specs=P("span", "rad", None, None, None, None, None),
        check_vma=False,
    )
```

```python
import functools
import math

import jax
import jax.numpy as jnp
import numpy as np
from jax import lax
from jax.experimental import pallas as pl
from jax.experimental.pallas import tpu as pltpu
from jax.sharding import PartitionSpec as P

KEEP = 2688


precise = lax.Precision.HIGHEST
contract_rows = (((1,), (1,)), ((), ()))


def partner_2(value, axis, distance):
    mask = 2**distance
    pairs = [(source, source ^ mask) for source in range(lax.axis_size(axis))]
    return lax.ppermute(value, axis, pairs)


def bit_reverse(value, bit_count):
    flipped = jnp.zeros_like(value)
    for section_bit in range(bit_count):
        flipped = flipped + (value >> section_bit & 1) * 2 ** (bit_count - 1 - section_bit)
    return flipped


def section_angles(device, section_bit):
    upper_half = device >> section_bit & 1 == 1
    twiddle_index = jnp.where(upper_half, device % 2**section_bit, 0)
    angles = twiddle_index.astype(jnp.float32) * (2.0 * math.pi / 2 ** (section_bit + 1))
    sign_factor = jnp.where(upper_half, -1.0, 1.0).astype(jnp.float32)
    return (sign_factor, jnp.cos(angles), jnp.sin(angles))


def butterfly(fields, bit_count):
    device = lax.axis_index("span")
    top_bit = bit_count - 1
    partner = partner_2(fields, "span", top_bit)
    sign_factor, cosine, sine_value = section_angles(device, top_bit)
    difference = partner + sign_factor * fields
    real_part = difference * cosine
    imag_part = -difference * sine_value
    for section_bit in range(bit_count - 2, -1, -1):
        other_real, other_imag = partner_2((real_part, imag_part), "span", section_bit)
        sign_factor, cosine, sine_value = section_angles(device, section_bit)
        diff_real = other_real + sign_factor * real_part
        diff_imag = other_imag + sign_factor * imag_part
        real_part = diff_real * cosine + diff_imag * sine_value
        imag_part = diff_imag * cosine - diff_real * sine_value
    return (real_part, imag_part)


def mode_transform(real_part, imag_part, bit_count):
    groups = lax.axis_size("span")
    line_width = real_part.shape[3]
    full_length = line_width * groups
    kept_modes = KEEP // groups
    residue = bit_reverse(lax.axis_index("span"), bit_count)
    mode_index = residue + groups * jnp.arange(kept_modes, dtype=jnp.int32)
    phases = mode_index[:, None] * jnp.arange(line_width, dtype=jnp.int32)[None, :] % full_length
    angles = phases.astype(jnp.float32) * (2.0 * math.pi / full_length)
    normalizer = 1.0 / math.sqrt(full_length)
    cosine_table = jnp.cos(angles) * normalizer
    sine_table = jnp.sin(angles) * normalizer
    line_real = real_part.reshape(-1, line_width)
    line_imag = imag_part.reshape(-1, line_width)
    cos_real = lax.dot_general(cosine_table, line_real, contract_rows, precision=precise)
    cos_imag = lax.dot_general(cosine_table, line_imag, contract_rows, precision=precise)
    sin_real = lax.dot_general(sine_table, line_real, contract_rows, precision=precise)
    sin_imag = lax.dot_general(sine_table, line_imag, contract_rows, precision=precise)
    return (jnp.stack([cos_real + sin_imag, cos_imag - sin_real]), mode_index)


def placement_table(column, group_count, capacity):
    groups = jnp.arange(group_count, dtype=jnp.int32)
    member = (column[None, :] == groups[:, None]).astype(jnp.int32)
    ranking = jnp.cumsum(member, axis=1, dtype=jnp.int32) - member
    slot_index = jnp.arange(capacity, dtype=jnp.int32)
    return member[None] * (ranking[None] == slot_index[:, None, None])


def damping_factor(half_step, decay, wave_index):
    wave_square = (wave_index.astype(jnp.float32) * (math.pi / KEEP)) ** 2
    damping = half_step[None, :, None] * (decay[None, :, :] + wave_square[:, None, None])
    return (1.0 - damping) / (1.0 + damping)


def on_device_any(fields, mode_group, half_step, decay, eigen_inverse, eigen_vectors):
    bit_count = lax.axis_size("span").bit_length() - 1
    real_part, imag_part = butterfly(fields, bit_count)
    spectra, mode_index = mode_transform(real_part, imag_part, bit_count)
    kept_modes = spectra.shape[1]
    group_count = lax.axis_size("rad")
    capacity = min(kept_modes, 2 * kept_modes // group_count)
    planes = fields.shape[1]
    radial_rows = fields.shape[2]
    arranged = spectra.reshape(2, kept_modes, 2, planes, radial_rows)
    placing = placement_table(mode_group[:, 0], group_count, capacity)
    placing_float = placing.astype(jnp.float32)
    packed = jnp.einsum("sgb,cbfal->scfagl", placing_float, arranged, precision=precise)
    packed = packed.reshape(capacity, 2, 2, planes, group_count * radial_rows)
    regrouped = lax.all_to_all(packed, "rad", split_axis=4, concat_axis=4, tiled=True)
    own_slots = lax.dynamic_index_in_dim(placing, lax.axis_index("rad"), 1, keepdims=False)
    slot_modes = jnp.sum(own_slots * mode_index[None, :], axis=1)
    factor = damping_factor(half_step, decay, slot_modes)
    inner_part = jnp.einsum("scfar,fir->scfai", regrouped, eigen_inverse, precision=precise)
    inner_part = inner_part * factor[:, None, :, None, :]
    result = jnp.einsum("scfai,fri->scfar", inner_part, eigen_vectors, precision=precise)
    return result.reshape(1, 1, capacity, 2, 2, planes, group_count * radial_rows)


HALF = 8
BLOCK = 64
PARTS = 3
LAST_PARTS = (2, 1)
VMEM_BYTES = 24 * 1024 * 1024


def flip3(value):
    return (value & 1) << 2 | value & 2 | value >> 2


def swap_span(value, distance):
    pairs = [(source, source ^ distance) for source in range(lax.axis_size("span"))]
    return lax.ppermute(value, "span", pairs)


def swap_rad(value):
    return lax.ppermute(value, "rad", [(0, 1), (1, 0)])


def split_pair(value):
    high = value.astype(jnp.bfloat16)
    low = (value - high.astype(jnp.float32)).astype(jnp.bfloat16)
    return high, low


def dot_rows(left, right):
    return lax.dot_general(left, right, contract_rows, preferred_element_type=jnp.float32)


def dot_split(left, right):
    left_high, left_low = left
    right_high, right_low = right
    total = dot_rows(left_high, right_high)
    total = total + dot_rows(left_low, right_high)
    return total + dot_rows(left_high, right_low)


def transform_8(real, imag):
    root = math.sqrt(0.5)
    er, ei, orr, oi = [], [], [], []
    for j in range(4):
        er.append(real[j] + real[j + 4])
        ei.append(imag[j] + imag[j + 4])
        dr = real[j] - real[j + 4]
        di = imag[j] - imag[j + 4]
        if j == 0:
            orr.append(dr)
            oi.append(di)
        elif j == 1:
            orr.append((dr + di) * root)
            oi.append((di - dr) * root)
        elif j == 2:
            orr.append(di)
            oi.append(-dr)
        else:
            orr.append((di - dr) * root)
            oi.append((-di - dr) * root)

    def transform_4(r, i):
        ar, ai = r[0] + r[2], i[0] + i[2]
        br, bi = r[0] - r[2], i[0] - i[2]
        cr, ci = r[1] + r[3], i[1] + i[3]
        dr, di = r[1] - r[3], i[1] - i[3]
        return [(ar + cr, ai + ci), (br + di, bi - dr), (ar - cr, ai - ci), (br - di, bi + dr)]

    even = transform_4(er, ei)
    odd = transform_4(orr, oi)
    return [even[q // 2] if q % 2 == 0 else odd[q // 2] for q in range(8)]


def half_sums_kernel(counts, place, *refs):
    cells, refs = refs[: len(counts)], refs[len(counts) :]
    cos_turn, sin_turn, table_rows = refs[:3]
    outs, (ordered, high, low) = refs[3:-3], refs[-3:]
    me, parity = place[0], place[1]
    sign = place[2].astype(jnp.float32)
    width = ordered.shape[-1]
    distance = 0
    for ref, count in zip(cells, counts):
        for index in range(count):
            ordered[me ^ distance] = ref[index]
            distance += 1

    turn_real, turn_imag = [], []
    for j in range(HALF):
        angle = 2.0 * math.pi * j / 16
        turn_real.append(sign * jnp.where(parity == 1, math.cos(angle), 1.0))
        turn_imag.append(sign * jnp.where(parity == 1, -math.sin(angle), 0.0))

    def one_block(step, carry):
        rows = pl.ds(pl.multiple_of(step * 16, 16), 16)
        lower = pl.ds(pl.multiple_of(BLOCK + step * 16, 16), 16)
        for lane in range(0, width, 128):
            real, imag = [], []
            for j in range(HALF):
                value = ordered[j, rows, lane : lane + 128]
                real.append(value * turn_real[j])
                imag.append(value * turn_imag[j])
            sums = transform_8(real, imag)
            for q in range(HALF):
                sum_real, sum_imag = sums[q]
                cosine = cos_turn[parity, q : q + 1, lane : lane + 128]
                sine = sin_turn[parity, q : q + 1, lane : lane + 128]
                real_high, real_low = split_pair(sum_real * cosine + sum_imag * sine)
                imag_high, imag_low = split_pair(sum_imag * cosine - sum_real * sine)
                high[q, rows, lane : lane + 128] = real_high
                high[q, rows, width + lane : width + lane + 128] = imag_high
                high[q, lower, lane : lane + 128] = imag_high
                high[q, lower, width + lane : width + lane + 128] = -real_high
                low[q, rows, lane : lane + 128] = real_low
                low[q, rows, width + lane : width + lane + 128] = imag_low
                low[q, lower, lane : lane + 128] = imag_low
                low[q, lower, width + lane : width + lane + 128] = -real_low
        return carry

    lax.fori_loop(0, BLOCK // 16, one_block, 0)
    table = split_pair(table_rows[...])
    for q in range(0, HALF, 2):
        lines_high = high[q : q + 2].reshape(4 * BLOCK, 2 * width)
        lines_low = low[q : q + 2].reshape(4 * BLOCK, 2 * width)
        result = dot_split(table, (lines_high, lines_low))
        first = 0
        for out in outs:
            rows = slice(first, first + out.shape[1])
            out[me ^ flip3(q)] = result[rows, : 2 * BLOCK]
            out[me ^ flip3(q + 1)] = result[rows, 2 * BLOCK :]
            first += out.shape[1]


def half_sums(place, cells, tables, parts):
    width = cells[0][0].shape[-1]
    rows = tables[2].shape[0]
    counts = [array.shape[0] if count is None else count for array, count, _ in cells]

    def full(array):
        return pl.BlockSpec(array.shape, lambda i: (0,) * array.ndim)

    def some(count, inner):
        return pl.BlockSpec((count, BLOCK, width), lambda i: (0, inner, 0))

    return pl.pallas_call(
        functools.partial(half_sums_kernel, counts),
        grid=(1,),
        out_shape=[
            jax.ShapeDtypeStruct((HALF, part, 2 * BLOCK), jnp.float32) for part in parts
        ],
        in_specs=[pl.BlockSpec(memory_space=pltpu.SMEM)]
        + [some(count, inner) for count, (_, _, inner) in zip(counts, cells)]
        + [full(table) for table in tables],
        out_specs=[
            pl.BlockSpec((HALF, part, 2 * BLOCK), lambda i: (0, 0, 0)) for part in parts
        ],
        scratch_shapes=[
            pltpu.VMEM((HALF, BLOCK, width), jnp.float32),
            pltpu.VMEM((HALF, 2 * BLOCK, 2 * width), jnp.bfloat16),
            pltpu.VMEM((HALF, 2 * BLOCK, 2 * width), jnp.bfloat16),
        ],
        cost_estimate=pl.CostEstimate(
            flops=rows * BLOCK * width,
            bytes_accessed=BLOCK * width * 4,
            transcendentals=0,
        ),
        compiler_params=pltpu.CompilerParams(vmem_limit_bytes=VMEM_BYTES),
        name="half_sums",
    )(place, *[array for array, _, _ in cells], *tables)


def gather_planes_kernel(place, *refs):
    own, from_z, out, ordered = refs[0], refs[1], refs[-2], refs[-1]
    me = place[0]
    ordered[me] = own[0]
    ordered[me ^ 4] = from_z[0]
    for distance in range(1, 4):
        for index in range(2):
            ordered[me ^ (distance + 4 * index)] = refs[1 + distance][index]
    for plane in range(HALF):
        out[:, plane, :] = ordered[plane]


def gather_planes(place, own, from_z, others):
    modes, lanes = own.shape[-2:]
    one = pl.BlockSpec((1, modes, lanes), lambda i: (0, 0, 0))
    two = pl.BlockSpec((2, modes, lanes), lambda i: (0, 0, 0))
    return pl.pallas_call(
        gather_planes_kernel,
        grid=(1,),
        out_shape=jax.ShapeDtypeStruct((modes, HALF, lanes), jnp.float32),
        in_specs=[pl.BlockSpec(memory_space=pltpu.SMEM), one, one, two, two, two],
        out_specs=pl.BlockSpec((modes, HALF, lanes), lambda i: (0, 0, 0)),
        scratch_shapes=[pltpu.VMEM((HALF, modes, lanes), jnp.float32)],
        cost_estimate=pl.CostEstimate(
            flops=0, bytes_accessed=8 * HALF * modes * lanes, transcendentals=0
        ),
        compiler_params=pltpu.CompilerParams(vmem_limit_bytes=VMEM_BYTES),
        name="gather_planes",
    )(place, own, from_z, *others)


def solve_kernel(count, place, *refs):
    blocks = refs[: 2 * count]
    inverse, vectors, factor = refs[2 * count : 2 * count + 3]
    out = refs[-1]
    modes = out.shape[0]
    radial = out.shape[-1]

    @pl.when(place[3] == 1)
    def _():
        inverse_pair = split_pair(inverse[0])
        vectors_pair = split_pair(vectors[0])
        scale = jnp.broadcast_to(factor[0][:, None, :], (modes, HALF, radial))
        scale = scale.reshape(modes * HALF, radial)
        whole = [block[...].reshape(modes * HALF, 2 * BLOCK) for block in blocks]
        for part in range(2):
            lanes = slice(part * BLOCK, (part + 1) * BLOCK)
            lines = jnp.concatenate([value[:, lanes] for value in whole], axis=1)
            inner = dot_split(split_pair(lines), inverse_pair) * scale
            solved = dot_split(split_pair(inner), vectors_pair)
            out[:, part, 0] = solved.reshape(modes, HALF, radial)

    @pl.when(place[3] != 1)
    def _():
        out[...] = jnp.zeros_like(out)


def solve(place, field, first, count, blocks, inverse, vectors, factor, earlier):
    modes = factor.shape[1]
    radial = inverse.shape[-1]
    step = modes // PARTS

    def lines(array):
        offset = first if array.shape[0] == modes else 0
        return pl.BlockSpec((step, HALF, 2 * BLOCK), lambda i: (offset + i, 0, 0))

    matrix = pl.BlockSpec((1, radial, radial), lambda i: (field, 0, 0))
    in_specs = [pl.BlockSpec(memory_space=pltpu.SMEM)] + [lines(block) for block in blocks]
    in_specs += [matrix, matrix]
    in_specs += [pl.BlockSpec((1, step, radial), lambda i: (field, first + i, 0))]
    operands = [place, *blocks, inverse, vectors, factor]
    aliases = {}
    if earlier is not None:
        aliases = {len(operands): 0}
        operands.append(earlier)
        in_specs.append(pl.BlockSpec(memory_space=pl.ANY))

    def kernel(*refs):
        kept = refs if earlier is None else refs[: len(operands) - 1] + refs[-1:]
        solve_kernel(len(blocks) // 2, *kept)

    return pl.pallas_call(
        kernel,
        grid=(count,),
        out_shape=jax.ShapeDtypeStruct((modes, 2, 2, HALF, radial), jnp.float32),
        in_specs=in_specs,
        out_specs=pl.BlockSpec(
            (step, 2, 1, HALF, radial), lambda i: (first + i, 0, field, 0, 0)
        ),
        input_output_aliases=aliases,
        cost_estimate=pl.CostEstimate(
            flops=count * modes * radial * radial,
            bytes_accessed=count * modes * radial,
            transcendentals=0,
        ),
        compiler_params=pltpu.CompilerParams(vmem_limit_bytes=VMEM_BYTES),
        name="solve",
    )(*operands)


def mode_tables(width, modes):
    cells = np.arange(width)
    residue = 2 * np.arange(HALF)[None, :, None] + np.arange(2)[:, None, None]
    turn = 2.0 * np.pi * residue * cells / (2 * HALF * width)
    padded = -(-modes // 16) * 16
    angle = 2.0 * np.pi * (np.arange(padded)[:, None] * cells[None, :] % width) / width
    table = np.concatenate([np.cos(angle), np.sin(angle)], axis=1)
    table = table / math.sqrt(2 * HALF * width)
    table[modes:] = 0.0
    return tuple(array.astype(np.float32) for array in (np.cos(turn), np.sin(turn), table))


def on_device_halves(fields, mode_group, half_step, decay, eigen_inverse, eigen_vectors):
    span = lax.axis_index("span")
    rad = lax.axis_index("rad")
    me = span & 7
    half = span >> 3
    rows = fields.shape[2]
    width = fields.shape[3]
    modes = KEEP // 16
    tables = mode_tables(width, modes)

    heavy = (mode_group[0, 0] == rad).astype(jnp.int32)
    one = jnp.ones_like(me)
    place_send = jnp.stack([me, 1 - half, one, heavy])
    place_keep = jnp.stack([me, half, 1 - 2 * half, heavy])

    mode_index = bit_reverse(span, 4) + 16 * jnp.arange(modes, dtype=jnp.int32)
    factor = damping_factor(half_step, decay, mode_index).transpose(1, 0, 2)
    own = lax.dynamic_slice_in_dim(eigen_inverse, rad * rows, rows, 2)
    other = lax.dynamic_slice_in_dim(eigen_inverse, (1 - rad) * rows, rows, 2)
    inverse = jnp.concatenate([own, other], axis=2)

    units = [(field, block) for field in range(2) for block in range(rows // BLOCK)]
    total = len(units)
    per_field = rows // BLOCK
    last = total - 1

    def plane_rows(field, start, count, distance):
        piece = lax.dynamic_slice(
            fields, (field, me ^ distance, start, 0), (1, 1, count, width)
        )
        return piece.reshape(count, width)

    def swap_core(field, start, count):
        paired = fields.reshape(2, 4, 2, rows, width)
        piece = lax.dynamic_slice(
            paired, (field, 0, 1 - (me & 1), start, 0), (1, 4, 1, count, width)
        )
        return swap_span(piece.reshape(4, count, width), 1)

    def core_rows(core, start, count, distance):
        plane = (me ^ distance) >> 1
        piece = lax.dynamic_slice(core, (plane, start, 0), (1, count, width))
        return piece.reshape(count, width)

    def away_direct(core, field, start, count):
        return [
            jnp.stack([plane_rows(field, start, count, d), core_rows(core, start, count, d)])
            for d in (2, 4, 6)
        ]

    def swap_direct(away):
        return [swap_span(value, distance) for value, distance in zip(away, (2, 4, 6))]

    def near_cells(core, field, start, core_start):
        mine = plane_rows(field, start, BLOCK, 0)
        return [(mine[None], 1, 0), (core_rows(core, core_start, BLOCK, 0)[None], 1, 0)]

    def away_x(core, inner, count):
        rows_of = (inner * BLOCK, count * BLOCK)
        away = []
        for distance in (2, 6):
            away.append(plane_rows(1, *rows_of, distance))
            away.append(core_rows(core, *rows_of, distance))
        return jnp.stack(away)

    def away_z(core, inner, from_x, place):
        rows_of = (inner * BLOCK, BLOCK)
        away = [plane_rows(1, *rows_of, 4)[None], core_rows(core, *rows_of, 4)[None]]
        away += [from_x[2:, place * BLOCK : (place + 1) * BLOCK]]
        return jnp.concatenate(away)

    def share(kept, came):
        return kept[:4] + came[:4], swap_span(kept[4:] + came[4:], 4)

    def swap_modes(near, from_z):
        return [
            swap_span(jnp.stack([near[distance], from_z[distance]]), distance)
            for distance in range(1, 4)
        ]

    def finish(near, from_z):
        return gather_planes(place_keep, near, from_z, swap_modes(near, from_z))

    def tie(*values):
        return lax.optimization_barrier(values)

    def sums(place, unit):
        step = modes // PARTS
        parts = [step * count for count in LAST_PARTS] if unit == last else [modes]
        return half_sums(place, cells[unit], tables, parts)

    cells = {}
    sent, kept, came, mine, other = {}, {}, {}, {}, {}
    def direct_unit(core, unit, arrays):
        start = units[unit][1] * BLOCK
        return near_cells(core, 0, start, start) + [(array, 2, 0) for array in arrays]

    core_a = swap_core(0, 0, rows)
    away = [away_direct(core_a, 0, n * BLOCK, BLOCK) for n in range(per_field)]
    direct = [swap_direct(away[0]), swap_direct(away[1])]
    core_c = swap_core(1, 0, rows)
    cells[0] = direct_unit(core_a, 0, direct[0])
    sent[0] = sums(place_send, 0)
    later_x = [away_x(core_c, 0, 2), away_x(core_c, 2, 1)]
    sent[0], direct[1], away[2], later_x, core_c, me = tie(
        sent[0], direct[1], away[2], later_x, core_c, me
    )
    cells[1] = direct_unit(core_a, 1, direct[1])
    matrices = (inverse, eigen_vectors, factor)
    from_x, swapped = [], {}
    result = None
    for step in range(last):
        came[step] = swap_span(sent[step][0], HALF)
        extra = {}
        if step == 0:
            kept[0] = sums(place_keep, 0)
            extra["direct"] = swap_direct(away[2])
        if step < 2:
            extra["x"] = swap_span(later_x[step], 2)
        sent[step + 1] = sums(place_send, step + 1)
        kept[step + 1] = sums(place_keep, step + 1)
        if 1 <= step <= 3:
            unit = step + 2
            inner = unit - per_field
            source, place = (from_x[0], inner) if inner < 2 else (from_x[1], 0)
            extra["z"] = swap_span(away_z(core_c, inner, source, place), 4)
            cells[unit] = near_cells(core_c, 1, inner * BLOCK, inner * BLOCK)
            cells[unit] += [(source, 2, place)]
        if step >= 1:
            extra["swapped"] = share(kept[step - 1][0], came[step - 1])
        if step >= 2:
            extra["mine"] = finish(*swapped[step - 2])
        if step >= 3:
            extra["other"] = swap_rad(mine[step - 3])
        came[step], sent[step + 1], kept[step + 1], extra, me = tie(
            came[step], sent[step + 1], kept[step + 1], extra, me
        )
        if "direct" in extra:
            cells[2] = direct_unit(core_a, 2, extra["direct"])
        if "x" in extra:
            from_x.append(extra["x"])
        if "z" in extra:
            cells[step + 2].append((extra["z"], 4, 0))
        if step >= 1:
            swapped[step - 1] = extra["swapped"]
        if step >= 2:
            mine[step - 2] = extra["mine"]
        if step >= 3:
            other[step - 3] = extra["other"]

    def blocks_of(numbers, part=None):
        chosen = [mine[n] if n != last else mine[n][part] for n in numbers]
        return chosen + [other[n] if n != last else other[n][part] for n in numbers]

    came[last] = [swap_span(part, HALF) for part in sent[last]]
    other[last - 3] = swap_rad(mine[last - 3])
    swapped[last - 1] = share(kept[last - 1][0], came[last - 1])
    mine[last - 2] = finish(*swapped[last - 2])
    came[last][0], swapped[last - 1], mine[last - 2], other[last - 3] = tie(
        came[last][0], swapped[last - 1], mine[last - 2], other[last - 3]
    )
    other[last - 2] = swap_rad(mine[last - 2])
    mine[last - 1] = finish(*swapped[last - 1])
    ready = share(kept[last][0], came[last][0])
    ready, mine[last - 1] = tie(ready, mine[last - 1])
    other[last - 1] = swap_rad(mine[last - 1])
    blocks = blocks_of(range(per_field))
    result = solve(place_keep, 0, 0, 2, blocks, *matrices, None)
    others, result = tie(swap_modes(*ready), result)
    first = gather_planes(place_keep, *ready, others)
    first, came[last][1], other[last - 2] = tie(first, came[last][1], other[last - 2])
    other_first = swap_rad(first)
    ready = share(kept[last][1], came[last][1])
    result = solve(place_keep, 0, 2, 1, blocks, *matrices, result)
    others, result = tie(swap_modes(*ready), result)
    second = gather_planes(place_keep, *ready, others)
    second, other[last - 1] = tie(second, other[last - 1])
    mine[last] = [first, second]
    other[last] = [other_first, swap_rad(second)]
    start = 0
    for part, count in enumerate(LAST_PARTS):
        blocks = blocks_of(range(per_field, total), part)
        result = solve(place_keep, 1, start, count, blocks, *matrices, result)
        start += count
    return result[None, None]


def solution(mesh):
    placed = (P(None, None, "rad", "span"), P(None, "span"), P(), P(), P(), P())
    halves = mesh.shape["span"] == 2 * HALF and mesh.shape["rad"] == 2
    return jax.shard_map(
        on_device_halves if halves else on_device_any,
        mesh=mesh,
        in_specs=placed,
        out_specs=P("span", "rad", None, None, None, None, None),
        check_vma=False,
    )
```

```python
import functools
import math

import jax
import jax.numpy as jnp
import numpy as np
from jax import lax
from jax.experimental import pallas as pl
from jax.experimental.pallas import tpu as pltpu
from jax.sharding import PartitionSpec as P

KEEP = 2688


precise = lax.Precision.HIGHEST
contract_rows = (((1,), (1,)), ((), ()))


def partner_2(value, axis, distance):
    mask = 2**distance
    pairs = [(source, source ^ mask) for source in range(lax.axis_size(axis))]
    return lax.ppermute(value, axis, pairs)


def bit_reverse(value, bit_count):
    flipped = jnp.zeros_like(value)
    for section_bit in range(bit_count):
        flipped = flipped + (value >> section_bit & 1) * 2 ** (bit_count - 1 - section_bit)
    return flipped


def section_angles(device, section_bit):
    upper_half = device >> section_bit & 1 == 1
    twiddle_index = jnp.where(upper_half, device % 2**section_bit, 0)
    angles = twiddle_index.astype(jnp.float32) * (2.0 * math.pi / 2 ** (section_bit + 1))
    sign_factor = jnp.where(upper_half, -1.0, 1.0).astype(jnp.float32)
    return (sign_factor, jnp.cos(angles), jnp.sin(angles))


def butterfly(fields, bit_count):
    device = lax.axis_index("span")
    top_bit = bit_count - 1
    partner = partner_2(fields, "span", top_bit)
    sign_factor, cosine, sine_value = section_angles(device, top_bit)
    difference = partner + sign_factor * fields
    real_part = difference * cosine
    imag_part = -difference * sine_value
    for section_bit in range(bit_count - 2, -1, -1):
        other_real, other_imag = partner_2((real_part, imag_part), "span", section_bit)
        sign_factor, cosine, sine_value = section_angles(device, section_bit)
        diff_real = other_real + sign_factor * real_part
        diff_imag = other_imag + sign_factor * imag_part
        real_part = diff_real * cosine + diff_imag * sine_value
        imag_part = diff_imag * cosine - diff_real * sine_value
    return (real_part, imag_part)


def mode_transform(real_part, imag_part, bit_count):
    groups = lax.axis_size("span")
    line_width = real_part.shape[3]
    full_length = line_width * groups
    kept_modes = KEEP // groups
    residue = bit_reverse(lax.axis_index("span"), bit_count)
    mode_index = residue + groups * jnp.arange(kept_modes, dtype=jnp.int32)
    phases = mode_index[:, None] * jnp.arange(line_width, dtype=jnp.int32)[None, :] % full_length
    angles = phases.astype(jnp.float32) * (2.0 * math.pi / full_length)
    normalizer = 1.0 / math.sqrt(full_length)
    cosine_table = jnp.cos(angles) * normalizer
    sine_table = jnp.sin(angles) * normalizer
    line_real = real_part.reshape(-1, line_width)
    line_imag = imag_part.reshape(-1, line_width)
    cos_real = lax.dot_general(cosine_table, line_real, contract_rows, precision=precise)
    cos_imag = lax.dot_general(cosine_table, line_imag, contract_rows, precision=precise)
    sin_real = lax.dot_general(sine_table, line_real, contract_rows, precision=precise)
    sin_imag = lax.dot_general(sine_table, line_imag, contract_rows, precision=precise)
    return (jnp.stack([cos_real + sin_imag, cos_imag - sin_real]), mode_index)


def placement_table(column, group_count, capacity):
    groups = jnp.arange(group_count, dtype=jnp.int32)
    member = (column[None, :] == groups[:, None]).astype(jnp.int32)
    ranking = jnp.cumsum(member, axis=1, dtype=jnp.int32) - member
    slot_index = jnp.arange(capacity, dtype=jnp.int32)
    return member[None] * (ranking[None] == slot_index[:, None, None])


def damping_factor(half_step, decay, wave_index):
    wave_square = (wave_index.astype(jnp.float32) * (math.pi / KEEP)) ** 2
    damping = half_step[None, :, None] * (decay[None, :, :] + wave_square[:, None, None])
    return (1.0 - damping) / (1.0 + damping)


def on_device_any(fields, mode_group, half_step, decay, eigen_inverse, eigen_vectors):
    bit_count = lax.axis_size("span").bit_length() - 1
    real_part, imag_part = butterfly(fields, bit_count)
    spectra, mode_index = mode_transform(real_part, imag_part, bit_count)
    kept_modes = spectra.shape[1]
    group_count = lax.axis_size("rad")
    capacity = min(kept_modes, 2 * kept_modes // group_count)
    planes = fields.shape[1]
    radial_rows = fields.shape[2]
    arranged = spectra.reshape(2, kept_modes, 2, planes, radial_rows)
    placing = placement_table(mode_group[:, 0], group_count, capacity)
    placing_float = placing.astype(jnp.float32)
    packed = jnp.einsum("sgb,cbfal->scfagl", placing_float, arranged, precision=precise)
    packed = packed.reshape(capacity, 2, 2, planes, group_count * radial_rows)
    regrouped = lax.all_to_all(packed, "rad", split_axis=4, concat_axis=4, tiled=True)
    own_slots = lax.dynamic_index_in_dim(placing, lax.axis_index("rad"), 1, keepdims=False)
    slot_modes = jnp.sum(own_slots * mode_index[None, :], axis=1)
    factor = damping_factor(half_step, decay, slot_modes)
    inner_part = jnp.einsum("scfar,fir->scfai", regrouped, eigen_inverse, precision=precise)
    inner_part = inner_part * factor[:, None, :, None, :]
    result = jnp.einsum("scfai,fri->scfar", inner_part, eigen_vectors, precision=precise)
    return result.reshape(1, 1, capacity, 2, 2, planes, group_count * radial_rows)


HALF = 8
BLOCK = 64
PARTS = 3
LAST_PARTS = (2, 1)
VMEM_BYTES = 24 * 1024 * 1024


def flip3(value):
    return (value & 1) << 2 | value & 2 | value >> 2


def swap_span(value, distance):
    pairs = [(source, source ^ distance) for source in range(lax.axis_size("span"))]
    return lax.ppermute(value, "span", pairs)


def swap_rad(value):
    return lax.ppermute(value, "rad", [(0, 1), (1, 0)])


def split_pair(value):
    high = value.astype(jnp.bfloat16)
    low = (value - high.astype(jnp.float32)).astype(jnp.bfloat16)
    return high, low


def dot_rows(left, right):
    return lax.dot_general(left, right, contract_rows, preferred_element_type=jnp.float32)


def dot_split(left, right):
    left_high, left_low = left
    right_high, right_low = right
    total = dot_rows(left_high, right_high)
    total = total + dot_rows(left_low, right_high)
    return total + dot_rows(left_high, right_low)


def transform_8(real, imag):
    root = math.sqrt(0.5)
    er, ei, orr, oi = [], [], [], []
    for j in range(4):
        er.append(real[j] + real[j + 4])
        ei.append(imag[j] + imag[j + 4])
        dr = real[j] - real[j + 4]
        di = imag[j] - imag[j + 4]
        if j == 0:
            orr.append(dr)
            oi.append(di)
        elif j == 1:
            orr.append((dr + di) * root)
            oi.append((di - dr) * root)
        elif j == 2:
            orr.append(di)
            oi.append(-dr)
        else:
            orr.append((di - dr) * root)
            oi.append((-di - dr) * root)

    def transform_4(r, i):
        ar, ai = r[0] + r[2], i[0] + i[2]
        br, bi = r[0] - r[2], i[0] - i[2]
        cr, ci = r[1] + r[3], i[1] + i[3]
        dr, di = r[1] - r[3], i[1] - i[3]
        return [(ar + cr, ai + ci), (br + di, bi - dr), (ar - cr, ai - ci), (br - di, bi + dr)]

    even = transform_4(er, ei)
    odd = transform_4(orr, oi)
    return [even[q // 2] if q % 2 == 0 else odd[q // 2] for q in range(8)]


def half_sums_kernel(counts, place, *refs):
    cells, refs = refs[: len(counts)], refs[len(counts) :]
    cos_turn, sin_turn, table_rows = refs[:3]
    outs, (ordered, high, low) = refs[3:-3], refs[-3:]
    me, parity = place[0], place[1]
    sign = place[2].astype(jnp.float32)
    width = ordered.shape[-1]
    distance = 0
    for ref, count in zip(cells, counts):
        for index in range(count):
            ordered[me ^ distance] = ref[index]
            distance += 1

    turn_real, turn_imag = [], []
    for j in range(HALF):
        angle = 2.0 * math.pi * j / 16
        turn_real.append(sign * jnp.where(parity == 1, math.cos(angle), 1.0))
        turn_imag.append(sign * jnp.where(parity == 1, -math.sin(angle), 0.0))

    def one_block(step, carry):
        rows = pl.ds(pl.multiple_of(step * 16, 16), 16)
        lower = pl.ds(pl.multiple_of(BLOCK + step * 16, 16), 16)
        for lane in range(0, width, 128):
            real, imag = [], []
            for j in range(HALF):
                value = ordered[j, rows, lane : lane + 128]
                real.append(value * turn_real[j])
                imag.append(value * turn_imag[j])
            sums = transform_8(real, imag)
            for q in range(HALF):
                sum_real, sum_imag = sums[q]
                cosine = cos_turn[parity, q : q + 1, lane : lane + 128]
                sine = sin_turn[parity, q : q + 1, lane : lane + 128]
                real_high, real_low = split_pair(sum_real * cosine + sum_imag * sine)
                imag_high, imag_low = split_pair(sum_imag * cosine - sum_real * sine)
                high[q, rows, lane : lane + 128] = real_high
                high[q, rows, width + lane : width + lane + 128] = imag_high
                high[q, lower, lane : lane + 128] = imag_high
                high[q, lower, width + lane : width + lane + 128] = -real_high
                low[q, rows, lane : lane + 128] = real_low
                low[q, rows, width + lane : width + lane + 128] = imag_low
                low[q, lower, lane : lane + 128] = imag_low
                low[q, lower, width + lane : width + lane + 128] = -real_low
        return carry

    lax.fori_loop(0, BLOCK // 16, one_block, 0)
    table = split_pair(table_rows[...])
    for q in range(0, HALF, 2):
        lines_high = high[q : q + 2].reshape(4 * BLOCK, 2 * width)
        lines_low = low[q : q + 2].reshape(4 * BLOCK, 2 * width)
        result = dot_split(table, (lines_high, lines_low))
        first = 0
        for out in outs:
            rows = slice(first, first + out.shape[1])
            out[me ^ flip3(q)] = result[rows, : 2 * BLOCK]
            out[me ^ flip3(q + 1)] = result[rows, 2 * BLOCK :]
            first += out.shape[1]


def half_sums(place, cells, tables, parts):
    width = cells[0][0].shape[-1]
    rows = tables[2].shape[0]
    counts = [array.shape[0] if count is None else count for array, count, _ in cells]

    def full(array):
        return pl.BlockSpec(array.shape, lambda i: (0,) * array.ndim)

    def some(count, inner):
        return pl.BlockSpec((count, BLOCK, width), lambda i: (0, inner, 0))

    return pl.pallas_call(
        functools.partial(half_sums_kernel, counts),
        grid=(1,),
        out_shape=[
            jax.ShapeDtypeStruct((HALF, part, 2 * BLOCK), jnp.float32) for part in parts
        ],
        in_specs=[pl.BlockSpec(memory_space=pltpu.SMEM)]
        + [some(count, inner) for count, (_, _, inner) in zip(counts, cells)]
        + [full(table) for table in tables],
        out_specs=[
            pl.BlockSpec((HALF, part, 2 * BLOCK), lambda i: (0, 0, 0)) for part in parts
        ],
        scratch_shapes=[
            pltpu.VMEM((HALF, BLOCK, width), jnp.float32),
            pltpu.VMEM((HALF, 2 * BLOCK, 2 * width), jnp.bfloat16),
            pltpu.VMEM((HALF, 2 * BLOCK, 2 * width), jnp.bfloat16),
        ],
        cost_estimate=pl.CostEstimate(
            flops=rows * BLOCK * width,
            bytes_accessed=BLOCK * width * 4,
            transcendentals=0,
        ),
        compiler_params=pltpu.CompilerParams(vmem_limit_bytes=VMEM_BYTES),
        name="half_sums",
    )(place, *[array for array, _, _ in cells], *tables)


def gather_planes_kernel(place, *refs):
    own, from_z, out, ordered = refs[0], refs[1], refs[-2], refs[-1]
    me = place[0]
    ordered[me] = own[0]
    ordered[me ^ 4] = from_z[0]
    for distance in range(1, 4):
        for index in range(2):
            ordered[me ^ (distance + 4 * index)] = refs[1 + distance][index]
    for plane in range(HALF):
        out[:, plane, :] = ordered[plane]


def gather_planes(place, own, from_z, others):
    modes, lanes = own.shape[-2:]
    one = pl.BlockSpec((1, modes, lanes), lambda i: (0, 0, 0))
    two = pl.BlockSpec((2, modes, lanes), lambda i: (0, 0, 0))
    return pl.pallas_call(
        gather_planes_kernel,
        grid=(1,),
        out_shape=jax.ShapeDtypeStruct((modes, HALF, lanes), jnp.float32),
        in_specs=[pl.BlockSpec(memory_space=pltpu.SMEM), one, one, two, two, two],
        out_specs=pl.BlockSpec((modes, HALF, lanes), lambda i: (0, 0, 0)),
        scratch_shapes=[pltpu.VMEM((HALF, modes, lanes), jnp.float32)],
        cost_estimate=pl.CostEstimate(
            flops=0, bytes_accessed=8 * HALF * modes * lanes, transcendentals=0
        ),
        compiler_params=pltpu.CompilerParams(vmem_limit_bytes=VMEM_BYTES),
        name="gather_planes",
    )(place, own, from_z, *others)


def solve_kernel(count, place, *refs):
    blocks = refs[: 2 * count]
    inverse, vectors, factor = refs[2 * count : 2 * count + 3]
    out = refs[-1]
    modes = out.shape[0]
    radial = out.shape[-1]

    @pl.when(place[3] == 1)
    def _():
        inverse_pair = split_pair(inverse[0])
        vectors_pair = split_pair(vectors[0])
        scale = jnp.broadcast_to(factor[0][:, None, :], (modes, HALF, radial))
        scale = scale.reshape(modes * HALF, radial)
        whole = [block[...].reshape(modes * HALF, 2 * BLOCK) for block in blocks]
        for part in range(2):
            lanes = slice(part * BLOCK, (part + 1) * BLOCK)
            lines = jnp.concatenate([value[:, lanes] for value in whole], axis=1)
            inner = dot_split(split_pair(lines), inverse_pair) * scale
            solved = dot_split(split_pair(inner), vectors_pair)
            out[:, part, 0] = solved.reshape(modes, HALF, radial)

    @pl.when(place[3] != 1)
    def _():
        out[...] = jnp.zeros_like(out)


def solve(place, field, first, count, blocks, inverse, vectors, factor, earlier):
    modes = factor.shape[1]
    radial = inverse.shape[-1]
    step = modes // PARTS

    def lines(array):
        offset = first if array.shape[0] == modes else 0
        return pl.BlockSpec((step, HALF, 2 * BLOCK), lambda i: (offset + i, 0, 0))

    matrix = pl.BlockSpec((1, radial, radial), lambda i: (field, 0, 0))
    in_specs = [pl.BlockSpec(memory_space=pltpu.SMEM)] + [lines(block) for block in blocks]
    in_specs += [matrix, matrix]
    in_specs += [pl.BlockSpec((1, step, radial), lambda i: (field, first + i, 0))]
    operands = [place, *blocks, inverse, vectors, factor]
    aliases = {}
    if earlier is not None:
        aliases = {len(operands): 0}
        operands.append(earlier)
        in_specs.append(pl.BlockSpec(memory_space=pl.ANY))

    def kernel(*refs):
        kept = refs if earlier is None else refs[: len(operands) - 1] + refs[-1:]
        solve_kernel(len(blocks) // 2, *kept)

    return pl.pallas_call(
        kernel,
        grid=(count,),
        out_shape=jax.ShapeDtypeStruct((modes, 2, 2, HALF, radial), jnp.float32),
        in_specs=in_specs,
        out_specs=pl.BlockSpec(
            (step, 2, 1, HALF, radial), lambda i: (first + i, 0, field, 0, 0)
        ),
        input_output_aliases=aliases,
        cost_estimate=pl.CostEstimate(
            flops=count * modes * radial * radial,
            bytes_accessed=count * modes * radial,
            transcendentals=0,
        ),
        compiler_params=pltpu.CompilerParams(vmem_limit_bytes=VMEM_BYTES),
        name="solve",
    )(*operands)


def mode_tables(width, modes):
    cells = np.arange(width)
    residue = 2 * np.arange(HALF)[None, :, None] + np.arange(2)[:, None, None]
    turn = 2.0 * np.pi * residue * cells / (2 * HALF * width)
    padded = -(-modes // 16) * 16
    angle = 2.0 * np.pi * (np.arange(padded)[:, None] * cells[None, :] % width) / width
    table = np.concatenate([np.cos(angle), np.sin(angle)], axis=1)
    table = table / math.sqrt(2 * HALF * width)
    table[modes:] = 0.0
    return tuple(array.astype(np.float32) for array in (np.cos(turn), np.sin(turn), table))


def on_device_halves(fields, mode_group, half_step, decay, eigen_inverse, eigen_vectors):
    span = lax.axis_index("span")
    rad = lax.axis_index("rad")
    me = span & 7
    half = span >> 3
    rows = fields.shape[2]
    width = fields.shape[3]
    modes = KEEP // 16
    tables = mode_tables(width, modes)

    heavy = (mode_group[0, 0] == rad).astype(jnp.int32)
    one = jnp.ones_like(me)
    place_send = jnp.stack([me, 1 - half, one, heavy])
    place_keep = jnp.stack([me, half, 1 - 2 * half, heavy])

    mode_index = bit_reverse(span, 4) + 16 * jnp.arange(modes, dtype=jnp.int32)
    factor = damping_factor(half_step, decay, mode_index).transpose(1, 0, 2)
    own = lax.dynamic_slice_in_dim(eigen_inverse, rad * rows, rows, 2)
    other = lax.dynamic_slice_in_dim(eigen_inverse, (1 - rad) * rows, rows, 2)
    inverse = jnp.concatenate([own, other], axis=2)

    units = [(field, block) for field in range(2) for block in range(rows // BLOCK)]
    total = len(units)
    per_field = rows // BLOCK
    last = total - 1

    def plane_rows(field, start, count, distance):
        piece = lax.dynamic_slice(
            fields, (field, me ^ distance, start, 0), (1, 1, count, width)
        )
        return piece.reshape(count, width)

    def swap_core(field, start, count):
        paired = fields.reshape(2, 4, 2, rows, width)
        piece = lax.dynamic_slice(
            paired, (field, 0, 1 - (me & 1), start, 0), (1, 4, 1, count, width)
        )
        return swap_span(piece.reshape(4, count, width), 1)

    def core_rows(core, start, count, distance):
        plane = (me ^ distance) >> 1
        piece = lax.dynamic_slice(core, (plane, start, 0), (1, count, width))
        return piece.reshape(count, width)

    def away_direct(core, field, start, count):
        return [
            jnp.stack([plane_rows(field, start, count, d), core_rows(core, start, count, d)])
            for d in (2, 4, 6)
        ]

    def swap_direct(away):
        return [swap_span(value, distance) for value, distance in zip(away, (2, 4, 6))]

    def near_cells(core, field, start, core_start):
        mine = plane_rows(field, start, BLOCK, 0)
        return [(mine[None], 1, 0), (core_rows(core, core_start, BLOCK, 0)[None], 1, 0)]

    def away_x(core, inner, count):
        rows_of = (inner * BLOCK, count * BLOCK)
        away = []
        for distance in (2, 6):
            away.append(plane_rows(1, *rows_of, distance))
            away.append(core_rows(core, *rows_of, distance))
        return jnp.stack(away)

    def away_z(core, inner, from_x, place):
        rows_of = (inner * BLOCK, BLOCK)
        away = [plane_rows(1, *rows_of, 4)[None], core_rows(core, *rows_of, 4)[None]]
        away += [from_x[2:, place * BLOCK : (place + 1) * BLOCK]]
        return jnp.concatenate(away)

    def share(kept, came):
        return kept[:4] + came[:4], swap_span(kept[4:] + came[4:], 4)

    def swap_modes(near, from_z):
        return [
            swap_span(jnp.stack([near[distance], from_z[distance]]), distance)
            for distance in range(1, 4)
        ]

    def finish(near, from_z):
        return gather_planes(place_keep, near, from_z, swap_modes(near, from_z))

    def tie(*values):
        return lax.optimization_barrier(values)

    def sums(place, unit):
        step = modes // PARTS
        parts = [step * count for count in LAST_PARTS] if unit == last else [modes]
        return half_sums(place, cells[unit], tables, parts)

    cells = {}
    sent, kept, came, mine, other = {}, {}, {}, {}, {}
    def direct_unit(core, unit, arrays):
        start = units[unit][1] * BLOCK
        return near_cells(core, 0, start, start) + [(array, 2, 0) for array in arrays]

    core_a = swap_core(0, 0, rows)
    away = [away_direct(core_a, 0, n * BLOCK, BLOCK) for n in range(per_field)]
    direct = [swap_direct(away[0]), swap_direct(away[1])]
    core_c = swap_core(1, 0, rows)
    cells[0] = direct_unit(core_a, 0, direct[0])
    sent[0] = sums(place_send, 0)
    later_x = [away_x(core_c, 0, 2), away_x(core_c, 2, 1)]
    sent[0], direct[1], away[2], later_x, core_c, me = tie(
        sent[0], direct[1], away[2], later_x, core_c, me
    )
    cells[1] = direct_unit(core_a, 1, direct[1])
    matrices = (inverse, eigen_vectors, factor)
    from_x, swapped = [], {}
    result = None
    for step in range(last):
        came[step] = swap_span(sent[step][0], HALF)
        extra = {}
        if step == 0:
            kept[0] = sums(place_keep, 0)
            extra["direct"] = swap_direct(away[2])
            extra["near"] = [
                [cell[0] for cell in near_cells(core_c, 1, inner * BLOCK, inner * BLOCK)]
                for inner in range(per_field)
            ]
        if step < 2:
            extra["x"] = swap_span(later_x[step], 2)
        sent[step + 1] = sums(place_send, step + 1)
        kept[step + 1] = sums(place_keep, step + 1)
        if 1 <= step <= 3:
            unit = step + 2
            inner = unit - per_field
            source, place = (from_x[0], inner) if inner < 2 else (from_x[1], 0)
            if inner == 0:
                next_z = away_z(core_c, 0, source, place)
            extra["z"] = swap_span(next_z, 4)
            if inner < 2:
                following = (from_x[0], 1) if inner == 0 else (from_x[1], 0)
                extra["away"] = away_z(core_c, inner + 1, *following)
            cells[unit] = [(array, 1, 0) for array in near[inner]]
            cells[unit] += [(source, 2, place)]
        if step >= 1:
            extra["swapped"] = share(kept[step - 1][0], came[step - 1])
        if step >= 2:
            extra["mine"] = finish(*swapped[step - 2])
        if step >= 3:
            extra["other"] = swap_rad(mine[step - 3])
        came[step], sent[step + 1], kept[step + 1], extra, me = tie(
            came[step], sent[step + 1], kept[step + 1], extra, me
        )
        if "direct" in extra:
            cells[2] = direct_unit(core_a, 2, extra["direct"])
            near = extra["near"]
        if "away" in extra:
            next_z = extra["away"]
        if "x" in extra:
            from_x.append(extra["x"])
        if "z" in extra:
            cells[step + 2].append((extra["z"], 4, 0))
        if step >= 1:
            swapped[step - 1] = extra["swapped"]
        if step >= 2:
            mine[step - 2] = extra["mine"]
        if step >= 3:
            other[step - 3] = extra["other"]

    def blocks_of(numbers, part=None):
        chosen = [mine[n] if n != last else mine[n][part] for n in numbers]
        return chosen + [other[n] if n != last else other[n][part] for n in numbers]

    came[last] = [swap_span(part, HALF) for part in sent[last]]
    other[last - 3] = swap_rad(mine[last - 3])
    swapped[last - 1] = share(kept[last - 1][0], came[last - 1])
    mine[last - 2] = finish(*swapped[last - 2])
    other[last - 2] = swap_rad(mine[last - 2])
    blocks = blocks_of(range(per_field))
    result = solve(place_keep, 0, 0, 2, blocks, *matrices, None)
    came[last][0], swapped[last - 1], result = tie(
        came[last][0], swapped[last - 1], result
    )
    mine[last - 1] = finish(*swapped[last - 1])
    ready = share(kept[last][0], came[last][0])
    ready, mine[last - 1], other[last - 2] = tie(ready, mine[last - 1], other[last - 2])
    other[last - 1] = swap_rad(mine[last - 1])
    first = finish(*ready)
    first, came[last][1] = tie(first, came[last][1])
    other_first = swap_rad(first)
    ready = share(kept[last][1], came[last][1])
    ready, other[last - 1] = tie(ready, other[last - 1])
    result = solve(place_keep, 0, 2, 1, blocks, *matrices, result)
    others, result = tie(swap_modes(*ready), result)
    second = gather_planes(place_keep, *ready, others)
    mine[last] = [first, second]
    other[last] = [other_first, swap_rad(second)]
    start = 0
    for part, count in enumerate(LAST_PARTS):
        blocks = blocks_of(range(per_field, total), part)
        result = solve(place_keep, 1, start, count, blocks, *matrices, result)
        start += count
    return result[None, None]


def solution(mesh):
    placed = (P(None, None, "rad", "span"), P(None, "span"), P(), P(), P(), P())
    halves = mesh.shape["span"] == 2 * HALF and mesh.shape["rad"] == 2
    return jax.shard_map(
        on_device_halves if halves else on_device_any,
        mesh=mesh,
        in_specs=placed,
        out_specs=P("span", "rad", None, None, None, None, None),
        check_vma=False,
    )
```

```python
import functools
import math

import jax
import jax.numpy as jnp
import numpy as np
from jax import lax
from jax.experimental import pallas as pl
from jax.experimental.pallas import tpu as pltpu
from jax.sharding import PartitionSpec as P

KEEP = 2688


precise = lax.Precision.HIGHEST
contract_rows = (((1,), (1,)), ((), ()))


def partner_2(value, axis, distance):
    mask = 2**distance
    pairs = [(source, source ^ mask) for source in range(lax.axis_size(axis))]
    return lax.ppermute(value, axis, pairs)


def bit_reverse(value, bit_count):
    flipped = jnp.zeros_like(value)
    for section_bit in range(bit_count):
        flipped = flipped + (value >> section_bit & 1) * 2 ** (bit_count - 1 - section_bit)
    return flipped


def section_angles(device, section_bit):
    upper_half = device >> section_bit & 1 == 1
    twiddle_index = jnp.where(upper_half, device % 2**section_bit, 0)
    angles = twiddle_index.astype(jnp.float32) * (2.0 * math.pi / 2 ** (section_bit + 1))
    sign_factor = jnp.where(upper_half, -1.0, 1.0).astype(jnp.float32)
    return (sign_factor, jnp.cos(angles), jnp.sin(angles))


def butterfly(fields, bit_count):
    device = lax.axis_index("span")
    top_bit = bit_count - 1
    partner = partner_2(fields, "span", top_bit)
    sign_factor, cosine, sine_value = section_angles(device, top_bit)
    difference = partner + sign_factor * fields
    real_part = difference * cosine
    imag_part = -difference * sine_value
    for section_bit in range(bit_count - 2, -1, -1):
        other_real, other_imag = partner_2((real_part, imag_part), "span", section_bit)
        sign_factor, cosine, sine_value = section_angles(device, section_bit)
        diff_real = other_real + sign_factor * real_part
        diff_imag = other_imag + sign_factor * imag_part
        real_part = diff_real * cosine + diff_imag * sine_value
        imag_part = diff_imag * cosine - diff_real * sine_value
    return (real_part, imag_part)


def mode_transform(real_part, imag_part, bit_count):
    groups = lax.axis_size("span")
    line_width = real_part.shape[3]
    full_length = line_width * groups
    kept_modes = KEEP // groups
    residue = bit_reverse(lax.axis_index("span"), bit_count)
    mode_index = residue + groups * jnp.arange(kept_modes, dtype=jnp.int32)
    phases = mode_index[:, None] * jnp.arange(line_width, dtype=jnp.int32)[None, :] % full_length
    angles = phases.astype(jnp.float32) * (2.0 * math.pi / full_length)
    normalizer = 1.0 / math.sqrt(full_length)
    cosine_table = jnp.cos(angles) * normalizer
    sine_table = jnp.sin(angles) * normalizer
    line_real = real_part.reshape(-1, line_width)
    line_imag = imag_part.reshape(-1, line_width)
    cos_real = lax.dot_general(cosine_table, line_real, contract_rows, precision=precise)
    cos_imag = lax.dot_general(cosine_table, line_imag, contract_rows, precision=precise)
    sin_real = lax.dot_general(sine_table, line_real, contract_rows, precision=precise)
    sin_imag = lax.dot_general(sine_table, line_imag, contract_rows, precision=precise)
    return (jnp.stack([cos_real + sin_imag, cos_imag - sin_real]), mode_index)


def placement_table(column, group_count, capacity):
    groups = jnp.arange(group_count, dtype=jnp.int32)
    member = (column[None, :] == groups[:, None]).astype(jnp.int32)
    ranking = jnp.cumsum(member, axis=1, dtype=jnp.int32) - member
    slot_index = jnp.arange(capacity, dtype=jnp.int32)
    return member[None] * (ranking[None] == slot_index[:, None, None])


def damping_factor(half_step, decay, wave_index):
    wave_square = (wave_index.astype(jnp.float32) * (math.pi / KEEP)) ** 2
    damping = half_step[None, :, None] * (decay[None, :, :] + wave_square[:, None, None])
    return (1.0 - damping) / (1.0 + damping)


def on_device_any(fields, mode_group, half_step, decay, eigen_inverse, eigen_vectors):
    bit_count = lax.axis_size("span").bit_length() - 1
    real_part, imag_part = butterfly(fields, bit_count)
    spectra, mode_index = mode_transform(real_part, imag_part, bit_count)
    kept_modes = spectra.shape[1]
    group_count = lax.axis_size("rad")
    capacity = min(kept_modes, 2 * kept_modes // group_count)
    planes = fields.shape[1]
    radial_rows = fields.shape[2]
    arranged = spectra.reshape(2, kept_modes, 2, planes, radial_rows)
    placing = placement_table(mode_group[:, 0], group_count, capacity)
    placing_float = placing.astype(jnp.float32)
    packed = jnp.einsum("sgb,cbfal->scfagl", placing_float, arranged, precision=precise)
    packed = packed.reshape(capacity, 2, 2, planes, group_count * radial_rows)
    regrouped = lax.all_to_all(packed, "rad", split_axis=4, concat_axis=4, tiled=True)
    own_slots = lax.dynamic_index_in_dim(placing, lax.axis_index("rad"), 1, keepdims=False)
    slot_modes = jnp.sum(own_slots * mode_index[None, :], axis=1)
    factor = damping_factor(half_step, decay, slot_modes)
    inner_part = jnp.einsum("scfar,fir->scfai", regrouped, eigen_inverse, precision=precise)
    inner_part = inner_part * factor[:, None, :, None, :]
    result = jnp.einsum("scfai,fri->scfar", inner_part, eigen_vectors, precision=precise)
    return result.reshape(1, 1, capacity, 2, 2, planes, group_count * radial_rows)


HALF = 8
BLOCK = 64
PARTS = 3
LAST_PARTS = (2, 1)
VMEM_BYTES = 24 * 1024 * 1024


def flip3(value):
    return (value & 1) << 2 | value & 2 | value >> 2


def swap_span(value, distance):
    pairs = [(source, source ^ distance) for source in range(lax.axis_size("span"))]
    return lax.ppermute(value, "span", pairs)


def swap_rad(value):
    return lax.ppermute(value, "rad", [(0, 1), (1, 0)])


def split_pair(value):
    high = value.astype(jnp.bfloat16)
    low = (value - high.astype(jnp.float32)).astype(jnp.bfloat16)
    return high, low


def dot_rows(left, right):
    return lax.dot_general(left, right, contract_rows, preferred_element_type=jnp.float32)


def dot_split(left, right):
    left_high, left_low = left
    right_high, right_low = right
    total = dot_rows(left_high, right_high)
    total = total + dot_rows(left_low, right_high)
    return total + dot_rows(left_high, right_low)


def transform_8(real, imag):
    root = math.sqrt(0.5)
    er, ei, orr, oi = [], [], [], []
    for j in range(4):
        er.append(real[j] + real[j + 4])
        ei.append(imag[j] + imag[j + 4])
        dr = real[j] - real[j + 4]
        di = imag[j] - imag[j + 4]
        if j == 0:
            orr.append(dr)
            oi.append(di)
        elif j == 1:
            orr.append((dr + di) * root)
            oi.append((di - dr) * root)
        elif j == 2:
            orr.append(di)
            oi.append(-dr)
        else:
            orr.append((di - dr) * root)
            oi.append((-di - dr) * root)

    def transform_4(r, i):
        ar, ai = r[0] + r[2], i[0] + i[2]
        br, bi = r[0] - r[2], i[0] - i[2]
        cr, ci = r[1] + r[3], i[1] + i[3]
        dr, di = r[1] - r[3], i[1] - i[3]
        return [(ar + cr, ai + ci), (br + di, bi - dr), (ar - cr, ai - ci), (br - di, bi + dr)]

    even = transform_4(er, ei)
    odd = transform_4(orr, oi)
    return [even[q // 2] if q % 2 == 0 else odd[q // 2] for q in range(8)]


def half_sums_kernel(counts, place, *refs):
    cells, refs = refs[: len(counts)], refs[len(counts) :]
    cos_turn, sin_turn, table_rows = refs[:3]
    outs, (ordered, high, low) = refs[3:-3], refs[-3:]
    me, parity = place[0], place[1]
    sign = place[2].astype(jnp.float32)
    width = ordered.shape[-1]
    distance = 0
    for ref, count in zip(cells, counts):
        for index in range(count):
            ordered[me ^ distance] = ref[index]
            distance += 1

    turn_real, turn_imag = [], []
    for j in range(HALF):
        angle = 2.0 * math.pi * j / 16
        turn_real.append(sign * jnp.where(parity == 1, math.cos(angle), 1.0))
        turn_imag.append(sign * jnp.where(parity == 1, -math.sin(angle), 0.0))

    def one_block(step, carry):
        rows = pl.ds(pl.multiple_of(step * 16, 16), 16)
        lower = pl.ds(pl.multiple_of(BLOCK + step * 16, 16), 16)
        for lane in range(0, width, 128):
            real, imag = [], []
            for j in range(HALF):
                value = ordered[j, rows, lane : lane + 128]
                real.append(value * turn_real[j])
                imag.append(value * turn_imag[j])
            sums = transform_8(real, imag)
            for q in range(HALF):
                sum_real, sum_imag = sums[q]
                cosine = cos_turn[parity, q : q + 1, lane : lane + 128]
                sine = sin_turn[parity, q : q + 1, lane : lane + 128]
                real_high, real_low = split_pair(sum_real * cosine + sum_imag * sine)
                imag_high, imag_low = split_pair(sum_imag * cosine - sum_real * sine)
                high[q, rows, lane : lane + 128] = real_high
                high[q, rows, width + lane : width + lane + 128] = imag_high
                high[q, lower, lane : lane + 128] = imag_high
                high[q, lower, width + lane : width + lane + 128] = -real_high
                low[q, rows, lane : lane + 128] = real_low
                low[q, rows, width + lane : width + lane + 128] = imag_low
                low[q, lower, lane : lane + 128] = imag_low
                low[q, lower, width + lane : width + lane + 128] = -real_low
        return carry

    lax.fori_loop(0, BLOCK // 16, one_block, 0)
    table = split_pair(table_rows[...])
    for q in range(0, HALF, 2):
        lines_high = high[q : q + 2].reshape(4 * BLOCK, 2 * width)
        lines_low = low[q : q + 2].reshape(4 * BLOCK, 2 * width)
        result = dot_split(table, (lines_high, lines_low))
        first = 0
        for out in outs:
            rows = slice(first, first + out.shape[1])
            out[me ^ flip3(q)] = result[rows, : 2 * BLOCK]
            out[me ^ flip3(q + 1)] = result[rows, 2 * BLOCK :]
            first += out.shape[1]


def half_sums(place, cells, tables, parts):
    width = cells[0][0].shape[-1]
    rows = tables[2].shape[0]
    counts = [array.shape[0] if count is None else count for array, count, _ in cells]

    def full(array):
        return pl.BlockSpec(array.shape, lambda i: (0,) * array.ndim)

    def some(count, inner):
        return pl.BlockSpec((count, BLOCK, width), lambda i: (0, inner, 0))

    return pl.pallas_call(
        functools.partial(half_sums_kernel, counts),
        grid=(1,),
        out_shape=[
            jax.ShapeDtypeStruct((HALF, part, 2 * BLOCK), jnp.float32) for part in parts
        ],
        in_specs=[pl.BlockSpec(memory_space=pltpu.SMEM)]
        + [some(count, inner) for count, (_, _, inner) in zip(counts, cells)]
        + [full(table) for table in tables],
        out_specs=[
            pl.BlockSpec((HALF, part, 2 * BLOCK), lambda i: (0, 0, 0)) for part in parts
        ],
        scratch_shapes=[
            pltpu.VMEM((HALF, BLOCK, width), jnp.float32),
            pltpu.VMEM((HALF, 2 * BLOCK, 2 * width), jnp.bfloat16),
            pltpu.VMEM((HALF, 2 * BLOCK, 2 * width), jnp.bfloat16),
        ],
        cost_estimate=pl.CostEstimate(
            flops=rows * BLOCK * width,
            bytes_accessed=BLOCK * width * 4,
            transcendentals=0,
        ),
        compiler_params=pltpu.CompilerParams(vmem_limit_bytes=VMEM_BYTES),
        name="half_sums",
    )(place, *[array for array, _, _ in cells], *tables)


def gather_planes_kernel(place, *refs):
    own, from_z, out, ordered = refs[0], refs[1], refs[-2], refs[-1]
    me = place[0]
    ordered[me] = own[0]
    ordered[me ^ 4] = from_z[0]
    for distance in range(1, 4):
        for index in range(2):
            ordered[me ^ (distance + 4 * index)] = refs[1 + distance][index]
    for plane in range(HALF):
        out[:, plane, :] = ordered[plane]


def gather_planes(place, own, from_z, others):
    modes, lanes = own.shape[-2:]
    one = pl.BlockSpec((1, modes, lanes), lambda i: (0, 0, 0))
    two = pl.BlockSpec((2, modes, lanes), lambda i: (0, 0, 0))
    return pl.pallas_call(
        gather_planes_kernel,
        grid=(1,),
        out_shape=jax.ShapeDtypeStruct((modes, HALF, lanes), jnp.float32),
        in_specs=[pl.BlockSpec(memory_space=pltpu.SMEM), one, one, two, two, two],
        out_specs=pl.BlockSpec((modes, HALF, lanes), lambda i: (0, 0, 0)),
        scratch_shapes=[pltpu.VMEM((HALF, modes, lanes), jnp.float32)],
        cost_estimate=pl.CostEstimate(
            flops=0, bytes_accessed=8 * HALF * modes * lanes, transcendentals=0
        ),
        compiler_params=pltpu.CompilerParams(vmem_limit_bytes=VMEM_BYTES),
        name="gather_planes",
    )(place, own, from_z, *others)


def solve_kernel(count, place, *refs):
    blocks = refs[: 2 * count]
    inverse, vectors, factor = refs[2 * count : 2 * count + 3]
    out = refs[-1]
    modes = out.shape[0]
    radial = out.shape[-1]

    @pl.when(place[3] == 1)
    def _():
        inverse_pair = split_pair(inverse[0])
        vectors_pair = split_pair(vectors[0])
        scale = jnp.broadcast_to(factor[0][:, None, :], (modes, HALF, radial))
        scale = scale.reshape(modes * HALF, radial)
        whole = [block[...].reshape(modes * HALF, 2 * BLOCK) for block in blocks]
        lines = jnp.concatenate(
            [
                jnp.concatenate(
                    [value[:, part * BLOCK : (part + 1) * BLOCK] for value in whole], axis=1
                )
                for part in range(2)
            ]
        )
        inner = dot_split(split_pair(lines), inverse_pair)
        inner = inner * jnp.concatenate([scale, scale])
        solved = dot_split(split_pair(inner), vectors_pair)
        solved = solved.reshape(2, modes, HALF, radial)
        for part in range(2):
            out[:, part, 0] = solved[part]

    @pl.when(place[3] != 1)
    def _():
        out[...] = jnp.zeros_like(out)


def solve(place, field, first, count, blocks, inverse, vectors, factor, earlier):
    modes = factor.shape[1]
    radial = inverse.shape[-1]
    step = modes // PARTS

    def lines(array):
        offset = first if array.shape[0] == modes else 0
        return pl.BlockSpec((step, HALF, 2 * BLOCK), lambda i: (offset + i, 0, 0))

    matrix = pl.BlockSpec((1, radial, radial), lambda i: (field, 0, 0))
    in_specs = [pl.BlockSpec(memory_space=pltpu.SMEM)] + [lines(block) for block in blocks]
    in_specs += [matrix, matrix]
    in_specs += [pl.BlockSpec((1, step, radial), lambda i: (field, first + i, 0))]
    operands = [place, *blocks, inverse, vectors, factor]
    aliases = {}
    if earlier is not None:
        aliases = {len(operands): 0}
        operands.append(earlier)
        in_specs.append(pl.BlockSpec(memory_space=pl.ANY))

    def kernel(*refs):
        kept = refs if earlier is None else refs[: len(operands) - 1] + refs[-1:]
        solve_kernel(len(blocks) // 2, *kept)

    return pl.pallas_call(
        kernel,
        grid=(count,),
        out_shape=jax.ShapeDtypeStruct((modes, 2, 2, HALF, radial), jnp.float32),
        in_specs=in_specs,
        out_specs=pl.BlockSpec(
            (step, 2, 1, HALF, radial), lambda i: (first + i, 0, field, 0, 0)
        ),
        input_output_aliases=aliases,
        cost_estimate=pl.CostEstimate(
            flops=count * modes * radial * radial,
            bytes_accessed=count * modes * radial,
            transcendentals=0,
        ),
        compiler_params=pltpu.CompilerParams(vmem_limit_bytes=VMEM_BYTES),
        name="solve",
    )(*operands)


def mode_tables(width, modes):
    cells = np.arange(width)
    residue = 2 * np.arange(HALF)[None, :, None] + np.arange(2)[:, None, None]
    turn = 2.0 * np.pi * residue * cells / (2 * HALF * width)
    padded = -(-modes // 16) * 16
    angle = 2.0 * np.pi * (np.arange(padded)[:, None] * cells[None, :] % width) / width
    table = np.concatenate([np.cos(angle), np.sin(angle)], axis=1)
    table = table / math.sqrt(2 * HALF * width)
    table[modes:] = 0.0
    return tuple(array.astype(np.float32) for array in (np.cos(turn), np.sin(turn), table))


def on_device_halves(fields, mode_group, half_step, decay, eigen_inverse, eigen_vectors):
    span = lax.axis_index("span")
    rad = lax.axis_index("rad")
    me = span & 7
    half = span >> 3
    rows = fields.shape[2]
    width = fields.shape[3]
    modes = KEEP // 16
    tables = mode_tables(width, modes)

    heavy = (mode_group[0, 0] == rad).astype(jnp.int32)
    one = jnp.ones_like(me)
    place_send = jnp.stack([me, 1 - half, one, heavy])
    place_keep = jnp.stack([me, half, 1 - 2 * half, heavy])

    mode_index = bit_reverse(span, 4) + 16 * jnp.arange(modes, dtype=jnp.int32)
    factor = damping_factor(half_step, decay, mode_index).transpose(1, 0, 2)
    own = lax.dynamic_slice_in_dim(eigen_inverse, rad * rows, rows, 2)
    other = lax.dynamic_slice_in_dim(eigen_inverse, (1 - rad) * rows, rows, 2)
    inverse = jnp.concatenate([own, other], axis=2)

    units = [(field, block) for field in range(2) for block in range(rows // BLOCK)]
    total = len(units)
    per_field = rows // BLOCK
    last = total - 1

    def plane_rows(field, start, count, distance):
        piece = lax.dynamic_slice(
            fields, (field, me ^ distance, start, 0), (1, 1, count, width)
        )
        return piece.reshape(count, width)

    def swap_core(field, start, count):
        paired = fields.reshape(2, 4, 2, rows, width)
        piece = lax.dynamic_slice(
            paired, (field, 0, 1 - (me & 1), start, 0), (1, 4, 1, count, width)
        )
        return swap_span(piece.reshape(4, count, width), 1)

    def core_rows(core, start, count, distance):
        plane = (me ^ distance) >> 1
        piece = lax.dynamic_slice(core, (plane, start, 0), (1, count, width))
        return piece.reshape(count, width)

    def away_direct(core, field, start, count):
        return [
            jnp.stack([plane_rows(field, start, count, d), core_rows(core, start, count, d)])
            for d in (2, 4, 6)
        ]

    def swap_direct(away):
        return [swap_span(value, distance) for value, distance in zip(away, (2, 4, 6))]

    def near_cells(core, field, start, core_start):
        mine = plane_rows(field, start, BLOCK, 0)
        return [(mine[None], 1, 0), (core_rows(core, core_start, BLOCK, 0)[None], 1, 0)]

    def away_x(core, inner, count):
        rows_of = (inner * BLOCK, count * BLOCK)
        away = []
        for distance in (2, 6):
            away.append(plane_rows(1, *rows_of, distance))
            away.append(core_rows(core, *rows_of, distance))
        return jnp.stack(away)

    def away_z(core, inner, from_x, place):
        rows_of = (inner * BLOCK, BLOCK)
        away = [plane_rows(1, *rows_of, 4)[None], core_rows(core, *rows_of, 4)[None]]
        away += [from_x[2:, place * BLOCK : (place + 1) * BLOCK]]
        return jnp.concatenate(away)

    def share(kept, came):
        return kept[:4] + came[:4], swap_span(kept[4:] + came[4:], 4)

    def swap_modes(near, from_z):
        return [
            swap_span(jnp.stack([near[distance], from_z[distance]]), distance)
            for distance in range(1, 4)
        ]

    def finish(near, from_z):
        return gather_planes(place_keep, near, from_z, swap_modes(near, from_z))

    def tie(*values):
        return lax.optimization_barrier(values)

    def sums(place, unit):
        step = modes // PARTS
        parts = [step * count for count in LAST_PARTS] if unit == last else [modes]
        return half_sums(place, cells[unit], tables, parts)

    cells = {}
    sent, kept, came, mine, other = {}, {}, {}, {}, {}
    def direct_unit(core, unit, arrays):
        start = units[unit][1] * BLOCK
        return near_cells(core, 0, start, start) + [(array, 2, 0) for array in arrays]

    core_a = swap_core(0, 0, rows)
    away = [away_direct(core_a, 0, n * BLOCK, BLOCK) for n in range(per_field)]
    direct = [swap_direct(away[0]), swap_direct(away[1])]
    core_c = swap_core(1, 0, rows)
    cells[0] = direct_unit(core_a, 0, direct[0])
    sent[0] = sums(place_send, 0)
    later_x = [away_x(core_c, 0, 2), away_x(core_c, 2, 1)]
    sent[0], direct[1], away[2], later_x, core_c, me = tie(
        sent[0], direct[1], away[2], later_x, core_c, me
    )
    cells[1] = direct_unit(core_a, 1, direct[1])
    matrices = (inverse, eigen_vectors, factor)
    from_x, swapped = [], {}
    result = None
    for step in range(last):
        came[step] = swap_span(sent[step][0], HALF)
        extra = {}
        if step == 0:
            kept[0] = sums(place_keep, 0)
            extra["direct"] = swap_direct(away[2])
            extra["z_parts"] = [
                plane_rows(1, 0, BLOCK, 4)[None], core_rows(core_c, 0, BLOCK, 4)[None]
            ]
            extra["near"] = [
                [cell[0] for cell in near_cells(core_c, 1, inner * BLOCK, inner * BLOCK)]
                for inner in range(per_field)
            ]
        if step < 2:
            extra["x"] = swap_span(later_x[step], 2)
        sent[step + 1] = sums(place_send, step + 1)
        kept[step + 1] = sums(place_keep, step + 1)
        if 1 <= step <= 3:
            unit = step + 2
            inner = unit - per_field
            source, place = (from_x[0], inner) if inner < 2 else (from_x[1], 0)
            if inner == 0:
                next_z = jnp.concatenate(z_parts + [source[2:, :BLOCK]])
            extra["z"] = swap_span(next_z, 4)
            if inner < 2:
                following = (from_x[0], 1) if inner == 0 else (from_x[1], 0)
                extra["away"] = away_z(core_c, inner + 1, *following)
            cells[unit] = [(array, 1, 0) for array in near[inner]]
            cells[unit] += [(source, 2, place)]
        if step >= 1:
            extra["swapped"] = share(kept[step - 1][0], came[step - 1])
        if step >= 2:
            extra["mine"] = finish(*swapped[step - 2])
        if step == last - 1:
            extra["other"] = [swap_rad(mine[unit]) for unit in range(last - 3)]
        came[step], sent[step + 1], kept[step + 1], extra, me = tie(
            came[step], sent[step + 1], kept[step + 1], extra, me
        )
        if "direct" in extra:
            cells[2] = direct_unit(core_a, 2, extra["direct"])
            near, z_parts = extra["near"], extra["z_parts"]
        if "away" in extra:
            next_z = extra["away"]
        if "x" in extra:
            from_x.append(extra["x"])
        if "z" in extra:
            cells[step + 2].append((extra["z"], 4, 0))
        if step >= 1:
            swapped[step - 1] = extra["swapped"]
        if step >= 2:
            mine[step - 2] = extra["mine"]
        if step == last - 1:
            other.update(enumerate(extra["other"]))

    def blocks_of(numbers, part=None):
        chosen = [mine[n] if n != last else mine[n][part] for n in numbers]
        return chosen + [other[n] if n != last else other[n][part] for n in numbers]

    came[last] = [swap_span(part, HALF) for part in sent[last]]
    other[last - 3] = swap_rad(mine[last - 3])
    swapped[last - 1] = share(kept[last - 1][0], came[last - 1])
    mine[last - 2] = finish(*swapped[last - 2])
    other[last - 2] = swap_rad(mine[last - 2])
    blocks = blocks_of(range(per_field))
    result = solve(place_keep, 0, 0, 2, blocks, *matrices, None)
    came[last][0], swapped[last - 1], result = tie(
        came[last][0], swapped[last - 1], result
    )
    mine[last - 1] = finish(*swapped[last - 1])
    ready = share(kept[last][0], came[last][0])
    ready, mine[last - 1], other[last - 2] = tie(ready, mine[last - 1], other[last - 2])
    other[last - 1] = swap_rad(mine[last - 1])
    first = finish(*ready)
    first, came[last][1] = tie(first, came[last][1])
    other_first = swap_rad(first)
    ready = share(kept[last][1], came[last][1])
    result = solve(place_keep, 0, 2, 1, blocks, *matrices, result)
    others, result, other[last - 1] = tie(swap_modes(*ready), result, other[last - 1])
    second = gather_planes(place_keep, *ready, others)
    mine[last] = [first, second]
    other[last] = [other_first, swap_rad(second)]
    start = 0
    for part, count in enumerate(LAST_PARTS):
        blocks = blocks_of(range(per_field, total), part)
        result = solve(place_keep, 1, start, count, blocks, *matrices, result)
        start += count
    return result[None, None]


def solution(mesh):
    placed = (P(None, None, "rad", "span"), P(None, "span"), P(), P(), P(), P())
    halves = mesh.shape["span"] == 2 * HALF and mesh.shape["rad"] == 2
    return jax.shard_map(
        on_device_halves if halves else on_device_any,
        mesh=mesh,
        in_specs=placed,
        out_specs=P("span", "rad", None, None, None, None, None),
        check_vma=False,
    )
```

```python
import functools
import math

import jax
import jax.numpy as jnp
import numpy as np
from jax import lax
from jax.experimental import pallas as pl
from jax.experimental.pallas import tpu as pltpu
from jax.sharding import PartitionSpec as P

KEEP = 2688


precise = lax.Precision.HIGHEST
contract_rows = (((1,), (1,)), ((), ()))


def partner_2(value, axis, distance):
    mask = 2**distance
    pairs = [(source, source ^ mask) for source in range(lax.axis_size(axis))]
    return lax.ppermute(value, axis, pairs)


def bit_reverse(value, bit_count):
    flipped = jnp.zeros_like(value)
    for section_bit in range(bit_count):
        flipped = flipped + (value >> section_bit & 1) * 2 ** (bit_count - 1 - section_bit)
    return flipped


def section_angles(device, section_bit):
    upper_half = device >> section_bit & 1 == 1
    twiddle_index = jnp.where(upper_half, device % 2**section_bit, 0)
    angles = twiddle_index.astype(jnp.float32) * (2.0 * math.pi / 2 ** (section_bit + 1))
    sign_factor = jnp.where(upper_half, -1.0, 1.0).astype(jnp.float32)
    return (sign_factor, jnp.cos(angles), jnp.sin(angles))


def butterfly(fields, bit_count):
    device = lax.axis_index("span")
    top_bit = bit_count - 1
    partner = partner_2(fields, "span", top_bit)
    sign_factor, cosine, sine_value = section_angles(device, top_bit)
    difference = partner + sign_factor * fields
    real_part = difference * cosine
    imag_part = -difference * sine_value
    for section_bit in range(bit_count - 2, -1, -1):
        other_real, other_imag = partner_2((real_part, imag_part), "span", section_bit)
        sign_factor, cosine, sine_value = section_angles(device, section_bit)
        diff_real = other_real + sign_factor * real_part
        diff_imag = other_imag + sign_factor * imag_part
        real_part = diff_real * cosine + diff_imag * sine_value
        imag_part = diff_imag * cosine - diff_real * sine_value
    return (real_part, imag_part)


def mode_transform(real_part, imag_part, bit_count):
    groups = lax.axis_size("span")
    line_width = real_part.shape[3]
    full_length = line_width * groups
    kept_modes = KEEP // groups
    residue = bit_reverse(lax.axis_index("span"), bit_count)
    mode_index = residue + groups * jnp.arange(kept_modes, dtype=jnp.int32)
    phases = mode_index[:, None] * jnp.arange(line_width, dtype=jnp.int32)[None, :] % full_length
    angles = phases.astype(jnp.float32) * (2.0 * math.pi / full_length)
    normalizer = 1.0 / math.sqrt(full_length)
    cosine_table = jnp.cos(angles) * normalizer
    sine_table = jnp.sin(angles) * normalizer
    line_real = real_part.reshape(-1, line_width)
    line_imag = imag_part.reshape(-1, line_width)
    cos_real = lax.dot_general(cosine_table, line_real, contract_rows, precision=precise)
    cos_imag = lax.dot_general(cosine_table, line_imag, contract_rows, precision=precise)
    sin_real = lax.dot_general(sine_table, line_real, contract_rows, precision=precise)
    sin_imag = lax.dot_general(sine_table, line_imag, contract_rows, precision=precise)
    return (jnp.stack([cos_real + sin_imag, cos_imag - sin_real]), mode_index)


def placement_table(column, group_count, capacity):
    groups = jnp.arange(group_count, dtype=jnp.int32)
    member = (column[None, :] == groups[:, None]).astype(jnp.int32)
    ranking = jnp.cumsum(member, axis=1, dtype=jnp.int32) - member
    slot_index = jnp.arange(capacity, dtype=jnp.int32)
    return member[None] * (ranking[None] == slot_index[:, None, None])


def damping_factor(half_step, decay, wave_index):
    wave_square = (wave_index.astype(jnp.float32) * (math.pi / KEEP)) ** 2
    damping = half_step[None, :, None] * (decay[None, :, :] + wave_square[:, None, None])
    return (1.0 - damping) / (1.0 + damping)


def on_device_any(fields, mode_group, half_step, decay, eigen_inverse, eigen_vectors):
    bit_count = lax.axis_size("span").bit_length() - 1
    real_part, imag_part = butterfly(fields, bit_count)
    spectra, mode_index = mode_transform(real_part, imag_part, bit_count)
    kept_modes = spectra.shape[1]
    group_count = lax.axis_size("rad")
    capacity = min(kept_modes, 2 * kept_modes // group_count)
    planes = fields.shape[1]
    radial_rows = fields.shape[2]
    arranged = spectra.reshape(2, kept_modes, 2, planes, radial_rows)
    placing = placement_table(mode_group[:, 0], group_count, capacity)
    placing_float = placing.astype(jnp.float32)
    packed = jnp.einsum("sgb,cbfal->scfagl", placing_float, arranged, precision=precise)
    packed = packed.reshape(capacity, 2, 2, planes, group_count * radial_rows)
    regrouped = lax.all_to_all(packed, "rad", split_axis=4, concat_axis=4, tiled=True)
    own_slots = lax.dynamic_index_in_dim(placing, lax.axis_index("rad"), 1, keepdims=False)
    slot_modes = jnp.sum(own_slots * mode_index[None, :], axis=1)
    factor = damping_factor(half_step, decay, slot_modes)
    inner_part = jnp.einsum("scfar,fir->scfai", regrouped, eigen_inverse, precision=precise)
    inner_part = inner_part * factor[:, None, :, None, :]
    result = jnp.einsum("scfai,fri->scfar", inner_part, eigen_vectors, precision=precise)
    return result.reshape(1, 1, capacity, 2, 2, planes, group_count * radial_rows)


HALF = 8
BLOCK = 64
PARTS = 3
LAST_PARTS = (2, 1)
VMEM_BYTES = 24 * 1024 * 1024


def flip3(value):
    return (value & 1) << 2 | value & 2 | value >> 2


def swap_span(value, distance):
    pairs = [(source, source ^ distance) for source in range(lax.axis_size("span"))]
    return lax.ppermute(value, "span", pairs)


def swap_rad(value):
    return lax.ppermute(value, "rad", [(0, 1), (1, 0)])


def split_pair(value):
    high = value.astype(jnp.bfloat16)
    low = (value - high.astype(jnp.float32)).astype(jnp.bfloat16)
    return high, low


def dot_rows(left, right):
    return lax.dot_general(left, right, contract_rows, preferred_element_type=jnp.float32)


def dot_split(left, right):
    left_high, left_low = left
    right_high, right_low = right
    total = dot_rows(left_high, right_high)
    total = total + dot_rows(left_low, right_high)
    return total + dot_rows(left_high, right_low)


def transform_8(real, imag):
    root = math.sqrt(0.5)
    er, ei, orr, oi = [], [], [], []
    for j in range(4):
        er.append(real[j] + real[j + 4])
        ei.append(imag[j] + imag[j + 4])
        dr = real[j] - real[j + 4]
        di = imag[j] - imag[j + 4]
        if j == 0:
            orr.append(dr)
            oi.append(di)
        elif j == 1:
            orr.append((dr + di) * root)
            oi.append((di - dr) * root)
        elif j == 2:
            orr.append(di)
            oi.append(-dr)
        else:
            orr.append((di - dr) * root)
            oi.append((-di - dr) * root)

    def transform_4(r, i):
        ar, ai = r[0] + r[2], i[0] + i[2]
        br, bi = r[0] - r[2], i[0] - i[2]
        cr, ci = r[1] + r[3], i[1] + i[3]
        dr, di = r[1] - r[3], i[1] - i[3]
        return [(ar + cr, ai + ci), (br + di, bi - dr), (ar - cr, ai - ci), (br - di, bi + dr)]

    even = transform_4(er, ei)
    odd = transform_4(orr, oi)
    return [even[q // 2] if q % 2 == 0 else odd[q // 2] for q in range(8)]


def half_sums_kernel(counts, place, *refs):
    cells, refs = refs[: len(counts)], refs[len(counts) :]
    cos_turn, sin_turn, table_rows = refs[:3]
    outs, (ordered, high, low) = refs[3:-3], refs[-3:]
    me, parity = place[0], place[1]
    sign = place[2].astype(jnp.float32)
    width = ordered.shape[-1]
    distance = 0
    for ref, count in zip(cells, counts):
        for index in range(count):
            ordered[me ^ distance] = ref[index]
            distance += 1

    turn_real, turn_imag = [], []
    for j in range(HALF):
        angle = 2.0 * math.pi * j / 16
        turn_real.append(sign * jnp.where(parity == 1, math.cos(angle), 1.0))
        turn_imag.append(sign * jnp.where(parity == 1, -math.sin(angle), 0.0))

    def one_block(step, carry):
        rows = pl.ds(pl.multiple_of(step * 16, 16), 16)
        lower = pl.ds(pl.multiple_of(BLOCK + step * 16, 16), 16)
        for lane in range(0, width, 128):
            real, imag = [], []
            for j in range(HALF):
                value = ordered[j, rows, lane : lane + 128]
                real.append(value * turn_real[j])
                imag.append(value * turn_imag[j])
            sums = transform_8(real, imag)
            for q in range(HALF):
                sum_real, sum_imag = sums[q]
                cosine = cos_turn[parity, q : q + 1, lane : lane + 128]
                sine = sin_turn[parity, q : q + 1, lane : lane + 128]
                real_high, real_low = split_pair(sum_real * cosine + sum_imag * sine)
                imag_high, imag_low = split_pair(sum_imag * cosine - sum_real * sine)
                high[q, rows, lane : lane + 128] = real_high
                high[q, rows, width + lane : width + lane + 128] = imag_high
                high[q, lower, lane : lane + 128] = imag_high
                high[q, lower, width + lane : width + lane + 128] = -real_high
                low[q, rows, lane : lane + 128] = real_low
                low[q, rows, width + lane : width + lane + 128] = imag_low
                low[q, lower, lane : lane + 128] = imag_low
                low[q, lower, width + lane : width + lane + 128] = -real_low
        return carry

    lax.fori_loop(0, BLOCK // 16, one_block, 0)
    table = split_pair(table_rows[...])
    for q in range(0, HALF, 2):
        lines_high = high[q : q + 2].reshape(4 * BLOCK, 2 * width)
        lines_low = low[q : q + 2].reshape(4 * BLOCK, 2 * width)
        result = dot_split(table, (lines_high, lines_low))
        first = 0
        for out in outs:
            rows = slice(first, first + out.shape[1])
            out[me ^ flip3(q)] = result[rows, : 2 * BLOCK]
            out[me ^ flip3(q + 1)] = result[rows, 2 * BLOCK :]
            first += out.shape[1]


def half_sums(place, cells, tables, parts):
    width = cells[0][0].shape[-1]
    rows = tables[2].shape[0]
    counts = [array.shape[0] if count is None else count for array, count, _ in cells]

    def full(array):
        return pl.BlockSpec(array.shape, lambda i: (0,) * array.ndim)

    def some(count, inner):
        return pl.BlockSpec((count, BLOCK, width), lambda i: (0, inner, 0))

    return pl.pallas_call(
        functools.partial(half_sums_kernel, counts),
        grid=(1,),
        out_shape=[
            jax.ShapeDtypeStruct((HALF, part, 2 * BLOCK), jnp.float32) for part in parts
        ],
        in_specs=[pl.BlockSpec(memory_space=pltpu.SMEM)]
        + [some(count, inner) for count, (_, _, inner) in zip(counts, cells)]
        + [full(table) for table in tables],
        out_specs=[
            pl.BlockSpec((HALF, part, 2 * BLOCK), lambda i: (0, 0, 0)) for part in parts
        ],
        scratch_shapes=[
            pltpu.VMEM((HALF, BLOCK, width), jnp.float32),
            pltpu.VMEM((HALF, 2 * BLOCK, 2 * width), jnp.bfloat16),
            pltpu.VMEM((HALF, 2 * BLOCK, 2 * width), jnp.bfloat16),
        ],
        cost_estimate=pl.CostEstimate(
            flops=rows * BLOCK * width,
            bytes_accessed=BLOCK * width * 4,
            transcendentals=0,
        ),
        compiler_params=pltpu.CompilerParams(vmem_limit_bytes=VMEM_BYTES),
        name="half_sums",
    )(place, *[array for array, _, _ in cells], *tables)


def gather_planes_kernel(place, *refs):
    own, from_z, out, ordered = refs[0], refs[1], refs[-2], refs[-1]
    me = place[0]
    ordered[me] = own[0]
    ordered[me ^ 4] = from_z[0]
    for distance in range(1, 4):
        for index in range(2):
            ordered[me ^ (distance + 4 * index)] = refs[1 + distance][index]
    for plane in range(HALF):
        out[:, plane, :] = ordered[plane]


def gather_planes(place, own, from_z, others):
    modes, lanes = own.shape[-2:]
    one = pl.BlockSpec((1, modes, lanes), lambda i: (0, 0, 0))
    two = pl.BlockSpec((2, modes, lanes), lambda i: (0, 0, 0))
    return pl.pallas_call(
        gather_planes_kernel,
        grid=(1,),
        out_shape=jax.ShapeDtypeStruct((modes, HALF, lanes), jnp.float32),
        in_specs=[pl.BlockSpec(memory_space=pltpu.SMEM), one, one, two, two, two],
        out_specs=pl.BlockSpec((modes, HALF, lanes), lambda i: (0, 0, 0)),
        scratch_shapes=[pltpu.VMEM((HALF, modes, lanes), jnp.float32)],
        cost_estimate=pl.CostEstimate(
            flops=0, bytes_accessed=8 * HALF * modes * lanes, transcendentals=0
        ),
        compiler_params=pltpu.CompilerParams(vmem_limit_bytes=VMEM_BYTES),
        name="gather_planes",
    )(place, own, from_z, *others)


def solve_kernel(count, place, *refs):
    blocks = refs[: 2 * count]
    inverse, vectors, factor = refs[2 * count : 2 * count + 3]
    out = refs[-1]
    modes = out.shape[0]
    radial = out.shape[-1]

    @pl.when(place[3] == 1)
    def _():
        inverse_pair = split_pair(inverse[0])
        vectors_pair = split_pair(vectors[0])
        scale = jnp.broadcast_to(factor[0][:, None, :], (modes, HALF, radial))
        scale = scale.reshape(modes * HALF, radial)
        whole = [block[...].reshape(modes * HALF, 2 * BLOCK) for block in blocks]
        for part in range(2):
            lanes = slice(part * BLOCK, (part + 1) * BLOCK)
            lines = jnp.concatenate([value[:, lanes] for value in whole], axis=1)
            inner = dot_split(split_pair(lines), inverse_pair) * scale
            solved = dot_split(split_pair(inner), vectors_pair)
            out[:, part, 0] = solved.reshape(modes, HALF, radial)

    @pl.when(place[3] != 1)
    def _():
        out[...] = jnp.zeros_like(out)


def solve(place, field, first, count, blocks, inverse, vectors, factor, earlier):
    modes = factor.shape[1]
    radial = inverse.shape[-1]
    step = modes // PARTS

    def lines(array):
        offset = first if array.shape[0] == modes else 0
        return pl.BlockSpec((step, HALF, 2 * BLOCK), lambda i: (offset + i, 0, 0))

    matrix = pl.BlockSpec((1, radial, radial), lambda i: (field, 0, 0))
    in_specs = [pl.BlockSpec(memory_space=pltpu.SMEM)] + [lines(block) for block in blocks]
    in_specs += [matrix, matrix]
    in_specs += [pl.BlockSpec((1, step, radial), lambda i: (field, first + i, 0))]
    operands = [place, *blocks, inverse, vectors, factor]
    aliases = {}
    if earlier is not None:
        aliases = {len(operands): 0}
        operands.append(earlier)
        in_specs.append(pl.BlockSpec(memory_space=pl.ANY))

    def kernel(*refs):
        kept = refs if earlier is None else refs[: len(operands) - 1] + refs[-1:]
        solve_kernel(len(blocks) // 2, *kept)

    return pl.pallas_call(
        kernel,
        grid=(count,),
        out_shape=jax.ShapeDtypeStruct((modes, 2, 2, HALF, radial), jnp.float32),
        in_specs=in_specs,
        out_specs=pl.BlockSpec(
            (step, 2, 1, HALF, radial), lambda i: (first + i, 0, field, 0, 0)
        ),
        input_output_aliases=aliases,
        cost_estimate=pl.CostEstimate(
            flops=count * modes * radial * radial,
            bytes_accessed=count * modes * radial,
            transcendentals=0,
        ),
        compiler_params=pltpu.CompilerParams(vmem_limit_bytes=VMEM_BYTES),
        name="solve",
    )(*operands)


def mode_tables(width, modes):
    cells = np.arange(width)
    residue = 2 * np.arange(HALF)[None, :, None] + np.arange(2)[:, None, None]
    turn = 2.0 * np.pi * residue * cells / (2 * HALF * width)
    padded = -(-modes // 16) * 16
    angle = 2.0 * np.pi * (np.arange(padded)[:, None] * cells[None, :] % width) / width
    table = np.concatenate([np.cos(angle), np.sin(angle)], axis=1)
    table = table / math.sqrt(2 * HALF * width)
    table[modes:] = 0.0
    return tuple(array.astype(np.float32) for array in (np.cos(turn), np.sin(turn), table))


def on_device_halves(fields, mode_group, half_step, decay, eigen_inverse, eigen_vectors):
    span = lax.axis_index("span")
    rad = lax.axis_index("rad")
    me = span & 7
    half = span >> 3
    rows = fields.shape[2]
    width = fields.shape[3]
    modes = KEEP // 16
    tables = mode_tables(width, modes)

    heavy = (mode_group[0, 0] == rad).astype(jnp.int32)
    one = jnp.ones_like(me)
    place_send = jnp.stack([me, 1 - half, one, heavy])
    place_keep = jnp.stack([me, half, 1 - 2 * half, heavy])

    mode_index = bit_reverse(span, 4) + 16 * jnp.arange(modes, dtype=jnp.int32)
    factor = damping_factor(half_step, decay, mode_index).transpose(1, 0, 2)
    own = lax.dynamic_slice_in_dim(eigen_inverse, rad * rows, rows, 2)
    other = lax.dynamic_slice_in_dim(eigen_inverse, (1 - rad) * rows, rows, 2)
    inverse = jnp.concatenate([own, other], axis=2)

    units = [(field, block) for field in range(2) for block in range(rows // BLOCK)]
    total = len(units)
    per_field = rows // BLOCK
    last = total - 1

    def plane_rows(field, start, count, distance):
        piece = lax.dynamic_slice(
            fields, (field, me ^ distance, start, 0), (1, 1, count, width)
        )
        return piece.reshape(count, width)

    def swap_core(field, start, count):
        paired = fields.reshape(2, 4, 2, rows, width)
        piece = lax.dynamic_slice(
            paired, (field, 0, 1 - (me & 1), start, 0), (1, 4, 1, count, width)
        )
        return swap_span(piece.reshape(4, count, width), 1)

    def core_rows(core, start, count, distance):
        plane = (me ^ distance) >> 1
        piece = lax.dynamic_slice(core, (plane, start, 0), (1, count, width))
        return piece.reshape(count, width)

    def away_direct(core, field, start, count):
        return [
            jnp.stack([plane_rows(field, start, count, d), core_rows(core, start, count, d)])
            for d in (2, 4, 6)
        ]

    def swap_direct(away):
        return [swap_span(value, distance) for value, distance in zip(away, (2, 4, 6))]

    def near_cells(core, field, start, core_start):
        mine = plane_rows(field, start, BLOCK, 0)
        return [(mine[None], 1, 0), (core_rows(core, core_start, BLOCK, 0)[None], 1, 0)]

    def away_x(core, inner, count):
        rows_of = (inner * BLOCK, count * BLOCK)
        away = []
        for distance in (2, 6):
            away.append(plane_rows(1, *rows_of, distance))
            away.append(core_rows(core, *rows_of, distance))
        return jnp.stack(away)

    def away_z(core, inner, from_x, place):
        rows_of = (inner * BLOCK, BLOCK)
        away = [plane_rows(1, *rows_of, 4)[None], core_rows(core, *rows_of, 4)[None]]
        away += [from_x[2:, place * BLOCK : (place + 1) * BLOCK]]
        return jnp.concatenate(away)

    def share(kept, came):
        return kept[:4] + came[:4], swap_span(kept[4:] + came[4:], 4)

    def swap_modes(near, from_z):
        return [
            swap_span(jnp.stack([near[distance], from_z[distance]]), distance)
            for distance in range(1, 4)
        ]

    def finish(near, from_z):
        return gather_planes(place_keep, near, from_z, swap_modes(near, from_z))

    def tie(*values):
        return lax.optimization_barrier(values)

    def sums(place, unit):
        step = modes // PARTS
        parts = [step * count for count in LAST_PARTS] if unit == last else [modes]
        return half_sums(place, cells[unit], tables, parts)

    cells = {}
    sent, kept, came, mine, other = {}, {}, {}, {}, {}
    def direct_unit(core, unit, arrays):
        start = units[unit][1] * BLOCK
        return near_cells(core, 0, start, start) + [(array, 2, 0) for array in arrays]

    core_a = swap_core(0, 0, rows)
    away = [away_direct(core_a, 0, n * BLOCK, BLOCK) for n in range(per_field)]
    direct = [swap_direct(away[0]), swap_direct(away[1])]
    core_c = swap_core(1, 0, rows)
    cells[0] = direct_unit(core_a, 0, direct[0])
    sent[0] = sums(place_send, 0)
    later_x = [away_x(core_c, 0, 2), away_x(core_c, 2, 1)]
    sent[0], direct[1], away[2], later_x, core_c, me = tie(
        sent[0], direct[1], away[2], later_x, core_c, me
    )
    cells[1] = direct_unit(core_a, 1, direct[1])
    matrices = (inverse, eigen_vectors, factor)
    from_x, swapped = [], {}
    result = None
    for step in range(last):
        came[step] = swap_span(sent[step][0], HALF)
        extra = {}
        if step == 0:
            kept[0] = sums(place_keep, 0)
            extra["direct"] = swap_direct(away[2])
            extra["z_parts"] = [
                plane_rows(1, 0, BLOCK, 4)[None], core_rows(core_c, 0, BLOCK, 4)[None]
            ]
            extra["near"] = [
                [cell[0] for cell in near_cells(core_c, 1, inner * BLOCK, inner * BLOCK)]
                for inner in range(per_field)
            ]
        if step < 2:
            extra["x"] = swap_span(later_x[step], 2)
        sent[step + 1] = sums(place_send, step + 1)
        kept[step + 1] = sums(place_keep, step + 1)
        if 1 <= step <= 3:
            unit = step + 2
            inner = unit - per_field
            source, place = (from_x[0], inner) if inner < 2 else (from_x[1], 0)
            if inner == 0:
                next_z = jnp.concatenate(z_parts + [source[2:, :BLOCK]])
            extra["z"] = swap_span(next_z, 4)
            if inner < 2:
                following = (from_x[0], 1) if inner == 0 else (from_x[1], 0)
                extra["away"] = away_z(core_c, inner + 1, *following)
            cells[unit] = [(array, 1, 0) for array in near[inner]]
            cells[unit] += [(source, 2, place)]
        if step >= 1:
            extra["swapped"] = share(kept[step - 1][0], came[step - 1])
        if step == last - 1:
            swapped[step - 2], extra["swapped"], sent[last], kept[last] = tie(
                swapped[step - 2], extra["swapped"], sent[last], kept[last]
            )
        if step >= 2:
            extra["mine"] = finish(*swapped[step - 2])
        if step == last - 1:
            extra["other"] = [swap_rad(mine[unit]) for unit in range(last - 3)]
        came[step], sent[step + 1], kept[step + 1], extra, me = tie(
            came[step], sent[step + 1], kept[step + 1], extra, me
        )
        if "direct" in extra:
            cells[2] = direct_unit(core_a, 2, extra["direct"])
            near, z_parts = extra["near"], extra["z_parts"]
        if "away" in extra:
            next_z = extra["away"]
        if "x" in extra:
            from_x.append(extra["x"])
        if "z" in extra:
            cells[step + 2].append((extra["z"], 4, 0))
        if step >= 1:
            swapped[step - 1] = extra["swapped"]
        if step >= 2:
            mine[step - 2] = extra["mine"]
        if step == last - 1:
            other.update(enumerate(extra["other"]))

    def blocks_of(numbers, part=None):
        chosen = [mine[n] if n != last else mine[n][part] for n in numbers]
        return chosen + [other[n] if n != last else other[n][part] for n in numbers]

    came[last] = [swap_span(part, HALF) for part in sent[last]]
    other[last - 3] = swap_rad(mine[last - 3])
    swapped[last - 1] = share(kept[last - 1][0], came[last - 1])
    mine[last - 2] = finish(*swapped[last - 2])
    other[last - 2] = swap_rad(mine[last - 2])
    blocks = blocks_of(range(per_field))
    result = solve(place_keep, 0, 0, 1, blocks, *matrices, None)
    came[last][0], swapped[last - 1], result = tie(
        came[last][0], swapped[last - 1], result
    )
    mine[last - 1] = finish(*swapped[last - 1])
    ready = share(kept[last][0], came[last][0])
    ready, mine[last - 1], other[last - 2] = tie(ready, mine[last - 1], other[last - 2])
    other[last - 1] = swap_rad(mine[last - 1])
    first = finish(*ready)
    first, came[last][1] = tie(first, came[last][1])
    other_first = swap_rad(first)
    ready = share(kept[last][1], came[last][1])
    result = solve(place_keep, 0, 1, 1, blocks, *matrices, result)
    others, result, other[last - 1] = tie(swap_modes(*ready), result, other[last - 1])
    second = gather_planes(place_keep, *ready, others)
    second, place = tie(second, place_keep)
    result = solve(place, 0, 2, 1, blocks, *matrices, result)
    mine[last] = [first, second]
    other[last] = [other_first, swap_rad(second)]
    start = 0
    for part, count in enumerate(LAST_PARTS):
        blocks = blocks_of(range(per_field, total), part)
        result = solve(place_keep, 1, start, count, blocks, *matrices, result)
        start += count
    return result[None, None]


def solution(mesh):
    placed = (P(None, None, "rad", "span"), P(None, "span"), P(), P(), P(), P())
    halves = mesh.shape["span"] == 2 * HALF and mesh.shape["rad"] == 2
    return jax.shard_map(
        on_device_halves if halves else on_device_any,
        mesh=mesh,
        in_specs=placed,
        out_specs=P("span", "rad", None, None, None, None, None),
        check_vma=False,
    )
```

```python
import functools
import math

import jax
import jax.numpy as jnp
import numpy as np
from jax import lax
from jax.experimental import pallas as pl
from jax.experimental.pallas import tpu as pltpu
from jax.sharding import PartitionSpec as P

KEEP = 2688


precise = lax.Precision.HIGHEST
contract_rows = (((1,), (1,)), ((), ()))


def partner_2(value, axis, distance):
    mask = 2**distance
    pairs = [(source, source ^ mask) for source in range(lax.axis_size(axis))]
    return lax.ppermute(value, axis, pairs)


def bit_reverse(value, bit_count):
    flipped = jnp.zeros_like(value)
    for section_bit in range(bit_count):
        flipped = flipped + (value >> section_bit & 1) * 2 ** (bit_count - 1 - section_bit)
    return flipped


def section_angles(device, section_bit):
    upper_half = device >> section_bit & 1 == 1
    twiddle_index = jnp.where(upper_half, device % 2**section_bit, 0)
    angles = twiddle_index.astype(jnp.float32) * (2.0 * math.pi / 2 ** (section_bit + 1))
    sign_factor = jnp.where(upper_half, -1.0, 1.0).astype(jnp.float32)
    return (sign_factor, jnp.cos(angles), jnp.sin(angles))


def butterfly(fields, bit_count):
    device = lax.axis_index("span")
    top_bit = bit_count - 1
    partner = partner_2(fields, "span", top_bit)
    sign_factor, cosine, sine_value = section_angles(device, top_bit)
    difference = partner + sign_factor * fields
    real_part = difference * cosine
    imag_part = -difference * sine_value
    for section_bit in range(bit_count - 2, -1, -1):
        other_real, other_imag = partner_2((real_part, imag_part), "span", section_bit)
        sign_factor, cosine, sine_value = section_angles(device, section_bit)
        diff_real = other_real + sign_factor * real_part
        diff_imag = other_imag + sign_factor * imag_part
        real_part = diff_real * cosine + diff_imag * sine_value
        imag_part = diff_imag * cosine - diff_real * sine_value
    return (real_part, imag_part)


def mode_transform(real_part, imag_part, bit_count):
    groups = lax.axis_size("span")
    line_width = real_part.shape[3]
    full_length = line_width * groups
    kept_modes = KEEP // groups
    residue = bit_reverse(lax.axis_index("span"), bit_count)
    mode_index = residue + groups * jnp.arange(kept_modes, dtype=jnp.int32)
    phases = mode_index[:, None] * jnp.arange(line_width, dtype=jnp.int32)[None, :] % full_length
    angles = phases.astype(jnp.float32) * (2.0 * math.pi / full_length)
    normalizer = 1.0 / math.sqrt(full_length)
    cosine_table = jnp.cos(angles) * normalizer
    sine_table = jnp.sin(angles) * normalizer
    line_real = real_part.reshape(-1, line_width)
    line_imag = imag_part.reshape(-1, line_width)
    cos_real = lax.dot_general(cosine_table, line_real, contract_rows, precision=precise)
    cos_imag = lax.dot_general(cosine_table, line_imag, contract_rows, precision=precise)
    sin_real = lax.dot_general(sine_table, line_real, contract_rows, precision=precise)
    sin_imag = lax.dot_general(sine_table, line_imag, contract_rows, precision=precise)
    return (jnp.stack([cos_real + sin_imag, cos_imag - sin_real]), mode_index)


def placement_table(column, group_count, capacity):
    groups = jnp.arange(group_count, dtype=jnp.int32)
    member = (column[None, :] == groups[:, None]).astype(jnp.int32)
    ranking = jnp.cumsum(member, axis=1, dtype=jnp.int32) - member
    slot_index = jnp.arange(capacity, dtype=jnp.int32)
    return member[None] * (ranking[None] == slot_index[:, None, None])


def damping_factor(half_step, decay, wave_index):
    wave_square = (wave_index.astype(jnp.float32) * (math.pi / KEEP)) ** 2
    damping = half_step[None, :, None] * (decay[None, :, :] + wave_square[:, None, None])
    return (1.0 - damping) / (1.0 + damping)


def on_device_any(fields, mode_group, half_step, decay, eigen_inverse, eigen_vectors):
    bit_count = lax.axis_size("span").bit_length() - 1
    real_part, imag_part = butterfly(fields, bit_count)
    spectra, mode_index = mode_transform(real_part, imag_part, bit_count)
    kept_modes = spectra.shape[1]
    group_count = lax.axis_size("rad")
    capacity = min(kept_modes, 2 * kept_modes // group_count)
    planes = fields.shape[1]
    radial_rows = fields.shape[2]
    arranged = spectra.reshape(2, kept_modes, 2, planes, radial_rows)
    placing = placement_table(mode_group[:, 0], group_count, capacity)
    placing_float = placing.astype(jnp.float32)
    packed = jnp.einsum("sgb,cbfal->scfagl", placing_float, arranged, precision=precise)
    packed = packed.reshape(capacity, 2, 2, planes, group_count * radial_rows)
    regrouped = lax.all_to_all(packed, "rad", split_axis=4, concat_axis=4, tiled=True)
    own_slots = lax.dynamic_index_in_dim(placing, lax.axis_index("rad"), 1, keepdims=False)
    slot_modes = jnp.sum(own_slots * mode_index[None, :], axis=1)
    factor = damping_factor(half_step, decay, slot_modes)
    inner_part = jnp.einsum("scfar,fir->scfai", regrouped, eigen_inverse, precision=precise)
    inner_part = inner_part * factor[:, None, :, None, :]
    result = jnp.einsum("scfai,fri->scfar", inner_part, eigen_vectors, precision=precise)
    return result.reshape(1, 1, capacity, 2, 2, planes, group_count * radial_rows)


HALF = 8
BLOCK = 64
PARTS = 3
LAST_PARTS = (2, 1)
VMEM_BYTES = 24 * 1024 * 1024


def flip3(value):
    return (value & 1) << 2 | value & 2 | value >> 2


def swap_span(value, distance):
    pairs = [(source, source ^ distance) for source in range(lax.axis_size("span"))]
    return lax.ppermute(value, "span", pairs)


def swap_rad(value):
    return lax.ppermute(value, "rad", [(0, 1), (1, 0)])


def split_pair(value):
    high = value.astype(jnp.bfloat16)
    low = (value - high.astype(jnp.float32)).astype(jnp.bfloat16)
    return high, low


def dot_rows(left, right):
    return lax.dot_general(left, right, contract_rows, preferred_element_type=jnp.float32)


def dot_split(left, right):
    left_high, left_low = left
    right_high, right_low = right
    total = dot_rows(left_high, right_high)
    total = total + dot_rows(left_low, right_high)
    return total + dot_rows(left_high, right_low)


def transform_8(real, imag):
    root = math.sqrt(0.5)
    er, ei, orr, oi = [], [], [], []
    for j in range(4):
        er.append(real[j] + real[j + 4])
        ei.append(imag[j] + imag[j + 4])
        dr = real[j] - real[j + 4]
        di = imag[j] - imag[j + 4]
        if j == 0:
            orr.append(dr)
            oi.append(di)
        elif j == 1:
            orr.append((dr + di) * root)
            oi.append((di - dr) * root)
        elif j == 2:
            orr.append(di)
            oi.append(-dr)
        else:
            orr.append((di - dr) * root)
            oi.append((-di - dr) * root)

    def transform_4(r, i):
        ar, ai = r[0] + r[2], i[0] + i[2]
        br, bi = r[0] - r[2], i[0] - i[2]
        cr, ci = r[1] + r[3], i[1] + i[3]
        dr, di = r[1] - r[3], i[1] - i[3]
        return [(ar + cr, ai + ci), (br + di, bi - dr), (ar - cr, ai - ci), (br - di, bi + dr)]

    even = transform_4(er, ei)
    odd = transform_4(orr, oi)
    return [even[q // 2] if q % 2 == 0 else odd[q // 2] for q in range(8)]


def half_sums_kernel(counts, place, *refs):
    cells, refs = refs[: len(counts)], refs[len(counts) :]
    cos_turn, sin_turn, table_rows = refs[:3]
    outs, (ordered, high, low) = refs[3:-3], refs[-3:]
    me, parity = place[0], place[1]
    sign = place[2].astype(jnp.float32)
    width = ordered.shape[-1]
    distance = 0
    for ref, count in zip(cells, counts):
        for index in range(count):
            ordered[me ^ distance] = ref[index]
            distance += 1

    turn_real, turn_imag = [], []
    for j in range(HALF):
        angle = 2.0 * math.pi * j / 16
        turn_real.append(sign * jnp.where(parity == 1, math.cos(angle), 1.0))
        turn_imag.append(sign * jnp.where(parity == 1, -math.sin(angle), 0.0))

    def one_block(step, carry):
        rows = pl.ds(pl.multiple_of(step * 16, 16), 16)
        lower = pl.ds(pl.multiple_of(BLOCK + step * 16, 16), 16)
        for lane in range(0, width, 128):
            real, imag = [], []
            for j in range(HALF):
                value = ordered[j, rows, lane : lane + 128]
                real.append(value * turn_real[j])
                imag.append(value * turn_imag[j])
            sums = transform_8(real, imag)
            for q in range(HALF):
                sum_real, sum_imag = sums[q]
                cosine = cos_turn[parity, q : q + 1, lane : lane + 128]
                sine = sin_turn[parity, q : q + 1, lane : lane + 128]
                real_high, real_low = split_pair(sum_real * cosine + sum_imag * sine)
                imag_high, imag_low = split_pair(sum_imag * cosine - sum_real * sine)
                high[q, rows, lane : lane + 128] = real_high
                high[q, rows, width + lane : width + lane + 128] = imag_high
                high[q, lower, lane : lane + 128] = imag_high
                high[q, lower, width + lane : width + lane + 128] = -real_high
                low[q, rows, lane : lane + 128] = real_low
                low[q, rows, width + lane : width + lane + 128] = imag_low
                low[q, lower, lane : lane + 128] = imag_low
                low[q, lower, width + lane : width + lane + 128] = -real_low
        return carry

    lax.fori_loop(0, BLOCK // 16, one_block, 0)
    table = split_pair(table_rows[...])
    for q in range(0, HALF, 2):
        lines_high = high[q : q + 2].reshape(4 * BLOCK, 2 * width)
        lines_low = low[q : q + 2].reshape(4 * BLOCK, 2 * width)
        result = dot_split(table, (lines_high, lines_low))
        first = 0
        for out in outs:
            rows = slice(first, first + out.shape[1])
            out[me ^ flip3(q)] = result[rows, : 2 * BLOCK]
            out[me ^ flip3(q + 1)] = result[rows, 2 * BLOCK :]
            first += out.shape[1]


def half_sums(place, cells, tables, parts):
    width = cells[0][0].shape[-1]
    rows = tables[2].shape[0]
    counts = [array.shape[0] if count is None else count for array, count, _ in cells]

    def full(array):
        return pl.BlockSpec(array.shape, lambda i: (0,) * array.ndim)

    def some(count, inner):
        return pl.BlockSpec((count, BLOCK, width), lambda i: (0, inner, 0))

    return pl.pallas_call(
        functools.partial(half_sums_kernel, counts),
        grid=(1,),
        out_shape=[
            jax.ShapeDtypeStruct((HALF, part, 2 * BLOCK), jnp.float32) for part in parts
        ],
        in_specs=[pl.BlockSpec(memory_space=pltpu.SMEM)]
        + [some(count, inner) for count, (_, _, inner) in zip(counts, cells)]
        + [full(table) for table in tables],
        out_specs=[
            pl.BlockSpec((HALF, part, 2 * BLOCK), lambda i: (0, 0, 0)) for part in parts
        ],
        scratch_shapes=[
            pltpu.VMEM((HALF, BLOCK, width), jnp.float32),
            pltpu.VMEM((HALF, 2 * BLOCK, 2 * width), jnp.bfloat16),
            pltpu.VMEM((HALF, 2 * BLOCK, 2 * width), jnp.bfloat16),
        ],
        cost_estimate=pl.CostEstimate(
            flops=rows * BLOCK * width,
            bytes_accessed=BLOCK * width * 4,
            transcendentals=0,
        ),
        compiler_params=pltpu.CompilerParams(vmem_limit_bytes=VMEM_BYTES),
        name="half_sums",
    )(place, *[array for array, _, _ in cells], *tables)


def gather_planes_kernel(place, *refs):
    own, from_z, out, ordered = refs[0], refs[1], refs[-2], refs[-1]
    me = place[0]
    ordered[me] = own[0]
    ordered[me ^ 4] = from_z[0]
    for distance in range(1, 4):
        for index in range(2):
            ordered[me ^ (distance + 4 * index)] = refs[1 + distance][index]
    for plane in range(HALF):
        out[:, plane, :] = ordered[plane]


def gather_planes(place, own, from_z, others):
    modes, lanes = own.shape[-2:]
    one = pl.BlockSpec((1, modes, lanes), lambda i: (0, 0, 0))
    two = pl.BlockSpec((2, modes, lanes), lambda i: (0, 0, 0))
    return pl.pallas_call(
        gather_planes_kernel,
        grid=(1,),
        out_shape=jax.ShapeDtypeStruct((modes, HALF, lanes), jnp.float32),
        in_specs=[pl.BlockSpec(memory_space=pltpu.SMEM), one, one, two, two, two],
        out_specs=pl.BlockSpec((modes, HALF, lanes), lambda i: (0, 0, 0)),
        scratch_shapes=[pltpu.VMEM((HALF, modes, lanes), jnp.float32)],
        cost_estimate=pl.CostEstimate(
            flops=0, bytes_accessed=8 * HALF * modes * lanes, transcendentals=0
        ),
        compiler_params=pltpu.CompilerParams(vmem_limit_bytes=VMEM_BYTES),
        name="gather_planes",
    )(place, own, from_z, *others)


def solve_kernel(count, place, *refs):
    blocks = refs[: 2 * count]
    inverse, vectors, factor = refs[2 * count : 2 * count + 3]
    out = refs[-1]
    modes = out.shape[0]
    radial = out.shape[-1]

    @pl.when(place[3] == 1)
    def _():
        inverse_pair = split_pair(inverse[0])
        vectors_pair = split_pair(vectors[0])
        scale = jnp.broadcast_to(factor[0][:, None, :], (modes, HALF, radial))
        scale = scale.reshape(modes * HALF, radial)
        whole = [block[...].reshape(modes * HALF, 2 * BLOCK) for block in blocks]
        for part in range(2):
            lanes = slice(part * BLOCK, (part + 1) * BLOCK)
            lines = jnp.concatenate([value[:, lanes] for value in whole], axis=1)
            inner = dot_split(split_pair(lines), inverse_pair) * scale
            solved = dot_split(split_pair(inner), vectors_pair)
            out[:, part, 0] = solved.reshape(modes, HALF, radial)

    @pl.when(place[3] != 1)
    def _():
        out[...] = jnp.zeros_like(out)


def solve(place, field, first, count, blocks, inverse, vectors, factor, earlier):
    modes = factor.shape[1]
    radial = inverse.shape[-1]
    step = modes // PARTS

    def lines(array):
        offset = first if array.shape[0] == modes else 0
        return pl.BlockSpec((step, HALF, 2 * BLOCK), lambda i: (offset + i, 0, 0))

    matrix = pl.BlockSpec((1, radial, radial), lambda i: (field, 0, 0))
    in_specs = [pl.BlockSpec(memory_space=pltpu.SMEM)] + [lines(block) for block in blocks]
    in_specs += [matrix, matrix]
    in_specs += [pl.BlockSpec((1, step, radial), lambda i: (field, first + i, 0))]
    operands = [place, *blocks, inverse, vectors, factor]
    aliases = {}
    if earlier is not None:
        aliases = {len(operands): 0}
        operands.append(earlier)
        in_specs.append(pl.BlockSpec(memory_space=pl.ANY))

    def kernel(*refs):
        kept = refs if earlier is None else refs[: len(operands) - 1] + refs[-1:]
        solve_kernel(len(blocks) // 2, *kept)

    return pl.pallas_call(
        kernel,
        grid=(count,),
        out_shape=jax.ShapeDtypeStruct((modes, 2, 2, HALF, radial), jnp.float32),
        in_specs=in_specs,
        out_specs=pl.BlockSpec(
            (step, 2, 1, HALF, radial), lambda i: (first + i, 0, field, 0, 0)
        ),
        input_output_aliases=aliases,
        cost_estimate=pl.CostEstimate(
            flops=count * modes * radial * radial,
            bytes_accessed=count * modes * radial,
            transcendentals=0,
        ),
        compiler_params=pltpu.CompilerParams(vmem_limit_bytes=VMEM_BYTES),
        name="solve",
    )(*operands)


def mode_tables(width, modes):
    cells = np.arange(width)
    residue = 2 * np.arange(HALF)[None, :, None] + np.arange(2)[:, None, None]
    turn = 2.0 * np.pi * residue * cells / (2 * HALF * width)
    padded = -(-modes // 16) * 16
    angle = 2.0 * np.pi * (np.arange(padded)[:, None] * cells[None, :] % width) / width
    table = np.concatenate([np.cos(angle), np.sin(angle)], axis=1)
    table = table / math.sqrt(2 * HALF * width)
    table[modes:] = 0.0
    return tuple(array.astype(np.float32) for array in (np.cos(turn), np.sin(turn), table))


def on_device_halves(fields, mode_group, half_step, decay, eigen_inverse, eigen_vectors):
    span = lax.axis_index("span")
    rad = lax.axis_index("rad")
    me = span & 7
    half = span >> 3
    rows = fields.shape[2]
    width = fields.shape[3]
    modes = KEEP // 16
    tables = mode_tables(width, modes)

    heavy = (mode_group[0, 0] == rad).astype(jnp.int32)
    one = jnp.ones_like(me)
    place_send = jnp.stack([me, 1 - half, one, heavy])
    place_keep = jnp.stack([me, half, 1 - 2 * half, heavy])

    mode_index = bit_reverse(span, 4) + 16 * jnp.arange(modes, dtype=jnp.int32)
    factor = damping_factor(half_step, decay, mode_index).transpose(1, 0, 2)
    own = lax.dynamic_slice_in_dim(eigen_inverse, rad * rows, rows, 2)
    other = lax.dynamic_slice_in_dim(eigen_inverse, (1 - rad) * rows, rows, 2)
    inverse = jnp.concatenate([own, other], axis=2)

    units = [(field, block) for field in range(2) for block in range(rows // BLOCK)]
    total = len(units)
    per_field = rows // BLOCK
    last = total - 1

    def plane_rows(field, start, count, distance):
        piece = lax.dynamic_slice(
            fields, (field, me ^ distance, start, 0), (1, 1, count, width)
        )
        return piece.reshape(count, width)

    def swap_core(field, start, count):
        paired = fields.reshape(2, 4, 2, rows, width)
        piece = lax.dynamic_slice(
            paired, (field, 0, 1 - (me & 1), start, 0), (1, 4, 1, count, width)
        )
        return swap_span(piece.reshape(4, count, width), 1)

    def core_rows(core, start, count, distance):
        plane = (me ^ distance) >> 1
        piece = lax.dynamic_slice(core, (plane, start, 0), (1, count, width))
        return piece.reshape(count, width)

    def away_direct(core, field, start, count):
        return [
            jnp.stack([plane_rows(field, start, count, d), core_rows(core, start, count, d)])
            for d in (2, 4, 6)
        ]

    def swap_direct(away):
        return [swap_span(value, distance) for value, distance in zip(away, (2, 4, 6))]

    def near_cells(core, field, start, core_start):
        mine = plane_rows(field, start, BLOCK, 0)
        return [(mine[None], 1, 0), (core_rows(core, core_start, BLOCK, 0)[None], 1, 0)]

    def away_x(core, inner, count):
        rows_of = (inner * BLOCK, count * BLOCK)
        away = []
        for distance in (2, 6):
            away.append(plane_rows(1, *rows_of, distance))
            away.append(core_rows(core, *rows_of, distance))
        return jnp.stack(away)

    def away_z(core, inner, from_x, place):
        rows_of = (inner * BLOCK, BLOCK)
        away = [plane_rows(1, *rows_of, 4)[None], core_rows(core, *rows_of, 4)[None]]
        away += [from_x[2:, place * BLOCK : (place + 1) * BLOCK]]
        return jnp.concatenate(away)

    def share(kept, came):
        return kept[:4] + came[:4], swap_span(kept[4:] + came[4:], 4)

    def swap_modes(near, from_z):
        return [
            swap_span(jnp.stack([near[distance], from_z[distance]]), distance)
            for distance in range(1, 4)
        ]

    def finish(near, from_z):
        return gather_planes(place_keep, near, from_z, swap_modes(near, from_z))

    def tie(*values):
        return lax.optimization_barrier(values)

    def sums(place, unit):
        step = modes // PARTS
        parts = [step * count for count in LAST_PARTS] if unit == last else [modes]
        return half_sums(place, cells[unit], tables, parts)

    cells = {}
    sent, kept, came, mine, other = {}, {}, {}, {}, {}
    def direct_unit(core, unit, arrays):
        start = units[unit][1] * BLOCK
        return near_cells(core, 0, start, start) + [(array, 2, 0) for array in arrays]

    core_a = swap_core(0, 0, rows)
    away = [away_direct(core_a, 0, n * BLOCK, BLOCK) for n in range(per_field)]
    direct = [swap_direct(away[0]), swap_direct(away[1])]
    core_c = swap_core(1, 0, rows)
    cells[0] = direct_unit(core_a, 0, direct[0])
    sent[0] = sums(place_send, 0)
    later_x = [away_x(core_c, 0, 2), away_x(core_c, 2, 1)]
    sent[0], direct[1], away[2], later_x, core_c, me = tie(
        sent[0], direct[1], away[2], later_x, core_c, me
    )
    cells[1] = direct_unit(core_a, 1, direct[1])
    matrices = (inverse, eigen_vectors, factor)
    from_x, swapped = [], {}
    result = None
    for step in range(last):
        came[step] = swap_span(sent[step][0], HALF)
        extra = {}
        if step == 0:
            kept[0] = sums(place_keep, 0)
            extra["direct"] = swap_direct(away[2])
            extra["z_parts"] = [
                plane_rows(1, 0, BLOCK, 4)[None], core_rows(core_c, 0, BLOCK, 4)[None]
            ]
            extra["near"] = [
                [cell[0] for cell in near_cells(core_c, 1, inner * BLOCK, inner * BLOCK)]
                for inner in range(per_field)
            ]
        if step < 2:
            extra["x"] = swap_span(later_x[step], 2)
        sent[step + 1] = sums(place_send, step + 1)
        kept[step + 1] = sums(place_keep, step + 1)
        if 1 <= step <= 3:
            unit = step + 2
            inner = unit - per_field
            source, place = (from_x[0], inner) if inner < 2 else (from_x[1], 0)
            if inner == 0:
                next_z = jnp.concatenate(z_parts + [source[2:, :BLOCK]])
            extra["z"] = swap_span(next_z, 4)
            if inner < 2:
                following = (from_x[0], 1) if inner == 0 else (from_x[1], 0)
                extra["away"] = away_z(core_c, inner + 1, *following)
            cells[unit] = [(array, 1, 0) for array in near[inner]]
            cells[unit] += [(source, 2, place)]
        if step >= 1:
            extra["swapped"] = share(kept[step - 1][0], came[step - 1])
        if step == last - 1:
            swapped[step - 2], extra["swapped"], sent[last], kept[last] = tie(
                swapped[step - 2], extra["swapped"], sent[last], kept[last]
            )
        if step >= 2:
            extra["mine"] = finish(*swapped[step - 2])
        if step == last - 1:
            extra["other"] = [swap_rad(mine[unit]) for unit in range(last - 3)]
        came[step], sent[step + 1], kept[step + 1], extra, me = tie(
            came[step], sent[step + 1], kept[step + 1], extra, me
        )
        if "direct" in extra:
            cells[2] = direct_unit(core_a, 2, extra["direct"])
            near, z_parts = extra["near"], extra["z_parts"]
        if "away" in extra:
            next_z = extra["away"]
        if "x" in extra:
            from_x.append(extra["x"])
        if "z" in extra:
            cells[step + 2].append((extra["z"], 4, 0))
        if step >= 1:
            swapped[step - 1] = extra["swapped"]
        if step >= 2:
            mine[step - 2] = extra["mine"]
        if step == last - 1:
            other.update(enumerate(extra["other"]))

    def blocks_of(numbers, part=None):
        chosen = [mine[n] if n != last else mine[n][part] for n in numbers]
        return chosen + [other[n] if n != last else other[n][part] for n in numbers]

    came[last] = [swap_span(part, HALF) for part in sent[last]]
    other[last - 3] = swap_rad(mine[last - 3])
    swapped[last - 1] = share(kept[last - 1][0], came[last - 1])
    mine[last - 2] = finish(*swapped[last - 2])
    other[last - 2] = swap_rad(mine[last - 2])
    blocks = blocks_of(range(per_field))
    result = solve(place_keep, 0, 0, 1, blocks, *matrices, None)
    came[last][0], swapped[last - 1], result = tie(
        came[last][0], swapped[last - 1], result
    )
    mine[last - 1] = finish(*swapped[last - 1])
    ready = share(kept[last][0], came[last][0])
    other[last - 1] = swap_rad(mine[last - 1])
    ready, mine[last - 1], other[last - 2] = tie(ready, mine[last - 1], other[last - 2])
    first = finish(*ready)
    first, came[last][1] = tie(first, came[last][1])
    other_first = swap_rad(first)
    ready = share(kept[last][1], came[last][1])
    result = solve(place_keep, 0, 1, 2, blocks, *matrices, result)
    others, result, other[last - 1] = tie(swap_modes(*ready), result, other[last - 1])
    second = gather_planes(place_keep, *ready, others)
    mine[last] = [first, second]
    other[last] = [other_first, swap_rad(second)]
    start = 0
    for part, count in enumerate(LAST_PARTS):
        blocks = blocks_of(range(per_field, total), part)
        result = solve(place_keep, 1, start, count, blocks, *matrices, result)
        start += count
    return result[None, None]


def solution(mesh):
    placed = (P(None, None, "rad", "span"), P(None, "span"), P(), P(), P(), P())
    halves = mesh.shape["span"] == 2 * HALF and mesh.shape["rad"] == 2
    return jax.shard_map(
        on_device_halves if halves else on_device_any,
        mesh=mesh,
        in_specs=placed,
        out_specs=P("span", "rad", None, None, None, None, None),
        check_vma=False,
    )
```

```python
import functools
import math

import jax
import jax.numpy as jnp
import numpy as np
from jax import lax
from jax.experimental import pallas as pl
from jax.experimental.pallas import tpu as pltpu
from jax.sharding import PartitionSpec as P

KEEP = 2688


precise = lax.Precision.HIGHEST
contract_rows = (((1,), (1,)), ((), ()))


def partner_2(value, axis, distance):
    mask = 2**distance
    pairs = [(source, source ^ mask) for source in range(lax.axis_size(axis))]
    return lax.ppermute(value, axis, pairs)


def bit_reverse(value, bit_count):
    flipped = jnp.zeros_like(value)
    for section_bit in range(bit_count):
        flipped = flipped + (value >> section_bit & 1) * 2 ** (bit_count - 1 - section_bit)
    return flipped


def section_angles(device, section_bit):
    upper_half = device >> section_bit & 1 == 1
    twiddle_index = jnp.where(upper_half, device % 2**section_bit, 0)
    angles = twiddle_index.astype(jnp.float32) * (2.0 * math.pi / 2 ** (section_bit + 1))
    sign_factor = jnp.where(upper_half, -1.0, 1.0).astype(jnp.float32)
    return (sign_factor, jnp.cos(angles), jnp.sin(angles))


def butterfly(fields, bit_count):
    device = lax.axis_index("span")
    top_bit = bit_count - 1
    partner = partner_2(fields, "span", top_bit)
    sign_factor, cosine, sine_value = section_angles(device, top_bit)
    difference = partner + sign_factor * fields
    real_part = difference * cosine
    imag_part = -difference * sine_value
    for section_bit in range(bit_count - 2, -1, -1):
        other_real, other_imag = partner_2((real_part, imag_part), "span", section_bit)
        sign_factor, cosine, sine_value = section_angles(device, section_bit)
        diff_real = other_real + sign_factor * real_part
        diff_imag = other_imag + sign_factor * imag_part
        real_part = diff_real * cosine + diff_imag * sine_value
        imag_part = diff_imag * cosine - diff_real * sine_value
    return (real_part, imag_part)


def mode_transform(real_part, imag_part, bit_count):
    groups = lax.axis_size("span")
    line_width = real_part.shape[3]
    full_length = line_width * groups
    kept_modes = KEEP // groups
    residue = bit_reverse(lax.axis_index("span"), bit_count)
    mode_index = residue + groups * jnp.arange(kept_modes, dtype=jnp.int32)
    phases = mode_index[:, None] * jnp.arange(line_width, dtype=jnp.int32)[None, :] % full_length
    angles = phases.astype(jnp.float32) * (2.0 * math.pi / full_length)
    normalizer = 1.0 / math.sqrt(full_length)
    cosine_table = jnp.cos(angles) * normalizer
    sine_table = jnp.sin(angles) * normalizer
    line_real = real_part.reshape(-1, line_width)
    line_imag = imag_part.reshape(-1, line_width)
    cos_real = lax.dot_general(cosine_table, line_real, contract_rows, precision=precise)
    cos_imag = lax.dot_general(cosine_table, line_imag, contract_rows, precision=precise)
    sin_real = lax.dot_general(sine_table, line_real, contract_rows, precision=precise)
    sin_imag = lax.dot_general(sine_table, line_imag, contract_rows, precision=precise)
    return (jnp.stack([cos_real + sin_imag, cos_imag - sin_real]), mode_index)


def placement_table(column, group_count, capacity):
    groups = jnp.arange(group_count, dtype=jnp.int32)
    member = (column[None, :] == groups[:, None]).astype(jnp.int32)
    ranking = jnp.cumsum(member, axis=1, dtype=jnp.int32) - member
    slot_index = jnp.arange(capacity, dtype=jnp.int32)
    return member[None] * (ranking[None] == slot_index[:, None, None])


def damping_factor(half_step, decay, wave_index):
    wave_square = (wave_index.astype(jnp.float32) * (math.pi / KEEP)) ** 2
    damping = half_step[None, :, None] * (decay[None, :, :] + wave_square[:, None, None])
    return (1.0 - damping) / (1.0 + damping)


def on_device_any(fields, mode_group, half_step, decay, eigen_inverse, eigen_vectors):
    bit_count = lax.axis_size("span").bit_length() - 1
    real_part, imag_part = butterfly(fields, bit_count)
    spectra, mode_index = mode_transform(real_part, imag_part, bit_count)
    kept_modes = spectra.shape[1]
    group_count = lax.axis_size("rad")
    capacity = min(kept_modes, 2 * kept_modes // group_count)
    planes = fields.shape[1]
    radial_rows = fields.shape[2]
    arranged = spectra.reshape(2, kept_modes, 2, planes, radial_rows)
    placing = placement_table(mode_group[:, 0], group_count, capacity)
    placing_float = placing.astype(jnp.float32)
    packed = jnp.einsum("sgb,cbfal->scfagl", placing_float, arranged, precision=precise)
    packed = packed.reshape(capacity, 2, 2, planes, group_count * radial_rows)
    regrouped = lax.all_to_all(packed, "rad", split_axis=4, concat_axis=4, tiled=True)
    own_slots = lax.dynamic_index_in_dim(placing, lax.axis_index("rad"), 1, keepdims=False)
    slot_modes = jnp.sum(own_slots * mode_index[None, :], axis=1)
    factor = damping_factor(half_step, decay, slot_modes)
    inner_part = jnp.einsum("scfar,fir->scfai", regrouped, eigen_inverse, precision=precise)
    inner_part = inner_part * factor[:, None, :, None, :]
    result = jnp.einsum("scfai,fri->scfar", inner_part, eigen_vectors, precision=precise)
    return result.reshape(1, 1, capacity, 2, 2, planes, group_count * radial_rows)


HALF = 8
BLOCK = 64
PARTS = 3
LAST_PARTS = (2, 1)
VMEM_BYTES = 36 * 1024 * 1024


def flip3(value):
    return (value & 1) << 2 | value & 2 | value >> 2


def swap_span(value, distance):
    pairs = [(source, source ^ distance) for source in range(lax.axis_size("span"))]
    return lax.ppermute(value, "span", pairs)


def swap_rad(value):
    return lax.ppermute(value, "rad", [(0, 1), (1, 0)])


def split_pair(value):
    high = value.astype(jnp.bfloat16)
    low = (value - high.astype(jnp.float32)).astype(jnp.bfloat16)
    return high, low


def dot_rows(left, right):
    return lax.dot_general(left, right, contract_rows, preferred_element_type=jnp.float32)


def dot_split(left, right):
    left_high, left_low = left
    right_high, right_low = right
    total = dot_rows(left_high, right_high)
    total = total + dot_rows(left_low, right_high)
    return total + dot_rows(left_high, right_low)


def transform_8(real, imag):
    root = math.sqrt(0.5)
    er, ei, orr, oi = [], [], [], []
    for j in range(4):
        er.append(real[j] + real[j + 4])
        ei.append(imag[j] + imag[j + 4])
        dr = real[j] - real[j + 4]
        di = imag[j] - imag[j + 4]
        if j == 0:
            orr.append(dr)
            oi.append(di)
        elif j == 1:
            orr.append((dr + di) * root)
            oi.append((di - dr) * root)
        elif j == 2:
            orr.append(di)
            oi.append(-dr)
        else:
            orr.append((di - dr) * root)
            oi.append((-di - dr) * root)

    def transform_4(r, i):
        ar, ai = r[0] + r[2], i[0] + i[2]
        br, bi = r[0] - r[2], i[0] - i[2]
        cr, ci = r[1] + r[3], i[1] + i[3]
        dr, di = r[1] - r[3], i[1] - i[3]
        return [(ar + cr, ai + ci), (br + di, bi - dr), (ar - cr, ai - ci), (br - di, bi + dr)]

    even = transform_4(er, ei)
    odd = transform_4(orr, oi)
    return [even[q // 2] if q % 2 == 0 else odd[q // 2] for q in range(8)]


def half_sums_kernel(counts, place, *refs):
    cells, refs = refs[: len(counts)], refs[len(counts) :]
    cos_turn, sin_turn, table_rows = refs[:3]
    outs, (ordered, high, low) = refs[3:-3], refs[-3:]
    me, parity = place[0], place[1]
    sign = place[2].astype(jnp.float32)
    width = ordered.shape[-1]
    distance = 0
    for ref, count in zip(cells, counts):
        for index in range(count):
            ordered[me ^ distance] = ref[index]
            distance += 1

    turn_real, turn_imag = [], []
    for j in range(HALF):
        angle = 2.0 * math.pi * j / 16
        turn_real.append(sign * jnp.where(parity == 1, math.cos(angle), 1.0))
        turn_imag.append(sign * jnp.where(parity == 1, -math.sin(angle), 0.0))

    def one_block(step, carry):
        rows = pl.ds(pl.multiple_of(step * 16, 16), 16)
        lower = pl.ds(pl.multiple_of(BLOCK + step * 16, 16), 16)
        for lane in range(0, width, 128):
            real, imag = [], []
            for j in range(HALF):
                value = ordered[j, rows, lane : lane + 128]
                real.append(value * turn_real[j])
                imag.append(value * turn_imag[j])
            sums = transform_8(real, imag)
            for q in range(HALF):
                sum_real, sum_imag = sums[q]
                cosine = cos_turn[parity, q : q + 1, lane : lane + 128]
                sine = sin_turn[parity, q : q + 1, lane : lane + 128]
                real_high, real_low = split_pair(sum_real * cosine + sum_imag * sine)
                imag_high, imag_low = split_pair(sum_imag * cosine - sum_real * sine)
                high[q, rows, lane : lane + 128] = real_high
                high[q, rows, width + lane : width + lane + 128] = imag_high
                high[q, lower, lane : lane + 128] = imag_high
                high[q, lower, width + lane : width + lane + 128] = -real_high
                low[q, rows, lane : lane + 128] = real_low
                low[q, rows, width + lane : width + lane + 128] = imag_low
                low[q, lower, lane : lane + 128] = imag_low
                low[q, lower, width + lane : width + lane + 128] = -real_low
        return carry

    lax.fori_loop(0, BLOCK // 16, one_block, 0)
    table = split_pair(table_rows[...])
    for q in range(0, HALF, 2):
        lines_high = high[q : q + 2].reshape(4 * BLOCK, 2 * width)
        lines_low = low[q : q + 2].reshape(4 * BLOCK, 2 * width)
        result = dot_split(table, (lines_high, lines_low))
        first = 0
        for out in outs:
            rows = slice(first, first + out.shape[1])
            out[me ^ flip3(q)] = result[rows, : 2 * BLOCK]
            out[me ^ flip3(q + 1)] = result[rows, 2 * BLOCK :]
            first += out.shape[1]


def half_sums(place, cells, tables, parts):
    width = cells[0][0].shape[-1]
    rows = tables[2].shape[0]
    counts = [array.shape[0] if count is None else count for array, count, _ in cells]

    def full(array):
        return pl.BlockSpec(array.shape, lambda i: (0,) * array.ndim)

    def some(count, inner):
        return pl.BlockSpec((count, BLOCK, width), lambda i: (0, inner, 0))

    return pl.pallas_call(
        functools.partial(half_sums_kernel, counts),
        grid=(1,),
        out_shape=[
            jax.ShapeDtypeStruct((HALF, part, 2 * BLOCK), jnp.float32) for part in parts
        ],
        in_specs=[pl.BlockSpec(memory_space=pltpu.SMEM)]
        + [some(count, inner) for count, (_, _, inner) in zip(counts, cells)]
        + [full(table) for table in tables],
        out_specs=[
            pl.BlockSpec((HALF, part, 2 * BLOCK), lambda i: (0, 0, 0)) for part in parts
        ],
        scratch_shapes=[
            pltpu.VMEM((HALF, BLOCK, width), jnp.float32),
            pltpu.VMEM((HALF, 2 * BLOCK, 2 * width), jnp.bfloat16),
            pltpu.VMEM((HALF, 2 * BLOCK, 2 * width), jnp.bfloat16),
        ],
        cost_estimate=pl.CostEstimate(
            flops=rows * BLOCK * width,
            bytes_accessed=BLOCK * width * 4,
            transcendentals=0,
        ),
        compiler_params=pltpu.CompilerParams(vmem_limit_bytes=VMEM_BYTES),
        name="half_sums",
    )(place, *[array for array, _, _ in cells], *tables)


def gather_planes_kernel(place, *refs):
    own, from_z, out, ordered = refs[0], refs[1], refs[-2], refs[-1]
    me = place[0]
    ordered[me] = own[0]
    ordered[me ^ 4] = from_z[0]
    for distance in range(1, 4):
        for index in range(2):
            ordered[me ^ (distance + 4 * index)] = refs[1 + distance][index]
    for plane in range(HALF):
        out[:, plane, :] = ordered[plane]


def gather_planes(place, own, from_z, others):
    modes, lanes = own.shape[-2:]
    one = pl.BlockSpec((1, modes, lanes), lambda i: (0, 0, 0))
    two = pl.BlockSpec((2, modes, lanes), lambda i: (0, 0, 0))
    return pl.pallas_call(
        gather_planes_kernel,
        grid=(1,),
        out_shape=jax.ShapeDtypeStruct((modes, HALF, lanes), jnp.float32),
        in_specs=[pl.BlockSpec(memory_space=pltpu.SMEM), one, one, two, two, two],
        out_specs=pl.BlockSpec((modes, HALF, lanes), lambda i: (0, 0, 0)),
        scratch_shapes=[pltpu.VMEM((HALF, modes, lanes), jnp.float32)],
        cost_estimate=pl.CostEstimate(
            flops=0, bytes_accessed=8 * HALF * modes * lanes, transcendentals=0
        ),
        compiler_params=pltpu.CompilerParams(vmem_limit_bytes=VMEM_BYTES),
        name="gather_planes",
    )(place, own, from_z, *others)


def solve_kernel(count, place, *refs):
    blocks = refs[: 2 * count]
    inverse, vectors, factor = refs[2 * count : 2 * count + 3]
    out = refs[-1]
    modes = out.shape[0]
    radial = out.shape[-1]

    @pl.when(place[3] == 1)
    def _():
        inverse_pair = split_pair(inverse[0])
        vectors_pair = split_pair(vectors[0])
        scale = jnp.broadcast_to(factor[0][:, None, :], (modes, HALF, radial))
        scale = scale.reshape(modes * HALF, radial)
        whole = [block[...].reshape(modes * HALF, 2 * BLOCK) for block in blocks]
        for part in range(2):
            lanes = slice(part * BLOCK, (part + 1) * BLOCK)
            lines = jnp.concatenate([value[:, lanes] for value in whole], axis=1)
            inner = dot_split(split_pair(lines), inverse_pair) * scale
            solved = dot_split(split_pair(inner), vectors_pair)
            out[:, part, 0] = solved.reshape(modes, HALF, radial)

    @pl.when(place[3] != 1)
    def _():
        out[...] = jnp.zeros_like(out)


def solve(place, field, first, count, blocks, inverse, vectors, factor, earlier):
    modes = factor.shape[1]
    radial = inverse.shape[-1]
    step = modes // PARTS

    def lines(array):
        offset = first if array.shape[0] == modes else 0
        return pl.BlockSpec((step, HALF, 2 * BLOCK), lambda i: (offset + i, 0, 0))

    matrix = pl.BlockSpec((1, radial, radial), lambda i: (field, 0, 0))
    in_specs = [pl.BlockSpec(memory_space=pltpu.SMEM)] + [lines(block) for block in blocks]
    in_specs += [matrix, matrix]
    in_specs += [pl.BlockSpec((1, step, radial), lambda i: (field, first + i, 0))]
    operands = [place, *blocks, inverse, vectors, factor]
    aliases = {}
    if earlier is not None:
        aliases = {len(operands): 0}
        operands.append(earlier)
        in_specs.append(pl.BlockSpec(memory_space=pl.ANY))

    def kernel(*refs):
        kept = refs if earlier is None else refs[: len(operands) - 1] + refs[-1:]
        solve_kernel(len(blocks) // 2, *kept)

    return pl.pallas_call(
        kernel,
        grid=(count,),
        out_shape=jax.ShapeDtypeStruct((modes, 2, 2, HALF, radial), jnp.float32),
        in_specs=in_specs,
        out_specs=pl.BlockSpec(
            (step, 2, 1, HALF, radial), lambda i: (first + i, 0, field, 0, 0)
        ),
        input_output_aliases=aliases,
        cost_estimate=pl.CostEstimate(
            flops=count * modes * radial * radial,
            bytes_accessed=count * modes * radial,
            transcendentals=0,
        ),
        compiler_params=pltpu.CompilerParams(vmem_limit_bytes=VMEM_BYTES),
        name="solve",
    )(*operands)


def mode_tables(width, modes):
    cells = np.arange(width)
    residue = 2 * np.arange(HALF)[None, :, None] + np.arange(2)[:, None, None]
    turn = 2.0 * np.pi * residue * cells / (2 * HALF * width)
    padded = -(-modes // 16) * 16
    angle = 2.0 * np.pi * (np.arange(padded)[:, None] * cells[None, :] % width) / width
    table = np.concatenate([np.cos(angle), np.sin(angle)], axis=1)
    table = table / math.sqrt(2 * HALF * width)
    table[modes:] = 0.0
    return tuple(array.astype(np.float32) for array in (np.cos(turn), np.sin(turn), table))


def on_device_halves(fields, mode_group, half_step, decay, eigen_inverse, eigen_vectors):
    span = lax.axis_index("span")
    rad = lax.axis_index("rad")
    me = span & 7
    half = span >> 3
    rows = fields.shape[2]
    width = fields.shape[3]
    modes = KEEP // 16
    tables = mode_tables(width, modes)

    heavy = (mode_group[0, 0] == rad).astype(jnp.int32)
    one = jnp.ones_like(me)
    place_send = jnp.stack([me, 1 - half, one, heavy])
    place_keep = jnp.stack([me, half, 1 - 2 * half, heavy])

    mode_index = bit_reverse(span, 4) + 16 * jnp.arange(modes, dtype=jnp.int32)
    factor = damping_factor(half_step, decay, mode_index).transpose(1, 0, 2)
    own = lax.dynamic_slice_in_dim(eigen_inverse, rad * rows, rows, 2)
    other = lax.dynamic_slice_in_dim(eigen_inverse, (1 - rad) * rows, rows, 2)
    inverse = jnp.concatenate([own, other], axis=2)

    units = [(field, block) for field in range(2) for block in range(rows // BLOCK)]
    total = len(units)
    per_field = rows // BLOCK
    last = total - 1

    def plane_rows(field, start, count, distance):
        piece = lax.dynamic_slice(
            fields, (field, me ^ distance, start, 0), (1, 1, count, width)
        )
        return piece.reshape(count, width)

    def swap_core(field, start, count):
        paired = fields.reshape(2, 4, 2, rows, width)
        piece = lax.dynamic_slice(
            paired, (field, 0, 1 - (me & 1), start, 0), (1, 4, 1, count, width)
        )
        return swap_span(piece.reshape(4, count, width), 1)

    def core_rows(core, start, count, distance):
        plane = (me ^ distance) >> 1
        piece = lax.dynamic_slice(core, (plane, start, 0), (1, count, width))
        return piece.reshape(count, width)

    def away_direct(core, field, start, count):
        return [
            jnp.stack([plane_rows(field, start, count, d), core_rows(core, start, count, d)])
            for d in (2, 4, 6)
        ]

    def swap_direct(away):
        return [swap_span(value, distance) for value, distance in zip(away, (2, 4, 6))]

    def near_cells(core, field, start, core_start):
        mine = plane_rows(field, start, BLOCK, 0)
        return [(mine[None], 1, 0), (core_rows(core, core_start, BLOCK, 0)[None], 1, 0)]

    def away_x(core, inner, count):
        rows_of = (inner * BLOCK, count * BLOCK)
        away = []
        for distance in (2, 6):
            away.append(plane_rows(1, *rows_of, distance))
            away.append(core_rows(core, *rows_of, distance))
        return jnp.stack(away)

    def away_z(core, inner, from_x, place):
        rows_of = (inner * BLOCK, BLOCK)
        away = [plane_rows(1, *rows_of, 4)[None], core_rows(core, *rows_of, 4)[None]]
        away += [from_x[2:, place * BLOCK : (place + 1) * BLOCK]]
        return jnp.concatenate(away)

    def share(kept, came):
        return kept[:4] + came[:4], swap_span(kept[4:] + came[4:], 4)

    def swap_modes(near, from_z):
        return [
            swap_span(jnp.stack([near[distance], from_z[distance]]), distance)
            for distance in range(1, 4)
        ]

    def finish(near, from_z):
        return gather_planes(place_keep, near, from_z, swap_modes(near, from_z))

    def tie(*values):
        return lax.optimization_barrier(values)

    def sums(place, unit):
        step = modes // PARTS
        parts = [step * count for count in LAST_PARTS] if unit == last else [modes]
        return half_sums(place, cells[unit], tables, parts)

    cells = {}
    sent, kept, came, mine, other = {}, {}, {}, {}, {}
    def direct_unit(core, unit, arrays):
        start = units[unit][1] * BLOCK
        return near_cells(core, 0, start, start) + [(array, 2, 0) for array in arrays]

    core_a = swap_core(0, 0, rows)
    away = [away_direct(core_a, 0, n * BLOCK, BLOCK) for n in range(per_field)]
    direct = [swap_direct(away[0]), swap_direct(away[1])]
    core_c = swap_core(1, 0, rows)
    cells[0] = direct_unit(core_a, 0, direct[0])
    sent[0] = sums(place_send, 0)
    later_x = [away_x(core_c, 0, 2), away_x(core_c, 2, 1)]
    sent[0], direct[1], away[2], later_x, core_c, me = tie(
        sent[0], direct[1], away[2], later_x, core_c, me
    )
    cells[1] = direct_unit(core_a, 1, direct[1])
    matrices = (inverse, eigen_vectors, factor)
    from_x, swapped = [], {}
    result = None
    for step in range(last):
        came[step] = swap_span(sent[step][0], HALF)
        extra = {}
        if step == 0:
            kept[0] = sums(place_keep, 0)
            extra["direct"] = swap_direct(away[2])
            extra["z_parts"] = [
                plane_rows(1, 0, BLOCK, 4)[None], core_rows(core_c, 0, BLOCK, 4)[None]
            ]
            extra["near"] = [
                [cell[0] for cell in near_cells(core_c, 1, inner * BLOCK, inner * BLOCK)]
                for inner in range(per_field)
            ]
        if step < 2:
            extra["x"] = swap_span(later_x[step], 2)
        sent[step + 1] = sums(place_send, step + 1)
        kept[step + 1] = sums(place_keep, step + 1)
        if 1 <= step <= 3:
            unit = step + 2
            inner = unit - per_field
            source, place = (from_x[0], inner) if inner < 2 else (from_x[1], 0)
            if inner == 0:
                next_z = jnp.concatenate(z_parts + [source[2:, :BLOCK]])
            extra["z"] = swap_span(next_z, 4)
            if inner < 2:
                following = (from_x[0], 1) if inner == 0 else (from_x[1], 0)
                extra["away"] = away_z(core_c, inner + 1, *following)
            cells[unit] = [(array, 1, 0) for array in near[inner]]
            cells[unit] += [(source, 2, place)]
        if step >= 1:
            extra["swapped"] = share(kept[step - 1][0], came[step - 1])
        if step == last - 1:
            swapped[step - 2], extra["swapped"], sent[last], kept[last] = tie(
                swapped[step - 2], extra["swapped"], sent[last], kept[last]
            )
        if step >= 2:
            extra["mine"] = finish(*swapped[step - 2])
        if step == last - 1:
            extra["other"] = [swap_rad(mine[unit]) for unit in range(last - 3)]
        came[step], sent[step + 1], kept[step + 1], extra, me = tie(
            came[step], sent[step + 1], kept[step + 1], extra, me
        )
        if "direct" in extra:
            cells[2] = direct_unit(core_a, 2, extra["direct"])
            near, z_parts = extra["near"], extra["z_parts"]
        if "away" in extra:
            next_z = extra["away"]
        if "x" in extra:
            from_x.append(extra["x"])
        if "z" in extra:
            cells[step + 2].append((extra["z"], 4, 0))
        if step >= 1:
            swapped[step - 1] = extra["swapped"]
        if step >= 2:
            mine[step - 2] = extra["mine"]
        if step == last - 1:
            other.update(enumerate(extra["other"]))

    def blocks_of(numbers, part=None):
        chosen = [mine[n] if n != last else mine[n][part] for n in numbers]
        return chosen + [other[n] if n != last else other[n][part] for n in numbers]

    came[last] = [swap_span(part, HALF) for part in sent[last]]
    other[last - 3] = swap_rad(mine[last - 3])
    swapped[last - 1] = share(kept[last - 1][0], came[last - 1])
    mine[last - 2] = finish(*swapped[last - 2])
    other[last - 2] = swap_rad(mine[last - 2])
    blocks = blocks_of(range(per_field))
    result = solve(place_keep, 0, 0, 1, blocks, *matrices, None)
    came[last][0], swapped[last - 1], result = tie(
        came[last][0], swapped[last - 1], result
    )
    mine[last - 1] = finish(*swapped[last - 1])
    ready = share(kept[last][0], came[last][0])
    other[last - 1] = swap_rad(mine[last - 1])
    ready, mine[last - 1], other[last - 2] = tie(ready, mine[last - 1], other[last - 2])
    first = finish(*ready)
    first, came[last][1] = tie(first, came[last][1])
    other_first = swap_rad(first)
    ready = share(kept[last][1], came[last][1])
    result = solve(place_keep, 0, 1, 2, blocks, *matrices, result)
    others, result, other[last - 1] = tie(swap_modes(*ready), result, other[last - 1])
    second = gather_planes(place_keep, *ready, others)
    mine[last] = [first, second]
    other[last] = [other_first, swap_rad(second)]
    start = 0
    for part, count in enumerate(LAST_PARTS):
        blocks = blocks_of(range(per_field, total), part)
        result = solve(place_keep, 1, start, count, blocks, *matrices, result)
        start += count
    return result[None, None]


def solution(mesh):
    placed = (P(None, None, "rad", "span"), P(None, "span"), P(), P(), P(), P())
    halves = mesh.shape["span"] == 2 * HALF and mesh.shape["rad"] == 2
    return jax.shard_map(
        on_device_halves if halves else on_device_any,
        mesh=mesh,
        in_specs=placed,
        out_specs=P("span", "rad", None, None, None, None, None),
        check_vma=False,
    )
```
